32 devices in a mesh: samp: 16 (over z, y, x), blk: 2 (over core).
Axes of the slice: x: 2, y: 2, z: 4, core: 2. Of those that a mesh axis runs over, the one named last changes fastest.
Arguments:
- tokens: bfloat16 [96, 800, 384], P('samp', 'blk')
- view_count: int32 [96], P('samp'), may hold values from 1 to 4, as said below
- norm1_gain: bfloat16 [384], replicated, may hold values from 0.5 to 1.5
- norm1_bias: bfloat16 [384], replicated, may hold values from -0.59765625 to 0.59765625
- w_qkv: bfloat16 [384, 1152], replicated, may hold values from -0.3125 to 0.3125
- qv_bias: bfloat16 [768], replicated, may hold values from -1.1953125 to 1.1953125
- w_out: bfloat16 [384, 384], replicated, may hold values from -3.5 to 3.5
- out_bias: bfloat16 [384], replicated, may hold values from -0.59765625 to 0.59765625
- norm2_gain: bfloat16 [384], replicated, may hold values from 0.5 to 1.5
- norm2_bias: bfloat16 [384], replicated, may hold values from -0.59765625 to 0.59765625
- w_fc1: bfloat16 [384, 1536], replicated, may hold values from -0.3125 to 0.3125
- fc1_bias: bfloat16 [1536], replicated, may hold values from -1.796875 to 1.796875
- w_fc2: bfloat16 [1536, 384], replicated, may hold values from -0.15625 to 0.15625
- fc2_bias: bfloat16 [384], replicated, may hold values from -0.59765625 to 0.59765625
- cot_tokens: bfloat16 [96, 800, 384], P('samp', 'blk'), may hold values from -6 to 6
- cot_cls: bfloat16 [96, 384], P(('samp', 'blk'))
Outputs:
- tokens_out: bfloat16 [96, 800, 384], P('samp', 'blk')
- cls_norm: bfloat16 [96, 384], P(('samp', 'blk'))
- grad_tokens: bfloat16 [96, 800, 384], P('samp', 'blk')
- grad_norm1_gain: float32 [384], replicated
- grad_norm1_bias: float32 [384], replicated
- grad_w_qkv: float32 [384, 1152], replicated
- grad_qv_bias: float32 [768], replicated
- grad_w_out: float32 [384, 384], replicated
- grad_out_bias: float32 [384], replicated
- grad_norm2_gain: float32 [384], replicated
- grad_norm2_bias: float32 [384], replicated
- grad_w_fc1: float32 [384, 1536], replicated
- grad_fc1_bias: float32 [1536], replicated
- grad_w_fc2: float32 [1536, 384], replicated
- grad_fc2_bias: float32 [384], replicated
The draws below stay inside these ranges and needn't reach their ends.
Inputs may be any that keep to these rules, and one draw needn't show every extreme that they name: `view_count`: each index of samp holds 6 samples in a row, and one of them has 4 views.
All inputs are finite; a program needn't handle non-finite values.
Results may differ from the reference program's by a relative error of at most 0.0096.
Values may be sent and summed in bfloat16 or wider, within the bound.
No kernel may reach another device: no remote copies, remote signals or barrier semaphores. Data moves between devices by JAX's collectives and lax.ppermute only.
A program may use at most 320 MiB of HBM per device.

```python
import jax
import jax.numpy as jnp
from jax import lax

D = 384
HEADS = 6
HEAD_DIM = 64
FF = 1536
VIEW_ROWS = 196
ROWS = 800
SAMP_DEV = 6
SAMPLES = 96


def draw_tokens(key, part):
    key = jax.random.fold_in(key, 11)
    noise_key, offset_key = jax.random.split(key)
    place = jnp.arange(SAMPLES, dtype=jnp.float32) / max(SAMPLES - 1, 1)
    noise = jax.random.normal(noise_key, (SAMPLES, ROWS, D), jnp.float32)
    offset = jax.random.normal(offset_key, (D,), jnp.float32)
    rising = 1.0 + 2.0 * place
    first_row = (jnp.arange(ROWS) == 0).astype(jnp.float32)
    values = rising[:, None, None] * (noise + first_row[None, :, None] * offset[None, None, :])
    return values.astype(jnp.bfloat16)


def draw_view_count(key, part):
    key = jax.random.fold_in(key, 23)
    tail_key, pick_key = jax.random.split(key)
    levels = jax.random.randint(tail_key, (SAMPLES,), 0, 16)
    counts = 1 + (levels >= 8).astype(jnp.int32) + (levels >= 12).astype(jnp.int32) + (levels >= 14).astype(jnp.int32)
    picked = jax.random.randint(pick_key, (SAMPLES // SAMP_DEV,), 0, SAMP_DEV)
    forced = jnp.arange(SAMPLES) % SAMP_DEV == jnp.repeat(picked, SAMP_DEV)
    return jnp.where(forced, 4, counts).astype(jnp.int32)


def draw_cot_cls(key, part):
    key = jax.random.fold_in(key, 37)
    noise_key, offset_key = jax.random.split(key)
    place = jnp.arange(SAMPLES, dtype=jnp.float32) / max(SAMPLES - 1, 1)
    noise = jax.random.normal(noise_key, (SAMPLES, D), jnp.float32)
    offset = jax.random.normal(offset_key, (D,), jnp.float32)
    rising = 0.6 + 1.2 * place
    values = rising[:, None] * (noise + offset[None, :])
    return values.astype(jnp.bfloat16)


def shard_levels(rng, dims, cuts, least, largest):
    level = 1.0
    for axis_at, shards_of in cuts:
        steps = jax.random.uniform(jax.random.fold_in(jax.random.fold_in(rng, 6), axis_at), (shards_of,), jnp.float32, least / len(cuts), largest / len(cuts))
        level = level * jnp.repeat(jnp.exp(steps), dims[axis_at] // shards_of).reshape((-1,) + (1,) * (len(dims) - 1 - axis_at))
    return level


def bell_draw(rng, shape, scale, most, shards=(), held_as=jnp.bfloat16):
    level = shard_levels(rng, shape, shards, -0.22, 0.18) if shards else 1.0
    entries = jax.random.normal(rng, shape, jnp.float32) * scale * level
    return jnp.minimum(jnp.maximum(entries, -most), most).astype(held_as)


def setup_inputs(seed: int = 0) -> dict:
    key_list = jax.random.split(jax.random.key(seed), 17)
    tokens = draw_tokens(jax.random.fold_in(key_list[16], 71), 0)
    view_count = draw_view_count(jax.random.fold_in(key_list[16], 71), 0)
    norm1_gain = jnp.clip(1.0 + 0.1 * jax.random.normal(key_list[2], (D,), jnp.float32), 0.5, 1.5).astype(jnp.bfloat16)
    norm1_bias = bell_draw(key_list[3], (D,), 0.1, 0.59765625)
    w_qkv = bell_draw(key_list[4], (D, 3 * D), D ** -0.5, 0.3125)
    qv_bias = bell_draw(key_list[5], (2 * D,), 0.2, 1.1953125)
    w_out = bell_draw(key_list[6], (D, D), (max(D // 128, 1)) ** -0.5, 3.5)
    out_bias = bell_draw(key_list[7], (D,), 0.1, 0.59765625)
    norm2_gain = jnp.clip(1.0 + 0.1 * jax.random.normal(key_list[8], (D,), jnp.float32), 0.5, 1.5).astype(jnp.bfloat16)
    norm2_bias = bell_draw(key_list[9], (D,), 0.1, 0.59765625)
    w_fc1 = bell_draw(key_list[10], (D, FF), D ** -0.5, 0.3125)
    fc1_bias = bell_draw(key_list[11], (FF,), 0.3, 1.796875)
    w_fc2 = bell_draw(key_list[12], (FF, D), FF ** -0.5, 0.15625)
    fc2_bias = bell_draw(key_list[13], (D,), 0.1, 0.59765625)
    cot_tokens = bell_draw(key_list[14], (SAMPLES, ROWS, D), 1.0, 6.0, ((0, 16), (1, 2)))
    cot_cls = draw_cot_cls(jax.random.fold_in(key_list[16], 71), 0)
    return dict(tokens=tokens, view_count=view_count, norm1_gain=norm1_gain, norm1_bias=norm1_bias, w_qkv=w_qkv, qv_bias=qv_bias, w_out=w_out, out_bias=out_bias, norm2_gain=norm2_gain, norm2_bias=norm2_bias, w_fc1=w_fc1, fc1_bias=fc1_bias, w_fc2=w_fc2, fc2_bias=fc2_bias, cot_tokens=cot_tokens, cot_cls=cot_cls)


NORM_EPS = 1e-06
CLS_EPS = 1e-05
MASKED = -1e+30
PRECISE = lax.Precision.HIGHEST

@jax.custom_vjp
def low(v):
    return lax.optimization_barrier(v.astype(jnp.bfloat16)).astype(jnp.float32)

@jax.custom_vjp
def low_back(v):
    return v

def low_keep(v):
    return (low(v), None)

def low_pass(kept, grad):
    return (grad,)

def back_keep(v):
    return (v, None)

def back_low(kept, grad):
    return (low(grad),)
low.defvjp(low_keep, low_pass)
low_back.defvjp(back_keep, back_low)

def norm_rows(values, norm_gain, norm_shift):
    centre = lax.optimization_barrier(jnp.mean(values, -1, keepdims=True))
    offset = values - centre
    spread = lax.optimization_barrier(jnp.mean(offset * offset, -1, keepdims=True))
    return offset * lax.rsqrt(spread + NORM_EPS) * norm_gain + norm_shift

def attend_sample(queries, key_rows, value_rows, limit_one):
    raw_scores = jnp.einsum('qhc,khc->hqk', queries, key_rows, precision=PRECISE) * HEAD_DIM ** (-0.5)
    live_keys = jnp.arange(ROWS, dtype=jnp.int32) < limit_one
    scores = low_back(jnp.where(live_keys[None, None, :], raw_scores, MASKED))
    row_top = lax.optimization_barrier(jnp.max(scores, -1, keepdims=True))
    powers = jnp.exp(scores - row_top)
    weights = low(powers / lax.optimization_barrier(jnp.sum(powers, -1, keepdims=True)))
    mixture = jnp.einsum('hqk,khc->qhc', weights, value_rows, precision=PRECISE)
    return low(low_back(mixture))

def layer_sample(params, sample, limit_one):
    norm1_gain, norm1_bias, w_qkv, qv_bias, w_out, out_bias, norm2_gain, norm2_bias, w_fc1, fc1_bias, w_fc2, fc2_bias = params
    width = sample.shape[-1]
    normed_first = low(norm_rows(sample, norm1_gain, norm1_bias))
    bias_full = jnp.concatenate((qv_bias[:width], jnp.zeros((width,), sample.dtype), qv_bias[width:]))
    projected = jnp.dot(normed_first, w_qkv, precision=PRECISE, preferred_element_type=jnp.float32)
    projected = low(low_back(projected + bias_full))
    split_heads = projected.reshape(ROWS, 3, HEADS, HEAD_DIM)
    attended = attend_sample(split_heads[:, 0], split_heads[:, 1], split_heads[:, 2], limit_one)
    attended = attended.reshape(ROWS, width)
    attn_branch = jnp.dot(attended, w_out, precision=PRECISE, preferred_element_type=jnp.float32) + out_bias
    middle = sample + low_back(attn_branch)
    normed_second = low(norm_rows(middle, norm2_gain, norm2_bias))
    pre_act = jnp.dot(normed_second, w_fc1, precision=PRECISE, preferred_element_type=jnp.float32) + fc1_bias
    pre_act = low_back(pre_act)
    activation = low(jax.nn.gelu(pre_act, approximate=False))
    mlp_branch = jnp.dot(activation, w_fc2, precision=PRECISE, preferred_element_type=jnp.float32) + fc2_bias
    return middle + low_back(mlp_branch)

def forward_all(params, token_values, limits):

    def one_sample(items):
        return layer_sample(params, items[0], items[1])
    output = lax.map(jax.checkpoint(one_sample), (token_values, limits))
    cls_rows = output[:, 0, :]
    cls_mean = lax.optimization_barrier(jnp.mean(cls_rows, 0))
    cls_scale = lax.rsqrt(lax.optimization_barrier(jnp.mean(cls_rows * cls_rows, 0)) - cls_mean * cls_mean + CLS_EPS)
    return (output, (cls_rows - cls_mean) * cls_scale)

def reference(tokens, view_count, norm1_gain, norm1_bias, w_qkv, qv_bias, w_out, out_bias, norm2_gain, norm2_bias, w_fc1, fc1_bias, w_fc2, fc2_bias, cot_tokens, cot_cls):
    params = (norm1_gain.astype(jnp.float32), norm1_bias.astype(jnp.float32), w_qkv.astype(jnp.float32), qv_bias.astype(jnp.float32), w_out.astype(jnp.float32), out_bias.astype(jnp.float32), norm2_gain.astype(jnp.float32), norm2_bias.astype(jnp.float32), w_fc1.astype(jnp.float32), fc1_bias.astype(jnp.float32), w_fc2.astype(jnp.float32), fc2_bias.astype(jnp.float32))
    limits = (1 + VIEW_ROWS * view_count).astype(jnp.int32)

    def wrapped(param_values, token_values):
        return forward_all(param_values, token_values, limits)
    (output, cls_values), pull = jax.vjp(wrapped, params, tokens.astype(jnp.float32))
    grads, grad_tokens = pull((cot_tokens.astype(jnp.float32), cot_cls.astype(jnp.float32)))
    return (output.astype(jnp.bfloat16), cls_values.astype(jnp.bfloat16), grad_tokens.astype(jnp.bfloat16), grads[0], grads[1], grads[2], grads[3], grads[4], grads[5], grads[6], grads[7], grads[8], grads[9], grads[10], grads[11])
```

```python
import functools
import math

import jax
import jax.numpy as jnp
from jax import lax
from jax.experimental import pallas as pl
from jax.experimental.pallas import tpu as pltpu
from jax.sharding import PartitionSpec as P

HEAD_DIM = 64
VIEW_ROWS = 196
NORM_EPS = 1e-06
CLS_EPS = 1e-05
MASKED = -1e30
LOG2E = math.log2(math.e)
LN2 = math.log(2.0)
SCALE = HEAD_DIM ** (-0.5)
SUM_LOW = 1e-15
SUM_HIGH = 1e15
BF = jnp.bfloat16
F32 = jnp.float32
VMEM_BYTES = 60 * 2**20


def dot(a, b, ca, cb):
    return lax.dot_general(a, b, (((ca,), (cb,)), ((), ())), preferred_element_type=F32)


def norm_parts(values):
    centre = jnp.mean(values, -1, keepdims=True)
    offset = values - centre
    rstd = lax.rsqrt(jnp.mean(offset * offset, -1, keepdims=True) + NORM_EPS)
    return offset * rstd, rstd


def gelu_cdf(values):
    return 0.5 + 0.5 * lax.erf(values * (0.5**0.5))


def params(semantics):
    return pltpu.CompilerParams(dimension_semantics=semantics, vmem_limit_bytes=VMEM_BYTES)


def whole(shape):
    return pl.BlockSpec(shape, lambda *_: (0,) * len(shape))


def key_counts(rows):
    views = (rows - 1) // VIEW_ROWS
    return [(v, min(rows, -(-(1 + VIEW_ROWS * v) // 16) * 16)) for v in range(1, views + 1)]


def project_kernel(
    blk_ref, views_ref, own_ref, far_ref, w_ref, bias_ref, gain_ref, shift_ref,
    w_out_ref, out_bias_ref, gain2_ref, shift2_ref, w1_ref, b1_ref, w2_ref, b2_ref,
    x_ref, hat_ref, rstd_ref, qkv_ref, cls_ref, mix_ref, first_ref,
):
    step = pl.program_id(0)
    half = own_ref.shape[1]
    rows = 2 * half
    width = own_ref.shape[2]
    mine = pl.multiple_of(blk_ref[0] * half, 16)
    other = pl.multiple_of((1 - blk_ref[0]) * half, 16)
    x_ref[0, pl.ds(mine, half), :] = own_ref[0]
    x_ref[0, pl.ds(other, half), :] = far_ref[0]
    values = x_ref[0].astype(F32)
    hat, rstd = norm_parts(values)
    hat_ref[0] = hat.astype(BF)
    rstd_ref[0] = rstd
    normed = (hat * gain_ref[...] + shift_ref[...]).astype(BF)
    for third in range(3):
        part = pl.ds(third * width, width)
        piece = dot(w_ref[part, :], normed, 1, 1) + bias_ref[part, :]
        if third == 0:
            piece = piece * (SCALE * LOG2E)
        qkv_ref[0, part, :] = piece.astype(BF)

    lead = qkv_ref[0, pl.ds(0, width), :128].astype(F32).T[0:1, :]
    head_of = lax.broadcasted_iota(jnp.int32, (8, width), 1) // HEAD_DIM
    pick = head_of == lax.broadcasted_iota(jnp.int32, (8, width), 0)
    queries = jnp.where(pick, lead, 0.0).astype(BF)
    scores = dot(queries, qkv_ref[0, pl.ds(width, width), :], 1, 0)
    limit = 1 + VIEW_ROWS * views_ref[step]
    place = lax.broadcasted_iota(jnp.int32, (8, rows), 1)
    scores = jnp.where(place < limit, scores, MASKED)
    powers = jnp.exp2(scores - jnp.max(scores, -1, keepdims=True))
    chances = (powers / jnp.sum(powers, -1, keepdims=True)).astype(BF)
    mixed = dot(chances, qkv_ref[0, pl.ds(2 * width, width), :], 1, 1)
    mix_ref[pl.ds(step, 1), :] = jnp.sum(jnp.where(pick, mixed, 0.0), 0, keepdims=True)
    first_ref[pl.ds(step, 1), :] = values[0:1, :]

    @pl.when(step == pl.num_programs(0) - 1)
    def _():
        middle = first_ref[...] + dot(mix_ref[...].astype(BF), w_out_ref[...], 1, 0) + out_bias_ref[...]
        normed2 = (norm_parts(middle)[0] * gain2_ref[...] + shift2_ref[...]).astype(BF)
        pre = dot(normed2, w1_ref[...], 1, 0) + b1_ref[...]
        act = (pre * gelu_cdf(pre)).astype(BF)
        cls_ref[...] = middle + dot(act, w2_ref[...], 1, 0) + b2_ref[...]


def forward_kernel(
    blk_ref, views_ref, q_ref, k_ref, v_ref, x_ref,
    w_out_ref, out_bias_ref, gain2_ref, shift2_ref, w1_ref, b1_ref, w2_ref, b2_ref,
    pow_ref, sum_ref, att_ref, hat_ref, rstd_ref, act_ref, slope_ref, own_ref, far_ref, out_ref,
):
    sample = pl.program_id(0)
    pair = pl.program_id(1)
    rows = x_ref.shape[1]
    half = rows // 2
    views = views_ref[sample]
    limit = 1 + VIEW_ROWS * views
    ones = jnp.ones((16, rows), BF)

    def heads():
        for h in range(2):
            yield h, pl.ds(h * HEAD_DIM, HEAD_DIM)

    def store(h, mixed):
        total = mixed[HEAD_DIM : HEAD_DIM + 1]
        sum_ref[0, pl.ds(2 * pair + h, 1), :] = total
        place = pl.ds(pl.multiple_of(pair * 128 + h * HEAD_DIM, HEAD_DIM), HEAD_DIM)
        att_ref[0, place, :] = (mixed[:HEAD_DIM] / total).astype(BF)

    for count, keys in key_counts(rows):

        @pl.when(views == count)
        def _(keys=keys):
            main = keys - 16
            for h, lanes in heads():
                scores = dot(k_ref[0, lanes, :keys], q_ref[0, lanes, :], 0, 0)
                pow_ref[0, h, :main, :] = jnp.exp2(scores[:main]).astype(BF)
                place = main + lax.broadcasted_iota(jnp.int32, (16, rows), 0)
                tail = jnp.where(place < limit, scores[main:], MASKED)
                pow_ref[0, h, main:keys, :] = jnp.exp2(tail).astype(BF)
                left = jnp.concatenate((v_ref[0, lanes, :keys], ones[:, :keys]), 0)
                store(h, dot(left, pow_ref[0, h, :keys, :], 1, 0))

    first = sum_ref[0, pl.ds(2 * pair, 1), :]
    second = sum_ref[0, pl.ds(2 * pair + 1, 1), :]
    least = jnp.min(jnp.minimum(first, second))
    plain = (least > SUM_LOW) & (jnp.max(jnp.maximum(first, second)) < SUM_HIGH)

    @pl.when(jnp.logical_not(plain))
    def _():
        for h, lanes in heads():
            scores = dot(k_ref[0, lanes, :], q_ref[0, lanes, :], 0, 0)
            place = lax.broadcasted_iota(jnp.int32, (rows, rows), 0)
            scores = jnp.where(place < limit, scores, MASKED)
            pow_ref[0, h] = jnp.exp2(scores - jnp.max(scores, 0, keepdims=True)).astype(BF)
            left = jnp.concatenate((v_ref[0, lanes, :], ones), 0)
            store(h, dot(left, pow_ref[0, h], 1, 0))

    @pl.when(pair == pl.num_programs(1) - 1)
    def _():
        branch = dot(att_ref[0], w_out_ref[...], 0, 0) + out_bias_ref[...]
        middle = x_ref[0].astype(F32) + branch
        hat, rstd = norm_parts(middle)
        hat_ref[0] = hat.astype(BF)
        rstd_ref[0] = rstd
        normed = (hat * gain2_ref[...] + shift2_ref[...]).astype(BF)
        hidden = w1_ref.shape[1]
        block = hidden // 2
        for r in range(2):
            part = slice(r * half, (r + 1) * half)
            for c in range(2):
                cols = slice(c * block, (c + 1) * block)
                pre = dot(normed[part], w1_ref[:, cols], 1, 0) + b1_ref[:, cols]
                cdf = gelu_cdf(pre)
                bell = jnp.exp(pre * pre * -0.5) * (1.0 / math.sqrt(2.0 * math.pi))
                act_ref[0, part, cols] = (pre * cdf).astype(BF)
                slope_ref[0, part, cols] = (cdf + pre * bell).astype(BF)
            output = middle[part] + dot(act_ref[0, part, :], w2_ref[...], 1, 0) + b2_ref[...]
            out_ref[part, :] = output.astype(BF)
        own_ref[0] = out_ref[pl.ds(pl.multiple_of(blk_ref[0] * half, 16), half), :]
        far_ref[0] = out_ref[pl.ds(pl.multiple_of((1 - blk_ref[0]) * half, 16), half), :]


def mlp_back_kernel(
    blk_ref, own_ref, far_ref, dcls_ref, act_ref, slope_ref, hat_ref, rstd_ref, att_ref, sum_ref,
    gain2_ref, w1_ref, w2_ref, w_out_ref,
    grads_ref, gmid_ref, dmix_ref, inner_ref,
    g_ref, dpre_ref, acc2_ref, acc1_ref, acc0_ref, accb_ref,
):
    step = pl.program_id(0)
    half = own_ref.shape[1]
    width = own_ref.shape[2]
    hidden = w1_ref.shape[1]

    @pl.when(step == 0)
    def _():
        acc2_ref[...] = jnp.zeros_like(acc2_ref)
        acc1_ref[...] = jnp.zeros_like(acc1_ref)
        acc0_ref[...] = jnp.zeros_like(acc0_ref)
        accb_ref[...] = jnp.zeros_like(accb_ref)

    g_ref[pl.ds(pl.multiple_of(blk_ref[0] * half, 16), half), :] = own_ref[0].astype(F32)
    g_ref[pl.ds(pl.multiple_of((1 - blk_ref[0]) * half, 16), half), :] = far_ref[0].astype(F32)
    g_ref[0:1, :] = g_ref[0:1, :] + dcls_ref[pl.ds(step, 1), :]
    g = g_ref[...]
    g_mlp = g.astype(BF)
    hat = hat_ref[0]
    for j in range(hidden // width):
        cols = slice(j * width, (j + 1) * width)
        d_act = dot(g_mlp, w2_ref[cols, :], 1, 1)
        d_pre = (d_act * slope_ref[0, :, cols].astype(F32)).astype(BF)
        dpre_ref[:, cols] = d_pre
        accb_ref[j : j + 1, :] += jnp.sum(d_pre.astype(F32), 0, keepdims=True)
        acc1_ref[:, cols] += dot(hat, d_pre, 0, 0)
        acc2_ref[cols, :] += dot(act_ref[0, :, cols], g_mlp, 0, 0)
    d_norm = dot(dpre_ref[...], w1_ref[...], 1, 1)
    u = d_norm * gain2_ref[...]
    hat = hat.astype(F32)
    g_mid = g + rstd_ref[0] * (
        u - jnp.mean(u, -1, keepdims=True) - hat * jnp.mean(u * hat, -1, keepdims=True)
    )
    g_attn = g_mid.astype(BF)
    gmid_ref[0] = g_attn
    acc0_ref[...] += dot(att_ref[0], g_attn, 1, 0)
    accb_ref[4:5, :] += jnp.sum(g_mlp.astype(F32), 0, keepdims=True)
    accb_ref[5:6, :] += jnp.sum(g_attn.astype(F32), 0, keepdims=True)
    d_mix = dot(w_out_ref[...], g_attn, 1, 1)
    for h in range(width // HEAD_DIM):
        part = slice(h * HEAD_DIM, (h + 1) * HEAD_DIM)
        piece = d_mix[part] / sum_ref[0, h : h + 1, :]
        dmix_ref[0, part, :] = piece.astype(BF)
        inner_ref[0, h : h + 1, :] = jnp.sum(piece * att_ref[0, part, :].astype(F32), 0, keepdims=True)

    @pl.when(step == pl.num_programs(0) - 1)
    def _():
        grads_ref[:hidden, :] = acc2_ref[...].astype(BF)
        for j in range(hidden // width):
            rows = slice(hidden + j * width, hidden + (j + 1) * width)
            grads_ref[rows, :] = acc1_ref[:, j * width : (j + 1) * width].astype(BF)
        grads_ref[2 * hidden : 2 * hidden + width, :] = acc0_ref[...].astype(BF)
        grads_ref[2 * hidden + width : 2 * hidden + width + 16, :] = accb_ref[...].astype(BF)
        rest = grads_ref.shape[0] - (2 * hidden + width + 16)
        if rest:
            grads_ref[2 * hidden + width + 16 :, :] = jnp.zeros((rest, width), BF)


def attention_back_kernel(
    views_ref, q_ref, k_ref, v_ref, pow_ref, dmix_ref, inner_ref, hat_ref,
    dqkv_ref, grads_ref, acc_ref, accb_ref,
):
    pair = pl.program_id(0)
    sample = pl.program_id(1)
    rows = hat_ref.shape[1]
    views = views_ref[sample]
    for count, keys in key_counts(rows):

        @pl.when(views == count)
        def _(keys=keys):
            for h in range(2):
                lanes = slice(h * HEAD_DIM, (h + 1) * HEAD_DIM)
                d_mix = dmix_ref[0, lanes, :]
                powers = pow_ref[0, h, :keys, :]
                d_weights = dot(v_ref[0, lanes, :keys], d_mix, 0, 0)
                inner = inner_ref[0, pl.ds(2 * pair + h, 1), :]
                d_scores = (powers.astype(F32) * (d_weights - inner)).astype(BF)
                d_query = dot(k_ref[0, lanes, :keys], d_scores, 1, 0) * SCALE
                d_key = dot(q_ref[0, lanes, :], d_scores, 1, 1) * LN2
                d_value = dot(d_mix, powers, 1, 1)
                base = h * HEAD_DIM
                dqkv_ref[0, base : base + HEAD_DIM, :] = d_query.astype(BF)
                dqkv_ref[0, 128 + base : 128 + base + HEAD_DIM, :keys] = d_key.astype(BF)
                dqkv_ref[0, 256 + base : 256 + base + HEAD_DIM, :keys] = d_value.astype(BF)
                if keys < rows:
                    blank = jnp.zeros((HEAD_DIM, rows - keys), BF)
                    dqkv_ref[0, 128 + base : 128 + base + HEAD_DIM, keys:] = blank
                    dqkv_ref[0, 256 + base : 256 + base + HEAD_DIM, keys:] = blank

    @pl.when(sample == 0)
    def _():
        acc_ref[...] = jnp.zeros_like(acc_ref)
        accb_ref[...] = jnp.zeros_like(accb_ref)

    d_part = dqkv_ref[0]
    acc_ref[...] += dot(d_part, hat_ref[0], 1, 0)
    accb_ref[...] += dot(jnp.ones((16, rows), BF), d_part, 1, 1)

    @pl.when(sample == pl.num_programs(1) - 1)
    def _():
        span = acc_ref.shape[0]
        grads_ref[0, :span, :] = acc_ref[...].astype(BF)
        grads_ref[0, span:, :] = accb_ref[...].astype(BF)


def tokens_back_kernel(
    blk_ref, dqkv_ref, w_ref, gain_ref, hat_ref, rstd_ref, gmid_ref, own_ref, far_ref, out_ref
):
    half = own_ref.shape[1]
    width = own_ref.shape[2]
    d_norm = jnp.zeros((2 * half, width), F32)
    for pair in range(dqkv_ref.shape[0]):
        d_norm = d_norm + dot(dqkv_ref[pair, 0], w_ref[pair], 0, 0)
    w = d_norm * gain_ref[...]
    hat = hat_ref[0].astype(F32)
    back = rstd_ref[0] * (
        w - jnp.mean(w, -1, keepdims=True) - hat * jnp.mean(w * hat, -1, keepdims=True)
    )
    out_ref[...] = (gmid_ref[0].astype(F32) + back).astype(BF)
    own_ref[0] = out_ref[pl.ds(pl.multiple_of(blk_ref[0] * half, 16), half), :]
    far_ref[0] = out_ref[pl.ds(pl.multiple_of((1 - blk_ref[0]) * half, 16), half), :]


def swap_cores(value):
    return lax.ppermute(value, "blk", [(0, 1), (1, 0)])


def stages(count):
    out = []
    stride = 1
    while stride < count:
        radix = 4 if (count // stride) % 4 == 0 else 2
        out.append((stride, radix))
        stride *= radix
    return out


def shifted(value, stride, radix, steps):
    count = lax.axis_size("samp")
    pairs = []
    for source in range(count):
        digit = (source // stride) % radix
        pairs.append((source, source + ((digit + steps) % radix - digit) * stride))
    return lax.ppermute(value, "samp", pairs)


def sum_small(value):
    value = value + swap_cores(value)
    for stride, radix in stages(lax.axis_size("samp")):
        value = value + sum(shifted(value, stride, radix, k) for k in range(1, radix))
    return value


def sum_large(value):
    core = lax.axis_index("blk")
    samp = lax.axis_index("samp")
    half = value.shape[0] // 2
    sent = lax.dynamic_slice_in_dim(value, (1 - core) * half, half, 0)
    kept = lax.dynamic_slice_in_dim(value, core * half, half, 0)
    value = (kept.astype(F32) + swap_cores(sent).astype(F32)).astype(BF)
    order = stages(lax.axis_size("samp"))
    for stride, radix in order:
        digit = (samp // stride) % radix
        size = value.shape[0] // radix
        total = lax.dynamic_slice_in_dim(value, digit * size, size, 0).astype(F32)
        for k in range(1, radix):
            piece = lax.dynamic_slice_in_dim(value, ((digit + k) % radix) * size, size, 0)
            total = total + shifted(piece, stride, radix, k).astype(F32)
        value = total.astype(BF)
    for stride, radix in reversed(order):
        digit = (samp // stride) % radix
        size = value.shape[0]
        whole_value = jnp.zeros((size * radix, value.shape[1]), BF)
        whole_value = lax.dynamic_update_slice_in_dim(whole_value, value, digit * size, 0)
        for k in range(1, radix):
            piece = shifted(value, stride, radix, k)
            whole_value = lax.dynamic_update_slice_in_dim(
                whole_value, piece, ((digit - k) % radix) * size, 0
            )
        value = whole_value
    other = swap_cores(value)
    first = core == 0
    return jnp.concatenate((jnp.where(first, value, other), jnp.where(first, other, value)), 0)


def pad_rows(count, unit):
    return -(-count // unit) * unit


def per_device(
    tokens, view_count, norm1_gain, norm1_bias, w_qkv, qv_bias, w_out, out_bias,
    norm2_gain, norm2_bias, w_fc1, fc1_bias, w_fc2, fc2_bias, cot_tokens, cot_cls,
):
    core = lax.axis_index("blk")
    cores = lax.axis_size("blk")
    samples, half, width = tokens.shape
    local = samples // cores
    rows = half * cores
    hidden = w_fc1.shape[1]
    heads = width // HEAD_DIM
    pairs = heads // 2
    units = lax.axis_size("samp") * cores * 8
    here = core.reshape(1).astype(jnp.int32)
    views = lax.dynamic_slice_in_dim(view_count, core * local, local, 0)
    row = lambda v: v.astype(F32).reshape(1, -1)

    theirs = (1 - core) * local
    far_tokens = swap_cores(lax.dynamic_slice_in_dim(tokens, theirs, local, 0))
    far_cot = swap_cores(lax.dynamic_slice_in_dim(cot_tokens, theirs, local, 0))

    w_turned = w_qkv.T
    bias_full = jnp.concatenate(
        (qv_bias[:width], jnp.zeros((width,), qv_bias.dtype), qv_bias[width:])
    ).astype(F32).reshape(-1, 1)
    gain1, shift1 = row(norm1_gain), row(norm1_bias)
    gain2, shift2 = row(norm2_gain), row(norm2_bias)
    mlp_args = (
        w_out, row(out_bias), gain2, shift2, w_fc1, row(fc1_bias), w_fc2, row(fc2_bias),
    )
    mlp_specs = [whole(a.shape) for a in mlp_args]
    sds = jax.ShapeDtypeStruct
    half_spec = lambda f: pl.BlockSpec((1, half, width), f)
    own_map = lambda s, b, *_: (b[0] * local + s, 0, 0)
    by_sample = lambda s, *_: (s, 0, 0)

    x_full, hat1, rstd1, qkv, cls_rows = pl.pallas_call(
        project_kernel,
        grid_spec=pltpu.PrefetchScalarGridSpec(
            num_scalar_prefetch=2,
            grid=(local,),
            in_specs=[
                half_spec(own_map),
                half_spec(by_sample),
                whole(w_turned.shape),
                whole(bias_full.shape),
                whole(gain1.shape),
                whole(shift1.shape),
                *mlp_specs,
            ],
            out_specs=[
                pl.BlockSpec((1, rows, width), by_sample),
                pl.BlockSpec((1, rows, width), by_sample),
                pl.BlockSpec((1, rows, 1), by_sample),
                pl.BlockSpec((1, 3 * width, rows), by_sample),
                whole((8, width)),
            ],
            scratch_shapes=[pltpu.VMEM((8, width), F32), pltpu.VMEM((8, width), F32)],
        ),
        out_shape=[
            sds((local, rows, width), BF),
            sds((local, rows, width), BF),
            sds((local, rows, 1), F32),
            sds((local, 3 * width, rows), BF),
            sds((8, width), F32),
        ],
        compiler_params=params(("arbitrary",)),
        cost_estimate=pl.CostEstimate(
            flops=2 * local * rows * width * 3 * width, bytes_accessed=12 * 2**20, transcendentals=0
        ),
        name="project",
    )(here, views, tokens, far_tokens, w_turned, bias_full, gain1, shift1, *mlp_args)

    cls = cls_rows[:local]
    grad_cls = cot_cls.astype(F32)
    sums = jnp.stack(
        (
            jnp.sum(cls, 0),
            jnp.sum(cls * cls, 0),
            jnp.sum(grad_cls, 0),
            jnp.sum(grad_cls * cls, 0),
        )
    )
    sums = sum_small(jnp.concatenate((sums, jnp.zeros((4, width), F32)), 0))

    pair_map = lambda base: (lambda s, p, *_: (s, base + p, 0))
    by_sample2 = lambda s, p, *_: (s, 0, 0)
    qkv_specs = [pl.BlockSpec((1, 128, rows), pair_map(t * pairs)) for t in range(3)]
    powers, totals, mixed, hat2, rstd2, act, slope, out_own, out_far = pl.pallas_call(
        forward_kernel,
        grid_spec=pltpu.PrefetchScalarGridSpec(
            num_scalar_prefetch=2,
            grid=(local, pairs),
            in_specs=[*qkv_specs, pl.BlockSpec((1, rows, width), by_sample2), *mlp_specs],
            out_specs=[
                pl.BlockSpec((1, 2, rows, rows), lambda s, p, *_: (s, p, 0, 0)),
                pl.BlockSpec((1, 8, rows), by_sample2),
                pl.BlockSpec((1, width, rows), by_sample2),
                pl.BlockSpec((1, rows, width), by_sample2),
                pl.BlockSpec((1, rows, 1), by_sample2),
                pl.BlockSpec((1, rows, hidden), by_sample2),
                pl.BlockSpec((1, rows, hidden), by_sample2),
                half_spec(lambda s, p, b, *_: (b[0] * local + s, 0, 0)),
                half_spec(by_sample2),
            ],
            scratch_shapes=[pltpu.VMEM((rows, width), BF)],
        ),
        out_shape=[
            sds((local, heads, rows, rows), BF),
            sds((local, 8, rows), F32),
            sds((local, width, rows), BF),
            sds((local, rows, width), BF),
            sds((local, rows, 1), F32),
            sds((local, rows, hidden), BF),
            sds((local, rows, hidden), BF),
            sds((samples, half, width), BF),
            sds((local, half, width), BF),
        ],
        compiler_params=params(("arbitrary", "arbitrary")),
        cost_estimate=pl.CostEstimate(
            flops=2 * local * rows * (width * width + 2 * width * hidden + 8 * rows * width),
            bytes_accessed=50 * 2**20,
            transcendentals=0,
        ),
        name="forward",
    )(here, views, qkv, qkv, qkv, x_full, *mlp_args)

    total_samples = local * cores * lax.axis_size("samp")
    cls_mean = sums[0] / total_samples
    cls_scale = lax.rsqrt(sums[1] / total_samples - cls_mean * cls_mean + CLS_EPS)
    cls_hat = (cls - cls_mean) * cls_scale
    cls_norm = cls_hat.astype(BF)
    cross = cls_scale * (sums[3] - cls_mean * sums[2])
    d_cls = cls_scale * (grad_cls - sums[2] / total_samples - cls_hat * (cross / total_samples))
    d_cls = jnp.concatenate((d_cls, jnp.zeros((8 - local, width), F32)), 0)

    tokens_out = lax.dynamic_update_slice_in_dim(out_own, swap_cores(out_far), theirs, 0)

    used1 = 2 * hidden + width + 16
    rows1 = pad_rows(used1, units)
    grads1, g_mid, d_mix, inner = pl.pallas_call(
        mlp_back_kernel,
        grid_spec=pltpu.PrefetchScalarGridSpec(
            num_scalar_prefetch=1,
            grid=(local,),
            in_specs=[
                half_spec(own_map),
                half_spec(by_sample),
                whole((8, width)),
                pl.BlockSpec((1, rows, hidden), by_sample),
                pl.BlockSpec((1, rows, hidden), by_sample),
                pl.BlockSpec((1, rows, width), by_sample),
                pl.BlockSpec((1, rows, 1), by_sample),
                pl.BlockSpec((1, width, rows), by_sample),
                pl.BlockSpec((1, 8, rows), by_sample),
                whole(gain2.shape),
                whole(w_fc1.shape),
                whole(w_fc2.shape),
                whole(w_out.shape),
            ],
            out_specs=[
                whole((rows1, width)),
                pl.BlockSpec((1, rows, width), by_sample),
                pl.BlockSpec((1, width, rows), by_sample),
                pl.BlockSpec((1, 8, rows), by_sample),
            ],
            scratch_shapes=[
                pltpu.VMEM((rows, width), F32),
                pltpu.VMEM((rows, hidden), BF),
                pltpu.VMEM((hidden, width), F32),
                pltpu.VMEM((width, hidden), F32),
                pltpu.VMEM((width, width), F32),
                pltpu.VMEM((16, width), F32),
            ],
        ),
        out_shape=[
            sds((rows1, width), BF),
            sds((local, rows, width), BF),
            sds((local, width, rows), BF),
            sds((local, 8, rows), F32),
        ],
        compiler_params=params(("arbitrary",)),
        cost_estimate=pl.CostEstimate(
            flops=2 * local * rows * (2 * width * width + 4 * width * hidden),
            bytes_accessed=30 * 2**20,
            transcendentals=0,
        ),
        name="mlp_back",
    )(
        here, cot_tokens, far_cot, d_cls, act, slope, hat2, rstd2, mixed, totals,
        gain2, w_fc1, w_fc2, w_out,
    )

    used2 = 3 * 128 + 16
    back_map = lambda base: (lambda p, s, *_: (s, base + p, 0))
    back_sample = lambda p, s, *_: (s, 0, 0)
    d_qkv, grads2 = pl.pallas_call(
        attention_back_kernel,
        grid_spec=pltpu.PrefetchScalarGridSpec(
            num_scalar_prefetch=1,
            grid=(pairs, local),
            in_specs=[
                *[pl.BlockSpec((1, 128, rows), back_map(t * pairs)) for t in range(3)],
                pl.BlockSpec((1, 2, rows, rows), lambda p, s, *_: (s, p, 0, 0)),
                pl.BlockSpec((1, 128, rows), back_map(0)),
                pl.BlockSpec((1, 8, rows), back_sample),
                pl.BlockSpec((1, rows, width), back_sample),
            ],
            out_specs=[
                pl.BlockSpec((None, 1, 384, rows), lambda p, s, *_: (p, s, 0, 0)),
                pl.BlockSpec((1, used2, width), lambda p, s, *_: (p, 0, 0)),
            ],
            scratch_shapes=[pltpu.VMEM((384, width), F32), pltpu.VMEM((16, 384), F32)],
        ),
        out_shape=[
            sds((pairs, local, 384, rows), BF),
            sds((pairs, used2, width), BF),
        ],
        compiler_params=params(("arbitrary", "arbitrary")),
        cost_estimate=pl.CostEstimate(
            flops=2 * local * rows * (3 * width * width + 16 * rows * width),
            bytes_accessed=40 * 2**20,
            transcendentals=0,
        ),
        name="attention_back",
    )(views, qkv, qkv, qkv, powers, d_mix, inner, hat1)

    w_pairs = w_turned.reshape(3, pairs, 128, width).transpose(1, 0, 2, 3).reshape(pairs, 384, width)
    grad_own, grad_far = pl.pallas_call(
        tokens_back_kernel,
        grid_spec=pltpu.PrefetchScalarGridSpec(
            num_scalar_prefetch=1,
            grid=(local,),
            in_specs=[
                pl.BlockSpec((pairs, 1, 384, rows), lambda s, *_: (0, s, 0, 0)),
                whole(w_pairs.shape),
                whole(gain1.shape),
                pl.BlockSpec((1, rows, width), by_sample),
                pl.BlockSpec((1, rows, 1), by_sample),
                pl.BlockSpec((1, rows, width), by_sample),
            ],
            out_specs=[half_spec(own_map), half_spec(by_sample)],
            scratch_shapes=[pltpu.VMEM((rows, width), BF)],
        ),
        out_shape=[sds((samples, half, width), BF), sds((local, half, width), BF)],
        compiler_params=params(("arbitrary",)),
        cost_estimate=pl.CostEstimate(
            flops=2 * local * rows * 3 * width * width, bytes_accessed=12 * 2**20, transcendentals=0
        ),
        name="tokens_back",
    )(here, d_qkv, w_pairs, gain1, hat1, rstd1, g_mid)
    grad_tokens = lax.dynamic_update_slice_in_dim(grad_own, swap_cores(grad_far), theirs, 0)

    total1 = sum_large(grads1).astype(F32)
    grad_w_fc2 = total1[:hidden]
    turned = jnp.concatenate(
        [total1[hidden + j * width : hidden + (j + 1) * width] for j in range(hidden // width)], 1
    )
    grad_w_out = total1[2 * hidden : 2 * hidden + width]
    vectors = total1[2 * hidden + width : used1]
    blocks = hidden // width
    grad_fc1_bias = vectors[:blocks].reshape(hidden)
    grad_fc2_bias = vectors[blocks]
    grad_out_bias = vectors[blocks + 1]
    grad_w_fc1 = gain2.T * turned + shift2.T * grad_fc1_bias
    w1 = w_fc1.astype(F32)
    grad_gain2 = jnp.sum(w1 * turned, 1)
    grad_shift2 = jnp.sum(w1 * grad_fc1_bias, 1)

    size2 = pairs * used2
    rows2 = pad_rows(size2, units)
    flat2 = grads2.reshape(size2, width)
    if rows2 > size2:
        flat2 = jnp.concatenate((flat2, jnp.zeros((rows2 - size2, width), BF)), 0)
    total2 = sum_large(flat2)[:size2].astype(F32).reshape(pairs, used2, width)
    hats = total2[:, :384].reshape(pairs, 3, 128, width).transpose(1, 0, 2, 3).reshape(3 * width, width)
    column_sums = total2[:, 384].reshape(pairs, 3, 128).transpose(1, 0, 2).reshape(3 * width)
    grad_w_qkv = hats.T * gain1.T + shift1.T * column_sums
    grad_qv_bias = jnp.concatenate((column_sums[:width], column_sums[2 * width :]))
    w0 = w_turned.astype(F32)
    grad_gain1 = jnp.sum(w0 * hats, 0)
    grad_shift1 = jnp.sum(w0 * column_sums[:, None], 0)
    return (
        tokens_out, cls_norm, grad_tokens, grad_gain1, grad_shift1, grad_w_qkv, grad_qv_bias,
        grad_w_out, grad_out_bias, grad_gain2, grad_shift2, grad_w_fc1, grad_fc1_bias,
        grad_w_fc2, grad_fc2_bias,
    )


def solution(mesh):
    split = P("samp", "blk", None)
    classes = P(("samp", "blk"), None)
    return jax.shard_map(
        per_device,
        mesh=mesh,
        in_specs=(split, P("samp"), *([P()] * 12), split, classes),
        out_specs=(split, classes, split, *([P()] * 12)),
        check_vma=False,
    )
```

```python
import functools
import math

import jax
import jax.numpy as jnp
import numpy as np
from jax import lax
from jax.experimental import pallas as pl
from jax.experimental.pallas import tpu as pltpu
from jax.sharding import PartitionSpec as P

HEAD_DIM = 64
VIEW_ROWS = 196
NORM_EPS = 1e-06
CLS_EPS = 1e-05
MASKED = -1e30
LOG2E = math.log2(math.e)
LN2 = math.log(2.0)
SCALE = HEAD_DIM ** (-0.5)
SUM_LOW = 1e-15
SUM_HIGH = 1e15
BF = jnp.bfloat16
F32 = jnp.float32
VMEM_BYTES = 60 * 2**20


def dot(a, b, ca, cb):
    return lax.dot_general(a, b, (((ca,), (cb,)), ((), ())), preferred_element_type=F32)


def norm_parts(values):
    centre = jnp.mean(values, -1, keepdims=True)
    offset = values - centre
    rstd = lax.rsqrt(jnp.mean(offset * offset, -1, keepdims=True) + NORM_EPS)
    return offset * rstd, rstd


def gelu_cdf(values):
    return 0.5 + 0.5 * lax.erf(values * (0.5**0.5))


def params(semantics):
    return pltpu.CompilerParams(dimension_semantics=semantics, vmem_limit_bytes=VMEM_BYTES)


def whole(shape):
    return pl.BlockSpec(shape, lambda *_: (0,) * len(shape))


def key_counts(rows):
    views = (rows - 1) // VIEW_ROWS
    return [(v, min(rows, -(-(1 + VIEW_ROWS * v) // 16) * 16)) for v in range(1, views + 1)]


GAIN1, SHIFT1, GAIN2, SHIFT2, OUT_BIAS, FC2_BIAS, QV_BIAS, FC1_BIAS = 0, 1, 2, 3, 4, 5, 6, 8


def row_of(pack_ref, index):
    return pack_ref[index : index + 1, :]


def place_halves(target_ref, core, own, far):
    half = own.shape[0]
    target_ref[pl.ds(pl.multiple_of(core * half, 16), half), :] = own
    target_ref[pl.ds(pl.multiple_of((1 - core) * half, 16), half), :] = far


def split_halves(source_ref, core, own_ref, far_ref):
    half = own_ref.shape[1]
    own_ref[0] = source_ref[pl.ds(pl.multiple_of(core * half, 16), half), :]
    far_ref[0] = source_ref[pl.ds(pl.multiple_of((1 - core) * half, 16), half), :]


def project_kernel(
    blk_ref, views_ref, own_ref, far_ref, w_ref, pack_ref, w_out_ref, w1_ref, w2_ref, cot_ref,
    x_ref, hat_ref, rstd_ref, qkv_ref, cls_ref, stat_ref, mix_ref, first_ref, full_ref,
):
    step = pl.program_id(0)
    rows = x_ref.shape[1]
    width = own_ref.shape[2]
    place_halves(full_ref, blk_ref[0], own_ref[0], far_ref[0])
    x_ref[0] = full_ref[...]
    values = full_ref[...].astype(F32)
    hat, rstd = norm_parts(values)
    hat_ref[0] = hat.astype(BF)
    rstd_ref[0] = rstd
    normed = (hat * row_of(pack_ref, GAIN1) + row_of(pack_ref, SHIFT1)).astype(BF)
    columns = pack_ref[0:8, :].T
    for third in range(3):
        part = pl.ds(third * width, width)
        piece = dot(w_ref[part, :], normed, 1, 1)
        if third == 0:
            piece = (piece + columns[:, QV_BIAS : QV_BIAS + 1]) * (SCALE * LOG2E)
        if third == 2:
            piece = piece + columns[:, QV_BIAS + 1 : QV_BIAS + 2]
        qkv_ref[0, part, :] = piece.astype(BF)

    lead = qkv_ref[0, pl.ds(0, width), :128].astype(F32).T[0:1, :]
    head_of = lax.broadcasted_iota(jnp.int32, (8, width), 1) // HEAD_DIM
    pick = head_of == lax.broadcasted_iota(jnp.int32, (8, width), 0)
    queries = jnp.where(pick, lead, 0.0).astype(BF)
    scores = dot(queries, qkv_ref[0, pl.ds(width, width), :], 1, 0)
    limit = 1 + VIEW_ROWS * views_ref[blk_ref[CORE] * pl.num_programs(0) + step]
    place = lax.broadcasted_iota(jnp.int32, (8, rows), 1)
    scores = jnp.where(place < limit, scores, MASKED)
    powers = jnp.exp2(scores - jnp.max(scores, -1, keepdims=True))
    chances = (powers / jnp.sum(powers, -1, keepdims=True)).astype(BF)
    mixed = dot(chances, qkv_ref[0, pl.ds(2 * width, width), :], 1, 1)
    mix_ref[pl.ds(step, 1), :] = jnp.sum(jnp.where(pick, mixed, 0.0), 0, keepdims=True)
    first_ref[pl.ds(step, 1), :] = values[0:1, :]

    @pl.when(step == pl.num_programs(0) - 1)
    def _():
        branch = dot(mix_ref[...].astype(BF), w_out_ref[...], 1, 0) + row_of(pack_ref, OUT_BIAS)
        middle = first_ref[...] + branch
        normed2 = norm_parts(middle)[0] * row_of(pack_ref, GAIN2) + row_of(pack_ref, SHIFT2)
        normed2 = normed2.astype(BF)
        output = middle + row_of(pack_ref, FC2_BIAS)
        for j in range(w1_ref.shape[1] // width):
            cols = slice(j * width, (j + 1) * width)
            pre = dot(normed2, w1_ref[:, cols], 1, 0) + row_of(pack_ref, FC1_BIAS + j)
            act = (pre * gelu_cdf(pre)).astype(BF)
            output = output + dot(act, w2_ref[cols, :], 1, 0)
        cls_ref[...] = output
        count = cot_ref.shape[0]
        cls = output[:count]
        cot = cot_ref[...].astype(F32)
        stat_ref[...] = jnp.zeros_like(stat_ref)
        for k, term in enumerate((cls, cls * cls, cot, cot * cls)):
            stat_ref[k : k + 1, :] = jnp.sum(term, 0, keepdims=True)


def attention_kernel(core_ref, views_ref, q_ref, k_ref, v_ref, pow_ref, sum_ref, att_ref):
    sample = pl.program_id(0)
    pair = pl.program_id(1)
    rows = q_ref.shape[2]
    views = views_ref[core_ref[CORE] * pl.num_programs(0) + sample]
    limit = 1 + VIEW_ROWS * views
    ones = jnp.ones((16, rows), BF)

    def heads():
        for h in range(2):
            yield h, pl.ds(h * HEAD_DIM, HEAD_DIM)

    def store(h, mixed):
        total = mixed[HEAD_DIM : HEAD_DIM + 1]
        sum_ref[0, pl.ds(2 * pair + h, 1), :] = total
        att_ref[0, h * HEAD_DIM : (h + 1) * HEAD_DIM, :] = (mixed[:HEAD_DIM] / total).astype(BF)

    for count, keys in key_counts(rows):

        @pl.when(views == count)
        def _(keys=keys):
            main = keys - 16
            for h, lanes in heads():
                scores = dot(k_ref[0, lanes, :keys], q_ref[0, lanes, :], 0, 0)
                pow_ref[0, h, :main, :] = jnp.exp2(scores[:main]).astype(BF)
                place = main + lax.broadcasted_iota(jnp.int32, (16, rows), 0)
                tail = jnp.where(place < limit, scores[main:], MASKED)
                pow_ref[0, h, main:keys, :] = jnp.exp2(tail).astype(BF)
                left = jnp.concatenate((v_ref[0, lanes, :keys], ones[:, :keys]), 0)
                store(h, dot(left, pow_ref[0, h, :keys, :], 1, 0))

    first = sum_ref[0, pl.ds(2 * pair, 1), :]
    second = sum_ref[0, pl.ds(2 * pair + 1, 1), :]
    least = jnp.min(jnp.minimum(first, second))
    plain = (least > SUM_LOW) & (jnp.max(jnp.maximum(first, second)) < SUM_HIGH)

    @pl.when(jnp.logical_not(plain))
    def _():
        for h, lanes in heads():
            scores = dot(k_ref[0, lanes, :], q_ref[0, lanes, :], 0, 0)
            place = lax.broadcasted_iota(jnp.int32, (rows, rows), 0)
            scores = jnp.where(place < limit, scores, MASKED)
            pow_ref[0, h] = jnp.exp2(scores - jnp.max(scores, 0, keepdims=True)).astype(BF)
            left = jnp.concatenate((v_ref[0, lanes, :], ones), 0)
            store(h, dot(left, pow_ref[0, h], 1, 0))


def mlp_kernel(
    blk_ref, x_ref, att_ref, w_out_ref, w1_ref, w2_ref, pack_ref,
    hat_ref, rstd_ref, act_ref, slope_ref, own_ref, far_ref, out_ref,
):
    half = own_ref.shape[1]
    width = own_ref.shape[2]
    branch = dot(att_ref[0], w_out_ref[...], 0, 0) + row_of(pack_ref, OUT_BIAS)
    middle = x_ref[0].astype(F32) + branch
    hat, rstd = norm_parts(middle)
    hat_ref[0] = hat.astype(BF)
    rstd_ref[0] = rstd
    normed = (hat * row_of(pack_ref, GAIN2) + row_of(pack_ref, SHIFT2)).astype(BF)
    for r in range(2):
        part = slice(r * half, (r + 1) * half)
        for j in range(w1_ref.shape[1] // width):
            cols = slice(j * width, (j + 1) * width)
            pre = dot(normed[part], w1_ref[:, cols], 1, 0) + row_of(pack_ref, FC1_BIAS + j)
            cdf = gelu_cdf(pre)
            bell = jnp.exp(pre * pre * -0.5) * (1.0 / math.sqrt(2.0 * math.pi))
            act_ref[0, part, cols] = (pre * cdf).astype(BF)
            slope_ref[0, part, cols] = (cdf + pre * bell).astype(BF)
        output = middle[part] + dot(act_ref[0, part, :], w2_ref[...], 1, 0)
        out_ref[part, :] = (output + row_of(pack_ref, FC2_BIAS)).astype(BF)
    split_halves(out_ref, blk_ref[0], own_ref, far_ref)


def mlp_grads_kernel(
    core_ref, own_ref, far_ref, cls_ref, cot_ref, *refs, samples, parts, peers
):
    stat_refs = refs[:peers]
    act_ref, slope_ref, hat_ref, w2_ref = refs[peers : peers + 4]
    dpre_ref, dcls_ref, norm_ref, bias_ref, kept_ref, sent_ref = refs[peers + 4 : peers + 10]
    g_ref, acc2_ref, acc1_ref, flat_ref = refs[peers + 10 :]
    step = pl.program_id(0)
    width = own_ref.shape[2]
    hidden = w2_ref.shape[0]

    @pl.when(step == 0)
    def _():
        acc2_ref[...] = jnp.zeros_like(acc2_ref)
        acc1_ref[...] = jnp.zeros_like(acc1_ref)
        bias_ref[...] = jnp.zeros_like(bias_ref)
        stats = stat_refs[0][...]
        for other in stat_refs[1:]:
            stats = stats + other[...]
        local = cot_ref.shape[0]
        cls = cls_ref[...][:local]
        cot = cot_ref[...].astype(F32)
        mean = stats[0:1] / samples
        scale = lax.rsqrt(stats[1:2] / samples - mean * mean + CLS_EPS)
        hat = (cls - mean) * scale
        norm_ref[...] = hat.astype(BF)
        cross = scale * (stats[3:4] - mean * stats[2:3])
        dcls_ref[...] = jnp.zeros_like(dcls_ref)
        dcls_ref[:local, :] = scale * (cot - stats[2:3] / samples - hat * (cross / samples))

    place_halves(g_ref, core_ref[0], own_ref[0].astype(F32), far_ref[0].astype(F32))
    g_ref[0:1, :] = g_ref[0:1, :] + dcls_ref[pl.ds(step, 1), :]
    g_mlp = g_ref[...].astype(BF)
    hat = hat_ref[0]
    blocks = hidden // width
    for j in range(blocks):
        cols = slice(j * width, (j + 1) * width)
        d_act = dot(g_mlp, w2_ref[cols, :], 1, 1)
        d_pre = (d_act * slope_ref[0, :, cols].astype(F32)).astype(BF)
        dpre_ref[0, :, cols] = d_pre
        bias_ref[j : j + 1, :] += jnp.sum(d_pre.astype(F32), 0, keepdims=True)
        acc1_ref[:, cols] += dot(hat, d_pre, 0, 0)
        acc2_ref[cols, :] += dot(act_ref[0, :, cols], g_mlp, 0, 0)
    bias_ref[blocks : blocks + 1, :] += jnp.sum(g_mlp.astype(F32), 0, keepdims=True)

    @pl.when(step == pl.num_programs(0) - 1)
    def _():
        flat_ref[:hidden, :] = acc2_ref[...].astype(BF)
        for j in range(blocks):
            rows = slice(hidden + j * width, hidden + (j + 1) * width)
            flat_ref[rows, :] = acc1_ref[:, j * width : (j + 1) * width].astype(BF)
        clear_rest(flat_ref, 2 * hidden)
        write_halves(core_ref[0], flat_ref, parts, kept_ref, sent_ref)


def mlp_back_kernel(
    blk_ref, own_ref, far_ref, dcls_ref, dpre_ref, hat_ref, rstd_ref, att_ref, sum_ref,
    bias_in_ref, pack_ref, w1_ref, w_out_ref,
    gmid_ref, dmix_ref, inner_ref, out_grad_ref, bias_ref, g_ref,
):
    step = pl.program_id(0)
    width = own_ref.shape[2]
    blocks = w1_ref.shape[1] // width

    @pl.when(step == 0)
    def _():
        out_grad_ref[...] = jnp.zeros_like(out_grad_ref)
        bias_ref[...] = bias_in_ref[...]

    place_halves(g_ref, blk_ref[0], own_ref[0].astype(F32), far_ref[0].astype(F32))
    g_ref[0:1, :] = g_ref[0:1, :] + dcls_ref[pl.ds(step, 1), :]
    d_norm = dot(dpre_ref[0], w1_ref[...], 1, 1)
    u = d_norm * row_of(pack_ref, GAIN2)
    hat = hat_ref[0].astype(F32)
    g_mid = g_ref[...] + rstd_ref[0] * (
        u - jnp.mean(u, -1, keepdims=True) - hat * jnp.mean(u * hat, -1, keepdims=True)
    )
    g_attn = g_mid.astype(BF)
    gmid_ref[0] = g_attn
    out_grad_ref[...] += dot(att_ref[0], g_attn, 1, 0)
    bias_ref[blocks + 1 : blocks + 2, :] += jnp.sum(g_attn.astype(F32), 0, keepdims=True)
    d_mix = dot(w_out_ref[...], g_attn, 1, 1)
    for h in range(width // HEAD_DIM):
        part = slice(h * HEAD_DIM, (h + 1) * HEAD_DIM)
        piece = d_mix[part] / sum_ref[0, h : h + 1, :]
        dmix_ref[0, part, :] = piece.astype(BF)
        inner_ref[0, h : h + 1, :] = jnp.sum(piece * att_ref[0, part, :].astype(F32), 0, keepdims=True)


def attention_back_kernel(
    core_ref, views_ref, q_ref, k_ref, v_ref, pow_ref, dmix_ref, inner_ref, hat_ref,
    dqkv_ref, grad_ref, sums_ref, *, pair
):
    sample = pl.program_id(0)
    rows = hat_ref.shape[1]
    views = views_ref[core_ref[CORE] * pl.num_programs(0) + sample]
    for count, keys in key_counts(rows):

        @pl.when(views == count)
        def _(keys=keys):
            for h in range(2):
                lanes = slice(h * HEAD_DIM, (h + 1) * HEAD_DIM)
                d_mix = dmix_ref[0, lanes, :]
                powers = pow_ref[0, h, :keys, :]
                d_weights = dot(v_ref[0, lanes, :keys], d_mix, 0, 0)
                inner = inner_ref[0, 2 * pair + h : 2 * pair + h + 1, :]
                d_scores = (powers.astype(F32) * (d_weights - inner)).astype(BF)
                d_query = dot(k_ref[0, lanes, :keys], d_scores, 1, 0) * SCALE
                d_key = dot(q_ref[0, lanes, :], d_scores, 1, 1) * LN2
                d_value = dot(d_mix, powers, 1, 1)
                base = h * HEAD_DIM
                dqkv_ref[0, base : base + HEAD_DIM, :] = d_query.astype(BF)
                dqkv_ref[0, 128 + base : 128 + base + HEAD_DIM, :keys] = d_key.astype(BF)
                dqkv_ref[0, 256 + base : 256 + base + HEAD_DIM, :keys] = d_value.astype(BF)
                if keys < rows:
                    blank = jnp.zeros((HEAD_DIM, rows - keys), BF)
                    dqkv_ref[0, 128 + base : 128 + base + HEAD_DIM, keys:] = blank
                    dqkv_ref[0, 256 + base : 256 + base + HEAD_DIM, keys:] = blank

    @pl.when(sample == 0)
    def _():
        grad_ref[...] = jnp.zeros_like(grad_ref)
        sums_ref[...] = jnp.zeros_like(sums_ref)

    d_part = dqkv_ref[0]
    grad_ref[...] += dot(d_part, hat_ref[0], 1, 0)
    sums_ref[...] += dot(jnp.ones((16, rows), BF), d_part, 1, 1)[:8]


def tokens_back_kernel(core_ref, *refs, pairs):
    dqkv_refs = refs[:pairs]
    w_ref, pack_ref, hat_ref, rstd_ref, gmid_ref, own_ref, far_ref, out_ref = refs[pairs:]
    width = own_ref.shape[2]
    d_norm = None
    for pair in range(pairs):
        w = jnp.concatenate(
            [w_ref[t * width + pair * 128 : t * width + (pair + 1) * 128, :] for t in range(3)], 0
        )
        piece = dot(dqkv_refs[pair][0], w, 0, 0)
        d_norm = piece if d_norm is None else d_norm + piece
    w = d_norm * row_of(pack_ref, GAIN1)
    hat = hat_ref[0].astype(F32)
    back = rstd_ref[0] * (
        w - jnp.mean(w, -1, keepdims=True) - hat * jnp.mean(w * hat, -1, keepdims=True)
    )
    out_ref[...] = (gmid_ref[0].astype(F32) + back).astype(BF)
    split_halves(out_ref, core_ref[0], own_ref, far_ref)


def clear_rest(ref, used):
    if ref.shape[0] > used:
        ref[used:, :] = jnp.zeros((ref.shape[0] - used, ref.shape[1]), ref.dtype)


def write_halves(core, flat_ref, parts, kept_ref, sent_ref):
    start = at = 0
    for size in parts:
        half = size // 2
        mine = pl.multiple_of(start + core * half, 16)
        other = pl.multiple_of(start + (1 - core) * half, 16)
        kept_ref[at : at + half, :] = flat_ref[pl.ds(mine, half), :]
        sent_ref[at : at + half, :] = flat_ref[pl.ds(other, half), :]
        start += size
        at += half


def pack_kernel(core_ref, *refs, pairs, parts):
    grad_refs = refs[:pairs]
    sums_refs = refs[pairs : 2 * pairs]
    out_grad_ref, bias_ref, kept_ref, sent_ref, flat_ref = refs[2 * pairs :]
    width = out_grad_ref.shape[0]
    for pair in range(pairs):
        flat_ref[pair * width : (pair + 1) * width, :] = grad_refs[pair][...].astype(BF)
    at = pairs * width
    flat_ref[at : at + width, :] = out_grad_ref[...].astype(BF)
    at += width
    clear_rest(flat_ref, at)
    vectors = [bias_ref[0:8, :]]
    rows = lax.broadcasted_iota(jnp.int32, (8, width), 0)
    extra = jnp.zeros((8, width), F32)
    for pair in range(pairs):
        extra = jnp.where(rows == pair, sums_refs[pair][0:1, :], extra)
    vectors.append(extra)
    flat_ref[at : at + 16, :] = jnp.concatenate(vectors, 0).astype(BF)
    write_halves(core_ref[0], flat_ref, parts, kept_ref, sent_ref)


def swap_cores(value):
    return lax.ppermute(value, "blk", [(0, 1), (1, 0)])


def stages(count, first=4):
    out = []
    stride = 1
    while stride < count:
        left = count // stride
        radix = first if not out and left % first == 0 else 4 if left % 4 == 0 else 2
        out.append((stride, radix))
        stride *= radix
    return out


def shifted(value, stage, steps, axis="samp"):
    stride, radix = stage
    count = lax.axis_size(axis)
    pairs = []
    for source in range(count):
        digit = (source // stride) % radix
        pairs.append((source, source + ((digit + steps) % radix - digit) * stride))
    return lax.ppermute(value, axis, pairs)


def small_call(kernel, args, outs, scratch=(), ties=(), name=None):
    def body(*refs):
        kernel(*refs[: len(args)], *refs[len(args) + len(ties) :])

    vmem = pl.BlockSpec(memory_space=pltpu.VMEM)
    size = lambda a: math.prod(a.shape) * jnp.dtype(a.dtype).itemsize
    total = sum(size(a) for a in (*args[1:], *outs)) + sum(
        math.prod(a.shape) * jnp.dtype(a.dtype).itemsize for a in scratch
    )
    return pl.pallas_call(
        body,
        in_specs=[
            pl.BlockSpec(memory_space=pltpu.SMEM),
            *[vmem] * (len(args) - 1),
            *[pl.BlockSpec(memory_space=pl.ANY)] * len(ties),
        ],
        out_specs=[vmem] * len(outs),
        out_shape=outs,
        scratch_shapes=list(scratch),
        compiler_params=pltpu.CompilerParams(vmem_limit_bytes=2 * total + 4 * 2**20),
        name=name,
    )(*args, *ties)


def spread_kernel(info_ref, *refs, groups):
    inputs = sum(count for count, *_ in groups)
    outputs = sum(radix for _, _, radix, _ in groups)
    at, out_at = 0, inputs
    for g, (count, rows, radix, slot) in enumerate(groups):
        part = slice(rows[0], rows[1])
        total = refs[at][part, :].astype(F32)
        for k in range(1, count):
            total = total + refs[at + k][part, :].astype(F32)
        if radix == 1:
            refs[out_at][...] = total.astype(BF)
        else:
            total_ref = refs[inputs + outputs + g]
            total_ref[...] = total.astype(BF)
            size = total_ref.shape[0] // radix
            for k in range(radix):
                start = lax.rem(info_ref[slot] + k, radix) * size
                refs[out_at + k][...] = total_ref[pl.ds(pl.multiple_of(start, 16), size), :]
        at += count
        out_at += radix


def collect_kernel(info_ref, *refs, groups):
    at, out_at = 0, sum(groups)
    for count in groups:
        size = refs[at].shape[0]
        for k in range(count):
            refs[out_at][k * size : (k + 1) * size, :] = refs[at + k][...]
        at += count
        out_at += 1


CORE = 0


class Layout:
    def __init__(self, count, chains):
        self.base = stages(count)
        self.count = count
        self.columns = {"core": 0}
        table = np.zeros((2 * count, 1 + len(self.base)), np.int32)
        for device in range(2 * count):
            samp = device // 2
            table[device, 0] = device % 2
            for i, (stride, radix) in enumerate(self.base):
                table[device, 1 + i] = (samp // stride) % radix
        tables = [table]
        self.place_at = []
        width = table.shape[1]
        for parts in chains:
            rows = np.stack([self.places(device, parts) for device in range(2 * count)])
            self.place_at.append(width)
            width += rows.shape[1]
            tables.append(rows)
        self.table = np.concatenate(tables, 1).astype(np.int32)

    def orders(self, parts):
        n = len(self.base)
        return [[(i + k) % n for k in range(n)] for i in range(len(parts))]

    def places(self, device, parts):
        core, samp = device % 2, device // 2
        out = []
        start = 0
        for size, order in zip(parts, self.orders(parts)):
            half = size // 2
            offsets = np.array([start + core * half, start + (1 - core) * half])
            unit = half
            for index in order:
                stride, radix = self.base[index]
                unit //= radix
                digit = ((samp // stride) % radix - np.arange(radix)) % radix
                offsets = (offsets[:, None] + (digit * unit)[None, :]).reshape(-1)
            out.append(offsets)
            start += size
        return np.concatenate(out)


class Chain:
    def __init__(self, layout, index, parts, info):
        self.layout = layout
        self.place = layout.place_at[index]
        self.parts = parts
        self.info = info
        self.orders = layout.orders(parts)
        self.rounds = len(layout.base)

    def start(self, kept, sent):
        self.pending = [[kept, swap_cores(sent)]]
        return kept

    def scatter(self, level, ties=()):
        groups, args = [], [self.info]
        at = 0
        last = level == self.rounds
        for part, order in enumerate(self.orders):
            arrays = self.pending[0] if level == 0 else self.pending[part]
            size = self.parts[part] // 2 if level == 0 else arrays[0].shape[0]
            rows = (at, at + size)
            if level == 0:
                at += size
            radix = 1 if last else self.layout.base[order[level]][1]
            slot = 0 if last else 1 + order[level]
            groups.append((len(arrays), rows, radix, slot))
            args += arrays
        width = args[1].shape[1]
        outs = []
        for _, rows, radix, _ in groups:
            outs += [jax.ShapeDtypeStruct(((rows[1] - rows[0]) // radix, width), BF)] * radix
        scratch = [pltpu.VMEM((rows[1] - rows[0], width), BF) for _, rows, _, _ in groups]
        result = small_call(
            functools.partial(spread_kernel, groups=tuple(groups)), args, outs, scratch, ties, "spread"
        )
        pieces = []
        at = 0
        for _, _, radix, _ in groups:
            pieces.append(list(result[at : at + radix]))
            at += radix
        if last:
            self.values = [group[0] for group in pieces]
            return self.gather(level - 1)
        self.pending = [
            [group[0]]
            + [shifted(group[k], self.layout.base[order[level]], k) for k in range(1, len(group))]
            for group, order in zip(pieces, self.orders)
        ]
        return pieces[0][0]

    def gather(self, level):
        self.pending = []
        for value, order in zip(self.values, self.orders):
            stage = self.layout.base[order[level]]
            self.pending.append([value] + [shifted(value, stage, k) for k in range(1, stage[1])])
        return self.values[0]

    def collect(self, level, ties=()):
        groups = tuple(len(group) for group in self.pending)
        args = [self.info] + [piece for group in self.pending for piece in group]
        outs = [
            jax.ShapeDtypeStruct((len(group) * group[0].shape[0], group[0].shape[1]), BF)
            for group in self.pending
        ]
        self.values = small_call(
            functools.partial(collect_kernel, groups=groups), args, outs, (), ties, "collect"
        )
        if level > 0:
            return self.gather(level - 1)
        self.pending = [[value, swap_cores(value)] for value in self.values]
        return self.values[0]

    def arrived(self):
        return [side for group in self.pending for side in group]

    def units(self):
        return [size // 2 // self.layout.count for size in self.parts]


def restore(info_ref, flat_ref, refs, units, chunks, at):
    for part, unit in enumerate(units):
        for side in range(2):
            ref = refs[2 * part + side]

            def body(i, carry, ref=ref, unit=unit, at=at):
                start = pl.multiple_of(info_ref[at + i], 16)
                source = pl.multiple_of(i * unit, 16)
                flat_ref[pl.ds(start, unit), :] = ref[pl.ds(source, unit), :]
                return carry

            lax.fori_loop(0, chunks, body, 0)
            at += chunks


def finish_mlp_kernel(info_ref, *refs, units, chunks, at):
    ins = 2 * len(units)
    g_refs = refs[:ins]
    fc2_ref, turned_ref, flat_ref = refs[ins:]
    restore(info_ref, flat_ref, g_refs, units, chunks, at)
    hidden, width = fc2_ref.shape
    fc2_ref[...] = flat_ref[:hidden, :].astype(F32)
    for j in range(hidden // width):
        rows = slice(hidden + j * width, hidden + (j + 1) * width)
        turned_ref[:, j * width : (j + 1) * width] = flat_ref[rows, :].astype(F32)


def finish_kernel(info_ref, *refs, units, chunks, at, pairs):
    ins = 2 * len(units)
    g_refs = refs[:ins]
    pack_ref, w_qkv_ref, w1_ref, turned_ref = refs[ins : ins + 4]
    w_qkv_grad_ref, w_out_grad_ref, fc1_grad_ref, vector_ref, flat_ref = refs[ins + 4 :]
    restore(info_ref, flat_ref, g_refs, units, chunks, at)
    width = w_out_grad_ref.shape[0]
    hidden = fc1_grad_ref.shape[1]
    blocks = hidden // width
    at = pairs * width
    w_out_grad_ref[...] = flat_ref[at : at + width, :].astype(F32)
    vectors = flat_ref[at + width : at + width + 16, :].astype(F32)
    columns = pack_ref[0:8, :].T
    gain = jnp.zeros((width, 1), F32)
    shift = jnp.zeros((width, 1), F32)
    for pair in range(pairs):
        hats = flat_ref[pair * width : (pair + 1) * width, :].astype(F32).T
        sums = vectors[8 + pair : 9 + pair]
        result = hats * columns[:, GAIN1 : GAIN1 + 1] + columns[:, SHIFT1 : SHIFT1 + 1] * sums
        for t in range(3):
            cols = slice(t * width + pair * 128, t * width + (pair + 1) * 128)
            own = slice(t * 128, (t + 1) * 128)
            w_qkv_grad_ref[:, cols] = result[:, own]
            w = w_qkv_ref[:, cols].astype(F32)
            gain = gain + jnp.sum(w * hats[:, own], -1, keepdims=True)
            shift = shift + jnp.sum(w * sums[:, own], -1, keepdims=True)
    gain2 = jnp.zeros((width, 1), F32)
    shift2 = jnp.zeros((width, 1), F32)
    for j in range(blocks):
        cols = slice(j * width, (j + 1) * width)
        hats = turned_ref[:, cols]
        sums = vectors[j : j + 1]
        fc1_grad_ref[:, cols] = hats * columns[:, GAIN2 : GAIN2 + 1] + columns[:, SHIFT2 : SHIFT2 + 1] * sums
        w = w1_ref[:, cols].astype(F32)
        gain2 = gain2 + jnp.sum(w * hats, -1, keepdims=True)
        shift2 = shift2 + jnp.sum(w * sums, -1, keepdims=True)
    vector_ref[0:16, :] = vectors
    lane = lax.broadcasted_iota(jnp.int32, (width, 128), 1)
    wide = jnp.where(lane == 0, gain, jnp.where(lane == 1, shift, jnp.where(lane == 2, gain2, shift2)))
    vector_ref[16:24, :] = wide.T[0:8]


def pad_rows(count, unit):
    return -(-count // unit) * unit


def per_device(
    tokens, view_count, norm1_gain, norm1_bias, w_qkv, qv_bias, w_out, out_bias,
    norm2_gain, norm2_bias, w_fc1, fc1_bias, w_fc2, fc2_bias, cot_tokens, cot_cls,
):
    core = lax.axis_index("blk")
    cores = lax.axis_size("blk")
    count = lax.axis_size("samp")
    samples, half, width = tokens.shape
    local = samples // cores
    rows = half * cores
    hidden = w_fc1.shape[1]
    blocks = hidden // width
    heads = width // HEAD_DIM
    pairs = heads // 2
    sds = jax.ShapeDtypeStruct

    unit = 32 * count

    def split_rows(used):
        total = pad_rows(used, unit)
        second = pad_rows(total // 3, unit)
        return [max(total - second, unit), second]

    parts1 = split_rows(2 * hidden)
    parts2 = split_rows(pairs * 384 + width + 16)
    layout = Layout(count, (parts1, parts2))
    device = lax.axis_index("samp") * cores + core
    info = lax.dynamic_index_in_dim(jnp.asarray(layout.table), device, 0, keepdims=False)

    theirs = (1 - core) * local
    far_tokens = swap_cores(lax.dynamic_slice_in_dim(tokens, theirs, local, 0))
    far_cot = swap_cores(lax.dynamic_slice_in_dim(cot_tokens, theirs, local, 0))

    w_turned = w_qkv.T
    pack = jnp.concatenate(
        (
            norm1_gain, norm1_bias, norm2_gain, norm2_bias, out_bias, fc2_bias, qv_bias, fc1_bias,
            jnp.zeros(((8 - blocks) * width,), BF),
        )
    ).astype(F32).reshape(16, width)

    vmem = pl.BlockSpec(memory_space=pltpu.VMEM)
    half_spec = lambda f: pl.BlockSpec((1, half, width), f)
    own_map = lambda s, b, *_: (b[CORE] * local + s, 0, 0)
    by_sample = lambda s, *_: (s, 0, 0)
    rows_spec = pl.BlockSpec((1, rows, width), by_sample)
    turned_spec = pl.BlockSpec((1, width, rows), by_sample)
    rstd_spec = pl.BlockSpec((1, rows, 1), by_sample)
    hidden_spec = pl.BlockSpec((1, rows, hidden), by_sample)
    eight_spec = pl.BlockSpec((1, 8, rows), by_sample)

    def big_call(kernel, prefetch, args, in_specs, outs, out_specs, scratch=(), ties=(), grid=(local,), name=None):
        n = len(prefetch) + len(args)

        def body(*refs):
            kernel(*refs[:n], *refs[n + len(ties) :])

        return pl.pallas_call(
            body,
            grid_spec=pltpu.PrefetchScalarGridSpec(
                num_scalar_prefetch=len(prefetch),
                grid=grid,
                in_specs=[*in_specs, *[pl.BlockSpec(memory_space=pl.ANY)] * len(ties)],
                out_specs=out_specs,
                scratch_shapes=list(scratch),
            ),
            out_shape=outs,
            compiler_params=params(("arbitrary",) * len(grid)),
            name=name,
        )(*prefetch, *args, *ties)

    x_full, hat1, rstd1, qkv, cls_rows, stats = big_call(
        project_kernel,
        (info, view_count),
        (tokens, far_tokens, w_turned, pack, w_out, w_fc1, w_fc2, cot_cls),
        [half_spec(own_map), half_spec(by_sample), *[vmem] * 6],
        [
            sds((local, rows, width), BF),
            sds((local, rows, width), BF),
            sds((local, rows, 1), F32),
            sds((local, 3 * width, rows), BF),
            sds((8, width), F32),
            sds((8, width), F32),
        ],
        [
            rows_spec, rows_spec, rstd_spec,
            pl.BlockSpec((1, 3 * width, rows), by_sample), vmem, vmem,
        ],
        [pltpu.VMEM((8, width), F32), pltpu.VMEM((8, width), F32), pltpu.VMEM((rows, width), BF)],
        name="project",
    )

    both = ("samp", "blk")
    first, *later = stages(count * cores, 8)
    stat_parts = [stats] + [shifted(stats, first, k, both) for k in range(1, first[1])]

    qkv_specs = lambda p: [
        pl.BlockSpec((1, 128, rows), lambda s, *a, t=t: (s, t * pairs + p(*a), 0)) for t in range(3)
    ]
    powers, totals, mixed = big_call(
        attention_kernel,
        (info, view_count),
        (qkv, qkv, qkv),
        qkv_specs(lambda p, *_: p),
        [
            sds((local, heads, rows, rows), BF),
            sds((local, 8, rows), F32),
            sds((local, width, rows), BF),
        ],
        [
            pl.BlockSpec((1, 2, rows, rows), lambda s, p, *_: (s, p, 0, 0)),
            pl.BlockSpec((1, 8, rows), lambda s, p, *_: (s, 0, 0)),
            pl.BlockSpec((1, 128, rows), lambda s, p, *_: (s, p, 0)),
        ],
        grid=(local, pairs),
        name="attention",
    )

    def add_kernel(info_ref, *refs):
        total = refs[0][...]
        for ref in refs[1:-1]:
            total = total + ref[...]
        refs[-1][...] = total

    tie = totals
    for stage in later:
        stats = small_call(
            add_kernel, [info, *stat_parts], [sds((8, width), F32)], (), (tie,), "add"
        )[0]
        stat_parts = [stats] + [shifted(stats, stage, k, both) for k in range(1, stage[1])]
        tie = stats

    hat2, rstd2, act, slope, out_own, out_far = big_call(
        mlp_kernel,
        (info,),
        (x_full, mixed, w_out, w_fc1, w_fc2, pack),
        [rows_spec, turned_spec, vmem, vmem, vmem, vmem],
        [
            sds((local, rows, width), BF),
            sds((local, rows, 1), F32),
            sds((local, rows, hidden), BF),
            sds((local, rows, hidden), BF),
            sds((samples, half, width), BF),
            sds((local, half, width), BF),
        ],
        [rows_spec, rstd_spec, hidden_spec, hidden_spec, half_spec(own_map), half_spec(by_sample)],
        [pltpu.VMEM((rows, width), BF)],
        (tie,),
        name="mlp",
    )
    out_came = swap_cores(out_far)

    d_pre, d_cls, cls_norm, biases, kept1, sent1 = big_call(
        functools.partial(
            mlp_grads_kernel, samples=local * cores * count, parts=parts1, peers=len(stat_parts)
        ),
        (info,),
        (cot_tokens, far_cot, cls_rows, cot_cls, *stat_parts, act, slope, hat2, w_fc2),
        [
            half_spec(own_map), half_spec(by_sample), vmem, vmem, *[vmem] * len(stat_parts),
            hidden_spec, hidden_spec, rows_spec, vmem,
        ],
        [
            sds((local, rows, hidden), BF),
            sds((8, width), F32),
            sds((local, width), BF),
            sds((8, width), F32),
            sds((sum(parts1) // 2, width), BF),
            sds((sum(parts1) // 2, width), BF),
        ],
        [hidden_spec, vmem, vmem, vmem, vmem, vmem],
        [
            pltpu.VMEM((rows, width), F32),
            pltpu.VMEM((hidden, width), F32),
            pltpu.VMEM((width, hidden), F32),
            pltpu.VMEM((sum(parts1), width), BF),
        ],
        name="mlp_grads",
    )
    chain1 = Chain(layout, 0, parts1, info)
    tie = chain1.start(kept1, sent1)

    g_mid, d_mix, inner, out_grad, biases = big_call(
        mlp_back_kernel,
        (info,),
        (cot_tokens, far_cot, d_cls, d_pre, hat2, rstd2, mixed, totals, biases, pack, w_fc1, w_out),
        [
            half_spec(own_map), half_spec(by_sample), vmem, hidden_spec, rows_spec, rstd_spec,
            turned_spec, eight_spec, vmem, vmem, vmem, vmem,
        ],
        [
            sds((local, rows, width), BF),
            sds((local, width, rows), BF),
            sds((local, 8, rows), F32),
            sds((width, width), F32),
            sds((8, width), F32),
        ],
        [rows_spec, turned_spec, eight_spec, vmem, vmem],
        [pltpu.VMEM((rows, width), F32)],
        name="mlp_back",
    )

    steps = [functools.partial(chain1.scatter, level) for level in range(chain1.rounds + 1)]
    steps += [functools.partial(chain1.collect, level) for level in reversed(range(chain1.rounds))]
    done = inner
    d_parts, grads, sums = [], [], []
    for pair in range(pairs):
        tie = steps.pop(0)(ties=(done,))
        d_part, grad, total = big_call(
            functools.partial(attention_back_kernel, pair=pair),
            (info, view_count),
            (qkv, qkv, qkv, powers, d_mix, inner, hat1),
            [
                *qkv_specs(lambda *_, p=pair: p),
                pl.BlockSpec((1, 2, rows, rows), lambda s, *_, p=pair: (s, p, 0, 0)),
                pl.BlockSpec((1, 128, rows), lambda s, *_, p=pair: (s, p, 0)),
                eight_spec,
                rows_spec,
            ],
            [
                sds((local, 384, rows), BF),
                sds((384, width), F32),
                sds((8, 384), F32),
            ],
            [pl.BlockSpec((1, 384, rows), by_sample), vmem, vmem],
            (),
            (tie,),
            name="attention_back",
        )
        d_parts.append(d_part)
        grads.append(grad)
        sums.append(total)
        done = total

    tie = steps.pop(0)(ties=(done,))
    chain2 = Chain(layout, 1, parts2, info)
    kept2, sent2 = small_call(
        functools.partial(pack_kernel, pairs=pairs, parts=parts2),
        (info, *grads, *sums, out_grad, biases),
        [sds((sum(parts2) // 2, width), BF)] * 2,
        [pltpu.VMEM((sum(parts2), width), BF)],
        (tie,),
        name="pack",
    )
    tie2 = chain2.start(kept2, sent2)
    steps2 = [functools.partial(chain2.scatter, level) for level in range(chain2.rounds + 1)]
    steps2 += [functools.partial(chain2.collect, level) for level in reversed(range(chain2.rounds))]

    grad_own, grad_far = big_call(
        functools.partial(tokens_back_kernel, pairs=pairs),
        (info,),
        (*d_parts, w_turned, pack, hat1, rstd1, g_mid),
        [
            *[pl.BlockSpec((1, 384, rows), by_sample)] * pairs,
            vmem, vmem, rows_spec, rstd_spec, rows_spec,
        ],
        [sds((samples, half, width), BF), sds((local, half, width), BF)],
        [half_spec(own_map), half_spec(by_sample)],
        [pltpu.VMEM((rows, width), BF)],
        (tie, tie2),
        name="tokens_back",
    )
    grad_came = swap_cores(grad_far)
    done = grad_far
    while steps or steps2:
        ties = (done,)
        if steps2:
            steps2.pop(0)(ties=ties)
        if steps:
            steps.pop(0)(ties=ties)
        done = info

    def finish(kernel, chain, args, outs, **options):
        return small_call(
            functools.partial(
                kernel, units=chain.units(), chunks=count, at=chain.place, **options
            ),
            (info, *chain.arrived(), *args),
            [sds(shape, F32) for shape in outs],
            [pltpu.VMEM((sum(chain.parts), width), BF)],
            name="finish",
        )

    grad_w_fc2, turned = finish(finish_mlp_kernel, chain1, (), ((hidden, width), (width, hidden)))
    grad_w_qkv, grad_w_out, grad_w_fc1, vectors = finish(
        finish_kernel, chain2, (pack, w_qkv, w_fc1, turned),
        ((width, 3 * width), (width, width), (width, hidden), (24, width)), pairs=pairs,
    )
    column_sums = vectors[8 : 8 + pairs].reshape(pairs, 3, 128)
    grad_qv_bias = jnp.concatenate((column_sums[:, 0].reshape(-1), column_sums[:, 2].reshape(-1)))
    tokens_out = lax.dynamic_update_slice_in_dim(out_own, out_came, theirs, 0)
    grad_tokens = lax.dynamic_update_slice_in_dim(grad_own, grad_came, theirs, 0)
    return (
        tokens_out, cls_norm, grad_tokens, vectors[16], vectors[17], grad_w_qkv, grad_qv_bias,
        grad_w_out, vectors[blocks + 1], vectors[18], vectors[19], grad_w_fc1,
        vectors[:blocks].reshape(hidden), grad_w_fc2, vectors[blocks],
    )


def solution(mesh):
    split = P("samp", "blk", None)
    classes = P(("samp", "blk"), None)
    return jax.shard_map(
        per_device,
        mesh=mesh,
        in_specs=(split, P("samp"), *([P()] * 12), split, classes),
        out_specs=(split, classes, split, *([P()] * 12)),
        check_vma=False,
    )
```

```python
import functools
import math

import jax
import jax.numpy as jnp
import numpy as np
from jax import lax
from jax.experimental import pallas as pl
from jax.experimental.pallas import tpu as pltpu
from jax.sharding import PartitionSpec as P

HEAD_DIM = 64
VIEW_ROWS = 196
NORM_EPS = 1e-06
CLS_EPS = 1e-05
MASKED = -1e30
LOG2E = math.log2(math.e)
LN2 = math.log(2.0)
SCALE = HEAD_DIM ** (-0.5)
SUM_LOW = 1e-15
SUM_HIGH = 1e15
BF = jnp.bfloat16
F32 = jnp.float32
VMEM_BYTES = 60 * 2**20
CORE = 0
BACK_SETS = (1, 1, 1)


def dot(a, b, ca, cb):
    return lax.dot_general(a, b, (((ca,), (cb,)), ((), ())), preferred_element_type=F32)


def norm_parts(values):
    centre = jnp.mean(values, -1, keepdims=True)
    offset = values - centre
    rstd = lax.rsqrt(jnp.mean(offset * offset, -1, keepdims=True) + NORM_EPS)
    return offset * rstd, rstd


def gelu_cdf(values):
    return 0.5 + 0.5 * lax.erf(values * (0.5**0.5))


def params(semantics):
    return pltpu.CompilerParams(dimension_semantics=semantics, vmem_limit_bytes=VMEM_BYTES)


def whole(shape):
    return pl.BlockSpec(shape, lambda *_: (0,) * len(shape))


def key_counts(rows):
    views = (rows - 1) // VIEW_ROWS
    return [(v, min(rows, -(-(1 + VIEW_ROWS * v) // 16) * 16)) for v in range(1, views + 1)]


GAIN1, SHIFT1, GAIN2, SHIFT2, OUT_BIAS, FC2_BIAS, QV_BIAS, FC1_BIAS = 0, 1, 2, 3, 4, 5, 6, 8


def row_of(pack_ref, index):
    return pack_ref[index : index + 1, :]


def place_halves(target_ref, core, own, far):
    half = own.shape[0]
    target_ref[pl.ds(pl.multiple_of(core * half, 16), half), :] = own
    target_ref[pl.ds(pl.multiple_of((1 - core) * half, 16), half), :] = far


def split_halves(source_ref, core, own_ref, far_ref):
    half = own_ref.shape[1]
    own_ref[0] = source_ref[pl.ds(pl.multiple_of(core * half, 16), half), :]
    far_ref[0] = source_ref[pl.ds(pl.multiple_of((1 - core) * half, 16), half), :]


def project_kernel(
    blk_ref, views_ref, own_ref, far_ref, w_ref, pack_ref, w_out_ref, w1_ref, w2_ref, cot_ref,
    hat_ref, qkv_ref, cls_ref, stat_ref, mix_ref, first_ref, full_ref,
):
    step = pl.program_id(0)
    rows = hat_ref.shape[1]
    width = own_ref.shape[2]
    place_halves(full_ref, blk_ref[0], own_ref[0], far_ref[0])
    values = full_ref[...].astype(F32)
    hat, _ = norm_parts(values)
    hat_ref[0] = hat.astype(BF)
    normed = (hat * row_of(pack_ref, GAIN1) + row_of(pack_ref, SHIFT1)).astype(BF)
    columns = pack_ref[0:8, :].T
    for third in range(3):
        part = pl.ds(third * width, width)
        piece = dot(w_ref[part, :], normed, 1, 1)
        if third == 0:
            piece = (piece + columns[:, QV_BIAS : QV_BIAS + 1]) * (SCALE * LOG2E)
        if third == 2:
            piece = piece + columns[:, QV_BIAS + 1 : QV_BIAS + 2]
        qkv_ref[0, part, :] = piece.astype(BF)

    lead = qkv_ref[0, pl.ds(0, width), :128].astype(F32).T[0:1, :]
    head_of = lax.broadcasted_iota(jnp.int32, (8, width), 1) // HEAD_DIM
    pick = head_of == lax.broadcasted_iota(jnp.int32, (8, width), 0)
    queries = jnp.where(pick, lead, 0.0).astype(BF)
    scores = dot(queries, qkv_ref[0, pl.ds(width, width), :], 1, 0)
    limit = 1 + VIEW_ROWS * views_ref[blk_ref[CORE] * pl.num_programs(0) + step]
    place = lax.broadcasted_iota(jnp.int32, (8, rows), 1)
    scores = jnp.where(place < limit, scores, MASKED)
    powers = jnp.exp2(scores - jnp.max(scores, -1, keepdims=True))
    chances = (powers / jnp.sum(powers, -1, keepdims=True)).astype(BF)
    mixed = dot(chances, qkv_ref[0, pl.ds(2 * width, width), :], 1, 1)
    mix_ref[pl.ds(step, 1), :] = jnp.sum(jnp.where(pick, mixed, 0.0), 0, keepdims=True)
    first_ref[pl.ds(step, 1), :] = values[0:1, :]

    @pl.when(step == pl.num_programs(0) - 1)
    def _():
        branch = dot(mix_ref[...].astype(BF), w_out_ref[...], 1, 0) + row_of(pack_ref, OUT_BIAS)
        middle = first_ref[...] + branch
        normed2 = norm_parts(middle)[0] * row_of(pack_ref, GAIN2) + row_of(pack_ref, SHIFT2)
        normed2 = normed2.astype(BF)
        output = middle + row_of(pack_ref, FC2_BIAS)
        for j in range(w1_ref.shape[1] // width):
            cols = slice(j * width, (j + 1) * width)
            pre = dot(normed2, w1_ref[:, cols], 1, 0) + row_of(pack_ref, FC1_BIAS + j)
            act = (pre * gelu_cdf(pre)).astype(BF)
            output = output + dot(act, w2_ref[cols, :], 1, 0)
        cls_ref[...] = output
        count = cot_ref.shape[0]
        cls = output[:count]
        cot = cot_ref[...].astype(F32)
        stat_ref[...] = jnp.zeros_like(stat_ref)
        for k, term in enumerate((cls, cls * cls, cot, cot * cls)):
            stat_ref[k : k + 1, :] = jnp.sum(term, 0, keepdims=True)


def masked_tail(scores, main, limit):
    place = main + lax.broadcasted_iota(jnp.int32, scores.shape, 0)
    return jnp.where(place < limit, scores, MASKED)


def attention_kernel(
    core_ref, views_ref, q_ref, k_ref, v_ref, sum_ref, top_ref, plain_ref, att_ref, pow_ref
):
    sample = pl.program_id(0)
    pair = pl.program_id(1)
    rows = q_ref.shape[2]
    views = views_ref[core_ref[CORE] * pl.num_programs(0) + sample]
    limit = 1 + VIEW_ROWS * views
    ones = jnp.ones((16, rows), BF)

    def heads():
        for h in range(2):
            yield h, pl.ds(h * HEAD_DIM, HEAD_DIM)

    def store(h, mixed):
        total = mixed[HEAD_DIM : HEAD_DIM + 1]
        sum_ref[0, pl.ds(2 * pair + h, 1), :] = total
        att_ref[0, h * HEAD_DIM : (h + 1) * HEAD_DIM, :] = (mixed[:HEAD_DIM] / total).astype(BF)

    for count, keys in key_counts(rows):

        @pl.when(views == count)
        def _(keys=keys):
            main = keys - 16
            for h, lanes in heads():
                scores = dot(k_ref[0, lanes, :keys], q_ref[0, lanes, :], 0, 0)
                pow_ref[h, :main, :] = jnp.exp2(scores[:main]).astype(BF)
                tail = masked_tail(scores[main:], main, limit)
                pow_ref[h, main:keys, :] = jnp.exp2(tail).astype(BF)
                left = jnp.concatenate((v_ref[0, lanes, :keys], ones[:, :keys]), 0)
                store(h, dot(left, pow_ref[h, :keys, :], 1, 0))

    first = sum_ref[0, pl.ds(2 * pair, 1), :]
    second = sum_ref[0, pl.ds(2 * pair + 1, 1), :]
    least = jnp.min(jnp.minimum(first, second))
    plain = (least > SUM_LOW) & (jnp.max(jnp.maximum(first, second)) < SUM_HIGH)
    plain_ref[sample, pair] = plain.astype(jnp.int32)

    @pl.when(jnp.logical_not(plain))
    def _():
        for h, lanes in heads():
            scores = dot(k_ref[0, lanes, :], q_ref[0, lanes, :], 0, 0)
            scores = masked_tail(scores, 0, limit)
            top = jnp.max(scores, 0, keepdims=True)
            top_ref[0, pl.ds(2 * pair + h, 1), :] = top
            pow_ref[h] = jnp.exp2(scores - top).astype(BF)
            left = jnp.concatenate((v_ref[0, lanes, :], ones), 0)
            store(h, dot(left, pow_ref[h], 1, 0))


def layer_kernel(
    core_ref, x_own_ref, x_far_ref, own_ref, far_ref, att_ref, sum_ref, cls_ref, cot_ref, *refs,
    samples, parts, peers
):
    stat_refs = refs[:peers]
    w_out_ref, w1_ref, w2_ref, pack_ref = refs[peers : peers + 4]
    (
        out_own_ref, out_far_ref, gmid_ref, dmix_ref, inner_ref, out_grad_ref, norm_ref, bias_ref,
        kept_ref, sent_ref,
    ) = refs[peers + 4 : peers + 14]
    full_ref, g_ref, act_ref, dpre_ref, dcls_ref, acc2_ref, acc1_ref, flat_ref = refs[peers + 14 :]
    step = pl.program_id(0)
    width = own_ref.shape[2]
    hidden = w2_ref.shape[0]
    blocks = hidden // width

    @pl.when(step == 0)
    def _():
        acc2_ref[...] = jnp.zeros_like(acc2_ref)
        acc1_ref[...] = jnp.zeros_like(acc1_ref)
        bias_ref[...] = jnp.zeros_like(bias_ref)
        out_grad_ref[...] = jnp.zeros_like(out_grad_ref)
        stats = stat_refs[0][...]
        for other in stat_refs[1:]:
            stats = stats + other[...]
        local = cot_ref.shape[0]
        cls = cls_ref[...][:local]
        cot = cot_ref[...].astype(F32)
        mean = stats[0:1] / samples
        scale = lax.rsqrt(stats[1:2] / samples - mean * mean + CLS_EPS)
        hat = (cls - mean) * scale
        norm_ref[...] = hat.astype(BF)
        cross = scale * (stats[3:4] - mean * stats[2:3])
        dcls_ref[...] = jnp.zeros_like(dcls_ref)
        dcls_ref[:local, :] = scale * (cot - stats[2:3] / samples - hat * (cross / samples))

    place_halves(full_ref, core_ref[CORE], x_own_ref[0], x_far_ref[0])
    place_halves(g_ref, core_ref[CORE], own_ref[0].astype(F32), far_ref[0].astype(F32))
    g_ref[0:1, :] = g_ref[0:1, :] + dcls_ref[pl.ds(step, 1), :]
    g_mlp = g_ref[...].astype(BF)
    bias_ref[blocks : blocks + 1, :] += jnp.sum(g_mlp.astype(F32), 0, keepdims=True)

    branch = dot(att_ref[0], w_out_ref[...], 0, 0) + row_of(pack_ref, OUT_BIAS)
    middle = full_ref[...].astype(F32) + branch
    hat, rstd = norm_parts(middle)
    normed = (hat * row_of(pack_ref, GAIN2) + row_of(pack_ref, SHIFT2)).astype(BF)
    hat_low = hat.astype(BF)
    for j in range(blocks):
        cols = slice(j * width, (j + 1) * width)
        pre = dot(normed, w1_ref[:, cols], 1, 0) + row_of(pack_ref, FC1_BIAS + j)
        d_act = dot(g_mlp, w2_ref[cols, :], 1, 1)
        cdf = gelu_cdf(pre)
        bell = jnp.exp(pre * pre * -0.5) * (1.0 / math.sqrt(2.0 * math.pi))
        act = (pre * cdf).astype(BF)
        act_ref[:, cols] = act
        d_pre = d_act * (cdf + pre * bell)
        bias_ref[j : j + 1, :] += jnp.sum(d_pre, 0, keepdims=True)
        d_pre = d_pre.astype(BF)
        dpre_ref[:, cols] = d_pre
        acc1_ref[:, cols] += dot(hat_low, d_pre, 0, 0)
        acc2_ref[cols, :] += dot(act, g_mlp, 0, 0)
    output = middle + dot(act_ref[...], w2_ref[...], 1, 0) + row_of(pack_ref, FC2_BIAS)
    full_ref[...] = output.astype(BF)
    split_halves(full_ref, core_ref[CORE], out_own_ref, out_far_ref)

    d_norm = dot(dpre_ref[...], w1_ref[...], 1, 1)
    u = d_norm * row_of(pack_ref, GAIN2)
    g_mid = g_ref[...] + rstd * (
        u - jnp.mean(u, -1, keepdims=True) - hat * jnp.mean(u * hat, -1, keepdims=True)
    )
    g_attn = g_mid.astype(BF)
    gmid_ref[0] = g_attn
    out_grad_ref[...] += dot(att_ref[0], g_attn, 1, 0)
    bias_ref[blocks + 1 : blocks + 2, :] += jnp.sum(g_attn.astype(F32), 0, keepdims=True)
    d_mix = dot(w_out_ref[...], g_attn, 1, 1)
    for h in range(width // HEAD_DIM):
        part = slice(h * HEAD_DIM, (h + 1) * HEAD_DIM)
        piece = d_mix[part] / sum_ref[0, h : h + 1, :]
        dmix_ref[0, part, :] = piece.astype(BF)
        inner_ref[0, h : h + 1, :] = jnp.sum(piece * att_ref[0, part, :].astype(F32), 0, keepdims=True)

    @pl.when(step == pl.num_programs(0) - 1)
    def _():
        flat_ref[:hidden, :] = acc2_ref[...].astype(BF)
        for j in range(blocks):
            rows = slice(hidden + j * width, hidden + (j + 1) * width)
            flat_ref[rows, :] = acc1_ref[:, j * width : (j + 1) * width].astype(BF)
        clear_rest(flat_ref, 2 * hidden)
        write_halves(core_ref[CORE], flat_ref, parts, kept_ref, sent_ref)


def attention_back_kernel(
    core_ref, views_ref, plain_ref, q_ref, k_ref, v_ref, top_ref, dmix_ref, inner_ref, hat_ref,
    dqkv_ref, grad_ref, sums_ref, pow_ref, *, first
):
    sample = pl.program_id(1)
    pair = first + pl.program_id(0)
    rows = hat_ref.shape[1]
    views = views_ref[core_ref[CORE] * pl.num_programs(1) + sample]
    limit = 1 + VIEW_ROWS * views
    plain = plain_ref[sample, pair] == 1

    def back(h, keys):
        lanes = slice(h * HEAD_DIM, (h + 1) * HEAD_DIM)
        d_mix = dmix_ref[0, lanes, :]
        powers = pow_ref[h, :keys, :]
        d_weights = dot(v_ref[0, lanes, :keys], d_mix, 0, 0)
        inner = inner_ref[0, pl.ds(2 * pair + h, 1), :]
        d_scores = (powers.astype(F32) * (d_weights - inner)).astype(BF)
        d_query = dot(k_ref[0, lanes, :keys], d_scores, 1, 0) * SCALE
        d_key = dot(q_ref[0, lanes, :], d_scores, 1, 1) * LN2
        d_value = dot(d_mix, powers, 1, 1)
        base = h * HEAD_DIM
        dqkv_ref[0, 0, base : base + HEAD_DIM, :] = d_query.astype(BF)
        dqkv_ref[0, 0, 128 + base : 128 + base + HEAD_DIM, :keys] = d_key.astype(BF)
        dqkv_ref[0, 0, 256 + base : 256 + base + HEAD_DIM, :keys] = d_value.astype(BF)
        if keys < rows:
            blank = jnp.zeros((HEAD_DIM, rows - keys), BF)
            dqkv_ref[0, 0, 128 + base : 128 + base + HEAD_DIM, keys:] = blank
            dqkv_ref[0, 0, 256 + base : 256 + base + HEAD_DIM, keys:] = blank

    for count, keys in key_counts(rows):

        @pl.when((views == count) & plain)
        def _(keys=keys):
            main = keys - 16
            for h in range(2):
                lanes = slice(h * HEAD_DIM, (h + 1) * HEAD_DIM)
                scores = dot(k_ref[0, lanes, :keys], q_ref[0, lanes, :], 0, 0)
                pow_ref[h, :main, :] = jnp.exp2(scores[:main]).astype(BF)
                tail = masked_tail(scores[main:], main, limit)
                pow_ref[h, main:keys, :] = jnp.exp2(tail).astype(BF)
                back(h, keys)

    @pl.when(jnp.logical_not(plain))
    def _():
        for h in range(2):
            lanes = slice(h * HEAD_DIM, (h + 1) * HEAD_DIM)
            scores = masked_tail(dot(k_ref[0, lanes, :], q_ref[0, lanes, :], 0, 0), 0, limit)
            top = top_ref[0, pl.ds(2 * pair + h, 1), :]
            pow_ref[h] = jnp.exp2(scores - top).astype(BF)
            back(h, rows)

    @pl.when(sample == 0)
    def _():
        grad_ref[...] = jnp.zeros_like(grad_ref)
        sums_ref[...] = jnp.zeros_like(sums_ref)

    d_part = dqkv_ref[0, 0]
    grad_ref[0] += dot(d_part, hat_ref[0], 1, 0)
    sums_ref[0] += dot(jnp.ones((16, rows), BF), d_part, 1, 1)[:8]


def tokens_back_kernel(core_ref, *refs, pairs, sets):
    dqkv_refs = refs[:sets]
    w_ref, pack_ref, x_own_ref, x_far_ref, gmid_ref, own_ref, far_ref, out_ref = refs[sets:]
    width = own_ref.shape[2]
    place_halves(out_ref, core_ref[CORE], x_own_ref[0], x_far_ref[0])
    hat, rstd = norm_parts(out_ref[...].astype(F32))
    d_norm = None
    pair = 0
    for ref in dqkv_refs:
        for k in range(ref.shape[0]):
            w = jnp.concatenate(
                [w_ref[t * width + pair * 128 : t * width + (pair + 1) * 128, :] for t in range(3)], 0
            )
            piece = dot(ref[k, 0], w, 0, 0)
            d_norm = piece if d_norm is None else d_norm + piece
            pair += 1
    w = d_norm * row_of(pack_ref, GAIN1)
    back = rstd * (w - jnp.mean(w, -1, keepdims=True) - hat * jnp.mean(w * hat, -1, keepdims=True))
    out_ref[...] = (gmid_ref[0].astype(F32) + back).astype(BF)
    split_halves(out_ref, core_ref[CORE], own_ref, far_ref)


def clear_rest(ref, used):
    if ref.shape[0] > used:
        ref[used:, :] = jnp.zeros((ref.shape[0] - used, ref.shape[1]), ref.dtype)


def write_halves(core, flat_ref, parts, kept_ref, sent_ref):
    start = at = 0
    for size in parts:
        half = size // 2
        mine = pl.multiple_of(start + core * half, 16)
        other = pl.multiple_of(start + (1 - core) * half, 16)
        kept_ref[at : at + half, :] = flat_ref[pl.ds(mine, half), :]
        sent_ref[at : at + half, :] = flat_ref[pl.ds(other, half), :]
        start += size
        at += half


def pack_kernel(core_ref, *refs, sets, parts):
    grad_refs = refs[:sets]
    sums_refs = refs[sets : 2 * sets]
    out_grad_ref, bias_ref, kept_ref, sent_ref, flat_ref = refs[2 * sets :]
    width = out_grad_ref.shape[0]
    rows = lax.broadcasted_iota(jnp.int32, (8, width), 0)
    extra = jnp.zeros((8, width), F32)
    pair = 0
    for grad_ref, sums_ref in zip(grad_refs, sums_refs):
        for k in range(grad_ref.shape[0]):
            flat_ref[pair * width : (pair + 1) * width, :] = grad_ref[k].astype(BF)
            extra = jnp.where(rows == pair, sums_ref[k][0:1, :], extra)
            pair += 1
    at = pair * width
    flat_ref[at : at + width, :] = out_grad_ref[...].astype(BF)
    at += width
    clear_rest(flat_ref, at)
    flat_ref[at : at + 16, :] = jnp.concatenate((bias_ref[0:8, :], extra), 0).astype(BF)
    write_halves(core_ref[CORE], flat_ref, parts, kept_ref, sent_ref)


def swap_cores(value):
    return lax.ppermute(value, "blk", [(0, 1), (1, 0)])


def stages(count, first=4):
    out = []
    stride = 1
    while stride < count:
        left = count // stride
        radix = first if not out and left % first == 0 else 4 if left % 4 == 0 else 2
        out.append((stride, radix))
        stride *= radix
    return out


def shifted(value, stage, steps, axis="samp"):
    stride, radix = stage
    count = lax.axis_size(axis)
    pairs = []
    for source in range(count):
        digit = (source // stride) % radix
        pairs.append((source, source + ((digit + steps) % radix - digit) * stride))
    return lax.ppermute(value, axis, pairs)


def small_call(kernel, args, outs, scratch=(), ties=(), name=None):
    def body(*refs):
        kernel(*refs[: len(args)], *refs[len(args) + len(ties) :])

    vmem = pl.BlockSpec(memory_space=pltpu.VMEM)
    size = lambda a: math.prod(a.shape) * jnp.dtype(a.dtype).itemsize
    total = sum(size(a) for a in (*args[1:], *outs)) + sum(
        math.prod(a.shape) * jnp.dtype(a.dtype).itemsize for a in scratch
    )
    return pl.pallas_call(
        body,
        in_specs=[
            pl.BlockSpec(memory_space=pltpu.SMEM),
            *[vmem] * (len(args) - 1),
            *[pl.BlockSpec(memory_space=pl.ANY)] * len(ties),
        ],
        out_specs=[vmem] * len(outs),
        out_shape=outs,
        scratch_shapes=list(scratch),
        compiler_params=pltpu.CompilerParams(vmem_limit_bytes=2 * total + 4 * 2**20),
        name=name,
    )(*args, *ties)


def spread_kernel(info_ref, *refs, groups):
    inputs = sum(count for count, *_ in groups)
    outputs = sum(radix for _, _, radix, _ in groups)
    at, out_at = 0, inputs
    for g, (count, rows, radix, slot) in enumerate(groups):
        part = slice(rows[0], rows[1])
        total = refs[at][part, :].astype(F32)
        for k in range(1, count):
            total = total + refs[at + k][part, :].astype(F32)
        if radix == 1:
            refs[out_at][...] = total.astype(BF)
        else:
            total_ref = refs[inputs + outputs + g]
            total_ref[...] = total.astype(BF)
            size = total_ref.shape[0] // radix
            for k in range(radix):
                start = lax.rem(info_ref[slot] + k, radix) * size
                refs[out_at + k][...] = total_ref[pl.ds(pl.multiple_of(start, 16), size), :]
        at += count
        out_at += radix


def collect_kernel(info_ref, *refs, groups):
    at, out_at = 0, sum(groups)
    for count in groups:
        size = refs[at].shape[0]
        for k in range(count):
            refs[out_at][k * size : (k + 1) * size, :] = refs[at + k][...]
        at += count
        out_at += 1


class Layout:
    def __init__(self, count, chains):
        self.base = stages(count)
        self.count = count
        self.columns = {"core": 0}
        table = np.zeros((2 * count, 1 + len(self.base)), np.int32)
        for device in range(2 * count):
            samp = device // 2
            table[device, 0] = device % 2
            for i, (stride, radix) in enumerate(self.base):
                table[device, 1 + i] = (samp // stride) % radix
        tables = [table]
        self.place_at = []
        width = table.shape[1]
        for parts in chains:
            rows = np.stack([self.places(device, parts) for device in range(2 * count)])
            self.place_at.append(width)
            width += rows.shape[1]
            tables.append(rows)
        self.table = np.concatenate(tables, 1).astype(np.int32)

    def orders(self, parts):
        n = len(self.base)
        return [[(i + k) % n for k in range(n)] for i in range(len(parts))]

    def places(self, device, parts):
        core, samp = device % 2, device // 2
        out = []
        start = 0
        for size, order in zip(parts, self.orders(parts)):
            half = size // 2
            offsets = np.array([start + core * half, start + (1 - core) * half])
            unit = half
            for index in order:
                stride, radix = self.base[index]
                unit //= radix
                digit = ((samp // stride) % radix - np.arange(radix)) % radix
                offsets = (offsets[:, None] + (digit * unit)[None, :]).reshape(-1)
            out.append(offsets)
            start += size
        return np.concatenate(out)


class Chain:
    def __init__(self, layout, index, parts, info):
        self.layout = layout
        self.place = layout.place_at[index]
        self.parts = parts
        self.info = info
        self.orders = layout.orders(parts)
        self.rounds = len(layout.base)

    def start(self, kept, sent):
        self.pending = [[kept, swap_cores(sent)]]
        return kept

    def scatter(self, level, ties=()):
        groups, args = [], [self.info]
        at = 0
        last = level == self.rounds
        for part, order in enumerate(self.orders):
            arrays = self.pending[0] if level == 0 else self.pending[part]
            size = self.parts[part] // 2 if level == 0 else arrays[0].shape[0]
            rows = (at, at + size)
            if level == 0:
                at += size
            radix = 1 if last else self.layout.base[order[level]][1]
            slot = 0 if last else 1 + order[level]
            groups.append((len(arrays), rows, radix, slot))
            args += arrays
        width = args[1].shape[1]
        outs = []
        for _, rows, radix, _ in groups:
            outs += [jax.ShapeDtypeStruct(((rows[1] - rows[0]) // radix, width), BF)] * radix
        scratch = [pltpu.VMEM((rows[1] - rows[0], width), BF) for _, rows, _, _ in groups]
        result = small_call(
            functools.partial(spread_kernel, groups=tuple(groups)), args, outs, scratch, ties, "spread"
        )
        pieces = []
        at = 0
        for _, _, radix, _ in groups:
            pieces.append(list(result[at : at + radix]))
            at += radix
        if last:
            self.values = [group[0] for group in pieces]
            return self.gather(level - 1)
        self.pending = [
            [group[0]]
            + [shifted(group[k], self.layout.base[order[level]], k) for k in range(1, len(group))]
            for group, order in zip(pieces, self.orders)
        ]
        return pieces[0][0]

    def gather(self, level):
        self.pending = []
        for value, order in zip(self.values, self.orders):
            stage = self.layout.base[order[level]]
            self.pending.append([value] + [shifted(value, stage, k) for k in range(1, stage[1])])
        return self.values[0]

    def collect(self, level, ties=()):
        groups = tuple(len(group) for group in self.pending)
        args = [self.info] + [piece for group in self.pending for piece in group]
        outs = [
            jax.ShapeDtypeStruct((len(group) * group[0].shape[0], group[0].shape[1]), BF)
            for group in self.pending
        ]
        self.values = small_call(
            functools.partial(collect_kernel, groups=groups), args, outs, (), ties, "collect"
        )
        if level > 0:
            return self.gather(level - 1)
        self.pending = [[value, swap_cores(value)] for value in self.values]
        return self.values[0]

    def arrived(self):
        return [side for group in self.pending for side in group]

    def units(self):
        return [size // 2 // self.layout.count for size in self.parts]


def restore(info_ref, flat_ref, refs, units, chunks, at):
    for part, unit in enumerate(units):
        for side in range(2):
            ref = refs[2 * part + side]

            def body(i, carry, ref=ref, unit=unit, at=at):
                start = pl.multiple_of(info_ref[at + i], 16)
                source = pl.multiple_of(i * unit, 16)
                flat_ref[pl.ds(start, unit), :] = ref[pl.ds(source, unit), :]
                return carry

            lax.fori_loop(0, chunks, body, 0)
            at += chunks


def finish_mlp_kernel(info_ref, *refs, units, chunks, at):
    ins = 2 * len(units)
    g_refs = refs[:ins]
    fc2_ref, turned_ref, flat_ref = refs[ins:]
    restore(info_ref, flat_ref, g_refs, units, chunks, at)
    hidden, width = fc2_ref.shape
    fc2_ref[...] = flat_ref[:hidden, :].astype(F32)
    for j in range(hidden // width):
        rows = slice(hidden + j * width, hidden + (j + 1) * width)
        turned_ref[:, j * width : (j + 1) * width] = flat_ref[rows, :].astype(F32)


def finish_kernel(info_ref, *refs, units, chunks, at, pairs):
    ins = 2 * len(units)
    g_refs = refs[:ins]
    pack_ref, w_qkv_ref, w1_ref, turned_ref = refs[ins : ins + 4]
    w_qkv_grad_ref, w_out_grad_ref, fc1_grad_ref, vector_ref, flat_ref = refs[ins + 4 :]
    restore(info_ref, flat_ref, g_refs, units, chunks, at)
    width = w_out_grad_ref.shape[0]
    hidden = fc1_grad_ref.shape[1]
    blocks = hidden // width
    at = pairs * width
    w_out_grad_ref[...] = flat_ref[at : at + width, :].astype(F32)
    vectors = flat_ref[at + width : at + width + 16, :].astype(F32)
    columns = pack_ref[0:8, :].T
    gain = jnp.zeros((width, 1), F32)
    shift = jnp.zeros((width, 1), F32)
    for pair in range(pairs):
        hats = flat_ref[pair * width : (pair + 1) * width, :].astype(F32).T
        sums = vectors[8 + pair : 9 + pair]
        result = hats * columns[:, GAIN1 : GAIN1 + 1] + columns[:, SHIFT1 : SHIFT1 + 1] * sums
        for t in range(3):
            cols = slice(t * width + pair * 128, t * width + (pair + 1) * 128)
            own = slice(t * 128, (t + 1) * 128)
            w_qkv_grad_ref[:, cols] = result[:, own]
            w = w_qkv_ref[:, cols].astype(F32)
            gain = gain + jnp.sum(w * hats[:, own], -1, keepdims=True)
            shift = shift + jnp.sum(w * sums[:, own], -1, keepdims=True)
    gain2 = jnp.zeros((width, 1), F32)
    shift2 = jnp.zeros((width, 1), F32)
    for j in range(blocks):
        cols = slice(j * width, (j + 1) * width)
        hats = turned_ref[:, cols]
        sums = vectors[j : j + 1]
        fc1_grad_ref[:, cols] = hats * columns[:, GAIN2 : GAIN2 + 1] + columns[:, SHIFT2 : SHIFT2 + 1] * sums
        w = w1_ref[:, cols].astype(F32)
        gain2 = gain2 + jnp.sum(w * hats, -1, keepdims=True)
        shift2 = shift2 + jnp.sum(w * sums, -1, keepdims=True)
    vector_ref[0:16, :] = vectors
    lane = lax.broadcasted_iota(jnp.int32, (width, 128), 1)
    wide = jnp.where(lane == 0, gain, jnp.where(lane == 1, shift, jnp.where(lane == 2, gain2, shift2)))
    vector_ref[16:24, :] = wide.T[0:8]


def pad_rows(count, unit):
    return -(-count // unit) * unit


def per_device(
    tokens, view_count, norm1_gain, norm1_bias, w_qkv, qv_bias, w_out, out_bias,
    norm2_gain, norm2_bias, w_fc1, fc1_bias, w_fc2, fc2_bias, cot_tokens, cot_cls,
):
    core = lax.axis_index("blk")
    cores = lax.axis_size("blk")
    count = lax.axis_size("samp")
    samples, half, width = tokens.shape
    local = samples // cores
    rows = half * cores
    hidden = w_fc1.shape[1]
    blocks = hidden // width
    heads = width // HEAD_DIM
    pairs = heads // 2
    sds = jax.ShapeDtypeStruct

    unit = 32 * count
    parts1 = [pad_rows(2 * hidden, unit)]
    parts2 = [pad_rows(pairs * 384 + width + 16, unit)]
    layout = Layout(count, (parts1, parts2))
    device = lax.axis_index("samp") * cores + core
    info = lax.dynamic_index_in_dim(jnp.asarray(layout.table), device, 0, keepdims=False)

    theirs = (1 - core) * local
    far_tokens = swap_cores(lax.dynamic_slice_in_dim(tokens, theirs, local, 0))
    far_cot = swap_cores(lax.dynamic_slice_in_dim(cot_tokens, theirs, local, 0))

    w_turned = w_qkv.T
    pack = jnp.concatenate(
        (
            norm1_gain, norm1_bias, norm2_gain, norm2_bias, out_bias, fc2_bias, qv_bias, fc1_bias,
            jnp.zeros(((8 - blocks) * width,), BF),
        )
    ).astype(F32).reshape(16, width)

    vmem = pl.BlockSpec(memory_space=pltpu.VMEM)
    half_spec = lambda f: pl.BlockSpec((1, half, width), f)
    own_map = lambda s, b, *_: (b[CORE] * local + s, 0, 0)
    by_sample = lambda s, *_: (s, 0, 0)
    rows_spec = pl.BlockSpec((1, rows, width), by_sample)
    turned_spec = pl.BlockSpec((1, width, rows), by_sample)
    rstd_spec = pl.BlockSpec((1, rows, 1), by_sample)
    hidden_spec = pl.BlockSpec((1, rows, hidden), by_sample)
    eight_spec = pl.BlockSpec((1, 8, rows), by_sample)

    def big_call(kernel, prefetch, args, in_specs, outs, out_specs, scratch=(), ties=(), grid=(local,), name=None):
        n = len(prefetch) + len(args)

        def body(*refs):
            kernel(*refs[:n], *refs[n + len(ties) :])

        return pl.pallas_call(
            body,
            grid_spec=pltpu.PrefetchScalarGridSpec(
                num_scalar_prefetch=len(prefetch),
                grid=grid,
                in_specs=[*in_specs, *[pl.BlockSpec(memory_space=pl.ANY)] * len(ties)],
                out_specs=out_specs,
                scratch_shapes=list(scratch),
            ),
            out_shape=outs,
            compiler_params=params(("arbitrary",) * len(grid)),
            name=name,
        )(*prefetch, *args, *ties)

    hat1, qkv, cls_rows, stats = big_call(
        project_kernel,
        (info, view_count),
        (tokens, far_tokens, w_turned, pack, w_out, w_fc1, w_fc2, cot_cls),
        [half_spec(own_map), half_spec(by_sample), *[vmem] * 6],
        [
            sds((local, rows, width), BF),
            sds((local, 3 * width, rows), BF),
            sds((8, width), F32),
            sds((8, width), F32),
        ],
        [rows_spec, pl.BlockSpec((1, 3 * width, rows), by_sample), vmem, vmem],
        [pltpu.VMEM((8, width), F32), pltpu.VMEM((8, width), F32), pltpu.VMEM((rows, width), BF)],
        name="project",
    )

    def add_kernel(info_ref, *refs):
        total = refs[0][...]
        for ref in refs[1:-1]:
            total = total + ref[...]
        refs[-1][...] = total

    first, *later = stages(count)
    stat_parts = [stats] + [shifted(stats, first, k) for k in range(1, first[1])]

    qkv_specs = lambda f: [
        pl.BlockSpec((1, 128, rows), lambda *a, t=t: (f(*a)[0], t * pairs + f(*a)[1], 0))
        for t in range(3)
    ]
    totals, tops, plain, mixed = big_call(
        attention_kernel,
        (info, view_count),
        (qkv, qkv, qkv),
        qkv_specs(lambda s, p, *_: (s, p)),
        [
            sds((local, 8, rows), F32),
            sds((local, 8, rows), F32),
            sds((local, pairs), jnp.int32),
            sds((local, width, rows), BF),
        ],
        [
            pl.BlockSpec((1, 8, rows), lambda s, p, *_: (s, 0, 0)),
            pl.BlockSpec((1, 8, rows), lambda s, p, *_: (s, 0, 0)),
            pl.BlockSpec(memory_space=pltpu.SMEM),
            pl.BlockSpec((1, 128, rows), lambda s, p, *_: (s, p, 0)),
        ],
        [pltpu.VMEM((2, rows, rows), BF)],
        grid=(local, pairs),
        name="attention",
    )

    tie = totals
    for send in [functools.partial(lambda v, stage: [shifted(v, stage, k) for k in range(1, stage[1])], stage=stage) for stage in later] + [lambda v: [swap_cores(v)]]:
        stats = small_call(
            add_kernel, [info, *stat_parts], [sds((8, width), F32)], (), (tie,), "add"
        )[0]
        stat_parts = [stats] + send(stats)
        tie = stats

    tokens_out_own, out_far, g_mid, d_mix, inner, out_grad, cls_norm, biases, kept1, sent1 = big_call(
        functools.partial(
            layer_kernel, samples=local * cores * count, parts=parts1, peers=len(stat_parts)
        ),
        (info,),
        (
            tokens, far_tokens, cot_tokens, far_cot, mixed, totals, cls_rows, cot_cls, *stat_parts,
            w_out, w_fc1, w_fc2, pack,
        ),
        [
            half_spec(own_map), half_spec(by_sample), half_spec(own_map), half_spec(by_sample),
            turned_spec, eight_spec, vmem, vmem, *[vmem] * len(stat_parts), vmem, vmem, vmem, vmem,
        ],
        [
            sds((samples, half, width), BF),
            sds((local, half, width), BF),
            sds((local, rows, width), BF),
            sds((local, width, rows), BF),
            sds((local, 8, rows), F32),
            sds((width, width), F32),
            sds((local, width), BF),
            sds((8, width), F32),
            sds((sum(parts1) // 2, width), BF),
            sds((sum(parts1) // 2, width), BF),
        ],
        [
            half_spec(own_map), half_spec(by_sample), rows_spec, turned_spec, eight_spec,
            vmem, vmem, vmem, vmem, vmem,
        ],
        [
            pltpu.VMEM((rows, width), BF),
            pltpu.VMEM((rows, width), F32),
            pltpu.VMEM((rows, hidden), BF),
            pltpu.VMEM((rows, hidden), BF),
            pltpu.VMEM((8, width), F32),
            pltpu.VMEM((hidden, width), F32),
            pltpu.VMEM((width, hidden), F32),
            pltpu.VMEM((sum(parts1), width), BF),
        ],
        name="layer",
    )
    out_own = tokens_out_own
    out_came = swap_cores(out_far)
    chain1 = Chain(layout, 0, parts1, info)
    chain1.start(kept1, sent1)

    def attention_back(first, number, ties):
        place = lambda p, s, *_: (s, first + p)
        return big_call(
            functools.partial(attention_back_kernel, first=first),
            (info, view_count, plain),
            (qkv, qkv, qkv, tops, d_mix, inner, hat1),
            [
                *qkv_specs(place),
                pl.BlockSpec((1, 8, rows), lambda p, s, *_: (s, 0, 0)),
                pl.BlockSpec((1, 128, rows), lambda p, s, *_: (s, first + p, 0)),
                pl.BlockSpec((1, 8, rows), lambda p, s, *_: (s, 0, 0)),
                pl.BlockSpec((1, rows, width), lambda p, s, *_: (s, 0, 0)),
            ],
            [
                sds((number, local, 384, rows), BF),
                sds((number, 384, width), F32),
                sds((number, 8, 384), F32),
            ],
            [
                pl.BlockSpec((1, 1, 384, rows), lambda p, s, *_: (p, s, 0, 0)),
                pl.BlockSpec((1, 384, width), lambda p, s, *_: (p, 0, 0)),
                pl.BlockSpec((1, 8, 384), lambda p, s, *_: (p, 0, 0)),
            ],
            [pltpu.VMEM((2, rows, rows), BF)],
            ties,
            grid=(number, local),
            name="attention_back",
        )

    steps = [functools.partial(chain1.scatter, level) for level in range(chain1.rounds + 1)]
    steps += [functools.partial(chain1.collect, level) for level in reversed(range(chain1.rounds))]
    done, tie = inner, inner
    d_parts, grads, sums = [], [], []
    at = 0
    for number in BACK_SETS:
        d_part, grad, total = attention_back(at, number, (tie,))
        at += number
        d_parts.append(d_part)
        grads.append(grad)
        sums.append(total)
        done = total
        tie = steps.pop(0)(ties=(done,))

    chain2 = Chain(layout, 1, parts2, info)
    kept2, sent2 = small_call(
        functools.partial(pack_kernel, sets=len(grads), parts=parts2),
        (info, *grads, *sums, out_grad, biases),
        [sds((sum(parts2) // 2, width), BF)] * 2,
        [pltpu.VMEM((sum(parts2), width), BF)],
        (tie,),
        name="pack",
    )
    tie2 = chain2.start(kept2, sent2)
    steps2 = [functools.partial(chain2.scatter, level) for level in range(chain2.rounds + 1)]
    steps2 += [functools.partial(chain2.collect, level) for level in reversed(range(chain2.rounds))]

    grad_own, grad_far = big_call(
        functools.partial(tokens_back_kernel, pairs=pairs, sets=len(d_parts)),
        (info,),
        (*d_parts, w_turned, pack, tokens, far_tokens, g_mid),
        [
            *[
                pl.BlockSpec((d.shape[0], 1, 384, rows), lambda s, *_: (0, s, 0, 0)) for d in d_parts
            ],
            vmem, vmem, half_spec(own_map), half_spec(by_sample), rows_spec,
        ],
        [sds((samples, half, width), BF), sds((local, half, width), BF)],
        [half_spec(own_map), half_spec(by_sample)],
        [pltpu.VMEM((rows, width), BF)],
        (tie, tie2),
        name="tokens_back",
    )
    grad_came = swap_cores(grad_far)
    done = grad_far
    while steps or steps2:
        ties = (done,)
        if steps:
            steps.pop(0)(ties=ties)
        if steps2:
            steps2.pop(0)(ties=ties)
        done = info

    def finish(kernel, chain, args, outs, **options):
        return small_call(
            functools.partial(
                kernel, units=chain.units(), chunks=count, at=chain.place, **options
            ),
            (info, *chain.arrived(), *args),
            [sds(shape, F32) for shape in outs],
            [pltpu.VMEM((sum(chain.parts), width), BF)],
            name="finish",
        )

    grad_w_fc2, turned = finish(finish_mlp_kernel, chain1, (), ((hidden, width), (width, hidden)))
    grad_w_qkv, grad_w_out, grad_w_fc1, vectors = finish(
        finish_kernel, chain2, (pack, w_qkv, w_fc1, turned),
        ((width, 3 * width), (width, width), (width, hidden), (24, width)), pairs=pairs,
    )
    column_sums = vectors[8 : 8 + pairs].reshape(pairs, 3, 128)
    grad_qv_bias = jnp.concatenate((column_sums[:, 0].reshape(-1), column_sums[:, 2].reshape(-1)))
    tokens_out = lax.dynamic_update_slice_in_dim(out_own, out_came, theirs, 0)
    grad_tokens = lax.dynamic_update_slice_in_dim(grad_own, grad_came, theirs, 0)
    return (
        tokens_out, cls_norm, grad_tokens, vectors[16], vectors[17], grad_w_qkv, grad_qv_bias,
        grad_w_out, vectors[blocks + 1], vectors[18], vectors[19], grad_w_fc1,
        vectors[:blocks].reshape(hidden), grad_w_fc2, vectors[blocks],
    )


def solution(mesh):
    split = P("samp", "blk", None)
    classes = P(("samp", "blk"), None)
    return jax.shard_map(
        per_device,
        mesh=mesh,
        in_specs=(split, P("samp"), *([P()] * 12), split, classes),
        out_specs=(split, classes, split, *([P()] * 12)),
        check_vma=False,
    )
```

```python
import functools
import math

import jax
import jax.numpy as jnp
import numpy as np
from jax import lax
from jax.experimental import pallas as pl
from jax.experimental.pallas import tpu as pltpu
from jax.sharding import PartitionSpec as P

HEAD_DIM = 64
VIEW_ROWS = 196
NORM_EPS = 1e-06
CLS_EPS = 1e-05
MASKED = -1e30
LOG2E = math.log2(math.e)
LN2 = math.log(2.0)
SCALE = HEAD_DIM ** (-0.5)
SUM_LOW = 1e-15
SUM_HIGH = 1e15
BF = jnp.bfloat16
F32 = jnp.float32
VMEM_BYTES = 60 * 2**20
CORE = 0
EXTRA = 16


def dot(a, b, ca, cb):
    return lax.dot_general(a, b, (((ca,), (cb,)), ((), ())), preferred_element_type=F32)


def norm_parts(values):
    centre = jnp.mean(values, -1, keepdims=True)
    offset = values - centre
    rstd = lax.rsqrt(jnp.mean(offset * offset, -1, keepdims=True) + NORM_EPS)
    return offset * rstd, rstd


def gelu_cdf(values):
    return 0.5 + 0.5 * lax.erf(values * (0.5**0.5))


def params(semantics):
    return pltpu.CompilerParams(dimension_semantics=semantics, vmem_limit_bytes=VMEM_BYTES)


def whole(shape):
    return pl.BlockSpec(shape, lambda *_: (0,) * len(shape))


def key_counts(rows):
    views = (rows - 1) // VIEW_ROWS
    return [(v, min(rows, -(-(1 + VIEW_ROWS * v) // 16) * 16)) for v in range(1, views + 1)]


GAIN1, SHIFT1, GAIN2, SHIFT2, OUT_BIAS, FC2_BIAS, QV_BIAS, FC1_BIAS = 0, 1, 2, 3, 4, 5, 6, 8


def row_of(pack_ref, index):
    return pack_ref[index : index + 1, :]


def place_halves(target_ref, core, own, far):
    half = own.shape[0]
    target_ref[pl.ds(pl.multiple_of(core * half, 16), half), :] = own
    target_ref[pl.ds(pl.multiple_of((1 - core) * half, 16), half), :] = far


def split_halves(source_ref, core, own_ref, far_ref):
    half = own_ref.shape[1]
    own_ref[0] = source_ref[pl.ds(pl.multiple_of(core * half, 16), half), :]
    far_ref[0] = source_ref[pl.ds(pl.multiple_of((1 - core) * half, 16), half), :]


def project_kernel(
    blk_ref, views_ref, own_ref, far_ref, w_ref, pack_ref, w_out_ref, w1_ref, w2_ref, cot_ref,
    hat_ref, qkv_ref, cls_ref, stat_ref, mix_ref, first_ref, full_ref,
):
    step = pl.program_id(0)
    rows = hat_ref.shape[1]
    width = own_ref.shape[2]
    place_halves(full_ref, blk_ref[0], own_ref[0], far_ref[0])
    values = full_ref[...].astype(F32)
    hat, _ = norm_parts(values)
    hat_ref[0] = hat.astype(BF)
    normed = (hat * row_of(pack_ref, GAIN1) + row_of(pack_ref, SHIFT1)).astype(BF)
    columns = pack_ref[0:8, :].T
    for third in range(3):
        part = pl.ds(third * width, width)
        piece = dot(w_ref[part, :], normed, 1, 1)
        if third == 0:
            piece = (piece + columns[:, QV_BIAS : QV_BIAS + 1]) * (SCALE * LOG2E)
        if third == 2:
            piece = piece + columns[:, QV_BIAS + 1 : QV_BIAS + 2]
        qkv_ref[0, part, :] = piece.astype(BF)

    lead = qkv_ref[0, pl.ds(0, width), :128].astype(F32).T[0:1, :]
    head_of = lax.broadcasted_iota(jnp.int32, (8, width), 1) // HEAD_DIM
    pick = head_of == lax.broadcasted_iota(jnp.int32, (8, width), 0)
    queries = jnp.where(pick, lead, 0.0).astype(BF)
    scores = dot(queries, qkv_ref[0, pl.ds(width, width), :], 1, 0)
    limit = 1 + VIEW_ROWS * views_ref[blk_ref[CORE] * pl.num_programs(0) + step]
    place = lax.broadcasted_iota(jnp.int32, (8, rows), 1)
    scores = jnp.where(place < limit, scores, MASKED)
    powers = jnp.exp2(scores - jnp.max(scores, -1, keepdims=True))
    chances = (powers / jnp.sum(powers, -1, keepdims=True)).astype(BF)
    mixed = dot(chances, qkv_ref[0, pl.ds(2 * width, width), :], 1, 1)
    mix_ref[pl.ds(step, 1), :] = jnp.sum(jnp.where(pick, mixed, 0.0), 0, keepdims=True)
    first_ref[pl.ds(step, 1), :] = values[0:1, :]

    @pl.when(step == pl.num_programs(0) - 1)
    def _():
        branch = dot(mix_ref[...].astype(BF), w_out_ref[...], 1, 0) + row_of(pack_ref, OUT_BIAS)
        middle = first_ref[...] + branch
        normed2 = norm_parts(middle)[0] * row_of(pack_ref, GAIN2) + row_of(pack_ref, SHIFT2)
        normed2 = normed2.astype(BF)
        output = middle + row_of(pack_ref, FC2_BIAS)
        for j in range(w1_ref.shape[1] // width):
            cols = slice(j * width, (j + 1) * width)
            pre = dot(normed2, w1_ref[:, cols], 1, 0) + row_of(pack_ref, FC1_BIAS + j)
            act = (pre * gelu_cdf(pre)).astype(BF)
            output = output + dot(act, w2_ref[cols, :], 1, 0)
        cls_ref[...] = output
        count = cot_ref.shape[0]
        cls = output[:count]
        cot = cot_ref[...].astype(F32)
        stat_ref[...] = jnp.zeros_like(stat_ref)
        for k, term in enumerate((cls, cls * cls, cot, cot * cls)):
            stat_ref[k : k + 1, :] = jnp.sum(term, 0, keepdims=True)


def masked_tail(scores, main, limit):
    place = main + lax.broadcasted_iota(jnp.int32, scores.shape, 0)
    return jnp.where(place < limit, scores, MASKED)


def attention_kernel(
    core_ref, views_ref, qkv_ref, sum_ref, top_ref, plain_ref, att_ref, pow_ref
):
    sample = pl.program_id(0)
    rows = qkv_ref.shape[2]
    width = att_ref.shape[1]
    heads = width // HEAD_DIM
    views = views_ref[core_ref[CORE] * pl.num_programs(0) + sample]
    limit = 1 + VIEW_ROWS * views
    ones = jnp.ones((16, rows), BF)

    def store(h, mixed):
        total = mixed[HEAD_DIM : HEAD_DIM + 1]
        sum_ref[0, h : h + 1, :] = total
        att_ref[0, h * HEAD_DIM : (h + 1) * HEAD_DIM, :] = (mixed[:HEAD_DIM] * (1.0 / total)).astype(BF)

    sum_ref[0, heads:8, :] = jnp.ones((8 - heads, rows), F32)
    for count, keys in key_counts(rows):

        @pl.when(views == count)
        def _(keys=keys):
            main = keys - 16
            for h in range(heads):
                query, key, value = head_parts(qkv_ref, h, width, keys)
                slot = h % pow_ref.shape[0]
                scores = dot(key, query, 0, 0)
                pow_ref[slot, :main, :] = jnp.exp2(scores[:main]).astype(BF)
                tail = masked_tail(scores[main:], main, limit)
                pow_ref[slot, main:keys, :] = jnp.exp2(tail).astype(BF)
                left = jnp.concatenate((value, ones[:, :keys]), 0)
                store(h, dot(left, pow_ref[slot, :keys, :], 1, 0))

    totals = sum_ref[0]
    plain = (jnp.min(totals) > SUM_LOW) & (jnp.max(totals) < SUM_HIGH)
    plain_ref[sample] = plain.astype(jnp.int32)

    @pl.when(jnp.logical_not(plain))
    def _():
        for h in range(heads):
            query, key, value = head_parts(qkv_ref, h, width, rows)
            slot = h % pow_ref.shape[0]
            scores = masked_tail(dot(key, query, 0, 0), 0, limit)
            top = jnp.max(scores, 0, keepdims=True)
            top_ref[0, h : h + 1, :] = top
            pow_ref[slot] = jnp.exp2(scores - top).astype(BF)
            left = jnp.concatenate((value, ones), 0)
            store(h, dot(left, pow_ref[slot], 1, 0))


def head_parts(qkv_ref, h, width, keys):
    part = lambda t: slice(t * width + h * HEAD_DIM, t * width + (h + 1) * HEAD_DIM)
    return qkv_ref[0, part(0), :], qkv_ref[0, part(1), :keys], qkv_ref[0, part(2), :keys]


def layer_kernel(
    core_ref, x_own_ref, x_far_ref, own_ref, far_ref, att_ref, sum_ref, cls_ref, cot_ref, *refs,
    samples, parts, peers
):
    stat_refs = refs[:peers]
    w_out_ref, w1_ref, w2_ref, pack_ref = refs[peers : peers + 4]
    (
        out_own_ref, out_far_ref, gmid_ref, dmix_ref, inner_ref, out_grad_ref, norm_ref, bias_ref,
        kept_ref, sent_ref,
    ) = refs[peers + 4 : peers + 14]
    full_ref, g_ref, act_ref, dpre_ref, dcls_ref, acc2_ref, acc1_ref, flat_ref = refs[peers + 14 :]
    step = pl.program_id(0)
    width = own_ref.shape[2]
    hidden = w2_ref.shape[0]
    blocks = hidden // width

    @pl.when(step == 0)
    def _():
        acc2_ref[...] = jnp.zeros_like(acc2_ref)
        acc1_ref[...] = jnp.zeros_like(acc1_ref)
        bias_ref[...] = jnp.zeros_like(bias_ref)
        out_grad_ref[...] = jnp.zeros_like(out_grad_ref)
        stats = stat_refs[0][...]
        for other in stat_refs[1:]:
            stats = stats + other[...]
        local = cot_ref.shape[0]
        cls = cls_ref[...][:local]
        cot = cot_ref[...].astype(F32)
        mean = stats[0:1] / samples
        scale = lax.rsqrt(stats[1:2] / samples - mean * mean + CLS_EPS)
        hat = (cls - mean) * scale
        norm_ref[...] = hat.astype(BF)
        cross = scale * (stats[3:4] - mean * stats[2:3])
        dcls_ref[...] = jnp.zeros_like(dcls_ref)
        dcls_ref[:local, :] = scale * (cot - stats[2:3] / samples - hat * (cross / samples))

    place_halves(full_ref, core_ref[CORE], x_own_ref[0], x_far_ref[0])
    place_halves(g_ref, core_ref[CORE], own_ref[0].astype(F32), far_ref[0].astype(F32))
    g_ref[0:1, :] = g_ref[0:1, :] + dcls_ref[pl.ds(step, 1), :]
    g_mlp = g_ref[...].astype(BF)
    bias_ref[blocks : blocks + 1, :] += jnp.sum(g_mlp.astype(F32), 0, keepdims=True)

    branch = dot(att_ref[0], w_out_ref[...], 0, 0) + row_of(pack_ref, OUT_BIAS)
    middle = full_ref[...].astype(F32) + branch
    hat, rstd = norm_parts(middle)
    normed = (hat * row_of(pack_ref, GAIN2) + row_of(pack_ref, SHIFT2)).astype(BF)
    hat_low = hat.astype(BF)
    for j in range(blocks):
        cols = slice(j * width, (j + 1) * width)
        pre = dot(normed, w1_ref[:, cols], 1, 0) + row_of(pack_ref, FC1_BIAS + j)
        d_act = dot(g_mlp, w2_ref[cols, :], 1, 1)
        cdf = gelu_cdf(pre)
        bell = jnp.exp2(pre * pre * (-0.5 * LOG2E) - 0.5 * math.log2(2.0 * math.pi))
        act_ref[:, cols] = (pre * cdf).astype(BF)
        d_pre = d_act * (cdf + pre * bell)
        bias_ref[j : j + 1, :] += jnp.sum(d_pre, 0, keepdims=True)
        dpre_ref[:, cols] = d_pre.astype(BF)
    acc1_ref[...] += dot(hat_low, dpre_ref[...], 0, 0)
    acc2_ref[...] += dot(act_ref[...], g_mlp, 0, 0)
    output = middle + dot(act_ref[...], w2_ref[...], 1, 0) + row_of(pack_ref, FC2_BIAS)
    full_ref[...] = output.astype(BF)
    split_halves(full_ref, core_ref[CORE], out_own_ref, out_far_ref)

    d_norm = dot(dpre_ref[...], w1_ref[...], 1, 1)
    u = d_norm * row_of(pack_ref, GAIN2)
    g_mid = g_ref[...] + rstd * (
        u - jnp.mean(u, -1, keepdims=True) - hat * jnp.mean(u * hat, -1, keepdims=True)
    )
    g_attn = g_mid.astype(BF)
    gmid_ref[0] = g_attn
    out_grad_ref[...] += dot(att_ref[0], g_attn, 1, 0)
    bias_ref[blocks + 1 : blocks + 2, :] += jnp.sum(g_attn.astype(F32), 0, keepdims=True)
    d_mix = dot(w_out_ref[...], g_attn, 1, 1)
    for h in range(width // HEAD_DIM):
        part = slice(h * HEAD_DIM, (h + 1) * HEAD_DIM)
        piece = d_mix[part] * (1.0 / sum_ref[0, h : h + 1, :])
        dmix_ref[0, part, :] = piece.astype(BF)
        inner_ref[0, h : h + 1, :] = jnp.sum(piece * att_ref[0, part, :].astype(F32), 0, keepdims=True)

    @pl.when(step == pl.num_programs(0) - 1)
    def _():
        flat_ref[:hidden, :] = acc2_ref[...].astype(BF)
        for j in range(blocks):
            rows = slice(hidden + j * width, hidden + (j + 1) * width)
            flat_ref[rows, :] = acc1_ref[:, j * width : (j + 1) * width].astype(BF)
        clear_rest(flat_ref, 2 * hidden)
        write_halves(core_ref[CORE], flat_ref, parts, kept_ref, sent_ref)


def attention_back_kernel(
    core_ref, views_ref, plain_ref, qkv_ref, top_ref, dmix_ref, inner_ref, hat_ref,
    dqkv_ref, grad_ref, sums_ref, pow_ref, *, sample, samples
):
    rows, width = hat_ref.shape[1:]
    heads = width // HEAD_DIM
    views = views_ref[core_ref[CORE] * samples + sample]
    limit = 1 + VIEW_ROWS * views
    plain = plain_ref[sample] == 1

    def back(h, parts, slot, keys):
        query, key, value = parts
        place = lambda t: slice(t * width + h * HEAD_DIM, t * width + (h + 1) * HEAD_DIM)
        d_mix = dmix_ref[0, place(0), :]
        powers = pow_ref[slot, :keys, :]
        d_weights = dot(value, d_mix, 0, 0)
        inner = inner_ref[0, h : h + 1, :]
        d_scores = (powers.astype(F32) * (d_weights - inner)).astype(BF)
        d_query = dot(key, d_scores, 1, 0) * SCALE
        d_key = dot(query, d_scores, 1, 1) * LN2
        d_value = dot(d_mix, powers, 1, 1)
        dqkv_ref[0, place(0), :] = d_query.astype(BF)
        dqkv_ref[0, place(1), :keys] = d_key.astype(BF)
        dqkv_ref[0, place(2), :keys] = d_value.astype(BF)
        if keys < rows:
            blank = jnp.zeros((HEAD_DIM, rows - keys), BF)
            dqkv_ref[0, place(1), keys:] = blank
            dqkv_ref[0, place(2), keys:] = blank

    for count, keys in key_counts(rows):

        @pl.when((views == count) & plain)
        def _(keys=keys):
            main = keys - 16
            for h in range(heads):
                slot = h % pow_ref.shape[0]
                parts = head_parts(qkv_ref, h, width, keys)
                scores = dot(parts[1], parts[0], 0, 0)
                pow_ref[slot, :main, :] = jnp.exp2(scores[:main]).astype(BF)
                tail = masked_tail(scores[main:], main, limit)
                pow_ref[slot, main:keys, :] = jnp.exp2(tail).astype(BF)
                back(h, parts, slot, keys)

    @pl.when(jnp.logical_not(plain))
    def _():
        for h in range(heads):
            slot = h % pow_ref.shape[0]
            parts = head_parts(qkv_ref, h, width, rows)
            scores = masked_tail(dot(parts[1], parts[0], 0, 0), 0, limit)
            pow_ref[slot] = jnp.exp2(scores - top_ref[0, h : h + 1, :]).astype(BF)
            back(h, parts, slot, rows)

    right = jnp.concatenate((hat_ref[0], jnp.ones((rows, 128), BF)), 1)
    result = dot(dqkv_ref[0], right, 1, 0)
    grad_ref[...] = result[:, :width].astype(BF)
    sums_ref[...] = result[:, width:].T[:8]


def tokens_back_kernel(core_ref, *refs, sets):
    dqkv_refs = refs[:sets]
    w_ref, pack_ref, x_own_ref, x_far_ref, gmid_ref, own_ref, far_ref, out_ref, d_ref, sems = refs[sets:]
    step = pl.program_id(0)

    def fetch(k):
        return pltpu.make_async_copy(dqkv_refs[k].at[0], d_ref.at[k], sems.at[k])

    @pl.when(step == 0)
    def _():
        for k in range(sets):
            fetch(k).start()

    for k in range(sets):

        @pl.when(step == k)
        def _(k=k):
            fetch(k).wait()

    d_norm = dot(d_ref[step], w_ref[...], 0, 0)
    place_halves(out_ref, core_ref[CORE], x_own_ref[0], x_far_ref[0])
    hat, rstd = norm_parts(out_ref[...].astype(F32))
    w = d_norm * row_of(pack_ref, GAIN1)
    back = rstd * (w - jnp.mean(w, -1, keepdims=True) - hat * jnp.mean(w * hat, -1, keepdims=True))
    out_ref[...] = (gmid_ref[0].astype(F32) + back).astype(BF)
    split_halves(out_ref, core_ref[CORE], own_ref, far_ref)


def clear_rest(ref, used):
    if ref.shape[0] > used:
        ref[used:, :] = jnp.zeros((ref.shape[0] - used, ref.shape[1]), ref.dtype)


def write_halves(core, flat_ref, parts, kept_ref, sent_ref):
    start = at = 0
    for size in parts:
        half = size // 2
        mine = pl.multiple_of(start + core * half, 16)
        other = pl.multiple_of(start + (1 - core) * half, 16)
        kept_ref[at : at + half, :] = flat_ref[pl.ds(mine, half), :]
        sent_ref[at : at + half, :] = flat_ref[pl.ds(other, half), :]
        start += size
        at += half


def pack_kernel(core_ref, *refs, sets, parts):
    grad_refs = refs[:sets]
    sums_refs = refs[sets : 2 * sets]
    out_grad_ref, bias_ref, kept_ref, sent_ref, flat_ref = refs[2 * sets :]
    width = out_grad_ref.shape[0]
    used = grad_refs[0].shape[0]
    total, sums = grad_refs[0][...].astype(F32), sums_refs[0][...]
    for grad_ref, sums_ref in zip(grad_refs[1:], sums_refs[1:]):
        total = total + grad_ref[...].astype(F32)
        sums = sums + sums_ref[...]
    flat_ref[:used, :] = total.astype(BF)
    flat_ref[used : used + width, :] = out_grad_ref[...].astype(BF)
    clear_rest(flat_ref, used + width)
    write_halves(core_ref[CORE], flat_ref, parts, kept_ref, sent_ref)
    rows = lax.broadcasted_iota(jnp.int32, (8, width), 0)
    extra = jnp.zeros((8, width), F32)
    for t in range(used // width):
        extra = jnp.where(rows == t, sums[0:1, t * width : (t + 1) * width], extra)
    vectors = jnp.concatenate((bias_ref[0:8, :], extra), 0).astype(BF)
    at = sum(parts) // 2
    kept_ref[at : at + EXTRA, :] = vectors
    sent_ref[at : at + EXTRA, :] = vectors


def swap_cores(value):
    return lax.ppermute(value, "blk", [(0, 1), (1, 0)])


def stages(count, first=4):
    out = []
    stride = 1
    while stride < count:
        left = count // stride
        radix = first if not out and left % first == 0 else 4 if left % 4 == 0 else 2
        out.append((stride, radix))
        stride *= radix
    return out


def shifted(value, stage, steps, axis="samp"):
    stride, radix = stage
    count = lax.axis_size(axis)
    pairs = []
    for source in range(count):
        digit = (source // stride) % radix
        pairs.append((source, source + ((digit + steps) % radix - digit) * stride))
    return lax.ppermute(value, axis, pairs)


def small_call(kernel, args, outs, scratch=(), ties=(), name=None):
    def body(*refs):
        kernel(*refs[: len(args)], *refs[len(args) + len(ties) :])

    vmem = pl.BlockSpec(memory_space=pltpu.VMEM)
    size = lambda a: math.prod(a.shape) * jnp.dtype(a.dtype).itemsize
    total = sum(size(a) for a in (*args[1:], *outs)) + sum(
        math.prod(a.shape) * jnp.dtype(a.dtype).itemsize for a in scratch
    )
    return pl.pallas_call(
        body,
        in_specs=[
            pl.BlockSpec(memory_space=pltpu.SMEM),
            *[vmem] * (len(args) - 1),
            *[pl.BlockSpec(memory_space=pl.ANY)] * len(ties),
        ],
        out_specs=[vmem] * len(outs),
        out_shape=outs,
        scratch_shapes=list(scratch),
        compiler_params=pltpu.CompilerParams(vmem_limit_bytes=2 * total + 4 * 2**20),
        name=name,
    )(*args, *ties)


def spread_kernel(info_ref, *refs, count, radix, slot, extra):
    outputs = radix + (1 if extra and radix == 1 else 0)
    outs, total_ref = refs[count : count + outputs], refs[count + outputs]
    total = refs[0][...].astype(F32)
    for ref in refs[1:count]:
        total = total + ref[...].astype(F32)
    rows = total_ref.shape[0] - extra
    size = rows // radix
    total_ref[...] = total.astype(BF)
    if radix == 1:
        outs[0][...] = total_ref[:rows, :]
        if extra:
            outs[1][...] = total[rows:]
        return
    for k in range(radix):
        start = lax.rem(info_ref[slot] + k, radix) * size
        outs[k][:size, :] = total_ref[pl.ds(pl.multiple_of(start, 16), size), :]
        if extra:
            outs[k][size:, :] = total_ref[rows:, :]


def collect_kernel(info_ref, *refs, groups):
    at, out_at = 0, sum(groups)
    for count in groups:
        size = refs[at].shape[0]
        for k in range(count):
            refs[out_at][k * size : (k + 1) * size, :] = refs[at + k][...]
        at += count
        out_at += 1


class Layout:
    def __init__(self, count, rows):
        self.base = stages(count)
        self.count = count
        self.rows = rows
        table = np.zeros((2 * count, 1 + len(self.base)), np.int32)
        for device in range(2 * count):
            table[device, 0] = device % 2
            for i in range(len(self.base)):
                table[device, 1 + i] = self.digit(device, i)
        self.place = table.shape[1]
        places = np.stack([self.places(device, rows) for device in range(2 * count)])
        self.table = np.concatenate((table, places), 1).astype(np.int32)

    def digit(self, device, index):
        stride, radix = self.base[index]
        return (device // 2 // stride) % radix

    def places(self, device, rows):
        core = device % 2
        unit = rows // 2
        offsets = np.array([core * unit, (1 - core) * unit])
        for index, (_, radix) in enumerate(self.base):
            unit //= radix
            digit = (self.digit(device, index) - np.arange(radix)) % radix
            offsets = (offsets[:, None] + (digit * unit)[None, :]).reshape(-1)
        return offsets

    def own_places(self, rows):
        return np.array([self.places(device, rows)[0] for device in range(2 * self.count)], np.int32)


class Chain:
    def __init__(self, layout, info, extra=0):
        self.layout = layout
        self.info = info
        self.extra = extra
        self.rounds = len(layout.base)

    def start(self, kept, sent):
        self.pending = [kept, swap_cores(sent)]

    def scatter(self, level, ties=()):
        last = level == self.rounds
        radix = 1 if last else self.layout.base[level][1]
        rows, width = self.pending[0].shape
        size = (rows - self.extra) // radix
        if last:
            outs = [jax.ShapeDtypeStruct((size, width), BF)]
            if self.extra:
                outs.append(jax.ShapeDtypeStruct((self.extra, width), F32))
        else:
            outs = [jax.ShapeDtypeStruct((size + self.extra, width), BF)] * radix
        pieces = small_call(
            functools.partial(
                spread_kernel, count=len(self.pending), radix=radix, slot=1 + level, extra=self.extra
            ),
            (self.info, *self.pending), outs, [pltpu.VMEM((rows, width), BF)], ties, "spread",
        )
        if last:
            self.value = pieces[0]
            self.vectors = pieces[1] if self.extra else None
        else:
            stage = self.layout.base[level]
            self.pending = [pieces[0]] + [shifted(pieces[k], stage, k) for k in range(1, radix)]
        return pieces[0]

    def gather(self, level):
        stage = self.layout.base[level]
        self.pending = [self.value] + [shifted(self.value, stage, k) for k in range(1, stage[1])]

    def collect(self, ties=()):
        size, width = self.pending[0].shape
        outs = [jax.ShapeDtypeStruct((len(self.pending) * size, width), BF)]
        self.value = small_call(
            functools.partial(collect_kernel, groups=(len(self.pending),)),
            (self.info, *self.pending), outs, (), ties, "collect",
        )[0]
        return self.value


def restore(place_ref, flat_ref, ref, unit, at):
    def body(i, carry):
        start = pl.multiple_of(place_ref[at + i], 16)
        source = pl.multiple_of(i * unit, 16)
        chunk = ref[pl.ds(source, unit), :]
        flat_ref[pl.ds(start, unit), :] = chunk
        return carry

    lax.fori_loop(0, ref.shape[0] // unit, body, 0)


def finish_mlp_kernel(place_ref, all_ref, vectors_ref, pack_ref, w1_ref, fc2_ref, fc1_ref, rows_ref, flat_ref, *, unit):
    restore(place_ref, flat_ref, all_ref, unit, 0)
    hidden, width = fc2_ref.shape
    fc2_ref[...] = flat_ref[:hidden, :].astype(F32)
    columns = pack_ref[0:8, :].T
    gain = jnp.zeros((width, 1), F32)
    shift = jnp.zeros((width, 1), F32)
    for j in range(hidden // width):
        cols = slice(j * width, (j + 1) * width)
        hats = flat_ref[hidden + j * width : hidden + (j + 1) * width, :].astype(F32)
        sums = vectors_ref[j : j + 1, :]
        fc1_ref[:, cols] = hats * columns[:, GAIN2 : GAIN2 + 1] + columns[:, SHIFT2 : SHIFT2 + 1] * sums
        w = w1_ref[:, cols].astype(F32)
        gain = gain + jnp.sum(w * hats, -1, keepdims=True)
        shift = shift + jnp.sum(w * sums, -1, keepdims=True)
    lane = lax.broadcasted_iota(jnp.int32, (width, 128), 1)
    rows_ref[...] = jnp.where(lane == 0, gain, jnp.where(lane == 1, shift, 0.0)).T[0:8]


def finish_kernel(
    info_ref, own_ref, far_ref, vectors_ref, pack_ref, w_ref, qkv_ref, out_ref, rows_ref, flat_ref, *, unit, at
):
    restore(info_ref, flat_ref, own_ref, unit, at)
    restore(info_ref, flat_ref, far_ref, unit, at + own_ref.shape[0] // unit)
    width = out_ref.shape[0]
    columns = qkv_ref.shape[1]
    out_ref[...] = flat_ref[columns : columns + width, :].astype(F32)
    gain = jnp.zeros((1, width), F32)
    shift = jnp.zeros((1, width), F32)
    turned = vectors_ref[8:16, :].T
    for t in range(columns // width):
        part = slice(t * width, (t + 1) * width)
        hats = flat_ref[part, :].astype(F32)
        sums = turned[:, t : t + 1]
        result = hats * row_of(pack_ref, GAIN1) + sums * row_of(pack_ref, SHIFT1)
        qkv_ref[:, part] = result.T
        w = w_ref[part, :].astype(F32)
        gain = gain + jnp.sum(w * hats, 0, keepdims=True)
        shift = shift + jnp.sum(w * sums, 0, keepdims=True)
    rows_ref[...] = jnp.concatenate((gain, shift, jnp.zeros((6, width), F32)), 0)


def pad_rows(count, unit):
    return -(-count // unit) * unit


def per_device(
    tokens, view_count, norm1_gain, norm1_bias, w_qkv, qv_bias, w_out, out_bias,
    norm2_gain, norm2_bias, w_fc1, fc1_bias, w_fc2, fc2_bias, cot_tokens, cot_cls,
):
    core = lax.axis_index("blk")
    cores = lax.axis_size("blk")
    count = lax.axis_size("samp")
    samples, half, width = tokens.shape
    local = samples // cores
    rows = half * cores
    hidden = w_fc1.shape[1]
    blocks = hidden // width
    heads = width // HEAD_DIM
    pairs = heads // 2
    sds = jax.ShapeDtypeStruct

    unit = 32 * count
    parts1 = [pad_rows(2 * hidden, unit)]
    parts2 = [pad_rows(4 * width, unit)]
    layout = Layout(count, parts2[0])
    device = lax.axis_index("samp") * cores + core
    info = lax.dynamic_index_in_dim(jnp.asarray(layout.table), device, 0, keepdims=False)

    theirs = (1 - core) * local
    far_tokens = swap_cores(lax.dynamic_slice_in_dim(tokens, theirs, local, 0))
    far_cot = swap_cores(lax.dynamic_slice_in_dim(cot_tokens, theirs, local, 0))

    w_turned = w_qkv.T
    pack = jnp.concatenate(
        (
            norm1_gain, norm1_bias, norm2_gain, norm2_bias, out_bias, fc2_bias, qv_bias, fc1_bias,
            jnp.zeros(((8 - blocks) * width,), BF),
        )
    ).astype(F32).reshape(16, width)

    vmem = pl.BlockSpec(memory_space=pltpu.VMEM)
    half_spec = lambda f: pl.BlockSpec((1, half, width), f)
    own_map = lambda s, b, *_: (b[CORE] * local + s, 0, 0)
    by_sample = lambda s, *_: (s, 0, 0)
    rows_spec = pl.BlockSpec((1, rows, width), by_sample)
    turned_spec = pl.BlockSpec((1, width, rows), by_sample)
    rstd_spec = pl.BlockSpec((1, rows, 1), by_sample)
    hidden_spec = pl.BlockSpec((1, rows, hidden), by_sample)
    eight_spec = pl.BlockSpec((1, 8, rows), by_sample)

    def big_call(kernel, prefetch, args, in_specs, outs, out_specs, scratch=(), ties=(), grid=(local,), name=None):
        n = len(prefetch) + len(args)

        def body(*refs):
            kernel(*refs[:n], *refs[n + len(ties) :])

        return pl.pallas_call(
            body,
            grid_spec=pltpu.PrefetchScalarGridSpec(
                num_scalar_prefetch=len(prefetch),
                grid=grid,
                in_specs=[*in_specs, *[pl.BlockSpec(memory_space=pl.ANY)] * len(ties)],
                out_specs=out_specs,
                scratch_shapes=list(scratch),
            ),
            out_shape=outs,
            compiler_params=params(("arbitrary",) * len(grid)),
            name=name,
        )(*prefetch, *args, *ties)

    hat1, qkv, cls_rows, stats = big_call(
        project_kernel,
        (info, view_count),
        (tokens, far_tokens, w_turned, pack, w_out, w_fc1, w_fc2, cot_cls),
        [half_spec(own_map), half_spec(by_sample), *[vmem] * 6],
        [
            sds((local, rows, width), BF),
            sds((local, 3 * width, rows), BF),
            sds((8, width), F32),
            sds((8, width), F32),
        ],
        [rows_spec, pl.BlockSpec((1, 3 * width, rows), by_sample), vmem, vmem],
        [pltpu.VMEM((8, width), F32), pltpu.VMEM((8, width), F32), pltpu.VMEM((rows, width), BF)],
        name="project",
    )

    def add_kernel(info_ref, *refs):
        total = refs[0][...]
        for ref in refs[1:-1]:
            total = total + ref[...]
        refs[-1][...] = total

    first, *later = stages(count)
    stat_parts = [stats] + [shifted(stats, first, k) for k in range(1, first[1])]

    qkv_spec = lambda f: pl.BlockSpec((1, 3 * width, rows), f)
    totals, tops, plain, mixed = big_call(
        attention_kernel,
        (info, view_count),
        (qkv,),
        [qkv_spec(by_sample)],
        [
            sds((local, 8, rows), F32),
            sds((local, 8, rows), F32),
            sds((local,), jnp.int32),
            sds((local, width, rows), BF),
        ],
        [eight_spec, eight_spec, pl.BlockSpec(memory_space=pltpu.SMEM), turned_spec],
        [pltpu.VMEM((2, rows, rows), BF)],
        name="attention",
    )

    tie = totals
    for send in [functools.partial(lambda v, stage: [shifted(v, stage, k) for k in range(1, stage[1])], stage=stage) for stage in later] + [lambda v: [swap_cores(v)]]:
        stats = small_call(
            add_kernel, [info, *stat_parts], [sds((8, width), F32)], (), (tie,), "add"
        )[0]
        stat_parts = [stats] + send(stats)
        tie = stats

    tokens_out_own, out_far, g_mid, d_mix, inner, out_grad, cls_norm, biases, kept1, sent1 = big_call(
        functools.partial(
            layer_kernel, samples=local * cores * count, parts=parts1, peers=len(stat_parts)
        ),
        (info,),
        (
            tokens, far_tokens, cot_tokens, far_cot, mixed, totals, cls_rows, cot_cls, *stat_parts,
            w_out, w_fc1, w_fc2, pack,
        ),
        [
            half_spec(own_map), half_spec(by_sample), half_spec(own_map), half_spec(by_sample),
            turned_spec, eight_spec, vmem, vmem, *[vmem] * len(stat_parts), vmem, vmem, vmem, vmem,
        ],
        [
            sds((samples, half, width), BF),
            sds((local, half, width), BF),
            sds((local, rows, width), BF),
            sds((local, width, rows), BF),
            sds((local, 8, rows), F32),
            sds((width, width), F32),
            sds((local, width), BF),
            sds((8, width), F32),
            sds((sum(parts1) // 2, width), BF),
            sds((sum(parts1) // 2, width), BF),
        ],
        [
            half_spec(own_map), half_spec(by_sample), rows_spec, turned_spec, eight_spec,
            vmem, vmem, vmem, vmem, vmem,
        ],
        [
            pltpu.VMEM((rows, width), BF),
            pltpu.VMEM((rows, width), F32),
            pltpu.VMEM((rows, hidden), BF),
            pltpu.VMEM((rows, hidden), BF),
            pltpu.VMEM((8, width), F32),
            pltpu.VMEM((hidden, width), F32),
            pltpu.VMEM((width, hidden), F32),
            pltpu.VMEM((sum(parts1), width), BF),
        ],
        name="layer",
    )
    chain1 = Chain(layout, info)
    chain1.start(kept1, sent1)
    out_came = swap_cores(out_far)

    def attention_back(sample, ties):
        place = lambda *_: (sample, 0, 0)
        return big_call(
            functools.partial(attention_back_kernel, sample=sample, samples=local),
            (info, view_count, plain),
            (qkv, tops, d_mix, inner, hat1),
            [
                qkv_spec(place),
                pl.BlockSpec((1, 8, rows), place),
                pl.BlockSpec((1, width, rows), place),
                pl.BlockSpec((1, 8, rows), place),
                pl.BlockSpec((1, rows, width), place),
            ],
            [
                sds((1, 3 * width, rows), BF),
                sds((3 * width, width), BF),
                sds((8, 3 * width), F32),
            ],
            [qkv_spec(lambda *_: (0, 0, 0)), vmem, vmem],
            [pltpu.VMEM((2, rows, rows), BF)],
            ties,
            grid=(1,),
            name="attention_back",
        )

    ties = (inner,)
    d_parts, grads, sums = [], [], []
    for sample in range(local):
        d_part, grad, total = attention_back(sample, ties)
        d_parts.append(d_part)
        grads.append(grad)
        sums.append(total)
        if sample <= chain1.rounds:
            ties = (chain1.scatter(sample, (total,)),)
        if sample == 0:
            tokens_out = lax.dynamic_update_slice_in_dim(tokens_out_own, out_came, theirs, 0)
            ties = (*ties, tokens_out)
    for level in range(local, chain1.rounds + 1):
        ties = (chain1.scatter(level),)
    gathered = lax.all_gather(chain1.value, ("samp", "blk"), axis=0, tiled=True)

    chain2 = Chain(layout, info, EXTRA)
    kept2, sent2 = small_call(
        functools.partial(pack_kernel, sets=len(grads), parts=parts2),
        (info, *grads, *sums, out_grad, biases),
        [sds((sum(parts2) // 2 + EXTRA, width), BF)] * 2,
        [pltpu.VMEM((sum(parts2), width), BF)],
        ties,
        name="pack",
    )
    chain2.start(kept2, sent2)
    tie = chain2.scatter(0)

    grad_own, grad_far = big_call(
        functools.partial(tokens_back_kernel, sets=len(d_parts)),
        (info,),
        (*d_parts, w_turned, pack, tokens, far_tokens, g_mid),
        [
            *[pl.BlockSpec(memory_space=pl.ANY)] * len(d_parts),
            vmem, vmem, half_spec(own_map), half_spec(by_sample), rows_spec,
        ],
        [sds((samples, half, width), BF), sds((local, half, width), BF)],
        [half_spec(own_map), half_spec(by_sample)],
        [
            pltpu.VMEM((rows, width), BF),
            pltpu.VMEM((len(d_parts), 3 * width, rows), BF),
            pltpu.SemaphoreType.DMA((len(d_parts),)),
        ],
        (tie,),
        name="tokens_back",
    )
    grad_came = swap_cores(grad_far)
    ties = (grad_far,)
    for level in range(1, chain2.rounds + 1):
        chain2.scatter(level, ties)
        ties = ()
    for level in reversed(range(chain2.rounds)):
        chain2.gather(level)
        if level == chain2.rounds - 1:
            grad_tokens = lax.dynamic_update_slice_in_dim(grad_own, grad_came, theirs, 0)
            ties = (grad_tokens,)
        chain2.collect(ties)
        ties = ()
    other = swap_cores(chain2.value)

    grad_w_fc2, grad_w_fc1, rows2 = small_call(
        functools.partial(finish_mlp_kernel, unit=parts1[0] // (2 * count)),
        (jnp.asarray(layout.own_places(parts1[0])), gathered, chain2.vectors, pack, w_fc1),
        [sds((hidden, width), F32), sds((width, hidden), F32), sds((8, width), F32)],
        [pltpu.VMEM((parts1[0], width), BF)],
        (chain2.value,),
        name="finish_mlp",
    )
    grad_w_qkv, grad_w_out, rows1 = small_call(
        functools.partial(finish_kernel, unit=parts2[0] // (2 * count), at=layout.place),
        (info, chain2.value, other, chain2.vectors, pack, w_turned),
        [sds((width, 3 * width), F32), sds((width, width), F32), sds((8, width), F32)],
        [pltpu.VMEM((parts2[0], width), BF)],
        name="finish",
    )
    vectors = chain2.vectors
    grad_qv_bias = jnp.concatenate((vectors[8], vectors[10]))
    return (
        tokens_out, cls_norm, grad_tokens, rows1[0], rows1[1], grad_w_qkv, grad_qv_bias,
        grad_w_out, vectors[blocks + 1], rows2[0], rows2[1], grad_w_fc1,
        vectors[:blocks].reshape(hidden), grad_w_fc2, vectors[blocks],
    )


def solution(mesh):
    split = P("samp", "blk", None)
    classes = P(("samp", "blk"), None)
    return jax.shard_map(
        per_device,
        mesh=mesh,
        in_specs=(split, P("samp"), *([P()] * 12), split, classes),
        out_specs=(split, classes, split, *([P()] * 12)),
        check_vma=False,
    )
```

```python
import functools
import math

import jax
import jax.numpy as jnp
import numpy as np
from jax import lax
from jax.experimental import pallas as pl
from jax.experimental.pallas import tpu as pltpu
from jax.sharding import PartitionSpec as P

HEAD_DIM = 64
VIEW_ROWS = 196
NORM_EPS = 1e-06
CLS_EPS = 1e-05
MASKED = -1e30
LOG2E = math.log2(math.e)
LN2 = math.log(2.0)
SCALE = HEAD_DIM ** (-0.5)
SUM_LOW = 1e-15
SUM_HIGH = 1e15
BF = jnp.bfloat16
F32 = jnp.float32
VMEM_BYTES = 60 * 2**20
CORE = 0
EXTRA = 16


def dot(a, b, ca, cb):
    return lax.dot_general(a, b, (((ca,), (cb,)), ((), ())), preferred_element_type=F32)


def norm_parts(values):
    centre = jnp.mean(values, -1, keepdims=True)
    offset = values - centre
    rstd = lax.rsqrt(jnp.mean(offset * offset, -1, keepdims=True) + NORM_EPS)
    return offset * rstd, rstd


def gelu_cdf(values):
    return 0.5 + 0.5 * lax.erf(values * (0.5**0.5))


def params(semantics):
    return pltpu.CompilerParams(dimension_semantics=semantics, vmem_limit_bytes=VMEM_BYTES)


def whole(shape):
    return pl.BlockSpec(shape, lambda *_: (0,) * len(shape))


def key_counts(rows):
    views = (rows - 1) // VIEW_ROWS
    return [(v, min(rows, -(-(1 + VIEW_ROWS * v) // 16) * 16)) for v in range(1, views + 1)]


GAIN1, SHIFT1, GAIN2, SHIFT2, OUT_BIAS, FC2_BIAS, QV_BIAS, FC1_BIAS = 0, 1, 2, 3, 4, 5, 6, 8


def row_of(pack_ref, index):
    return pack_ref[index : index + 1, :]


def place_halves(target_ref, core, own, far):
    half = own.shape[0]
    target_ref[pl.ds(pl.multiple_of(core * half, 16), half), :] = own
    target_ref[pl.ds(pl.multiple_of((1 - core) * half, 16), half), :] = far


def split_halves(source_ref, core, own_ref, far_ref):
    half = own_ref.shape[1]
    own_ref[0] = source_ref[pl.ds(pl.multiple_of(core * half, 16), half), :]
    far_ref[0] = source_ref[pl.ds(pl.multiple_of((1 - core) * half, 16), half), :]


def project_kernel(
    blk_ref, views_ref, own_ref, far_ref, w_in_ref, pack_ref, w_out_ref, w1_ref, w2_ref, cot_ref,
    hat_ref, qkv_ref, cls_ref, stat_ref, w_ref, mix_ref, first_ref, full_ref,
):
    step = pl.program_id(0)

    @pl.when(step == 0)
    def _():
        w_ref[...] = w_in_ref[...].T

    rows = hat_ref.shape[1]
    width = own_ref.shape[2]
    place_halves(full_ref, blk_ref[0], own_ref[0], far_ref[0])
    values = full_ref[...].astype(F32)
    hat, _ = norm_parts(values)
    hat_ref[0] = hat.astype(BF)
    normed = (hat * row_of(pack_ref, GAIN1) + row_of(pack_ref, SHIFT1)).astype(BF)
    columns = pack_ref[0:8, :].T
    for third in range(3):
        part = pl.ds(third * width, width)
        piece = dot(w_ref[part, :], normed, 1, 1)
        if third == 0:
            piece = (piece + columns[:, QV_BIAS : QV_BIAS + 1]) * (SCALE * LOG2E)
        if third == 2:
            piece = piece + columns[:, QV_BIAS + 1 : QV_BIAS + 2]
        qkv_ref[0, part, :] = piece.astype(BF)

    lead = qkv_ref[0, pl.ds(0, width), :128].astype(F32).T[0:1, :]
    head_of = lax.broadcasted_iota(jnp.int32, (8, width), 1) // HEAD_DIM
    pick = head_of == lax.broadcasted_iota(jnp.int32, (8, width), 0)
    queries = jnp.where(pick, lead, 0.0).astype(BF)
    scores = dot(queries, qkv_ref[0, pl.ds(width, width), :], 1, 0)
    limit = 1 + VIEW_ROWS * views_ref[blk_ref[CORE] * pl.num_programs(0) + step]
    place = lax.broadcasted_iota(jnp.int32, (8, rows), 1)
    scores = jnp.where(place < limit, scores, MASKED)
    powers = jnp.exp2(scores - jnp.max(scores, -1, keepdims=True))
    chances = (powers / jnp.sum(powers, -1, keepdims=True)).astype(BF)
    mixed = dot(chances, qkv_ref[0, pl.ds(2 * width, width), :], 1, 1)
    mix_ref[pl.ds(step, 1), :] = jnp.sum(jnp.where(pick, mixed, 0.0), 0, keepdims=True)
    first_ref[pl.ds(step, 1), :] = values[0:1, :]

    @pl.when(step == pl.num_programs(0) - 1)
    def _():
        branch = dot(mix_ref[...].astype(BF), w_out_ref[...], 1, 0) + row_of(pack_ref, OUT_BIAS)
        middle = first_ref[...] + branch
        normed2 = norm_parts(middle)[0] * row_of(pack_ref, GAIN2) + row_of(pack_ref, SHIFT2)
        normed2 = normed2.astype(BF)
        output = middle + row_of(pack_ref, FC2_BIAS)
        for j in range(w1_ref.shape[1] // width):
            cols = slice(j * width, (j + 1) * width)
            pre = dot(normed2, w1_ref[:, cols], 1, 0) + row_of(pack_ref, FC1_BIAS + j)
            act = (pre * gelu_cdf(pre)).astype(BF)
            output = output + dot(act, w2_ref[cols, :], 1, 0)
        cls_ref[...] = output
        count = cot_ref.shape[0]
        cls = output[:count]
        cot = cot_ref[...].astype(F32)
        stat_ref[...] = jnp.zeros_like(stat_ref)
        for k, term in enumerate((cls, cls * cls, cot, cot * cls)):
            stat_ref[k : k + 1, :] = jnp.sum(term, 0, keepdims=True)


def masked_tail(scores, main, limit):
    place = main + lax.broadcasted_iota(jnp.int32, scores.shape, 0)
    return jnp.where(place < limit, scores, MASKED)


def attention_kernel(
    core_ref, views_ref, qkv_ref, sum_ref, top_ref, plain_ref, att_ref, pow_ref
):
    sample = pl.program_id(0)
    rows = qkv_ref.shape[2]
    width = att_ref.shape[1]
    heads = width // HEAD_DIM
    views = views_ref[core_ref[CORE] * pl.num_programs(0) + sample]
    limit = 1 + VIEW_ROWS * views
    ones = jnp.ones((16, rows), BF)

    def store(h, mixed):
        total = mixed[HEAD_DIM : HEAD_DIM + 1]
        sum_ref[0, pl.ds(h, 1), :] = total
        att_ref[0, head_rows(h, 0), :] = (mixed[:HEAD_DIM] * (1.0 / total)).astype(BF)

    sum_ref[0, heads:8, :] = jnp.ones((8 - heads, rows), F32)
    for count, keys in key_counts(rows):

        @pl.when(views == count)
        def _(keys=keys):
            main = keys - 16

            def pair(p, carry):
                both = range(2)
                parts = [head_parts(qkv_ref, 2 * p + k, width, keys) for k in both]
                scores = [dot(key, query, 0, 0) for query, key, _ in parts]
                for k in both:
                    pow_ref[k, :main, :] = jnp.exp2(scores[k][:main]).astype(BF)
                    tail = masked_tail(scores[k][main:], main, limit)
                    pow_ref[k, main:keys, :] = jnp.exp2(tail).astype(BF)
                lefts = [jnp.concatenate((value, ones[:, :keys]), 0) for _, _, value in parts]
                mixed = [dot(lefts[k], pow_ref[k, :keys, :], 1, 0) for k in both]
                for k in both:
                    store(2 * p + k, mixed[k])
                return carry

            lax.fori_loop(0, heads // 2, pair, 0)

    totals = sum_ref[0]
    plain = (jnp.min(totals) > SUM_LOW) & (jnp.max(totals) < SUM_HIGH)
    plain_ref[sample] = plain.astype(jnp.int32)

    @pl.when(jnp.logical_not(plain))
    def _():
        @each_head(heads)
        def _(h, slot):
            query, key, value = head_parts(qkv_ref, h, width, rows)
            scores = masked_tail(dot(key, query, 0, 0), 0, limit)
            top = jnp.max(scores, 0, keepdims=True)
            top_ref[0, pl.ds(h, 1), :] = top
            pow_ref[slot] = jnp.exp2(scores - top).astype(BF)
            left = jnp.concatenate((value, ones), 0)
            store(h, dot(left, pow_ref[slot], 1, 0))


def each_head(heads):
    def run(body):
        def pair(p, carry):
            for slot in range(2):
                body(2 * p + slot, slot)
            return carry

        lax.fori_loop(0, heads // 2, pair, 0)

    return run


def head_rows(h, base):
    return pl.ds(pl.multiple_of(base + h * HEAD_DIM, HEAD_DIM), HEAD_DIM)


def head_parts(qkv_ref, h, width, keys):
    return (
        qkv_ref[0, head_rows(h, 0), :],
        qkv_ref[0, head_rows(h, width), :keys],
        qkv_ref[0, head_rows(h, 2 * width), :keys],
    )


def layer_kernel(
    core_ref, x_own_ref, x_far_ref, own_ref, far_ref, att_ref, sum_ref, cls_ref, cot_ref, *refs,
    samples, parts, peers
):
    stat_refs = refs[:peers]
    w_out_ref, w1_ref, w2_ref, pack_ref = refs[peers : peers + 4]
    (
        out_own_ref, out_far_ref, gmid_ref, dmix_ref, inner_ref, out_grad_ref, norm_ref, bias_ref,
        kept_ref, sent_ref,
    ) = refs[peers + 4 : peers + 14]
    full_ref, g_ref, act_ref, dpre_ref, dcls_ref, acc2_ref, acc1_ref, flat_ref = refs[peers + 14 :]
    step = pl.program_id(0)
    width = own_ref.shape[2]
    hidden = w2_ref.shape[0]
    blocks = hidden // width

    @pl.when(step == 0)
    def _():
        acc2_ref[...] = jnp.zeros_like(acc2_ref)
        acc1_ref[...] = jnp.zeros_like(acc1_ref)
        bias_ref[...] = jnp.zeros_like(bias_ref)
        out_grad_ref[...] = jnp.zeros_like(out_grad_ref)
        stats = stat_refs[0][...]
        for other in stat_refs[1:]:
            stats = stats + other[...]
        local = cot_ref.shape[0]
        cls = cls_ref[...][:local]
        cot = cot_ref[...].astype(F32)
        mean = stats[0:1] / samples
        scale = lax.rsqrt(stats[1:2] / samples - mean * mean + CLS_EPS)
        hat = (cls - mean) * scale
        norm_ref[...] = hat.astype(BF)
        cross = scale * (stats[3:4] - mean * stats[2:3])
        dcls_ref[...] = jnp.zeros_like(dcls_ref)
        dcls_ref[:local, :] = scale * (cot - stats[2:3] / samples - hat * (cross / samples))

    place_halves(full_ref, core_ref[CORE], x_own_ref[0], x_far_ref[0])
    place_halves(g_ref, core_ref[CORE], own_ref[0].astype(F32), far_ref[0].astype(F32))
    g_ref[0:1, :] = g_ref[0:1, :] + dcls_ref[pl.ds(step, 1), :]
    g_mlp = g_ref[...].astype(BF)
    bias_ref[blocks : blocks + 1, :] += jnp.sum(g_mlp.astype(F32), 0, keepdims=True)

    branch = dot(att_ref[0], w_out_ref[...], 0, 0) + row_of(pack_ref, OUT_BIAS)
    middle = full_ref[...].astype(F32) + branch
    hat, rstd = norm_parts(middle)
    normed = (hat * row_of(pack_ref, GAIN2) + row_of(pack_ref, SHIFT2)).astype(BF)
    hat_low = hat.astype(BF)
    for j in range(blocks):
        cols = slice(j * width, (j + 1) * width)
        pre = dot(normed, w1_ref[:, cols], 1, 0) + row_of(pack_ref, FC1_BIAS + j)
        d_act = dot(g_mlp, w2_ref[cols, :], 1, 1)
        cdf = gelu_cdf(pre)
        bell = jnp.exp2(pre * pre * (-0.5 * LOG2E) - 0.5 * math.log2(2.0 * math.pi))
        act_ref[:, cols] = (pre * cdf).astype(BF)
        d_pre = d_act * (cdf + pre * bell)
        bias_ref[j : j + 1, :] += jnp.sum(d_pre, 0, keepdims=True)
        dpre_ref[:, cols] = d_pre.astype(BF)
    acc1_ref[...] += dot(hat_low, dpre_ref[...], 0, 0)
    acc2_ref[...] += dot(act_ref[...], g_mlp, 0, 0)
    output = middle + dot(act_ref[...], w2_ref[...], 1, 0) + row_of(pack_ref, FC2_BIAS)
    full_ref[...] = output.astype(BF)
    split_halves(full_ref, core_ref[CORE], out_own_ref, out_far_ref)

    d_norm = dot(dpre_ref[...], w1_ref[...], 1, 1)
    u = d_norm * row_of(pack_ref, GAIN2)
    g_mid = g_ref[...] + rstd * (
        u - jnp.mean(u, -1, keepdims=True) - hat * jnp.mean(u * hat, -1, keepdims=True)
    )
    g_attn = g_mid.astype(BF)
    gmid_ref[0] = g_attn
    out_grad_ref[...] += dot(att_ref[0], g_attn, 1, 0)
    bias_ref[blocks + 1 : blocks + 2, :] += jnp.sum(g_attn.astype(F32), 0, keepdims=True)
    d_mix = dot(w_out_ref[...], g_attn, 1, 1)
    for h in range(width // HEAD_DIM):
        part = slice(h * HEAD_DIM, (h + 1) * HEAD_DIM)
        piece = d_mix[part] * (1.0 / sum_ref[0, h : h + 1, :])
        dmix_ref[0, part, :] = piece.astype(BF)
        inner_ref[0, h : h + 1, :] = jnp.sum(piece * att_ref[0, part, :].astype(F32), 0, keepdims=True)

    @pl.when(step == pl.num_programs(0) - 1)
    def _():
        flat_ref[:hidden, :] = acc2_ref[...].astype(BF)
        for j in range(blocks):
            rows = slice(hidden + j * width, hidden + (j + 1) * width)
            flat_ref[rows, :] = acc1_ref[:, j * width : (j + 1) * width].astype(BF)
        clear_rest(flat_ref, 2 * hidden)
        write_halves(core_ref[CORE], flat_ref, parts, kept_ref, sent_ref)


def attention_back_kernel(
    core_ref, views_ref, plain_ref, qkv_ref, top_ref, dmix_ref, inner_ref, hat_ref,
    dqkv_ref, grad_ref, sums_ref, pow_ref, *, sample, samples
):
    pair = pl.program_id(0)
    rows, width = hat_ref.shape[1:]
    views = views_ref[core_ref[CORE] * samples + sample]
    limit = 1 + VIEW_ROWS * views
    plain = plain_ref[sample] == 1
    both = range(2)
    lanes = [slice(k * HEAD_DIM, (k + 1) * HEAD_DIM) for k in both]

    def back(keys, powers_of):
        query = [qkv_ref[0, 0, part, :] for part in lanes]
        key = [qkv_ref[0, 1, part, :keys] for part in lanes]
        value = [qkv_ref[0, 2, part, :keys] for part in lanes]
        d_mix = [dmix_ref[0, part, :] for part in lanes]
        scores = [dot(key[k], query[k], 0, 0) for k in both]
        for k in both:
            powers_of(k, scores[k])
        d_weights = [dot(value[k], d_mix[k], 0, 0) for k in both]
        d_scores = []
        for k in both:
            inner = inner_ref[0, pl.ds(2 * pair + k, 1), :]
            powers = pow_ref[k, :keys, :].astype(F32)
            d_scores.append((powers * (d_weights[k] - inner)).astype(BF))
        for k in both:
            d_value = dot(d_mix[k], pow_ref[k, :keys, :], 1, 1)
            dqkv_ref[0, 2, lanes[k], :keys] = d_value.astype(BF)
        for k in both:
            d_query = dot(key[k], d_scores[k], 1, 0) * SCALE
            dqkv_ref[0, 0, lanes[k], :] = d_query.astype(BF)
            d_key = dot(query[k], d_scores[k], 1, 1) * LN2
            dqkv_ref[0, 1, lanes[k], :keys] = d_key.astype(BF)
        if keys < rows:
            blank = jnp.zeros((2 * HEAD_DIM, rows - keys), BF)
            dqkv_ref[0, 1, :, keys:] = blank
            dqkv_ref[0, 2, :, keys:] = blank

    for count, keys in key_counts(rows):

        @pl.when((views == count) & plain)
        def _(keys=keys):
            main = keys - 16

            def powers_of(k, scores):
                pow_ref[k, :main, :] = jnp.exp2(scores[:main]).astype(BF)
                tail = masked_tail(scores[main:], main, limit)
                pow_ref[k, main:keys, :] = jnp.exp2(tail).astype(BF)

            back(keys, powers_of)

    @pl.when(jnp.logical_not(plain))
    def _():
        def powers_of(k, scores):
            top = top_ref[0, pl.ds(2 * pair + k, 1), :]
            pow_ref[k] = jnp.exp2(masked_tail(scores, 0, limit) - top).astype(BF)

        back(rows, powers_of)

    right = jnp.concatenate((hat_ref[0], jnp.ones((rows, 128), BF)), 1)
    result = dot(dqkv_ref[0].reshape(3 * 2 * HEAD_DIM, rows), right, 1, 0)
    grad_ref[...] = result[:, :width].astype(BF).reshape(grad_ref.shape)
    sums_ref[0] = result[:, width:].T[:8]


def tokens_back_kernel(core_ref, *refs, sets):
    dqkv_refs = refs[:sets]
    w_ref, pack_ref, x_own_ref, x_far_ref, gmid_ref, own_ref, far_ref, out_ref, d_ref, sems = refs[sets:]
    step = pl.program_id(0)

    def fetch(k):
        return pltpu.make_async_copy(dqkv_refs[k].at[0], d_ref.at[k], sems.at[k])

    @pl.when(step == 0)
    def _():
        for k in range(sets):
            fetch(k).start()

    for k in range(sets):

        @pl.when(step == k)
        def _(k=k):
            fetch(k).wait()

    d_norm = dot(d_ref[step], w_ref[...], 0, 0)
    place_halves(out_ref, core_ref[CORE], x_own_ref[0], x_far_ref[0])
    hat, rstd = norm_parts(out_ref[...].astype(F32))
    w = d_norm * row_of(pack_ref, GAIN1)
    back = rstd * (w - jnp.mean(w, -1, keepdims=True) - hat * jnp.mean(w * hat, -1, keepdims=True))
    out_ref[...] = (gmid_ref[0].astype(F32) + back).astype(BF)
    split_halves(out_ref, core_ref[CORE], own_ref, far_ref)


def clear_rest(ref, used):
    if ref.shape[0] > used:
        ref[used:, :] = jnp.zeros((ref.shape[0] - used, ref.shape[1]), ref.dtype)


def write_halves(core, flat_ref, parts, kept_ref, sent_ref):
    start = at = 0
    for size in parts:
        half = size // 2
        mine = pl.multiple_of(start + core * half, 16)
        other = pl.multiple_of(start + (1 - core) * half, 16)
        kept_ref[at : at + half, :] = flat_ref[pl.ds(mine, half), :]
        sent_ref[at : at + half, :] = flat_ref[pl.ds(other, half), :]
        start += size
        at += half


def pack_kernel(core_ref, *refs, sets, parts):
    grad_refs = refs[:sets]
    sums_refs = refs[sets : 2 * sets]
    out_grad_ref, bias_ref, kept_ref, sent_ref, flat_ref = refs[2 * sets :]
    width = out_grad_ref.shape[0]
    used = grad_refs[0].shape[0]
    total, sums = grad_refs[0][...].astype(F32), sums_refs[0][...]
    for grad_ref, sums_ref in zip(grad_refs[1:], sums_refs[1:]):
        total = total + grad_ref[...].astype(F32)
        sums = sums + sums_ref[...]
    flat_ref[:used, :] = total.astype(BF)
    flat_ref[used : used + width, :] = out_grad_ref[...].astype(BF)
    clear_rest(flat_ref, used + width)
    write_halves(core_ref[CORE], flat_ref, parts, kept_ref, sent_ref)
    rows = lax.broadcasted_iota(jnp.int32, (8, width), 0)
    extra = jnp.zeros((8, width), F32)
    for t in range(used // width):
        row = jnp.concatenate([sums[p, 0:1, t * 128 : (t + 1) * 128] for p in range(width // 128)], 1)
        extra = jnp.where(rows == t, row, extra)
    vectors = jnp.concatenate((bias_ref[0:8, :], extra), 0).astype(BF)
    at = sum(parts) // 2
    kept_ref[at : at + EXTRA, :] = vectors
    sent_ref[at : at + EXTRA, :] = vectors


def insert_rows(info, base, came):
    count = came.shape[0]

    def body(info_ref, came_ref, base_ref, out_ref, sem):
        start = (1 - info_ref[CORE]) * count
        copy = pltpu.make_async_copy(came_ref, out_ref.at[pl.ds(start, count)], sem)
        copy.start()
        copy.wait()

    anywhere = pl.BlockSpec(memory_space=pl.ANY)
    return pl.pallas_call(
        body,
        in_specs=[pl.BlockSpec(memory_space=pltpu.SMEM), anywhere, anywhere],
        out_specs=anywhere,
        out_shape=jax.ShapeDtypeStruct(base.shape, base.dtype),
        scratch_shapes=[pltpu.SemaphoreType.DMA],
        input_output_aliases={2: 0},
        name="insert",
    )(info, came, base)


def swap_cores(value):
    return lax.ppermute(value, "blk", [(0, 1), (1, 0)])


def stages(count, first=4):
    out = []
    stride = 1
    while stride < count:
        left = count // stride
        radix = first if not out and left % first == 0 else 4 if left % 4 == 0 else 2
        out.append((stride, radix))
        stride *= radix
    return out


def shifted(value, stage, steps, axis="samp"):
    stride, radix = stage
    count = lax.axis_size(axis)
    pairs = []
    for source in range(count):
        digit = (source // stride) % radix
        pairs.append((source, source + ((digit + steps) % radix - digit) * stride))
    return lax.ppermute(value, axis, pairs)


def small_call(kernel, args, outs, scratch=(), ties=(), name=None, through=()):
    n, t, m, o = len(args), len(ties), len(through), len(outs)

    def body(*refs):
        kernel(*refs[:n], *refs[n + t + m : n + t + m + o], *refs[n + t + 2 * m + o :])

    vmem = pl.BlockSpec(memory_space=pltpu.VMEM)
    size = lambda a: math.prod(a.shape) * jnp.dtype(a.dtype).itemsize
    total = sum(size(a) for a in (*args[1:], *outs)) + sum(
        math.prod(a.shape) * jnp.dtype(a.dtype).itemsize for a in scratch
    )
    return pl.pallas_call(
        body,
        in_specs=[
            pl.BlockSpec(memory_space=pltpu.SMEM),
            *[vmem] * (len(args) - 1),
            *[pl.BlockSpec(memory_space=pl.ANY)] * (t + m),
        ],
        out_specs=[vmem] * o + [pl.BlockSpec(memory_space=pl.ANY)] * m,
        out_shape=[*outs, *[jax.ShapeDtypeStruct(a.shape, a.dtype) for a in through]],
        scratch_shapes=list(scratch),
        input_output_aliases={n + t + k: o + k for k in range(m)},
        compiler_params=pltpu.CompilerParams(vmem_limit_bytes=2 * total + 4 * 2**20),
        name=name,
    )(*args, *ties, *through)


def spread_kernel(info_ref, *refs, count, radix, slot, extra):
    outputs = radix + (1 if extra and radix == 1 else 0)
    outs, total_ref = refs[count : count + outputs], refs[count + outputs]
    total = refs[0][...].astype(F32)
    for ref in refs[1:count]:
        total = total + ref[...].astype(F32)
    rows = total_ref.shape[0] - extra
    size = rows // radix
    total_ref[...] = total.astype(BF)
    if radix == 1:
        outs[0][...] = total_ref[:rows, :]
        if extra:
            outs[1][...] = total[rows:]
        return
    for k in range(radix):
        start = lax.rem(info_ref[slot] + k, radix) * size
        outs[k][:size, :] = total_ref[pl.ds(pl.multiple_of(start, 16), size), :]
        if extra:
            outs[k][size:, :] = total_ref[rows:, :]


def collect_kernel(info_ref, *refs, groups):
    at, out_at = 0, sum(groups)
    for count in groups:
        size = refs[at].shape[0]
        for k in range(count):
            refs[out_at][k * size : (k + 1) * size, :] = refs[at + k][...]
        at += count
        out_at += 1


class Layout:
    def __init__(self, count, rows):
        self.base = stages(count)
        self.count = count
        self.rows = rows
        table = np.zeros((2 * count, 1 + len(self.base)), np.int32)
        for device in range(2 * count):
            table[device, 0] = device % 2
            for i in range(len(self.base)):
                table[device, 1 + i] = self.digit(device, i)
        self.place = table.shape[1]
        places = np.stack([self.places(device, rows) for device in range(2 * count)])
        self.table = np.concatenate((table, places), 1).astype(np.int32)

    def digit(self, device, index):
        stride, radix = self.base[index]
        return (device // 2 // stride) % radix

    def places(self, device, rows):
        core = device % 2
        unit = rows // 2
        offsets = np.array([core * unit, (1 - core) * unit])
        for index, (_, radix) in enumerate(self.base):
            unit //= radix
            digit = (self.digit(device, index) - np.arange(radix)) % radix
            offsets = (offsets[:, None] + (digit * unit)[None, :]).reshape(-1)
        return offsets

    def own_places(self, rows):
        return np.array([self.places(device, rows)[0] for device in range(2 * self.count)], np.int32)


class Chain:
    def __init__(self, layout, info, extra=0):
        self.layout = layout
        self.info = info
        self.extra = extra
        self.rounds = len(layout.base)

    def start(self, kept, sent):
        self.pending = [kept, swap_cores(sent)]

    def scatter(self, level, ties=(), through=()):
        last = level == self.rounds
        radix = 1 if last else self.layout.base[level][1]
        rows, width = self.pending[0].shape
        size = (rows - self.extra) // radix
        if last:
            outs = [jax.ShapeDtypeStruct((size, width), BF)]
            if self.extra:
                outs.append(jax.ShapeDtypeStruct((self.extra, width), F32))
        else:
            outs = [jax.ShapeDtypeStruct((size + self.extra, width), BF)] * radix
        pieces = small_call(
            functools.partial(
                spread_kernel, count=len(self.pending), radix=radix, slot=1 + level, extra=self.extra
            ),
            (self.info, *self.pending), outs, [pltpu.VMEM((rows, width), BF)], ties, "spread", through,
        )
        self.through = pieces[len(outs) :]
        if last:
            self.value = pieces[0]
            self.vectors = pieces[1] if self.extra else None
        else:
            stage = self.layout.base[level]
            self.pending = [pieces[0]] + [shifted(pieces[k], stage, k) for k in range(1, radix)]
        return pieces[0]

    def gather(self, level):
        stage = self.layout.base[level]
        self.pending = [self.value] + [shifted(self.value, stage, k) for k in range(1, stage[1])]

    def collect(self, ties=()):
        size, width = self.pending[0].shape
        outs = [jax.ShapeDtypeStruct((len(self.pending) * size, width), BF)]
        self.value = small_call(
            functools.partial(collect_kernel, groups=(len(self.pending),)),
            (self.info, *self.pending), outs, (), ties, "collect",
        )[0]
        return self.value


def restore(place_ref, flat_ref, ref, unit, at):
    def body(i, carry):
        start = pl.multiple_of(place_ref[at + i], 16)
        source = pl.multiple_of(i * unit, 16)
        chunk = ref[pl.ds(source, unit), :]
        flat_ref[pl.ds(start, unit), :] = chunk
        return carry

    lax.fori_loop(0, ref.shape[0] // unit, body, 0)


def finish_mlp_kernel(place_ref, all_ref, vectors_ref, pack_ref, w1_ref, fc2_ref, fc1_ref, rows_ref, flat_ref, *, unit):
    restore(place_ref, flat_ref, all_ref, unit, 0)
    hidden, width = fc2_ref.shape
    fc2_ref[...] = flat_ref[:hidden, :].astype(F32)
    columns = pack_ref[0:8, :].T
    gain = jnp.zeros((width, 1), F32)
    shift = jnp.zeros((width, 1), F32)
    for j in range(hidden // width):
        cols = slice(j * width, (j + 1) * width)
        hats = flat_ref[hidden + j * width : hidden + (j + 1) * width, :].astype(F32)
        sums = vectors_ref[j : j + 1, :]
        fc1_ref[:, cols] = hats * columns[:, GAIN2 : GAIN2 + 1] + columns[:, SHIFT2 : SHIFT2 + 1] * sums
        w = w1_ref[:, cols].astype(F32)
        gain = gain + jnp.sum(w * hats, -1, keepdims=True)
        shift = shift + jnp.sum(w * sums, -1, keepdims=True)
    lane = lax.broadcasted_iota(jnp.int32, (width, 128), 1)
    rows_ref[...] = jnp.where(lane == 0, gain, jnp.where(lane == 1, shift, 0.0)).T[0:8]


def finish_kernel(
    info_ref, own_ref, far_ref, vectors_ref, pack_ref, w_ref, qkv_ref, out_ref, rows_ref, flat_ref, *, unit, at
):
    restore(info_ref, flat_ref, own_ref, unit, at)
    restore(info_ref, flat_ref, far_ref, unit, at + own_ref.shape[0] // unit)
    width = out_ref.shape[0]
    columns = qkv_ref.shape[1]
    out_ref[...] = flat_ref[columns : columns + width, :].astype(F32)
    gain = jnp.zeros((1, width), F32)
    shift = jnp.zeros((1, width), F32)
    turned = vectors_ref[8:16, :].T
    for t in range(columns // width):
        part = slice(t * width, (t + 1) * width)
        hats = flat_ref[part, :].astype(F32)
        sums = turned[:, t : t + 1]
        result = hats * row_of(pack_ref, GAIN1) + sums * row_of(pack_ref, SHIFT1)
        qkv_ref[:, part] = result.T
        w = w_ref[part, :].astype(F32)
        gain = gain + jnp.sum(w * hats, 0, keepdims=True)
        shift = shift + jnp.sum(w * sums, 0, keepdims=True)
    rows_ref[...] = jnp.concatenate((gain, shift, jnp.zeros((6, width), F32)), 0)


def pad_rows(count, unit):
    return -(-count // unit) * unit


def per_device(
    tokens, view_count, norm1_gain, norm1_bias, w_qkv, qv_bias, w_out, out_bias,
    norm2_gain, norm2_bias, w_fc1, fc1_bias, w_fc2, fc2_bias, cot_tokens, cot_cls,
):
    core = lax.axis_index("blk")
    cores = lax.axis_size("blk")
    count = lax.axis_size("samp")
    samples, half, width = tokens.shape
    local = samples // cores
    rows = half * cores
    hidden = w_fc1.shape[1]
    blocks = hidden // width
    heads = width // HEAD_DIM
    pairs = heads // 2
    sds = jax.ShapeDtypeStruct

    unit = 32 * count
    parts1 = [pad_rows(2 * hidden, unit)]
    parts2 = [pad_rows(4 * width, unit)]
    layout = Layout(count, parts2[0])
    device = lax.axis_index("samp") * cores + core
    info = lax.dynamic_index_in_dim(jnp.asarray(layout.table), device, 0, keepdims=False)

    theirs = (1 - core) * local
    far_tokens = swap_cores(lax.dynamic_slice_in_dim(tokens, theirs, local, 0))
    far_cot = swap_cores(lax.dynamic_slice_in_dim(cot_tokens, theirs, local, 0))

    pack = jnp.concatenate(
        (
            norm1_gain, norm1_bias, norm2_gain, norm2_bias, out_bias, fc2_bias, qv_bias, fc1_bias,
            jnp.zeros(((8 - blocks) * width,), BF),
        )
    ).astype(F32).reshape(16, width)

    vmem = pl.BlockSpec(memory_space=pltpu.VMEM)
    half_spec = lambda f: pl.BlockSpec((1, half, width), f)
    own_map = lambda s, b, *_: (b[CORE] * local + s, 0, 0)
    by_sample = lambda s, *_: (s, 0, 0)
    rows_spec = pl.BlockSpec((1, rows, width), by_sample)
    turned_spec = pl.BlockSpec((1, width, rows), by_sample)
    rstd_spec = pl.BlockSpec((1, rows, 1), by_sample)
    hidden_spec = pl.BlockSpec((1, rows, hidden), by_sample)
    eight_spec = pl.BlockSpec((1, 8, rows), by_sample)

    def big_call(kernel, prefetch, args, in_specs, outs, out_specs, scratch=(), ties=(), grid=(local,), name=None):
        n = len(prefetch) + len(args)

        def body(*refs):
            kernel(*refs[:n], *refs[n + len(ties) :])

        return pl.pallas_call(
            body,
            grid_spec=pltpu.PrefetchScalarGridSpec(
                num_scalar_prefetch=len(prefetch),
                grid=grid,
                in_specs=[*in_specs, *[pl.BlockSpec(memory_space=pl.ANY)] * len(ties)],
                out_specs=out_specs,
                scratch_shapes=list(scratch),
            ),
            out_shape=outs,
            compiler_params=params(("arbitrary",) * len(grid)),
            name=name,
        )(*prefetch, *args, *ties)

    hat1, qkv, cls_rows, stats, w_turned = big_call(
        project_kernel,
        (info, view_count),
        (tokens, far_tokens, w_qkv, pack, w_out, w_fc1, w_fc2, cot_cls),
        [half_spec(own_map), half_spec(by_sample), *[vmem] * 6],
        [
            sds((local, rows, width), BF),
            sds((local, 3 * width, rows), BF),
            sds((8, width), F32),
            sds((8, width), F32),
            sds((3 * width, width), BF),
        ],
        [rows_spec, pl.BlockSpec((1, 3 * width, rows), by_sample), vmem, vmem, vmem],
        [pltpu.VMEM((8, width), F32), pltpu.VMEM((8, width), F32), pltpu.VMEM((rows, width), BF)],
        name="project",
    )

    def add_kernel(info_ref, *refs):
        total = refs[0][...]
        for ref in refs[1:-1]:
            total = total + ref[...]
        refs[-1][...] = total

    *later, first = stages(count)

    def add_all(values, ties=()):
        return small_call(add_kernel, [info, *values], [sds((8, width), F32)], (), ties, "add")[0]

    stats = add_all([stats, swap_cores(stats)])
    stat_parts = [stats] + [shifted(stats, first, k) for k in range(1, first[1])]

    qkv_spec = lambda f: pl.BlockSpec((1, 3 * width, rows), f)
    totals, tops, plain, mixed = big_call(
        attention_kernel,
        (info, view_count),
        (qkv,),
        [qkv_spec(by_sample)],
        [
            sds((local, 8, rows), F32),
            sds((local, 8, rows), F32),
            sds((local,), jnp.int32),
            sds((local, width, rows), BF),
        ],
        [eight_spec, eight_spec, pl.BlockSpec(memory_space=pltpu.SMEM), turned_spec],
        [pltpu.VMEM((2, rows, rows), BF)],
        (stats,),
        name="attention",
    )

    tie = totals
    for stage in later:
        stats = add_all(stat_parts, (tie,))
        stat_parts = [stats] + [shifted(stats, stage, k) for k in range(1, stage[1])]
        tie = stats

    tokens_out_own, out_far, g_mid, d_mix, inner, out_grad, cls_norm, biases, kept1, sent1 = big_call(
        functools.partial(
            layer_kernel, samples=local * cores * count, parts=parts1, peers=len(stat_parts)
        ),
        (info,),
        (
            tokens, far_tokens, cot_tokens, far_cot, mixed, totals, cls_rows, cot_cls, *stat_parts,
            w_out, w_fc1, w_fc2, pack,
        ),
        [
            half_spec(own_map), half_spec(by_sample), half_spec(own_map), half_spec(by_sample),
            turned_spec, eight_spec, vmem, vmem, *[vmem] * len(stat_parts), vmem, vmem, vmem, vmem,
        ],
        [
            sds((samples, half, width), BF),
            sds((local, half, width), BF),
            sds((local, rows, width), BF),
            sds((local, width, rows), BF),
            sds((local, 8, rows), F32),
            sds((width, width), F32),
            sds((local, width), BF),
            sds((8, width), F32),
            sds((sum(parts1) // 2, width), BF),
            sds((sum(parts1) // 2, width), BF),
        ],
        [
            half_spec(own_map), half_spec(by_sample), rows_spec, turned_spec, eight_spec,
            vmem, vmem, vmem, vmem, vmem,
        ],
        [
            pltpu.VMEM((rows, width), BF),
            pltpu.VMEM((rows, width), F32),
            pltpu.VMEM((rows, hidden), BF),
            pltpu.VMEM((rows, hidden), BF),
            pltpu.VMEM((8, width), F32),
            pltpu.VMEM((hidden, width), F32),
            pltpu.VMEM((width, hidden), F32),
            pltpu.VMEM((sum(parts1), width), BF),
        ],
        name="layer",
    )
    chain1 = Chain(layout, info)
    chain1.start(kept1, sent1)
    out_came = swap_cores(out_far)

    def attention_back(sample, ties):
        place = lambda *_: (sample, 0, 0)
        return big_call(
            functools.partial(attention_back_kernel, sample=sample, samples=local),
            (info, view_count, plain),
            (qkv.reshape(local, 3, width, rows), tops, d_mix, inner, hat1),
            [
                pl.BlockSpec((1, 3, 128, rows), lambda p, *_: (sample, 0, p, 0)),
                pl.BlockSpec((1, 8, rows), place),
                pl.BlockSpec((1, 128, rows), lambda p, *_: (sample, p, 0)),
                pl.BlockSpec((1, 8, rows), place),
                pl.BlockSpec((1, rows, width), place),
            ],
            [
                sds((1, 3, width, rows), BF),
                sds((3, width, width), BF),
                sds((pairs, 8, 384), F32),
            ],
            [
                pl.BlockSpec((1, 3, 128, rows), lambda p, *_: (0, 0, p, 0)),
                pl.BlockSpec((3, 128, width), lambda p, *_: (0, p, 0)),
                pl.BlockSpec((1, 8, 384), lambda p, *_: (p, 0, 0)),
            ],
            [pltpu.VMEM((2, rows, rows), BF)],
            ties,
            grid=(pairs,),
            name="attention_back",
        )

    ties = (chain1.scatter(0),)
    d_parts, grads, sums = [], [], []
    for sample in range(local):
        d_part, grad, total = attention_back(sample, ties)
        d_parts.append(d_part.reshape(1, 3 * width, rows))
        grads.append(grad.reshape(3 * width, width))
        sums.append(total)
        ties = (total,)
        if sample < chain1.rounds:
            ties = (chain1.scatter(sample + 1, (total,)),)
        if sample == 0:
            tokens_out = insert_rows(info, tokens_out_own, out_came)
            ties = (*ties, tokens_out)
        if sample + 1 == chain1.rounds:
            gathered = lax.all_gather(chain1.value, ("samp", "blk"), axis=0, tiled=True)
    if chain1.rounds > local:
        for level in range(local + 1, chain1.rounds + 1):
            ties = (chain1.scatter(level),)
        gathered = lax.all_gather(chain1.value, ("samp", "blk"), axis=0, tiled=True)

    chain2 = Chain(layout, info, EXTRA)
    kept2, sent2 = small_call(
        functools.partial(pack_kernel, sets=len(grads), parts=parts2),
        (info, *grads, *sums, out_grad, biases),
        [sds((sum(parts2) // 2 + EXTRA, width), BF)] * 2,
        [pltpu.VMEM((sum(parts2), width), BF)],
        ties,
        name="pack",
    )
    chain2.start(kept2, sent2)
    tie = chain2.scatter(0)

    grad_own, grad_far = big_call(
        functools.partial(tokens_back_kernel, sets=len(d_parts)),
        (info,),
        (*d_parts, w_turned, pack, tokens, far_tokens, g_mid),
        [
            *[pl.BlockSpec(memory_space=pl.ANY)] * len(d_parts),
            vmem, vmem, half_spec(own_map), half_spec(by_sample), rows_spec,
        ],
        [sds((samples, half, width), BF), sds((local, half, width), BF)],
        [half_spec(own_map), half_spec(by_sample)],
        [
            pltpu.VMEM((rows, width), BF),
            pltpu.VMEM((len(d_parts), 3 * width, rows), BF),
            pltpu.SemaphoreType.DMA((len(d_parts),)),
        ],
        (tie,),
        name="tokens_back",
    )
    for level in range(1, chain2.rounds + 1):
        chain2.scatter(level, (), (grad_far,) if level == 1 else ())
        if level == 1:
            grad_came = swap_cores(chain2.through[0])
    ties = ()
    for level in reversed(range(chain2.rounds)):
        chain2.gather(level)
        if level == chain2.rounds - 1:
            grad_tokens = insert_rows(info, grad_own, grad_came)
            ties = (grad_tokens,)
        chain2.collect(ties)
        ties = ()
    other = swap_cores(chain2.value)

    grad_w_fc2, grad_w_fc1, rows2 = small_call(
        functools.partial(finish_mlp_kernel, unit=parts1[0] // (2 * count)),
        (jnp.asarray(layout.own_places(parts1[0])), gathered, chain2.vectors, pack, w_fc1),
        [sds((hidden, width), F32), sds((width, hidden), F32), sds((8, width), F32)],
        [pltpu.VMEM((parts1[0], width), BF)],
        (chain2.value,),
        name="finish_mlp",
    )
    grad_w_qkv, grad_w_out, rows1 = small_call(
        functools.partial(finish_kernel, unit=parts2[0] // (2 * count), at=layout.place),
        (info, chain2.value, other, chain2.vectors, pack, w_turned),
        [sds((width, 3 * width), F32), sds((width, width), F32), sds((8, width), F32)],
        [pltpu.VMEM((parts2[0], width), BF)],
        name="finish",
    )
    vectors = chain2.vectors
    grad_qv_bias = jnp.concatenate((vectors[8], vectors[10]))
    return (
        tokens_out, cls_norm, grad_tokens, rows1[0], rows1[1], grad_w_qkv, grad_qv_bias,
        grad_w_out, vectors[blocks + 1], rows2[0], rows2[1], grad_w_fc1,
        vectors[:blocks].reshape(hidden), grad_w_fc2, vectors[blocks],
    )


def solution(mesh):
    split = P("samp", "blk", None)
    classes = P(("samp", "blk"), None)
    return jax.shard_map(
        per_device,
        mesh=mesh,
        in_specs=(split, P("samp"), *([P()] * 12), split, classes),
        out_specs=(split, classes, split, *([P()] * 12)),
        check_vma=False,
    )
```

```python
import functools
import math

import jax
import jax.numpy as jnp
import numpy as np
from jax import lax
from jax.experimental import pallas as pl
from jax.experimental.pallas import tpu as pltpu
from jax.sharding import PartitionSpec as P

HEAD_DIM = 64
VIEW_ROWS = 196
NORM_EPS = 1e-06
CLS_EPS = 1e-05
MASKED = -1e30
LOG2E = math.log2(math.e)
LN2 = math.log(2.0)
SCALE = HEAD_DIM ** (-0.5)
SUM_LOW = 1e-15
SUM_HIGH = 1e15
BF = jnp.bfloat16
F32 = jnp.float32
VMEM_BYTES = 60 * 2**20
CORE = 0
EXTRA = 16


def dot(a, b, ca, cb):
    return lax.dot_general(a, b, (((ca,), (cb,)), ((), ())), preferred_element_type=F32)


def norm_parts(values):
    centre = jnp.mean(values, -1, keepdims=True)
    offset = values - centre
    rstd = lax.rsqrt(jnp.mean(offset * offset, -1, keepdims=True) + NORM_EPS)
    return offset * rstd, rstd


def gelu_cdf(values):
    return 0.5 + 0.5 * lax.erf(values * (0.5**0.5))


def params(semantics):
    return pltpu.CompilerParams(dimension_semantics=semantics, vmem_limit_bytes=VMEM_BYTES)


def whole(shape):
    return pl.BlockSpec(shape, lambda *_: (0,) * len(shape))


def key_counts(rows):
    views = (rows - 1) // VIEW_ROWS
    return [(v, min(rows, -(-(1 + VIEW_ROWS * v) // 16) * 16)) for v in range(1, views + 1)]


GAIN1, SHIFT1, GAIN2, SHIFT2, OUT_BIAS, FC2_BIAS, QV_BIAS, FC1_BIAS = 0, 1, 2, 3, 4, 5, 6, 8


def row_of(pack_ref, index):
    return pack_ref[index : index + 1, :]


def place_halves(target_ref, core, own, far):
    half = own.shape[0]
    target_ref[pl.ds(pl.multiple_of(core * half, 16), half), :] = own
    target_ref[pl.ds(pl.multiple_of((1 - core) * half, 16), half), :] = far


def split_halves(source_ref, core, own_ref, far_ref):
    half = own_ref.shape[1]
    own_ref[0] = source_ref[pl.ds(pl.multiple_of(core * half, 16), half), :]
    far_ref[0] = source_ref[pl.ds(pl.multiple_of((1 - core) * half, 16), half), :]


def rank_samples(views_ref, base, order_ref):
    count = order_ref.shape[0]
    views = [views_ref[base + i] for i in range(count)]
    for i in range(count):
        rank = jnp.int32(0)
        for j in range(count):
            if j != i:
                ahead = views[j] >= views[i] if j < i else views[j] > views[i]
                rank = rank + ahead.astype(jnp.int32)
        order_ref[rank] = jnp.int32(i)


def project_kernel(
    blk_ref, views_ref, own_ref, far_ref, w_in_ref, pack_ref, w_out_ref, w1_ref, w2_ref, cot_ref,
    hat_ref, qkv_ref, cls_ref, stat_ref, w_ref, order_ref, mix_ref, first_ref, full_ref,
):
    step = pl.program_id(0)

    @pl.when(step == 0)
    def _():
        w_ref[...] = w_in_ref[...].T
        rank_samples(views_ref, blk_ref[CORE] * order_ref.shape[0], order_ref)

    rows = hat_ref.shape[1]
    width = own_ref.shape[2]
    place_halves(full_ref, blk_ref[0], own_ref[0], far_ref[0])
    values = full_ref[...].astype(F32)
    hat, _ = norm_parts(values)
    hat_ref[0] = hat.astype(BF)
    normed = (hat * row_of(pack_ref, GAIN1) + row_of(pack_ref, SHIFT1)).astype(BF)
    columns = pack_ref[0:8, :].T
    for third in range(3):
        part = pl.ds(third * width, width)
        piece = dot(w_ref[part, :], normed, 1, 1)
        if third == 0:
            piece = (piece + columns[:, QV_BIAS : QV_BIAS + 1]) * (SCALE * LOG2E)
        if third == 2:
            piece = piece + columns[:, QV_BIAS + 1 : QV_BIAS + 2]
        qkv_ref[0, part, :] = piece.astype(BF)

    lead = qkv_ref[0, pl.ds(0, width), :128].astype(F32).T[0:1, :]
    head_of = lax.broadcasted_iota(jnp.int32, (8, width), 1) // HEAD_DIM
    pick = head_of == lax.broadcasted_iota(jnp.int32, (8, width), 0)
    queries = jnp.where(pick, lead, 0.0).astype(BF)
    scores = dot(queries, qkv_ref[0, pl.ds(width, width), :], 1, 0)
    limit = 1 + VIEW_ROWS * views_ref[blk_ref[CORE] * pl.num_programs(0) + step]
    place = lax.broadcasted_iota(jnp.int32, (8, rows), 1)
    scores = jnp.where(place < limit, scores, MASKED)
    powers = jnp.exp2(scores - jnp.max(scores, -1, keepdims=True))
    chances = (powers / jnp.sum(powers, -1, keepdims=True)).astype(BF)
    mixed = dot(chances, qkv_ref[0, pl.ds(2 * width, width), :], 1, 1)
    mix_ref[pl.ds(step, 1), :] = jnp.sum(jnp.where(pick, mixed, 0.0), 0, keepdims=True)
    first_ref[pl.ds(step, 1), :] = values[0:1, :]

    @pl.when(step == pl.num_programs(0) - 1)
    def _():
        branch = dot(mix_ref[...].astype(BF), w_out_ref[...], 1, 0) + row_of(pack_ref, OUT_BIAS)
        middle = first_ref[...] + branch
        normed2 = norm_parts(middle)[0] * row_of(pack_ref, GAIN2) + row_of(pack_ref, SHIFT2)
        normed2 = normed2.astype(BF)
        output = middle + row_of(pack_ref, FC2_BIAS)
        for j in range(w1_ref.shape[1] // width):
            cols = slice(j * width, (j + 1) * width)
            pre = dot(normed2, w1_ref[:, cols], 1, 0) + row_of(pack_ref, FC1_BIAS + j)
            act = (pre * gelu_cdf(pre)).astype(BF)
            output = output + dot(act, w2_ref[cols, :], 1, 0)
        cls_ref[...] = output
        count = cot_ref.shape[0]
        cls = output[:count]
        cot = cot_ref[...].astype(F32)
        stat_ref[...] = jnp.zeros_like(stat_ref)
        for k, term in enumerate((cls, cls * cls, cot, cot * cls)):
            stat_ref[k : k + 1, :] = jnp.sum(term, 0, keepdims=True)


def masked_tail(scores, main, limit):
    place = main + lax.broadcasted_iota(jnp.int32, scores.shape, 0)
    return jnp.where(place < limit, scores, MASKED)


def attention_kernel(
    core_ref, views_ref, qkv_ref, sum_ref, top_ref, plain_ref, att_ref, pow_ref
):
    sample = pl.program_id(0)
    rows = qkv_ref.shape[2]
    width = att_ref.shape[1]
    heads = width // HEAD_DIM
    views = views_ref[core_ref[CORE] * pl.num_programs(0) + sample]
    limit = 1 + VIEW_ROWS * views
    ones = jnp.ones((16, rows), BF)

    def store(h, mixed):
        total = mixed[HEAD_DIM : HEAD_DIM + 1]
        sum_ref[0, pl.ds(h, 1), :] = total
        att_ref[0, head_rows(h, 0), :] = (mixed[:HEAD_DIM] * (1.0 / total)).astype(BF)

    sum_ref[0, heads:8, :] = jnp.ones((8 - heads, rows), F32)
    for count, keys in key_counts(rows):

        @pl.when(views == count)
        def _(keys=keys):
            main = keys - 16

            def pair(p, carry):
                both = range(2)
                parts = [head_parts(qkv_ref, 2 * p + k, width, keys) for k in both]
                scores = [dot(key, query, 0, 0) for query, key, _ in parts]
                for k in both:
                    pow_ref[k, :main, :] = jnp.exp2(scores[k][:main]).astype(BF)
                    tail = masked_tail(scores[k][main:], main, limit)
                    pow_ref[k, main:keys, :] = jnp.exp2(tail).astype(BF)
                lefts = [jnp.concatenate((value, ones[:, :keys]), 0) for _, _, value in parts]
                mixed = [dot(lefts[k], pow_ref[k, :keys, :], 1, 0) for k in both]
                for k in both:
                    store(2 * p + k, mixed[k])
                return carry

            lax.fori_loop(0, heads // 2, pair, 0)

    totals = sum_ref[0]
    plain = (jnp.min(totals) > SUM_LOW) & (jnp.max(totals) < SUM_HIGH)
    plain_ref[sample] = plain.astype(jnp.int32)

    @pl.when(jnp.logical_not(plain))
    def _():
        @each_head(heads)
        def _(h, slot):
            query, key, value = head_parts(qkv_ref, h, width, rows)
            scores = masked_tail(dot(key, query, 0, 0), 0, limit)
            top = jnp.max(scores, 0, keepdims=True)
            top_ref[0, pl.ds(h, 1), :] = top
            pow_ref[slot] = jnp.exp2(scores - top).astype(BF)
            left = jnp.concatenate((value, ones), 0)
            store(h, dot(left, pow_ref[slot], 1, 0))


def each_head(heads):
    def run(body):
        def pair(p, carry):
            for slot in range(2):
                body(2 * p + slot, slot)
            return carry

        lax.fori_loop(0, heads // 2, pair, 0)

    return run


def head_rows(h, base):
    return pl.ds(pl.multiple_of(base + h * HEAD_DIM, HEAD_DIM), HEAD_DIM)


def head_parts(qkv_ref, h, width, keys):
    return (
        qkv_ref[0, head_rows(h, 0), :],
        qkv_ref[0, head_rows(h, width), :keys],
        qkv_ref[0, head_rows(h, 2 * width), :keys],
    )


def layer_kernel(
    core_ref, x_own_ref, x_far_ref, own_ref, far_ref, att_ref, sum_ref, cls_ref, cot_ref, *refs,
    samples, parts, peers
):
    stat_refs = refs[:peers]
    w_out_ref, w1_ref, w2_ref, pack_ref = refs[peers : peers + 4]
    (
        out_own_ref, out_far_ref, gmid_ref, dmix_ref, inner_ref, out_grad_ref, norm_ref, bias_ref,
        kept_ref, sent_ref,
    ) = refs[peers + 4 : peers + 14]
    full_ref, g_ref, act_ref, dpre_ref, dcls_ref, acc2_ref, acc1_ref, flat_ref = refs[peers + 14 :]
    step = pl.program_id(0)
    width = own_ref.shape[2]
    hidden = w2_ref.shape[0]
    blocks = hidden // width

    @pl.when(step == 0)
    def _():
        acc2_ref[...] = jnp.zeros_like(acc2_ref)
        acc1_ref[...] = jnp.zeros_like(acc1_ref)
        bias_ref[...] = jnp.zeros_like(bias_ref)
        out_grad_ref[...] = jnp.zeros_like(out_grad_ref)
        stats = stat_refs[0][...]
        for other in stat_refs[1:]:
            stats = stats + other[...]
        local = cot_ref.shape[0]
        cls = cls_ref[...][:local]
        cot = cot_ref[...].astype(F32)
        mean = stats[0:1] / samples
        scale = lax.rsqrt(stats[1:2] / samples - mean * mean + CLS_EPS)
        hat = (cls - mean) * scale
        norm_ref[...] = hat.astype(BF)
        cross = scale * (stats[3:4] - mean * stats[2:3])
        dcls_ref[...] = jnp.zeros_like(dcls_ref)
        dcls_ref[:local, :] = scale * (cot - stats[2:3] / samples - hat * (cross / samples))

    place_halves(full_ref, core_ref[CORE], x_own_ref[0], x_far_ref[0])
    place_halves(g_ref, core_ref[CORE], own_ref[0].astype(F32), far_ref[0].astype(F32))
    g_ref[0:1, :] = g_ref[0:1, :] + dcls_ref[pl.ds(step, 1), :]
    g_mlp = g_ref[...].astype(BF)
    bias_ref[blocks : blocks + 1, :] += jnp.sum(g_mlp.astype(F32), 0, keepdims=True)

    branch = dot(att_ref[0], w_out_ref[...], 0, 0) + row_of(pack_ref, OUT_BIAS)
    middle = full_ref[...].astype(F32) + branch
    hat, rstd = norm_parts(middle)
    normed = (hat * row_of(pack_ref, GAIN2) + row_of(pack_ref, SHIFT2)).astype(BF)
    hat_low = hat.astype(BF)
    for j in range(blocks):
        cols = slice(j * width, (j + 1) * width)
        pre = dot(normed, w1_ref[:, cols], 1, 0) + row_of(pack_ref, FC1_BIAS + j)
        d_act = dot(g_mlp, w2_ref[cols, :], 1, 1)
        cdf = gelu_cdf(pre)
        bell = jnp.exp2(pre * pre * (-0.5 * LOG2E) - 0.5 * math.log2(2.0 * math.pi))
        act_ref[:, cols] = (pre * cdf).astype(BF)
        d_pre = d_act * (cdf + pre * bell)
        bias_ref[j : j + 1, :] += jnp.sum(d_pre, 0, keepdims=True)
        dpre_ref[:, cols] = d_pre.astype(BF)
    acc1_ref[...] += dot(hat_low, dpre_ref[...], 0, 0)
    acc2_ref[...] += dot(act_ref[...], g_mlp, 0, 0)
    output = middle + dot(act_ref[...], w2_ref[...], 1, 0) + row_of(pack_ref, FC2_BIAS)
    full_ref[...] = output.astype(BF)
    split_halves(full_ref, core_ref[CORE], out_own_ref, out_far_ref)

    d_norm = dot(dpre_ref[...], w1_ref[...], 1, 1)
    u = d_norm * row_of(pack_ref, GAIN2)
    g_mid = g_ref[...] + rstd * (
        u - jnp.mean(u, -1, keepdims=True) - hat * jnp.mean(u * hat, -1, keepdims=True)
    )
    g_attn = g_mid.astype(BF)
    gmid_ref[0] = g_attn
    out_grad_ref[...] += dot(att_ref[0], g_attn, 1, 0)
    bias_ref[blocks + 1 : blocks + 2, :] += jnp.sum(g_attn.astype(F32), 0, keepdims=True)
    d_mix = dot(w_out_ref[...], g_attn, 1, 1)
    for h in range(width // HEAD_DIM):
        part = slice(h * HEAD_DIM, (h + 1) * HEAD_DIM)
        piece = d_mix[part] * (1.0 / sum_ref[0, h : h + 1, :])
        dmix_ref[0, part, :] = piece.astype(BF)
        inner_ref[0, h : h + 1, :] = jnp.sum(piece * att_ref[0, part, :].astype(F32), 0, keepdims=True)

    @pl.when(step == pl.num_programs(0) - 1)
    def _():
        flat_ref[:hidden, :] = acc2_ref[...].astype(BF)
        for j in range(blocks):
            rows = slice(hidden + j * width, hidden + (j + 1) * width)
            flat_ref[rows, :] = acc1_ref[:, j * width : (j + 1) * width].astype(BF)
        clear_rest(flat_ref, 2 * hidden)
        write_halves(core_ref[CORE], flat_ref, parts, kept_ref, sent_ref)


def attention_back_kernel(
    core_ref, views_ref, plain_ref, order_ref, qkv_ref, top_ref, dmix_ref, inner_ref, hat_ref,
    dqkv_ref, grad_ref, sums_ref, pow_ref, *, turn, samples
):
    pair = pl.program_id(0)
    sample = order_ref[turn]
    rows, width = hat_ref.shape[1:]
    views = views_ref[core_ref[CORE] * samples + sample]
    limit = 1 + VIEW_ROWS * views
    plain = plain_ref[sample] == 1
    both = range(2)
    lanes = [slice(k * HEAD_DIM, (k + 1) * HEAD_DIM) for k in both]

    def back(keys, powers_of):
        query = [qkv_ref[0, 0, part, :] for part in lanes]
        key = [qkv_ref[0, 1, part, :keys] for part in lanes]
        value = [qkv_ref[0, 2, part, :keys] for part in lanes]
        d_mix = [dmix_ref[0, part, :] for part in lanes]
        scores = [dot(key[k], query[k], 0, 0) for k in both]
        for k in both:
            powers_of(k, scores[k])
        d_weights = [dot(value[k], d_mix[k], 0, 0) for k in both]
        d_scores = []
        for k in both:
            inner = inner_ref[0, pl.ds(2 * pair + k, 1), :]
            powers = pow_ref[k, :keys, :].astype(F32)
            d_scores.append((powers * (d_weights[k] - inner)).astype(BF))
        for k in both:
            d_value = dot(d_mix[k], pow_ref[k, :keys, :], 1, 1)
            dqkv_ref[0, 2, lanes[k], :keys] = d_value.astype(BF)
        for k in both:
            d_query = dot(key[k], d_scores[k], 1, 0) * SCALE
            dqkv_ref[0, 0, lanes[k], :] = d_query.astype(BF)
            d_key = dot(query[k], d_scores[k], 1, 1) * LN2
            dqkv_ref[0, 1, lanes[k], :keys] = d_key.astype(BF)
        if keys < rows:
            blank = jnp.zeros((2 * HEAD_DIM, rows - keys), BF)
            dqkv_ref[0, 1, :, keys:] = blank
            dqkv_ref[0, 2, :, keys:] = blank

    for count, keys in key_counts(rows):

        @pl.when((views == count) & plain)
        def _(keys=keys):
            main = keys - 16

            def powers_of(k, scores):
                pow_ref[k, :main, :] = jnp.exp2(scores[:main]).astype(BF)
                tail = masked_tail(scores[main:], main, limit)
                pow_ref[k, main:keys, :] = jnp.exp2(tail).astype(BF)

            back(keys, powers_of)

    @pl.when(jnp.logical_not(plain))
    def _():
        def powers_of(k, scores):
            top = top_ref[0, pl.ds(2 * pair + k, 1), :]
            pow_ref[k] = jnp.exp2(masked_tail(scores, 0, limit) - top).astype(BF)

        back(rows, powers_of)

    right = jnp.concatenate((hat_ref[0], jnp.ones((rows, 128), BF)), 1)
    result = dot(dqkv_ref[0].reshape(3 * 2 * HEAD_DIM, rows), right, 1, 0)
    grad_ref[...] = result[:, :width].astype(BF).reshape(grad_ref.shape)
    sums_ref[0] = result[:, width:].T[:8]


def tokens_back_kernel(core_ref, order_ref, *refs, sets):
    dqkv_refs = refs[:sets]
    w_ref, pack_ref, x_own_ref, x_far_ref, gmid_ref, own_ref, far_ref, out_ref, d_ref, sems = refs[sets:]
    step = pl.program_id(0)

    def fetch(k):
        return pltpu.make_async_copy(dqkv_refs[k].at[0], d_ref.at[k], sems.at[k])

    @pl.when(step == 0)
    def _():
        for k in range(sets):
            fetch(k).start()

    for k in range(sets):

        @pl.when(step == k)
        def _(k=k):
            fetch(k).wait()

    d_norm = dot(d_ref[step], w_ref[...], 0, 0)
    place_halves(out_ref, core_ref[CORE], x_own_ref[0], x_far_ref[0])
    hat, rstd = norm_parts(out_ref[...].astype(F32))
    w = d_norm * row_of(pack_ref, GAIN1)
    back = rstd * (w - jnp.mean(w, -1, keepdims=True) - hat * jnp.mean(w * hat, -1, keepdims=True))
    out_ref[...] = (gmid_ref[0].astype(F32) + back).astype(BF)
    split_halves(out_ref, core_ref[CORE], own_ref, far_ref)


def clear_rest(ref, used):
    if ref.shape[0] > used:
        ref[used:, :] = jnp.zeros((ref.shape[0] - used, ref.shape[1]), ref.dtype)


def write_halves(core, flat_ref, parts, kept_ref, sent_ref):
    start = at = 0
    for size in parts:
        half = size // 2
        mine = pl.multiple_of(start + core * half, 16)
        other = pl.multiple_of(start + (1 - core) * half, 16)
        kept_ref[at : at + half, :] = flat_ref[pl.ds(mine, half), :]
        sent_ref[at : at + half, :] = flat_ref[pl.ds(other, half), :]
        start += size
        at += half


def pack_kernel(core_ref, *refs, sets, parts):
    grad_refs = refs[:sets]
    sums_refs = refs[sets : 2 * sets]
    out_grad_ref, bias_ref, kept_ref, sent_ref, flat_ref = refs[2 * sets :]
    width = out_grad_ref.shape[0]
    used = grad_refs[0].shape[0]
    total, sums = grad_refs[0][...].astype(F32), sums_refs[0][...]
    for grad_ref, sums_ref in zip(grad_refs[1:], sums_refs[1:]):
        total = total + grad_ref[...].astype(F32)
        sums = sums + sums_ref[...]
    flat_ref[:used, :] = total.astype(BF)
    flat_ref[used : used + width, :] = out_grad_ref[...].astype(BF)
    clear_rest(flat_ref, used + width)
    write_halves(core_ref[CORE], flat_ref, parts, kept_ref, sent_ref)
    rows = lax.broadcasted_iota(jnp.int32, (8, width), 0)
    extra = jnp.zeros((8, width), F32)
    for t in range(used // width):
        row = jnp.concatenate([sums[p, 0:1, t * 128 : (t + 1) * 128] for p in range(width // 128)], 1)
        extra = jnp.where(rows == t, row, extra)
    vectors = jnp.concatenate((bias_ref[0:8, :], extra), 0).astype(BF)
    at = sum(parts) // 2
    kept_ref[at : at + EXTRA, :] = vectors
    sent_ref[at : at + EXTRA, :] = vectors


def insert_rows(info, base, came):
    count = came.shape[0]
    block = (1, *came.shape[1:])

    def body(info_ref, came_ref, base_ref, out_ref):
        out_ref[...] = came_ref[...]

    return pl.pallas_call(
        body,
        grid_spec=pltpu.PrefetchScalarGridSpec(
            num_scalar_prefetch=1,
            grid=(count,),
            in_specs=[
                pl.BlockSpec(block, lambda s, *_: (s, 0, 0)), pl.BlockSpec(memory_space=pltpu.HBM),
            ],
            out_specs=pl.BlockSpec(block, lambda s, b: ((1 - b[CORE]) * count + s, 0, 0)),
        ),
        out_shape=jax.ShapeDtypeStruct(base.shape, base.dtype),
        input_output_aliases={2: 0},
        compiler_params=params(("arbitrary",)),
        name="insert",
    )(info, came, base)


def swap_cores(value):
    return lax.ppermute(value, "blk", [(0, 1), (1, 0)])


def stages(count, first=4):
    out = []
    stride = 1
    while stride < count:
        left = count // stride
        radix = first if not out and left % first == 0 else 4 if left % 4 == 0 else 2
        out.append((stride, radix))
        stride *= radix
    return out


def shifted(value, stage, steps, axis="samp"):
    stride, radix = stage
    count = lax.axis_size(axis)
    pairs = []
    for source in range(count):
        digit = (source // stride) % radix
        pairs.append((source, source + ((digit + steps) % radix - digit) * stride))
    return lax.ppermute(value, axis, pairs)


def small_call(kernel, args, outs, scratch=(), ties=(), name=None, through=()):
    n, t, m, o = len(args), len(ties), len(through), len(outs)

    def body(*refs):
        kernel(*refs[:n], *refs[n + t + m : n + t + m + o], *refs[n + t + 2 * m + o :])

    vmem = pl.BlockSpec(memory_space=pltpu.VMEM)
    size = lambda a: math.prod(a.shape) * jnp.dtype(a.dtype).itemsize
    total = sum(size(a) for a in (*args[1:], *outs)) + sum(
        math.prod(a.shape) * jnp.dtype(a.dtype).itemsize for a in scratch
    )
    return pl.pallas_call(
        body,
        in_specs=[
            pl.BlockSpec(memory_space=pltpu.SMEM),
            *[vmem] * (len(args) - 1),
            *[pl.BlockSpec(memory_space=pltpu.HBM)] * (t + m),
        ],
        out_specs=[vmem] * o + [pl.BlockSpec(memory_space=pltpu.HBM)] * m,
        out_shape=[*outs, *[jax.ShapeDtypeStruct(a.shape, a.dtype) for a in through]],
        scratch_shapes=list(scratch),
        input_output_aliases={n + t + k: o + k for k in range(m)},
        compiler_params=pltpu.CompilerParams(vmem_limit_bytes=2 * total + 4 * 2**20),
        name=name,
    )(*args, *ties, *through)


def spread_kernel(info_ref, *refs, count, radix, slot, extra):
    outputs = radix + (1 if extra and radix == 1 else 0)
    outs, total_ref = refs[count : count + outputs], refs[count + outputs]
    total = refs[0][...].astype(F32)
    for ref in refs[1:count]:
        total = total + ref[...].astype(F32)
    rows = total_ref.shape[0] - extra
    size = rows // radix
    total_ref[...] = total.astype(BF)
    if radix == 1:
        outs[0][...] = total_ref[:rows, :]
        if extra:
            outs[1][...] = total[rows:]
        return
    for k in range(radix):
        start = lax.rem(info_ref[slot] + k, radix) * size
        outs[k][:size, :] = total_ref[pl.ds(pl.multiple_of(start, 16), size), :]
        if extra:
            outs[k][size:, :] = total_ref[rows:, :]


def collect_kernel(info_ref, *refs, groups):
    at, out_at = 0, sum(groups)
    for count in groups:
        size = refs[at].shape[0]
        for k in range(count):
            refs[out_at][k * size : (k + 1) * size, :] = refs[at + k][...]
        at += count
        out_at += 1


class Layout:
    def __init__(self, count, rows):
        self.base = stages(count)
        self.count = count
        self.rows = rows
        table = np.zeros((2 * count, 1 + len(self.base)), np.int32)
        for device in range(2 * count):
            table[device, 0] = device % 2
            for i in range(len(self.base)):
                table[device, 1 + i] = self.digit(device, i)
        self.place = table.shape[1]
        places = np.stack([self.places(device, rows) for device in range(2 * count)])
        self.table = np.concatenate((table, places), 1).astype(np.int32)

    def digit(self, device, index):
        stride, radix = self.base[index]
        return (device // 2 // stride) % radix

    def places(self, device, rows):
        core = device % 2
        unit = rows // 2
        offsets = np.array([core * unit, (1 - core) * unit])
        for index, (_, radix) in enumerate(self.base):
            unit //= radix
            digit = (self.digit(device, index) - np.arange(radix)) % radix
            offsets = (offsets[:, None] + (digit * unit)[None, :]).reshape(-1)
        return offsets

    def own_places(self, rows):
        return np.array([self.places(device, rows)[0] for device in range(2 * self.count)], np.int32)


class Chain:
    def __init__(self, layout, info, extra=0):
        self.layout = layout
        self.info = info
        self.extra = extra
        self.rounds = len(layout.base)

    def start(self, kept, sent):
        self.pending = [kept, swap_cores(sent)]

    def scatter(self, level, ties=(), through=()):
        last = level == self.rounds
        radix = 1 if last else self.layout.base[level][1]
        rows, width = self.pending[0].shape
        size = (rows - self.extra) // radix
        if last:
            outs = [jax.ShapeDtypeStruct((size, width), BF)]
            if self.extra:
                outs.append(jax.ShapeDtypeStruct((self.extra, width), F32))
        else:
            outs = [jax.ShapeDtypeStruct((size + self.extra, width), BF)] * radix
        pieces = small_call(
            functools.partial(
                spread_kernel, count=len(self.pending), radix=radix, slot=1 + level, extra=self.extra
            ),
            (self.info, *self.pending), outs, [pltpu.VMEM((rows, width), BF)], ties, "spread", through,
        )
        self.through = pieces[len(outs) :]
        if last:
            self.value = pieces[0]
            self.vectors = pieces[1] if self.extra else None
        else:
            stage = self.layout.base[level]
            self.pending = [pieces[0]] + [shifted(pieces[k], stage, k) for k in range(1, radix)]
        return pieces[0]

    def gather(self, level):
        stage = self.layout.base[level]
        self.pending = [self.value] + [shifted(self.value, stage, k) for k in range(1, stage[1])]

    def collect(self, ties=()):
        size, width = self.pending[0].shape
        outs = [jax.ShapeDtypeStruct((len(self.pending) * size, width), BF)]
        self.value = small_call(
            functools.partial(collect_kernel, groups=(len(self.pending),)),
            (self.info, *self.pending), outs, (), ties, "collect",
        )[0]
        return self.value


def restore(place_ref, flat_ref, ref, unit, at):
    def body(i, carry):
        start = pl.multiple_of(place_ref[at + i], 16)
        source = pl.multiple_of(i * unit, 16)
        chunk = ref[pl.ds(source, unit), :]
        flat_ref[pl.ds(start, unit), :] = chunk
        return carry

    lax.fori_loop(0, ref.shape[0] // unit, body, 0)


def finish_mlp_kernel(place_ref, all_ref, vectors_ref, pack_ref, w1_ref, fc2_ref, fc1_ref, gain_ref, shift_ref, fc1_bias_ref, fc2_bias_ref, flat_ref, *, unit):
    restore(place_ref, flat_ref, all_ref, unit, 0)
    hidden, width = fc2_ref.shape
    fc2_ref[...] = flat_ref[:hidden, :].astype(F32)
    columns = pack_ref[0:8, :].T
    gain = jnp.zeros((width, 1), F32)
    shift = jnp.zeros((width, 1), F32)
    for j in range(hidden // width):
        cols = slice(j * width, (j + 1) * width)
        hats = flat_ref[hidden + j * width : hidden + (j + 1) * width, :].astype(F32)
        sums = vectors_ref[j : j + 1, :]
        fc1_ref[:, cols] = hats * columns[:, GAIN2 : GAIN2 + 1] + columns[:, SHIFT2 : SHIFT2 + 1] * sums
        w = w1_ref[:, cols].astype(F32)
        gain = gain + jnp.sum(w * hats, -1, keepdims=True)
        shift = shift + jnp.sum(w * sums, -1, keepdims=True)
    lane = lax.broadcasted_iota(jnp.int32, (width, 128), 1)
    both = jnp.where(lane == 0, gain, jnp.where(lane == 1, shift, 0.0)).T[0:8]
    gain_ref[...] = both[0]
    shift_ref[...] = both[1]
    blocks = hidden // width
    for j in range(blocks):
        fc1_bias_ref[j * width : (j + 1) * width] = vectors_ref[j, :]
    fc2_bias_ref[...] = vectors_ref[blocks, :]


def finish_kernel(
    info_ref, own_ref, far_ref, vectors_ref, pack_ref, w_ref, qkv_ref, out_ref, gain_ref, shift_ref, qv_ref, out_bias_ref, flat_ref,
    *, unit, at, blocks
):
    restore(info_ref, flat_ref, own_ref, unit, at)
    restore(info_ref, flat_ref, far_ref, unit, at + own_ref.shape[0] // unit)
    width = out_ref.shape[0]
    columns = qkv_ref.shape[1]
    out_ref[...] = flat_ref[columns : columns + width, :].astype(F32)
    gain = jnp.zeros((1, width), F32)
    shift = jnp.zeros((1, width), F32)
    turned = vectors_ref[8:16, :].T
    for t in range(columns // width):
        part = slice(t * width, (t + 1) * width)
        hats = flat_ref[part, :].astype(F32)
        sums = turned[:, t : t + 1]
        result = hats * row_of(pack_ref, GAIN1) + sums * row_of(pack_ref, SHIFT1)
        qkv_ref[:, part] = result.T
        w = w_ref[part, :].astype(F32)
        gain = gain + jnp.sum(w * hats, 0, keepdims=True)
        shift = shift + jnp.sum(w * sums, 0, keepdims=True)
    gain_ref[...] = gain[0]
    shift_ref[...] = shift[0]
    qv_ref[:width] = vectors_ref[8, :]
    qv_ref[width:] = vectors_ref[10, :]
    out_bias_ref[...] = vectors_ref[blocks + 1, :]


def pad_rows(count, unit):
    return -(-count // unit) * unit


def per_device(
    tokens, view_count, norm1_gain, norm1_bias, w_qkv, qv_bias, w_out, out_bias,
    norm2_gain, norm2_bias, w_fc1, fc1_bias, w_fc2, fc2_bias, cot_tokens, cot_cls,
):
    core = lax.axis_index("blk")
    cores = lax.axis_size("blk")
    count = lax.axis_size("samp")
    samples, half, width = tokens.shape
    local = samples // cores
    rows = half * cores
    hidden = w_fc1.shape[1]
    blocks = hidden // width
    heads = width // HEAD_DIM
    pairs = heads // 2
    sds = jax.ShapeDtypeStruct

    unit = 32 * count
    parts1 = [pad_rows(2 * hidden, unit)]
    parts2 = [pad_rows(4 * width, unit)]
    layout = Layout(count, parts2[0])
    device = lax.axis_index("samp") * cores + core
    info = lax.dynamic_index_in_dim(jnp.asarray(layout.table), device, 0, keepdims=False)

    theirs = (1 - core) * local
    far_tokens = swap_cores(lax.dynamic_slice_in_dim(tokens, theirs, local, 0))
    far_cot = swap_cores(lax.dynamic_slice_in_dim(cot_tokens, theirs, local, 0))

    pack = jnp.concatenate(
        (
            norm1_gain, norm1_bias, norm2_gain, norm2_bias, out_bias, fc2_bias, qv_bias, fc1_bias,
            jnp.zeros(((8 - blocks) * width,), BF),
        )
    ).astype(F32).reshape(16, width)

    vmem = pl.BlockSpec(memory_space=pltpu.VMEM)
    half_spec = lambda f: pl.BlockSpec((1, half, width), f)
    own_map = lambda s, b, *_: (b[CORE] * local + s, 0, 0)
    by_sample = lambda s, *_: (s, 0, 0)
    rows_spec = pl.BlockSpec((1, rows, width), by_sample)
    turned_spec = pl.BlockSpec((1, width, rows), by_sample)
    rstd_spec = pl.BlockSpec((1, rows, 1), by_sample)
    hidden_spec = pl.BlockSpec((1, rows, hidden), by_sample)
    eight_spec = pl.BlockSpec((1, 8, rows), by_sample)

    def big_call(kernel, prefetch, args, in_specs, outs, out_specs, scratch=(), ties=(), grid=(local,), name=None):
        n = len(prefetch) + len(args)

        def body(*refs):
            kernel(*refs[:n], *refs[n + len(ties) :])

        return pl.pallas_call(
            body,
            grid_spec=pltpu.PrefetchScalarGridSpec(
                num_scalar_prefetch=len(prefetch),
                grid=grid,
                in_specs=[*in_specs, *[pl.BlockSpec(memory_space=pl.ANY)] * len(ties)],
                out_specs=out_specs,
                scratch_shapes=list(scratch),
            ),
            out_shape=outs,
            compiler_params=params(("arbitrary",) * len(grid)),
            name=name,
        )(*prefetch, *args, *ties)

    hat1, qkv, cls_rows, stats, w_turned, order = big_call(
        project_kernel,
        (info, view_count),
        (tokens, far_tokens, w_qkv, pack, w_out, w_fc1, w_fc2, cot_cls),
        [half_spec(own_map), half_spec(by_sample), *[vmem] * 6],
        [
            sds((local, rows, width), BF),
            sds((local, 3 * width, rows), BF),
            sds((8, width), F32),
            sds((8, width), F32),
            sds((3 * width, width), BF),
            sds((local,), jnp.int32),
        ],
        [
            rows_spec, pl.BlockSpec((1, 3 * width, rows), by_sample), vmem, vmem, vmem,
            pl.BlockSpec(memory_space=pltpu.SMEM),
        ],
        [pltpu.VMEM((8, width), F32), pltpu.VMEM((8, width), F32), pltpu.VMEM((rows, width), BF)],
        name="project",
    )

    def add_kernel(info_ref, *refs):
        total = refs[0][...]
        for ref in refs[1:-1]:
            total = total + ref[...]
        refs[-1][...] = total

    *later, first = stages(count)

    def add_all(values, ties=()):
        return small_call(add_kernel, [info, *values], [sds((8, width), F32)], (), ties, "add")[0]

    stats = add_all([stats, swap_cores(stats)])
    stat_parts = [stats] + [shifted(stats, first, k) for k in range(1, first[1])]

    qkv_spec = lambda f: pl.BlockSpec((1, 3 * width, rows), f)
    totals, tops, plain, mixed = big_call(
        attention_kernel,
        (info, view_count),
        (qkv,),
        [qkv_spec(by_sample)],
        [
            sds((local, 8, rows), F32),
            sds((local, 8, rows), F32),
            sds((local,), jnp.int32),
            sds((local, width, rows), BF),
        ],
        [eight_spec, eight_spec, pl.BlockSpec(memory_space=pltpu.SMEM), turned_spec],
        [pltpu.VMEM((2, rows, rows), BF)],
        (stats,),
        name="attention",
    )

    tie = totals
    for stage in later:
        stats = add_all(stat_parts, (tie,))
        stat_parts = [stats] + [shifted(stats, stage, k) for k in range(1, stage[1])]
        tie = stats

    tokens_out_own, out_far, g_mid, d_mix, inner, out_grad, cls_norm, biases, kept1, sent1 = big_call(
        functools.partial(
            layer_kernel, samples=local * cores * count, parts=parts1, peers=len(stat_parts)
        ),
        (info,),
        (
            tokens, far_tokens, cot_tokens, far_cot, mixed, totals, cls_rows, cot_cls, *stat_parts,
            w_out, w_fc1, w_fc2, pack,
        ),
        [
            half_spec(own_map), half_spec(by_sample), half_spec(own_map), half_spec(by_sample),
            turned_spec, eight_spec, vmem, vmem, *[vmem] * len(stat_parts), vmem, vmem, vmem, vmem,
        ],
        [
            sds((samples, half, width), BF),
            sds((local, half, width), BF),
            sds((local, rows, width), BF),
            sds((local, width, rows), BF),
            sds((local, 8, rows), F32),
            sds((width, width), F32),
            sds((local, width), BF),
            sds((8, width), F32),
            sds((sum(parts1) // 2, width), BF),
            sds((sum(parts1) // 2, width), BF),
        ],
        [
            half_spec(own_map), half_spec(by_sample), rows_spec, turned_spec, eight_spec,
            vmem, vmem, vmem, vmem, vmem,
        ],
        [
            pltpu.VMEM((rows, width), BF),
            pltpu.VMEM((rows, width), F32),
            pltpu.VMEM((rows, hidden), BF),
            pltpu.VMEM((rows, hidden), BF),
            pltpu.VMEM((8, width), F32),
            pltpu.VMEM((hidden, width), F32),
            pltpu.VMEM((width, hidden), F32),
            pltpu.VMEM((sum(parts1), width), BF),
        ],
        name="layer",
    )
    chain1 = Chain(layout, info)
    chain1.start(kept1, sent1)
    out_came = swap_cores(out_far)

    def attention_back(turn, ties):
        place = lambda p, c, v, q, o: (o[turn], 0, 0)
        return big_call(
            functools.partial(attention_back_kernel, turn=turn, samples=local),
            (info, view_count, plain, order),
            (qkv.reshape(local, 3, width, rows), tops, d_mix, inner, hat1),
            [
                pl.BlockSpec((1, 3, 128, rows), lambda p, c, v, q, o: (o[turn], 0, p, 0)),
                pl.BlockSpec((1, 8, rows), place),
                pl.BlockSpec((1, 128, rows), lambda p, c, v, q, o: (o[turn], p, 0)),
                pl.BlockSpec((1, 8, rows), place),
                pl.BlockSpec((1, rows, width), place),
            ],
            [
                sds((1, 3, width, rows), BF),
                sds((3, width, width), BF),
                sds((pairs, 8, 384), F32),
            ],
            [
                pl.BlockSpec((1, 3, 128, rows), lambda p, *_: (0, 0, p, 0)),
                pl.BlockSpec((3, 128, width), lambda p, *_: (0, p, 0)),
                pl.BlockSpec((1, 8, 384), lambda p, *_: (p, 0, 0)),
            ],
            [pltpu.VMEM((2, rows, rows), BF)],
            ties,
            grid=(pairs,),
            name="attention_back",
        )

    ties = (chain1.scatter(0),)
    d_parts, grads, sums = [], [], []
    for sample in range(local):
        d_part, grad, total = attention_back(sample, ties)
        d_parts.append(d_part.reshape(1, 3 * width, rows))
        grads.append(grad.reshape(3 * width, width))
        sums.append(total)
        ties = (total,)
        if sample < chain1.rounds:
            ties = (chain1.scatter(sample + 1, (total,)),)
        if sample == 0:
            tokens_out = insert_rows(info, tokens_out_own, out_came)
            ties = (*ties, tokens_out)
        if sample + 1 == chain1.rounds:
            gathered = lax.all_gather(chain1.value, ("samp", "blk"), axis=0, tiled=True)
    if chain1.rounds > local:
        for level in range(local + 1, chain1.rounds + 1):
            ties = (chain1.scatter(level),)
        gathered = lax.all_gather(chain1.value, ("samp", "blk"), axis=0, tiled=True)

    chain2 = Chain(layout, info, EXTRA)
    kept2, sent2 = small_call(
        functools.partial(pack_kernel, sets=len(grads), parts=parts2),
        (info, *grads, *sums, out_grad, biases),
        [sds((sum(parts2) // 2 + EXTRA, width), BF)] * 2,
        [pltpu.VMEM((sum(parts2), width), BF)],
        ties,
        name="pack",
    )
    chain2.start(kept2, sent2)
    tie = chain2.scatter(0)

    own_turn = lambda s, c, o: (c[CORE] * local + o[s], 0, 0)
    turn = lambda s, c, o: (o[s], 0, 0)
    grad_own, grad_far = big_call(
        functools.partial(tokens_back_kernel, sets=len(d_parts)),
        (info, order),
        (*d_parts, w_turned, pack, tokens, far_tokens, g_mid),
        [
            *[pl.BlockSpec(memory_space=pl.ANY)] * len(d_parts),
            vmem, vmem, half_spec(own_turn), half_spec(turn), pl.BlockSpec((1, rows, width), turn),
        ],
        [sds((samples, half, width), BF), sds((local, half, width), BF)],
        [half_spec(own_turn), half_spec(turn)],
        [
            pltpu.VMEM((rows, width), BF),
            pltpu.VMEM((len(d_parts), 3 * width, rows), BF),
            pltpu.SemaphoreType.DMA((len(d_parts),)),
        ],
        (tie,),
        name="tokens_back",
    )
    for level in range(1, chain2.rounds + 1):
        chain2.scatter(level, (), (grad_far,) if level == 1 else ())
        if level == 1:
            grad_came = swap_cores(chain2.through[0])
    ties = ()
    for level in reversed(range(chain2.rounds)):
        chain2.gather(level)
        if level == chain2.rounds - 1:
            grad_tokens = insert_rows(info, grad_own, grad_came)
            ties = (grad_tokens,)
        chain2.collect(ties)
        ties = ()
    other = swap_cores(chain2.value)

    grad_w_fc2, grad_w_fc1, grad_gain2, grad_shift2, grad_fc1_bias, grad_fc2_bias = small_call(
        functools.partial(finish_mlp_kernel, unit=parts1[0] // (2 * count)),
        (jnp.asarray(layout.own_places(parts1[0])), gathered, chain2.vectors, pack, w_fc1),
        [
            sds((hidden, width), F32), sds((width, hidden), F32), sds((width,), F32), sds((width,), F32),
            sds((hidden,), F32), sds((width,), F32),
        ],
        [pltpu.VMEM((parts1[0], width), BF)],
        (chain2.value,),
        name="finish_mlp",
    )
    grad_w_qkv, grad_w_out, grad_gain1, grad_shift1, grad_qv_bias, grad_out_bias = small_call(
        functools.partial(finish_kernel, unit=parts2[0] // (2 * count), at=layout.place, blocks=blocks),
        (info, chain2.value, other, chain2.vectors, pack, w_turned),
        [
            sds((width, 3 * width), F32), sds((width, width), F32), sds((width,), F32), sds((width,), F32),
            sds((2 * width,), F32), sds((width,), F32),
        ],
        [pltpu.VMEM((parts2[0], width), BF)],
        (grad_w_fc2,),
        name="finish",
    )
    return (
        tokens_out, cls_norm, grad_tokens, grad_gain1, grad_shift1, grad_w_qkv, grad_qv_bias,
        grad_w_out, grad_out_bias, grad_gain2, grad_shift2, grad_w_fc1, grad_fc1_bias,
        grad_w_fc2, grad_fc2_bias,
    )


def solution(mesh):
    split = P("samp", "blk", None)
    classes = P(("samp", "blk"), None)
    return jax.shard_map(
        per_device,
        mesh=mesh,
        in_specs=(split, P("samp"), *([P()] * 12), split, classes),
        out_specs=(split, classes, split, *([P()] * 12)),
        check_vma=False,
    )
```

```python
import functools
import math

import jax
import jax.numpy as jnp
import numpy as np
from jax import lax
from jax.experimental import pallas as pl
from jax.experimental.pallas import tpu as pltpu
from jax.sharding import PartitionSpec as P

HEAD_DIM = 64
VIEW_ROWS = 196
NORM_EPS = 1e-06
CLS_EPS = 1e-05
MASKED = -1e30
LOG2E = math.log2(math.e)
LN2 = math.log(2.0)
SCALE = HEAD_DIM ** (-0.5)
SUM_LOW = 1e-15
SUM_HIGH = 1e15
BF = jnp.bfloat16
F32 = jnp.float32
VMEM_BYTES = 60 * 2**20
CORE = 0
EXTRA = 16


def dot(a, b, ca, cb):
    return lax.dot_general(a, b, (((ca,), (cb,)), ((), ())), preferred_element_type=F32)


def norm_parts(values):
    centre = jnp.mean(values, -1, keepdims=True)
    offset = values - centre
    rstd = lax.rsqrt(jnp.mean(offset * offset, -1, keepdims=True) + NORM_EPS)
    return offset * rstd, rstd


def gelu_cdf(values):
    return 0.5 + 0.5 * lax.erf(values * (0.5**0.5))


def params(semantics):
    return pltpu.CompilerParams(dimension_semantics=semantics, vmem_limit_bytes=VMEM_BYTES)


def whole(shape):
    return pl.BlockSpec(shape, lambda *_: (0,) * len(shape))


def key_counts(rows):
    views = (rows - 1) // VIEW_ROWS
    return [(v, min(rows, -(-(1 + VIEW_ROWS * v) // 16) * 16)) for v in range(1, views + 1)]


GAIN1, SHIFT1, GAIN2, SHIFT2, OUT_BIAS, FC2_BIAS, QV_BIAS, FC1_BIAS = 0, 1, 2, 3, 4, 5, 6, 8


def row_of(pack_ref, index):
    return pack_ref[index : index + 1, :]


def place_halves(target_ref, core, own, far):
    half = own.shape[0]
    target_ref[pl.ds(pl.multiple_of(core * half, 16), half), :] = own
    target_ref[pl.ds(pl.multiple_of((1 - core) * half, 16), half), :] = far


def split_halves(source_ref, core, own_ref, far_ref):
    half = own_ref.shape[1]
    own_ref[0] = source_ref[pl.ds(pl.multiple_of(core * half, 16), half), :]
    far_ref[0] = source_ref[pl.ds(pl.multiple_of((1 - core) * half, 16), half), :]


def rank_samples(views_ref, base, order_ref):
    count = order_ref.shape[0]
    views = [views_ref[base + i] for i in range(count)]
    for i in range(count):
        rank = jnp.int32(0)
        for j in range(count):
            if j != i:
                ahead = views[j] >= views[i] if j < i else views[j] > views[i]
                rank = rank + ahead.astype(jnp.int32)
        order_ref[rank] = jnp.int32(i)


def project_kernel(
    blk_ref, views_ref, own_ref, far_ref, w_in_ref, pack_ref, w_out_ref, w1_ref, w2_ref, cot_ref,
    hat_ref, qkv_ref, cls_ref, stat_ref, w_ref, order_ref, mix_ref, first_ref, full_ref,
):
    step = pl.program_id(0)

    @pl.when(step == 0)
    def _():
        w_ref[...] = w_in_ref[...].T
        rank_samples(views_ref, blk_ref[CORE] * order_ref.shape[0], order_ref)

    rows = hat_ref.shape[1]
    width = own_ref.shape[2]
    place_halves(full_ref, blk_ref[0], own_ref[0], far_ref[0])
    values = full_ref[...].astype(F32)
    hat, _ = norm_parts(values)
    hat_ref[0] = hat.astype(BF)
    normed = (hat * row_of(pack_ref, GAIN1) + row_of(pack_ref, SHIFT1)).astype(BF)
    columns = pack_ref[0:8, :].T
    for third in range(3):
        part = pl.ds(third * width, width)
        piece = dot(w_ref[part, :], normed, 1, 1)
        if third == 0:
            piece = (piece + columns[:, QV_BIAS : QV_BIAS + 1]) * (SCALE * LOG2E)
        if third == 2:
            piece = piece + columns[:, QV_BIAS + 1 : QV_BIAS + 2]
        qkv_ref[0, part, :] = piece.astype(BF)

    lead = qkv_ref[0, pl.ds(0, width), :128].astype(F32).T[0:1, :]
    head_of = lax.broadcasted_iota(jnp.int32, (8, width), 1) // HEAD_DIM
    pick = head_of == lax.broadcasted_iota(jnp.int32, (8, width), 0)
    queries = jnp.where(pick, lead, 0.0).astype(BF)
    scores = dot(queries, qkv_ref[0, pl.ds(width, width), :], 1, 0)
    limit = 1 + VIEW_ROWS * views_ref[blk_ref[CORE] * pl.num_programs(0) + step]
    place = lax.broadcasted_iota(jnp.int32, (8, rows), 1)
    scores = jnp.where(place < limit, scores, MASKED)
    powers = jnp.exp2(scores - jnp.max(scores, -1, keepdims=True))
    chances = (powers / jnp.sum(powers, -1, keepdims=True)).astype(BF)
    mixed = dot(chances, qkv_ref[0, pl.ds(2 * width, width), :], 1, 1)
    mix_ref[pl.ds(step, 1), :] = jnp.sum(jnp.where(pick, mixed, 0.0), 0, keepdims=True)
    first_ref[pl.ds(step, 1), :] = values[0:1, :]

    @pl.when(step == pl.num_programs(0) - 1)
    def _():
        branch = dot(mix_ref[...].astype(BF), w_out_ref[...], 1, 0) + row_of(pack_ref, OUT_BIAS)
        middle = first_ref[...] + branch
        normed2 = norm_parts(middle)[0] * row_of(pack_ref, GAIN2) + row_of(pack_ref, SHIFT2)
        normed2 = normed2.astype(BF)
        output = middle + row_of(pack_ref, FC2_BIAS)
        for j in range(w1_ref.shape[1] // width):
            cols = slice(j * width, (j + 1) * width)
            pre = dot(normed2, w1_ref[:, cols], 1, 0) + row_of(pack_ref, FC1_BIAS + j)
            act = (pre * gelu_cdf(pre)).astype(BF)
            output = output + dot(act, w2_ref[cols, :], 1, 0)
        cls_ref[...] = output
        count = cot_ref.shape[0]
        cls = output[:count]
        cot = cot_ref[...].astype(F32)
        stat_ref[...] = jnp.zeros_like(stat_ref)
        for k, term in enumerate((cls, cls * cls, cot, cot * cls)):
            stat_ref[k : k + 1, :] = jnp.sum(term, 0, keepdims=True)


def masked_tail(scores, main, limit):
    place = main + lax.broadcasted_iota(jnp.int32, scores.shape, 0)
    return jnp.where(place < limit, scores, MASKED)


def attention_kernel(
    core_ref, views_ref, qkv_ref, sum_ref, top_ref, plain_ref, att_ref, pow_ref
):
    sample = pl.program_id(0)
    rows = qkv_ref.shape[2]
    width = att_ref.shape[1]
    heads = width // HEAD_DIM
    views = views_ref[core_ref[CORE] * pl.num_programs(0) + sample]
    limit = 1 + VIEW_ROWS * views
    ones = jnp.ones((16, rows), BF)

    def store(h, mixed):
        total = mixed[HEAD_DIM : HEAD_DIM + 1]
        sum_ref[0, pl.ds(h, 1), :] = total
        att_ref[0, head_rows(h, 0), :] = (mixed[:HEAD_DIM] * (1.0 / total)).astype(BF)

    sum_ref[0, heads:8, :] = jnp.ones((8 - heads, rows), F32)
    for count, keys in key_counts(rows):

        @pl.when(views == count)
        def _(keys=keys):
            main = keys - 16

            def pair(p, carry):
                both = range(2)
                parts = [head_parts(qkv_ref, 2 * p + k, width, keys) for k in both]
                scores = [dot(key, query, 0, 0) for query, key, _ in parts]
                for k in both:
                    pow_ref[k, :main, :] = jnp.exp2(scores[k][:main]).astype(BF)
                    tail = masked_tail(scores[k][main:], main, limit)
                    pow_ref[k, main:keys, :] = jnp.exp2(tail).astype(BF)
                lefts = [jnp.concatenate((value, ones[:, :keys]), 0) for _, _, value in parts]
                mixed = [dot(lefts[k], pow_ref[k, :keys, :], 1, 0) for k in both]
                for k in both:
                    store(2 * p + k, mixed[k])
                return carry

            lax.fori_loop(0, heads // 2, pair, 0)

    totals = sum_ref[0]
    plain = (jnp.min(totals) > SUM_LOW) & (jnp.max(totals) < SUM_HIGH)
    plain_ref[sample] = plain.astype(jnp.int32)

    @pl.when(jnp.logical_not(plain))
    def _():
        @each_head(heads)
        def _(h, slot):
            query, key, value = head_parts(qkv_ref, h, width, rows)
            scores = masked_tail(dot(key, query, 0, 0), 0, limit)
            top = jnp.max(scores, 0, keepdims=True)
            top_ref[0, pl.ds(h, 1), :] = top
            pow_ref[slot] = jnp.exp2(scores - top).astype(BF)
            left = jnp.concatenate((value, ones), 0)
            store(h, dot(left, pow_ref[slot], 1, 0))


def each_head(heads):
    def run(body):
        def pair(p, carry):
            for slot in range(2):
                body(2 * p + slot, slot)
            return carry

        lax.fori_loop(0, heads // 2, pair, 0)

    return run


def head_rows(h, base):
    return pl.ds(pl.multiple_of(base + h * HEAD_DIM, HEAD_DIM), HEAD_DIM)


def head_parts(qkv_ref, h, width, keys):
    return (
        qkv_ref[0, head_rows(h, 0), :],
        qkv_ref[0, head_rows(h, width), :keys],
        qkv_ref[0, head_rows(h, 2 * width), :keys],
    )


def layer_kernel(
    core_ref, x_own_ref, x_far_ref, own_ref, far_ref, att_ref, sum_ref, cls_ref, cot_ref, *refs,
    samples, parts, peers
):
    stat_refs = refs[:peers]
    w_out_ref, w1_ref, w2_ref, pack_ref = refs[peers : peers + 4]
    (
        out_own_ref, out_far_ref, gmid_ref, dmix_ref, inner_ref, out_grad_ref, norm_ref, bias_ref,
        kept_ref, sent_ref,
    ) = refs[peers + 4 : peers + 14]
    full_ref, g_ref, act_ref, dpre_ref, dcls_ref, acc2_ref, acc1_ref, flat_ref = refs[peers + 14 :]
    step = pl.program_id(0)
    width = own_ref.shape[2]
    hidden = w2_ref.shape[0]
    blocks = hidden // width

    @pl.when(step == 0)
    def _():
        acc2_ref[...] = jnp.zeros_like(acc2_ref)
        acc1_ref[...] = jnp.zeros_like(acc1_ref)
        bias_ref[...] = jnp.zeros_like(bias_ref)
        out_grad_ref[...] = jnp.zeros_like(out_grad_ref)
        stats = stat_refs[0][...]
        for other in stat_refs[1:]:
            stats = stats + other[...]
        local = cot_ref.shape[0]
        cls = cls_ref[...][:local]
        cot = cot_ref[...].astype(F32)
        mean = stats[0:1] / samples
        scale = lax.rsqrt(stats[1:2] / samples - mean * mean + CLS_EPS)
        hat = (cls - mean) * scale
        norm_ref[...] = hat.astype(BF)
        cross = scale * (stats[3:4] - mean * stats[2:3])
        dcls_ref[...] = jnp.zeros_like(dcls_ref)
        dcls_ref[:local, :] = scale * (cot - stats[2:3] / samples - hat * (cross / samples))

    place_halves(full_ref, core_ref[CORE], x_own_ref[0], x_far_ref[0])
    place_halves(g_ref, core_ref[CORE], own_ref[0].astype(F32), far_ref[0].astype(F32))
    g_ref[0:1, :] = g_ref[0:1, :] + dcls_ref[pl.ds(step, 1), :]
    g_mlp = g_ref[...].astype(BF)
    bias_ref[blocks : blocks + 1, :] += jnp.sum(g_mlp.astype(F32), 0, keepdims=True)

    branch = dot(att_ref[0], w_out_ref[...], 0, 0) + row_of(pack_ref, OUT_BIAS)
    middle = full_ref[...].astype(F32) + branch
    hat, rstd = norm_parts(middle)
    normed = (hat * row_of(pack_ref, GAIN2) + row_of(pack_ref, SHIFT2)).astype(BF)
    hat_low = hat.astype(BF)
    for j in range(blocks):
        cols = slice(j * width, (j + 1) * width)
        pre = dot(normed, w1_ref[:, cols], 1, 0) + row_of(pack_ref, FC1_BIAS + j)
        d_act = dot(g_mlp, w2_ref[cols, :], 1, 1)
        cdf = gelu_cdf(pre)
        bell = jnp.exp2(pre * pre * (-0.5 * LOG2E) - 0.5 * math.log2(2.0 * math.pi))
        act_ref[:, cols] = (pre * cdf).astype(BF)
        d_pre = d_act * (cdf + pre * bell)
        bias_ref[j : j + 1, :] += jnp.sum(d_pre, 0, keepdims=True)
        dpre_ref[:, cols] = d_pre.astype(BF)
    acc1_ref[...] += dot(hat_low, dpre_ref[...], 0, 0)
    acc2_ref[...] += dot(act_ref[...], g_mlp, 0, 0)
    output = middle + dot(act_ref[...], w2_ref[...], 1, 0) + row_of(pack_ref, FC2_BIAS)
    full_ref[...] = output.astype(BF)
    split_halves(full_ref, core_ref[CORE], out_own_ref, out_far_ref)

    d_norm = dot(dpre_ref[...], w1_ref[...], 1, 1)
    u = d_norm * row_of(pack_ref, GAIN2)
    g_mid = g_ref[...] + rstd * (
        u - jnp.mean(u, -1, keepdims=True) - hat * jnp.mean(u * hat, -1, keepdims=True)
    )
    g_attn = g_mid.astype(BF)
    gmid_ref[0] = g_attn
    out_grad_ref[...] += dot(att_ref[0], g_attn, 1, 0)
    bias_ref[blocks + 1 : blocks + 2, :] += jnp.sum(g_attn.astype(F32), 0, keepdims=True)
    d_mix = dot(w_out_ref[...], g_attn, 1, 1)
    for h in range(width // HEAD_DIM):
        part = slice(h * HEAD_DIM, (h + 1) * HEAD_DIM)
        piece = d_mix[part] * (1.0 / sum_ref[0, h : h + 1, :])
        dmix_ref[0, part, :] = piece.astype(BF)
        inner_ref[0, h : h + 1, :] = jnp.sum(piece * att_ref[0, part, :].astype(F32), 0, keepdims=True)

    @pl.when(step == pl.num_programs(0) - 1)
    def _():
        flat_ref[:hidden, :] = acc2_ref[...].astype(BF)
        for j in range(blocks):
            rows = slice(hidden + j * width, hidden + (j + 1) * width)
            flat_ref[rows, :] = acc1_ref[:, j * width : (j + 1) * width].astype(BF)
        clear_rest(flat_ref, 2 * hidden)
        write_halves(core_ref[CORE], flat_ref, parts, kept_ref, sent_ref)


def attention_back_kernel(
    core_ref, views_ref, plain_ref, order_ref, qkv_ref, top_ref, dmix_ref, inner_ref, hat_ref,
    dqkv_ref, grad_ref, sums_ref, pow_ref, *, turn, samples
):
    pair = pl.program_id(0)
    sample = order_ref[turn]
    rows, width = hat_ref.shape[1:]
    views = views_ref[core_ref[CORE] * samples + sample]
    limit = 1 + VIEW_ROWS * views
    plain = plain_ref[sample] == 1
    both = range(2)
    lanes = [slice(k * HEAD_DIM, (k + 1) * HEAD_DIM) for k in both]

    def back(keys, powers_of):
        query = [qkv_ref[0, 0, part, :] for part in lanes]
        key = [qkv_ref[0, 1, part, :keys] for part in lanes]
        value = [qkv_ref[0, 2, part, :keys] for part in lanes]
        d_mix = [dmix_ref[0, part, :] for part in lanes]
        scores = [dot(key[k], query[k], 0, 0) for k in both]
        for k in both:
            powers_of(k, scores[k])
        d_weights = [dot(value[k], d_mix[k], 0, 0) for k in both]
        d_scores = []
        for k in both:
            inner = inner_ref[0, pl.ds(2 * pair + k, 1), :]
            powers = pow_ref[k, :keys, :].astype(F32)
            d_scores.append((powers * (d_weights[k] - inner)).astype(BF))
        for k in both:
            d_value = dot(d_mix[k], pow_ref[k, :keys, :], 1, 1)
            dqkv_ref[0, 2, lanes[k], :keys] = d_value.astype(BF)
        for k in both:
            d_query = dot(key[k], d_scores[k], 1, 0) * SCALE
            dqkv_ref[0, 0, lanes[k], :] = d_query.astype(BF)
            d_key = dot(query[k], d_scores[k], 1, 1) * LN2
            dqkv_ref[0, 1, lanes[k], :keys] = d_key.astype(BF)
        if keys < rows:
            blank = jnp.zeros((2 * HEAD_DIM, rows - keys), BF)
            dqkv_ref[0, 1, :, keys:] = blank
            dqkv_ref[0, 2, :, keys:] = blank

    for count, keys in key_counts(rows):

        @pl.when((views == count) & plain)
        def _(keys=keys):
            main = keys - 16

            def powers_of(k, scores):
                pow_ref[k, :main, :] = jnp.exp2(scores[:main]).astype(BF)
                tail = masked_tail(scores[main:], main, limit)
                pow_ref[k, main:keys, :] = jnp.exp2(tail).astype(BF)

            back(keys, powers_of)

    @pl.when(jnp.logical_not(plain))
    def _():
        def powers_of(k, scores):
            top = top_ref[0, pl.ds(2 * pair + k, 1), :]
            pow_ref[k] = jnp.exp2(masked_tail(scores, 0, limit) - top).astype(BF)

        back(rows, powers_of)

    right = jnp.concatenate((hat_ref[0], jnp.ones((rows, 128), BF)), 1)
    result = dot(dqkv_ref[0].reshape(3 * 2 * HEAD_DIM, rows), right, 1, 0)
    grad_ref[...] = result[:, :width].astype(BF).reshape(grad_ref.shape)
    sums_ref[0] = result[:, width:].T[:8]


def tokens_back_kernel(core_ref, order_ref, *refs, sets):
    dqkv_refs = refs[:sets]
    w_ref, pack_ref, x_own_ref, x_far_ref, gmid_ref, own_ref, far_ref, out_ref, d_ref, sems = refs[sets:]
    step = pl.program_id(0)

    def fetch(k):
        return pltpu.make_async_copy(dqkv_refs[k].at[0], d_ref.at[k], sems.at[k])

    @pl.when(step == 0)
    def _():
        for k in range(sets):
            fetch(k).start()

    for k in range(sets):

        @pl.when(step == k)
        def _(k=k):
            fetch(k).wait()

    d_norm = dot(d_ref[step], w_ref[...], 0, 0)
    place_halves(out_ref, core_ref[CORE], x_own_ref[0], x_far_ref[0])
    hat, rstd = norm_parts(out_ref[...].astype(F32))
    w = d_norm * row_of(pack_ref, GAIN1)
    back = rstd * (w - jnp.mean(w, -1, keepdims=True) - hat * jnp.mean(w * hat, -1, keepdims=True))
    out_ref[...] = (gmid_ref[0].astype(F32) + back).astype(BF)
    split_halves(out_ref, core_ref[CORE], own_ref, far_ref)


def clear_rest(ref, used):
    if ref.shape[0] > used:
        ref[used:, :] = jnp.zeros((ref.shape[0] - used, ref.shape[1]), ref.dtype)


def write_halves(core, flat_ref, parts, kept_ref, sent_ref):
    start = at = 0
    for size in parts:
        half = size // 2
        mine = pl.multiple_of(start + core * half, 16)
        other = pl.multiple_of(start + (1 - core) * half, 16)
        kept_ref[at : at + half, :] = flat_ref[pl.ds(mine, half), :]
        sent_ref[at : at + half, :] = flat_ref[pl.ds(other, half), :]
        start += size
        at += half


def pack_kernel(core_ref, *refs, sets, parts):
    grad_refs = refs[:sets]
    sums_refs = refs[sets : 2 * sets]
    out_grad_ref, bias_ref, kept_ref, sent_ref, flat_ref = refs[2 * sets :]
    width = out_grad_ref.shape[0]
    used = grad_refs[0].shape[0]
    total, sums = grad_refs[0][...].astype(F32), sums_refs[0][...]
    for grad_ref, sums_ref in zip(grad_refs[1:], sums_refs[1:]):
        total = total + grad_ref[...].astype(F32)
        sums = sums + sums_ref[...]
    flat_ref[:used, :] = total.astype(BF)
    flat_ref[used : used + width, :] = out_grad_ref[...].astype(BF)
    clear_rest(flat_ref, used + width)
    write_halves(core_ref[CORE], flat_ref, parts, kept_ref, sent_ref)
    rows = lax.broadcasted_iota(jnp.int32, (8, width), 0)
    extra = jnp.zeros((8, width), F32)
    for t in range(used // width):
        row = jnp.concatenate([sums[p, 0:1, t * 128 : (t + 1) * 128] for p in range(width // 128)], 1)
        extra = jnp.where(rows == t, row, extra)
    vectors = jnp.concatenate((bias_ref[0:8, :], extra), 0).astype(BF)
    at = sum(parts) // 2
    kept_ref[at : at + EXTRA, :] = vectors
    sent_ref[at : at + EXTRA, :] = vectors


def insert_rows(info, base, came):
    def body(info_ref, came_ref, base_ref, out_ref):
        out_ref[...] = came_ref[...]

    return pl.pallas_call(
        body,
        grid_spec=pltpu.PrefetchScalarGridSpec(
            num_scalar_prefetch=1,
            grid=(1,),
            in_specs=[
                pl.BlockSpec(came.shape, lambda *_: (0, 0, 0)), pl.BlockSpec(memory_space=pltpu.HBM),
            ],
            out_specs=pl.BlockSpec(came.shape, lambda s, b: (1 - b[CORE], 0, 0)),
        ),
        out_shape=jax.ShapeDtypeStruct(base.shape, base.dtype),
        input_output_aliases={2: 0},
        compiler_params=params(("arbitrary",)),
        name="insert",
    )(info, came, base)


def swap_cores(value):
    return lax.ppermute(value, "blk", [(0, 1), (1, 0)])


def stages(count, first=4):
    out = []
    stride = 1
    while stride < count:
        left = count // stride
        radix = first if not out and left % first == 0 else 4 if left % 4 == 0 else 2
        out.append((stride, radix))
        stride *= radix
    return out


def shifted(value, stage, steps, axis="samp"):
    stride, radix = stage
    count = lax.axis_size(axis)
    pairs = []
    for source in range(count):
        digit = (source // stride) % radix
        pairs.append((source, source + ((digit + steps) % radix - digit) * stride))
    return lax.ppermute(value, axis, pairs)


def small_call(kernel, args, outs, scratch=(), ties=(), name=None, through=()):
    n, t, m, o = len(args), len(ties), len(through), len(outs)

    def body(*refs):
        kernel(*refs[:n], *refs[n + t + m : n + t + m + o], *refs[n + t + 2 * m + o :])

    vmem = pl.BlockSpec(memory_space=pltpu.VMEM)
    size = lambda a: math.prod(a.shape) * jnp.dtype(a.dtype).itemsize
    total = sum(size(a) for a in (*args[1:], *outs)) + sum(
        math.prod(a.shape) * jnp.dtype(a.dtype).itemsize for a in scratch
    )
    return pl.pallas_call(
        body,
        in_specs=[
            pl.BlockSpec(memory_space=pltpu.SMEM),
            *[vmem] * (len(args) - 1),
            *[pl.BlockSpec(memory_space=pltpu.HBM)] * (t + m),
        ],
        out_specs=[vmem] * o + [pl.BlockSpec(memory_space=pltpu.HBM)] * m,
        out_shape=[*outs, *[jax.ShapeDtypeStruct(a.shape, a.dtype) for a in through]],
        scratch_shapes=list(scratch),
        input_output_aliases={n + t + k: o + k for k in range(m)},
        compiler_params=pltpu.CompilerParams(vmem_limit_bytes=2 * total + 4 * 2**20),
        name=name,
    )(*args, *ties, *through)


def spread_kernel(info_ref, *refs, count, radix, slot, extra):
    outputs = radix + (1 if extra and radix == 1 else 0)
    outs, total_ref = refs[count : count + outputs], refs[count + outputs]
    total = refs[0][...].astype(F32)
    for ref in refs[1:count]:
        total = total + ref[...].astype(F32)
    rows = total_ref.shape[0] - extra
    size = rows // radix
    total_ref[...] = total.astype(BF)
    if radix == 1:
        outs[0][...] = total_ref[:rows, :]
        if extra:
            outs[1][...] = total[rows:]
        return
    for k in range(radix):
        start = lax.rem(info_ref[slot] + k, radix) * size
        outs[k][:size, :] = total_ref[pl.ds(pl.multiple_of(start, 16), size), :]
        if extra:
            outs[k][size:, :] = total_ref[rows:, :]


def collect_kernel(info_ref, *refs, groups):
    at, out_at = 0, sum(groups)
    for count in groups:
        size = refs[at].shape[0]
        for k in range(count):
            refs[out_at][k * size : (k + 1) * size, :] = refs[at + k][...]
        at += count
        out_at += 1


class Layout:
    def __init__(self, count, sizes):
        self.base = stages(count)
        self.count = count
        table = np.zeros((2 * count, 1 + len(self.base)), np.int32)
        for device in range(2 * count):
            table[device, 0] = device % 2
            for i in range(len(self.base)):
                table[device, 1 + i] = self.digit(device, i)
        tables = [table]
        self.place = []
        for rows in sizes:
            self.place.append(sum(t.shape[1] for t in tables))
            tables.append(np.stack([self.places(device, rows) for device in range(2 * count)]))
        self.table = np.concatenate(tables, 1).astype(np.int32)

    def digit(self, device, index):
        stride, radix = self.base[index]
        return (device // 2 // stride) % radix

    def places(self, device, rows):
        core = device % 2
        unit = rows // 2
        offsets = np.array([core * unit, (1 - core) * unit])
        for index, (_, radix) in enumerate(self.base):
            unit //= radix
            digit = (self.digit(device, index) - np.arange(radix)) % radix
            offsets = (offsets[:, None] + (digit * unit)[None, :]).reshape(-1)
        return offsets


class Chain:
    def __init__(self, layout, info, extra=0):
        self.layout = layout
        self.info = info
        self.extra = extra
        self.rounds = len(layout.base)

    def start(self, kept, sent):
        self.pending = [kept, swap_cores(sent)]

    def scatter(self, level, ties=(), through=()):
        last = level == self.rounds
        radix = 1 if last else self.layout.base[level][1]
        rows, width = self.pending[0].shape
        size = (rows - self.extra) // radix
        if last:
            outs = [jax.ShapeDtypeStruct((size, width), BF)]
            if self.extra:
                outs.append(jax.ShapeDtypeStruct((self.extra, width), F32))
        else:
            outs = [jax.ShapeDtypeStruct((size + self.extra, width), BF)] * radix
        pieces = small_call(
            functools.partial(
                spread_kernel, count=len(self.pending), radix=radix, slot=1 + level, extra=self.extra
            ),
            (self.info, *self.pending), outs, [pltpu.VMEM((rows, width), BF)], ties, "spread", through,
        )
        self.through = pieces[len(outs) :]
        if last:
            self.value = pieces[0]
            self.vectors = pieces[1] if self.extra else None
        else:
            stage = self.layout.base[level]
            self.pending = [pieces[0]] + [shifted(pieces[k], stage, k) for k in range(1, radix)]
        return pieces[0]

    def gather(self, level):
        stage = self.layout.base[level]
        self.pending = [self.value] + [shifted(self.value, stage, k) for k in range(1, stage[1])]

    def collect(self, ties=()):
        size, width = self.pending[0].shape
        outs = [jax.ShapeDtypeStruct((len(self.pending) * size, width), BF)]
        self.value = small_call(
            functools.partial(collect_kernel, groups=(len(self.pending),)),
            (self.info, *self.pending), outs, (), ties, "collect",
        )[0]
        return self.value


def restore(place_ref, flat_ref, ref, unit, at):
    def body(i, carry):
        start = pl.multiple_of(place_ref[at + i], 16)
        source = pl.multiple_of(i * unit, 16)
        chunk = ref[pl.ds(source, unit), :]
        flat_ref[pl.ds(start, unit), :] = chunk
        return carry

    lax.fori_loop(0, ref.shape[0] // unit, body, 0)


def finish_mlp_kernel(
    info_ref, own_ref, far_ref, vectors_ref, pack_ref, w1_ref,
    fc2_ref, fc1_ref, gain_ref, shift_ref, fc1_bias_ref, fc2_bias_ref, flat_ref, *, unit, at
):
    restore(info_ref, flat_ref, own_ref, unit, at)
    restore(info_ref, flat_ref, far_ref, unit, at + own_ref.shape[0] // unit)
    hidden, width = fc2_ref.shape
    fc2_ref[...] = flat_ref[:hidden, :].astype(F32)
    columns = pack_ref[0:8, :].T
    gain = jnp.zeros((width, 1), F32)
    shift = jnp.zeros((width, 1), F32)
    for j in range(hidden // width):
        cols = slice(j * width, (j + 1) * width)
        hats = flat_ref[hidden + j * width : hidden + (j + 1) * width, :].astype(F32)
        sums = vectors_ref[j : j + 1, :]
        fc1_ref[:, cols] = hats * columns[:, GAIN2 : GAIN2 + 1] + columns[:, SHIFT2 : SHIFT2 + 1] * sums
        w = w1_ref[:, cols].astype(F32)
        gain = gain + jnp.sum(w * hats, -1, keepdims=True)
        shift = shift + jnp.sum(w * sums, -1, keepdims=True)
    lane = lax.broadcasted_iota(jnp.int32, (width, 128), 1)
    both = jnp.where(lane == 0, gain, jnp.where(lane == 1, shift, 0.0)).T[0:8]
    gain_ref[...] = both[0]
    shift_ref[...] = both[1]
    blocks = hidden // width
    for j in range(blocks):
        fc1_bias_ref[j * width : (j + 1) * width] = vectors_ref[j, :]
    fc2_bias_ref[...] = vectors_ref[blocks, :]


def finish_kernel(
    info_ref, own_ref, far_ref, vectors_ref, pack_ref, w_ref, qkv_ref, out_ref, gain_ref, shift_ref, qv_ref, out_bias_ref, flat_ref,
    *, unit, at, blocks
):
    restore(info_ref, flat_ref, own_ref, unit, at)
    restore(info_ref, flat_ref, far_ref, unit, at + own_ref.shape[0] // unit)
    width = out_ref.shape[0]
    columns = qkv_ref.shape[1]
    out_ref[...] = flat_ref[columns : columns + width, :].astype(F32)
    gain = jnp.zeros((1, width), F32)
    shift = jnp.zeros((1, width), F32)
    turned = vectors_ref[8:16, :].T
    for t in range(columns // width):
        part = slice(t * width, (t + 1) * width)
        hats = flat_ref[part, :].astype(F32)
        sums = turned[:, t : t + 1]
        result = hats * row_of(pack_ref, GAIN1) + sums * row_of(pack_ref, SHIFT1)
        qkv_ref[:, part] = result.T
        w = w_ref[part, :].astype(F32)
        gain = gain + jnp.sum(w * hats, 0, keepdims=True)
        shift = shift + jnp.sum(w * sums, 0, keepdims=True)
    gain_ref[...] = gain[0]
    shift_ref[...] = shift[0]
    qv_ref[:width] = vectors_ref[8, :]
    qv_ref[width:] = vectors_ref[10, :]
    out_bias_ref[...] = vectors_ref[blocks + 1, :]


def pad_rows(count, unit):
    return -(-count // unit) * unit


def per_device(
    tokens, view_count, norm1_gain, norm1_bias, w_qkv, qv_bias, w_out, out_bias,
    norm2_gain, norm2_bias, w_fc1, fc1_bias, w_fc2, fc2_bias, cot_tokens, cot_cls,
):
    core = lax.axis_index("blk")
    cores = lax.axis_size("blk")
    count = lax.axis_size("samp")
    samples, half, width = tokens.shape
    local = samples // cores
    rows = half * cores
    hidden = w_fc1.shape[1]
    blocks = hidden // width
    heads = width // HEAD_DIM
    pairs = heads // 2
    sds = jax.ShapeDtypeStruct

    unit = 32 * count
    parts1 = [pad_rows(2 * hidden, unit)]
    parts2 = [pad_rows(4 * width, unit)]
    layout = Layout(count, (parts1[0], parts2[0]))
    device = lax.axis_index("samp") * cores + core
    info = lax.dynamic_index_in_dim(jnp.asarray(layout.table), device, 0, keepdims=False)

    theirs = (1 - core) * local
    far_tokens = swap_cores(lax.dynamic_slice_in_dim(tokens, theirs, local, 0))
    far_cot = swap_cores(lax.dynamic_slice_in_dim(cot_tokens, theirs, local, 0))

    pack = jnp.concatenate(
        (
            norm1_gain, norm1_bias, norm2_gain, norm2_bias, out_bias, fc2_bias, qv_bias, fc1_bias,
            jnp.zeros(((8 - blocks) * width,), BF),
        )
    ).astype(F32).reshape(16, width)

    vmem = pl.BlockSpec(memory_space=pltpu.VMEM)
    half_spec = lambda f: pl.BlockSpec((1, half, width), f)
    own_map = lambda s, b, *_: (b[CORE] * local + s, 0, 0)
    by_sample = lambda s, *_: (s, 0, 0)
    rows_spec = pl.BlockSpec((1, rows, width), by_sample)
    turned_spec = pl.BlockSpec((1, width, rows), by_sample)
    rstd_spec = pl.BlockSpec((1, rows, 1), by_sample)
    hidden_spec = pl.BlockSpec((1, rows, hidden), by_sample)
    eight_spec = pl.BlockSpec((1, 8, rows), by_sample)

    def big_call(kernel, prefetch, args, in_specs, outs, out_specs, scratch=(), ties=(), grid=(local,), name=None):
        n = len(prefetch) + len(args)

        def body(*refs):
            kernel(*refs[:n], *refs[n + len(ties) :])

        return pl.pallas_call(
            body,
            grid_spec=pltpu.PrefetchScalarGridSpec(
                num_scalar_prefetch=len(prefetch),
                grid=grid,
                in_specs=[*in_specs, *[pl.BlockSpec(memory_space=pl.ANY)] * len(ties)],
                out_specs=out_specs,
                scratch_shapes=list(scratch),
            ),
            out_shape=outs,
            compiler_params=params(("arbitrary",) * len(grid)),
            name=name,
        )(*prefetch, *args, *ties)

    hat1, qkv, cls_rows, stats, w_turned, order = big_call(
        project_kernel,
        (info, view_count),
        (tokens, far_tokens, w_qkv, pack, w_out, w_fc1, w_fc2, cot_cls),
        [half_spec(own_map), half_spec(by_sample), *[vmem] * 6],
        [
            sds((local, rows, width), BF),
            sds((local, 3 * width, rows), BF),
            sds((8, width), F32),
            sds((8, width), F32),
            sds((3 * width, width), BF),
            sds((local,), jnp.int32),
        ],
        [
            rows_spec, pl.BlockSpec((1, 3 * width, rows), by_sample), vmem, vmem, vmem,
            pl.BlockSpec(memory_space=pltpu.SMEM),
        ],
        [pltpu.VMEM((8, width), F32), pltpu.VMEM((8, width), F32), pltpu.VMEM((rows, width), BF)],
        name="project",
    )

    def add_kernel(info_ref, *refs):
        total = refs[0][...]
        for ref in refs[1:-1]:
            total = total + ref[...]
        refs[-1][...] = total

    *later, first = stages(count)

    def add_all(values, ties=()):
        return small_call(add_kernel, [info, *values], [sds((8, width), F32)], (), ties, "add")[0]

    stats = add_all([stats, swap_cores(stats)])
    stat_parts = [stats] + [shifted(stats, first, k) for k in range(1, first[1])]

    qkv_spec = lambda f: pl.BlockSpec((1, 3 * width, rows), f)
    totals, tops, plain, mixed = big_call(
        attention_kernel,
        (info, view_count),
        (qkv,),
        [qkv_spec(by_sample)],
        [
            sds((local, 8, rows), F32),
            sds((local, 8, rows), F32),
            sds((local,), jnp.int32),
            sds((local, width, rows), BF),
        ],
        [eight_spec, eight_spec, pl.BlockSpec(memory_space=pltpu.SMEM), turned_spec],
        [pltpu.VMEM((2, rows, rows), BF)],
        (stats,),
        name="attention",
    )

    tie = totals
    for stage in later:
        stats = add_all(stat_parts, (tie,))
        stat_parts = [stats] + [shifted(stats, stage, k) for k in range(1, stage[1])]
        tie = stats

    tokens_out_own, out_far, g_mid, d_mix, inner, out_grad, cls_norm, biases, kept1, sent1 = big_call(
        functools.partial(
            layer_kernel, samples=local * cores * count, parts=parts1, peers=len(stat_parts)
        ),
        (info,),
        (
            tokens, far_tokens, cot_tokens, far_cot, mixed, totals, cls_rows, cot_cls, *stat_parts,
            w_out, w_fc1, w_fc2, pack,
        ),
        [
            half_spec(own_map), half_spec(by_sample), half_spec(own_map), half_spec(by_sample),
            turned_spec, eight_spec, vmem, vmem, *[vmem] * len(stat_parts), vmem, vmem, vmem, vmem,
        ],
        [
            sds((samples, half, width), BF),
            sds((local, half, width), BF),
            sds((local, rows, width), BF),
            sds((local, width, rows), BF),
            sds((local, 8, rows), F32),
            sds((width, width), F32),
            sds((local, width), BF),
            sds((8, width), F32),
            sds((sum(parts1) // 2, width), BF),
            sds((sum(parts1) // 2, width), BF),
        ],
        [
            half_spec(own_map), half_spec(by_sample), rows_spec, turned_spec, eight_spec,
            vmem, vmem, vmem, vmem, vmem,
        ],
        [
            pltpu.VMEM((rows, width), BF),
            pltpu.VMEM((rows, width), F32),
            pltpu.VMEM((rows, hidden), BF),
            pltpu.VMEM((rows, hidden), BF),
            pltpu.VMEM((8, width), F32),
            pltpu.VMEM((hidden, width), F32),
            pltpu.VMEM((width, hidden), F32),
            pltpu.VMEM((sum(parts1), width), BF),
        ],
        name="layer",
    )
    chain1 = Chain(layout, info)
    chain1.start(kept1, sent1)
    out_came = swap_cores(out_far)

    def attention_back(turn, ties):
        place = lambda p, c, v, q, o: (o[turn], 0, 0)
        return big_call(
            functools.partial(attention_back_kernel, turn=turn, samples=local),
            (info, view_count, plain, order),
            (qkv.reshape(local, 3, width, rows), tops, d_mix, inner, hat1),
            [
                pl.BlockSpec((1, 3, 128, rows), lambda p, c, v, q, o: (o[turn], 0, p, 0)),
                pl.BlockSpec((1, 8, rows), place),
                pl.BlockSpec((1, 128, rows), lambda p, c, v, q, o: (o[turn], p, 0)),
                pl.BlockSpec((1, 8, rows), place),
                pl.BlockSpec((1, rows, width), place),
            ],
            [
                sds((1, 3, width, rows), BF),
                sds((3, width, width), BF),
                sds((pairs, 8, 384), F32),
            ],
            [
                pl.BlockSpec((1, 3, 128, rows), lambda p, *_: (0, 0, p, 0)),
                pl.BlockSpec((3, 128, width), lambda p, *_: (0, p, 0)),
                pl.BlockSpec((1, 8, 384), lambda p, *_: (p, 0, 0)),
            ],
            [pltpu.VMEM((2, rows, rows), BF)],
            ties,
            grid=(pairs,),
            name="attention_back",
        )

    def scatter_step(level):
        def run(ties):
            piece = chain1.scatter(level, ties)
            if level == chain1.rounds:
                chain1.gather(level - 1)
            return piece

        return run

    def collect_step(level):
        def run(ties):
            value = chain1.collect(ties)
            if level > 0:
                chain1.gather(level - 1)
            return value

        return run

    steps = [scatter_step(level) for level in range(1, chain1.rounds + 1)]
    steps += [collect_step(level) for level in reversed(range(chain1.rounds))]
    ties = (chain1.scatter(0),)
    d_parts, grads, sums = [], [], []
    for sample in range(local):
        d_part, grad, total = attention_back(sample, ties)
        d_parts.append(d_part.reshape(1, 3 * width, rows))
        grads.append(grad.reshape(3 * width, width))
        sums.append(total)
        ties = (steps.pop(0)((total,)),)
        if sample == 0:
            tokens_out = insert_rows(info, tokens_out_own, out_came)
            ties = (*ties, tokens_out)

    chain2 = Chain(layout, info, EXTRA)
    kept2, sent2 = small_call(
        functools.partial(pack_kernel, sets=len(grads), parts=parts2),
        (info, *grads, *sums, out_grad, biases),
        [sds((sum(parts2) // 2 + EXTRA, width), BF)] * 2,
        [pltpu.VMEM((sum(parts2), width), BF)],
        ties,
        name="pack",
    )
    chain2.start(kept2, sent2)
    tie = chain2.scatter(0)

    own_turn = lambda s, c, o: (c[CORE] * local + o[s], 0, 0)
    turn = lambda s, c, o: (o[s], 0, 0)
    grad_own, grad_far = big_call(
        functools.partial(tokens_back_kernel, sets=len(d_parts)),
        (info, order),
        (*d_parts, w_turned, pack, tokens, far_tokens, g_mid),
        [
            *[pl.BlockSpec(memory_space=pl.ANY)] * len(d_parts),
            vmem, vmem, half_spec(own_turn), half_spec(turn), pl.BlockSpec((1, rows, width), turn),
        ],
        [sds((samples, half, width), BF), sds((local, half, width), BF)],
        [half_spec(own_turn), half_spec(turn)],
        [
            pltpu.VMEM((rows, width), BF),
            pltpu.VMEM((len(d_parts), 3 * width, rows), BF),
            pltpu.SemaphoreType.DMA((len(d_parts),)),
        ],
        (tie,),
        name="tokens_back",
    )
    for level in range(1, chain2.rounds + 1):
        piece = chain2.scatter(level, (), (grad_far,) if level == 1 else ())
        if level == 1:
            grad_came = swap_cores(chain2.through[0])
            while steps:
                piece = steps.pop(0)((piece,))
            other1 = swap_cores(chain1.value)
    ties = ()
    for level in reversed(range(chain2.rounds)):
        chain2.gather(level)
        if level == chain2.rounds - 1:
            (
                grad_w_fc2, grad_w_fc1, grad_gain2, grad_shift2, grad_fc1_bias, grad_fc2_bias,
            ) = small_call(
                functools.partial(
                    finish_mlp_kernel, unit=parts1[0] // (2 * count), at=layout.place[0]
                ),
                (info, chain1.value, other1, chain2.vectors, pack, w_fc1),
                [
                    sds((hidden, width), F32), sds((width, hidden), F32), sds((width,), F32),
                    sds((width,), F32), sds((hidden,), F32), sds((width,), F32),
                ],
                [pltpu.VMEM((parts1[0], width), BF)],
                name="finish_mlp",
            )
            ties = (grad_gain2,)
        chain2.collect(ties)
        ties = ()
    other = swap_cores(chain2.value)
    grad_tokens = insert_rows(info, grad_own, grad_came)

    grad_w_qkv, grad_w_out, grad_gain1, grad_shift1, grad_qv_bias, grad_out_bias = small_call(
        functools.partial(finish_kernel, unit=parts2[0] // (2 * count), at=layout.place[1], blocks=blocks),
        (info, chain2.value, other, chain2.vectors, pack, w_turned),
        [
            sds((width, 3 * width), F32), sds((width, width), F32), sds((width,), F32), sds((width,), F32),
            sds((2 * width,), F32), sds((width,), F32),
        ],
        [pltpu.VMEM((parts2[0], width), BF)],
        name="finish",
    )
    return (
        tokens_out, cls_norm, grad_tokens, grad_gain1, grad_shift1, grad_w_qkv, grad_qv_bias,
        grad_w_out, grad_out_bias, grad_gain2, grad_shift2, grad_w_fc1, grad_fc1_bias,
        grad_w_fc2, grad_fc2_bias,
    )


def solution(mesh):
    split = P("samp", "blk", None)
    classes = P(("samp", "blk"), None)
    return jax.shard_map(
        per_device,
        mesh=mesh,
        in_specs=(split, P("samp"), *([P()] * 12), split, classes),
        out_specs=(split, classes, split, *([P()] * 12)),
        check_vma=False,
    )
```

```python
import functools
import math

import jax
import jax.numpy as jnp
import numpy as np
from jax import lax
from jax.experimental import pallas as pl
from jax.experimental.pallas import tpu as pltpu
from jax.sharding import PartitionSpec as P

HEAD_DIM = 64
VIEW_ROWS = 196
NORM_EPS = 1e-06
CLS_EPS = 1e-05
MASKED = -1e30
LOG2E = math.log2(math.e)
LN2 = math.log(2.0)
SCALE = HEAD_DIM ** (-0.5)
SUM_LOW = 1e-15
SUM_HIGH = 1e15
BF = jnp.bfloat16
F32 = jnp.float32
VMEM_BYTES = 60 * 2**20
CORE = 0
EXTRA = 16


def dot(a, b, ca, cb):
    return lax.dot_general(a, b, (((ca,), (cb,)), ((), ())), preferred_element_type=F32)


def norm_parts(values):
    centre = jnp.mean(values, -1, keepdims=True)
    offset = values - centre
    rstd = lax.rsqrt(jnp.mean(offset * offset, -1, keepdims=True) + NORM_EPS)
    return offset * rstd, rstd


def gelu_cdf(values):
    return 0.5 + 0.5 * lax.erf(values * (0.5**0.5))


def params(semantics):
    return pltpu.CompilerParams(dimension_semantics=semantics, vmem_limit_bytes=VMEM_BYTES)


def whole(shape):
    return pl.BlockSpec(shape, lambda *_: (0,) * len(shape))


def key_counts(rows):
    views = (rows - 1) // VIEW_ROWS
    return [(v, min(rows, -(-(1 + VIEW_ROWS * v) // 16) * 16)) for v in range(1, views + 1)]


GAIN1, SHIFT1, GAIN2, SHIFT2, OUT_BIAS, FC2_BIAS, QV_BIAS, FC1_BIAS = 0, 1, 2, 3, 4, 5, 6, 8


def row_of(pack_ref, index):
    return pack_ref[index : index + 1, :]


def place_halves(target_ref, core, own, far):
    half = own.shape[0]
    target_ref[pl.ds(pl.multiple_of(core * half, 16), half), :] = own
    target_ref[pl.ds(pl.multiple_of((1 - core) * half, 16), half), :] = far


def split_halves(source_ref, core, own_ref, far_ref):
    half = own_ref.shape[1]
    own_ref[0] = source_ref[pl.ds(pl.multiple_of(core * half, 16), half), :]
    far_ref[0] = source_ref[pl.ds(pl.multiple_of((1 - core) * half, 16), half), :]


def rank_samples(views_ref, base, order_ref):
    count = order_ref.shape[0]
    views = [views_ref[base + i] for i in range(count)]
    for i in range(count):
        rank = jnp.int32(0)
        for j in range(count):
            if j != i:
                ahead = views[j] >= views[i] if j < i else views[j] > views[i]
                rank = rank + ahead.astype(jnp.int32)
        order_ref[rank] = jnp.int32(i)


def project_kernel(
    blk_ref, views_ref, own_ref, far_ref, w_in_ref, pack_ref, w_out_ref, w1_ref, w2_ref, cot_ref,
    hat_ref, qkv_ref, cls_ref, stat_ref, w_ref, order_ref, mix_ref, first_ref, full_ref,
):
    step = pl.program_id(0)

    @pl.when(step == 0)
    def _():
        w_ref[...] = w_in_ref[...].T
        rank_samples(views_ref, blk_ref[CORE] * order_ref.shape[0], order_ref)

    rows = hat_ref.shape[1]
    width = own_ref.shape[2]
    place_halves(full_ref, blk_ref[0], own_ref[0], far_ref[0])
    values = full_ref[...].astype(F32)
    hat, _ = norm_parts(values)
    hat_ref[0] = hat.astype(BF)
    normed = (hat * row_of(pack_ref, GAIN1) + row_of(pack_ref, SHIFT1)).astype(BF)
    columns = pack_ref[0:8, :].T
    for third in range(3):
        part = pl.ds(third * width, width)
        piece = dot(w_ref[part, :], normed, 1, 1)
        if third == 0:
            piece = (piece + columns[:, QV_BIAS : QV_BIAS + 1]) * (SCALE * LOG2E)
        if third == 2:
            piece = piece + columns[:, QV_BIAS + 1 : QV_BIAS + 2]
        qkv_ref[0, part, :] = piece.astype(BF)

    lead = qkv_ref[0, pl.ds(0, width), :128].astype(F32).T[0:1, :]
    head_of = lax.broadcasted_iota(jnp.int32, (8, width), 1) // HEAD_DIM
    pick = head_of == lax.broadcasted_iota(jnp.int32, (8, width), 0)
    queries = jnp.where(pick, lead, 0.0).astype(BF)
    scores = dot(queries, qkv_ref[0, pl.ds(width, width), :], 1, 0)
    limit = 1 + VIEW_ROWS * views_ref[blk_ref[CORE] * pl.num_programs(0) + step]
    place = lax.broadcasted_iota(jnp.int32, (8, rows), 1)
    scores = jnp.where(place < limit, scores, MASKED)
    powers = jnp.exp2(scores - jnp.max(scores, -1, keepdims=True))
    chances = (powers / jnp.sum(powers, -1, keepdims=True)).astype(BF)
    mixed = dot(chances, qkv_ref[0, pl.ds(2 * width, width), :], 1, 1)
    mix_ref[pl.ds(step, 1), :] = jnp.sum(jnp.where(pick, mixed, 0.0), 0, keepdims=True)
    first_ref[pl.ds(step, 1), :] = values[0:1, :]

    @pl.when(step == pl.num_programs(0) - 1)
    def _():
        branch = dot(mix_ref[...].astype(BF), w_out_ref[...], 1, 0) + row_of(pack_ref, OUT_BIAS)
        middle = first_ref[...] + branch
        normed2 = norm_parts(middle)[0] * row_of(pack_ref, GAIN2) + row_of(pack_ref, SHIFT2)
        normed2 = normed2.astype(BF)
        output = middle + row_of(pack_ref, FC2_BIAS)
        for j in range(w1_ref.shape[1] // width):
            cols = slice(j * width, (j + 1) * width)
            pre = dot(normed2, w1_ref[:, cols], 1, 0) + row_of(pack_ref, FC1_BIAS + j)
            act = (pre * gelu_cdf(pre)).astype(BF)
            output = output + dot(act, w2_ref[cols, :], 1, 0)
        cls_ref[...] = output
        count = cot_ref.shape[0]
        cls = output[:count]
        cot = cot_ref[...].astype(F32)
        stat_ref[...] = jnp.zeros_like(stat_ref)
        for k, term in enumerate((cls, cls * cls, cot, cot * cls)):
            stat_ref[k : k + 1, :] = jnp.sum(term, 0, keepdims=True)


def masked_tail(scores, main, limit):
    place = main + lax.broadcasted_iota(jnp.int32, scores.shape, 0)
    return jnp.where(place < limit, scores, MASKED)


def attention_kernel(
    core_ref, views_ref, qkv_ref, sum_ref, top_ref, plain_ref, att_ref, pow_ref
):
    sample = pl.program_id(0)
    rows = qkv_ref.shape[2]
    width = att_ref.shape[1]
    heads = width // HEAD_DIM
    views = views_ref[core_ref[CORE] * pl.num_programs(0) + sample]
    limit = 1 + VIEW_ROWS * views
    ones = jnp.ones((16, rows), BF)

    def store(h, mixed):
        total = mixed[HEAD_DIM : HEAD_DIM + 1]
        sum_ref[0, pl.ds(h, 1), :] = total
        att_ref[0, head_rows(h, 0), :] = (mixed[:HEAD_DIM] * (1.0 / total)).astype(BF)

    sum_ref[0, heads:8, :] = jnp.ones((8 - heads, rows), F32)
    for count, keys in key_counts(rows):

        @pl.when(views == count)
        def _(keys=keys):
            main = keys - 16

            def pair(p, carry):
                both = range(2)
                parts = [head_parts(qkv_ref, 2 * p + k, width, keys) for k in both]
                scores = [dot(key, query, 0, 0) for query, key, _ in parts]
                for k in both:
                    pow_ref[k, :main, :] = jnp.exp2(scores[k][:main]).astype(BF)
                    tail = masked_tail(scores[k][main:], main, limit)
                    pow_ref[k, main:keys, :] = jnp.exp2(tail).astype(BF)
                lefts = [jnp.concatenate((value, ones[:, :keys]), 0) for _, _, value in parts]
                mixed = [dot(lefts[k], pow_ref[k, :keys, :], 1, 0) for k in both]
                for k in both:
                    store(2 * p + k, mixed[k])
                return carry

            lax.fori_loop(0, heads // 2, pair, 0)

    totals = sum_ref[0]
    plain = (jnp.min(totals) > SUM_LOW) & (jnp.max(totals) < SUM_HIGH)
    plain_ref[sample] = plain.astype(jnp.int32)

    @pl.when(jnp.logical_not(plain))
    def _():
        @each_head(heads)
        def _(h, slot):
            query, key, value = head_parts(qkv_ref, h, width, rows)
            scores = masked_tail(dot(key, query, 0, 0), 0, limit)
            top = jnp.max(scores, 0, keepdims=True)
            top_ref[0, pl.ds(h, 1), :] = top
            pow_ref[slot] = jnp.exp2(scores - top).astype(BF)
            left = jnp.concatenate((value, ones), 0)
            store(h, dot(left, pow_ref[slot], 1, 0))


def each_head(heads):
    def run(body):
        def pair(p, carry):
            for slot in range(2):
                body(2 * p + slot, slot)
            return carry

        lax.fori_loop(0, heads // 2, pair, 0)

    return run


def head_rows(h, base):
    return pl.ds(pl.multiple_of(base + h * HEAD_DIM, HEAD_DIM), HEAD_DIM)


def head_parts(qkv_ref, h, width, keys):
    return (
        qkv_ref[0, head_rows(h, 0), :],
        qkv_ref[0, head_rows(h, width), :keys],
        qkv_ref[0, head_rows(h, 2 * width), :keys],
    )


def layer_kernel(
    core_ref, x_own_ref, x_far_ref, own_ref, far_ref, att_ref, sum_ref, cls_ref, cot_ref, *refs,
    samples, parts, peers
):
    stat_refs = refs[:peers]
    w_out_ref, w1_ref, w2_ref, pack_ref = refs[peers : peers + 4]
    (
        out_own_ref, out_far_ref, gmid_ref, dmix_ref, inner_ref, out_grad_ref, norm_ref, bias_ref,
        kept_ref, sent_ref,
    ) = refs[peers + 4 : peers + 14]
    full_ref, g_ref, act_ref, dpre_ref, dcls_ref, acc2_ref, acc1_ref, flat_ref = refs[peers + 14 :]
    step = pl.program_id(0)
    width = own_ref.shape[2]
    hidden = w2_ref.shape[0]
    blocks = hidden // width

    @pl.when(step == 0)
    def _():
        acc2_ref[...] = jnp.zeros_like(acc2_ref)
        acc1_ref[...] = jnp.zeros_like(acc1_ref)
        bias_ref[...] = jnp.zeros_like(bias_ref)
        out_grad_ref[...] = jnp.zeros_like(out_grad_ref)
        stats = stat_refs[0][...]
        for other in stat_refs[1:]:
            stats = stats + other[...]
        local = cot_ref.shape[0]
        cls = cls_ref[...][:local]
        cot = cot_ref[...].astype(F32)
        mean = stats[0:1] / samples
        scale = lax.rsqrt(stats[1:2] / samples - mean * mean + CLS_EPS)
        hat = (cls - mean) * scale
        norm_ref[...] = hat.astype(BF)
        cross = scale * (stats[3:4] - mean * stats[2:3])
        dcls_ref[...] = jnp.zeros_like(dcls_ref)
        dcls_ref[:local, :] = scale * (cot - stats[2:3] / samples - hat * (cross / samples))

    place_halves(full_ref, core_ref[CORE], x_own_ref[0], x_far_ref[0])
    place_halves(g_ref, core_ref[CORE], own_ref[0].astype(F32), far_ref[0].astype(F32))
    g_ref[0:1, :] = g_ref[0:1, :] + dcls_ref[pl.ds(step, 1), :]
    g_mlp = g_ref[...].astype(BF)
    bias_ref[blocks : blocks + 1, :] += jnp.sum(g_mlp.astype(F32), 0, keepdims=True)

    branch = dot(att_ref[0], w_out_ref[...], 0, 0) + row_of(pack_ref, OUT_BIAS)
    middle = full_ref[...].astype(F32) + branch
    hat, rstd = norm_parts(middle)
    normed = (hat * row_of(pack_ref, GAIN2) + row_of(pack_ref, SHIFT2)).astype(BF)
    hat_low = hat.astype(BF)
    for j in range(blocks):
        cols = slice(j * width, (j + 1) * width)
        pre = dot(normed, w1_ref[:, cols], 1, 0) + row_of(pack_ref, FC1_BIAS + j)
        d_act = dot(g_mlp, w2_ref[cols, :], 1, 1)
        cdf = gelu_cdf(pre)
        bell = jnp.exp2(pre * pre * (-0.5 * LOG2E) - 0.5 * math.log2(2.0 * math.pi))
        act_ref[:, cols] = (pre * cdf).astype(BF)
        d_pre = d_act * (cdf + pre * bell)
        bias_ref[j : j + 1, :] += jnp.sum(d_pre, 0, keepdims=True)
        dpre_ref[:, cols] = d_pre.astype(BF)
    acc1_ref[...] += dot(hat_low, dpre_ref[...], 0, 0)
    acc2_ref[...] += dot(act_ref[...], g_mlp, 0, 0)
    output = middle + dot(act_ref[...], w2_ref[...], 1, 0) + row_of(pack_ref, FC2_BIAS)
    full_ref[...] = output.astype(BF)
    split_halves(full_ref, core_ref[CORE], out_own_ref, out_far_ref)

    d_norm = dot(dpre_ref[...], w1_ref[...], 1, 1)
    u = d_norm * row_of(pack_ref, GAIN2)
    g_mid = g_ref[...] + rstd * (
        u - jnp.mean(u, -1, keepdims=True) - hat * jnp.mean(u * hat, -1, keepdims=True)
    )
    g_attn = g_mid.astype(BF)
    gmid_ref[0] = g_attn
    out_grad_ref[...] += dot(att_ref[0], g_attn, 1, 0)
    bias_ref[blocks + 1 : blocks + 2, :] += jnp.sum(g_attn.astype(F32), 0, keepdims=True)
    d_mix = dot(w_out_ref[...], g_attn, 1, 1)
    for h in range(width // HEAD_DIM):
        part = slice(h * HEAD_DIM, (h + 1) * HEAD_DIM)
        piece = d_mix[part] * (1.0 / sum_ref[0, h : h + 1, :])
        dmix_ref[0, part, :] = piece.astype(BF)
        inner_ref[0, h : h + 1, :] = jnp.sum(piece * att_ref[0, part, :].astype(F32), 0, keepdims=True)

    @pl.when(step == pl.num_programs(0) - 1)
    def _():
        flat_ref[:hidden, :] = acc2_ref[...].astype(BF)
        for j in range(blocks):
            rows = slice(hidden + j * width, hidden + (j + 1) * width)
            flat_ref[rows, :] = acc1_ref[:, j * width : (j + 1) * width].astype(BF)
        clear_rest(flat_ref, 2 * hidden)
        write_halves(core_ref[CORE], flat_ref, parts, kept_ref, sent_ref)


def attention_back_kernel(
    core_ref, views_ref, plain_ref, order_ref, qkv_ref, top_ref, dmix_ref, inner_ref, hat_ref,
    dqkv_ref, grad_ref, sums_ref, pow_ref, *, turn, samples
):
    pair = pl.program_id(0)
    sample = order_ref[turn]
    rows, width = hat_ref.shape[1:]
    views = views_ref[core_ref[CORE] * samples + sample]
    limit = 1 + VIEW_ROWS * views
    plain = plain_ref[sample] == 1
    both = range(2)
    lanes = [slice(k * HEAD_DIM, (k + 1) * HEAD_DIM) for k in both]

    def back(keys, powers_of):
        query = [qkv_ref[0, 0, part, :] for part in lanes]
        key = [qkv_ref[0, 1, part, :keys] for part in lanes]
        value = [qkv_ref[0, 2, part, :keys] for part in lanes]
        d_mix = [dmix_ref[0, part, :] for part in lanes]
        scores = [dot(key[k], query[k], 0, 0) for k in both]
        for k in both:
            powers_of(k, scores[k])
        d_weights = [dot(value[k], d_mix[k], 0, 0) for k in both]
        d_scores = []
        for k in both:
            inner = inner_ref[0, pl.ds(2 * pair + k, 1), :]
            powers = pow_ref[k, :keys, :].astype(F32)
            d_scores.append((powers * (d_weights[k] - inner)).astype(BF))
        for k in both:
            d_value = dot(d_mix[k], pow_ref[k, :keys, :], 1, 1)
            dqkv_ref[0, 2, lanes[k], :keys] = d_value.astype(BF)
        for k in both:
            d_query = dot(key[k], d_scores[k], 1, 0) * SCALE
            dqkv_ref[0, 0, lanes[k], :] = d_query.astype(BF)
            d_key = dot(query[k], d_scores[k], 1, 1) * LN2
            dqkv_ref[0, 1, lanes[k], :keys] = d_key.astype(BF)
        if keys < rows:
            blank = jnp.zeros((2 * HEAD_DIM, rows - keys), BF)
            dqkv_ref[0, 1, :, keys:] = blank
            dqkv_ref[0, 2, :, keys:] = blank

    for count, keys in key_counts(rows):

        @pl.when((views == count) & plain)
        def _(keys=keys):
            main = keys - 16

            def powers_of(k, scores):
                pow_ref[k, :main, :] = jnp.exp2(scores[:main]).astype(BF)
                tail = masked_tail(scores[main:], main, limit)
                pow_ref[k, main:keys, :] = jnp.exp2(tail).astype(BF)

            back(keys, powers_of)

    @pl.when(jnp.logical_not(plain))
    def _():
        def powers_of(k, scores):
            top = top_ref[0, pl.ds(2 * pair + k, 1), :]
            pow_ref[k] = jnp.exp2(masked_tail(scores, 0, limit) - top).astype(BF)

        back(rows, powers_of)

    right = jnp.concatenate((hat_ref[0], jnp.ones((rows, 128), BF)), 1)
    result = dot(dqkv_ref[0].reshape(3 * 2 * HEAD_DIM, rows), right, 1, 0)
    grad_ref[...] = result[:, :width].astype(BF).reshape(grad_ref.shape)
    sums_ref[0] = result[:, width:].T[:8]


def tokens_back_kernel(core_ref, order_ref, *refs, sets):
    dqkv_refs = refs[:sets]
    w_ref, pack_ref, x_own_ref, x_far_ref, gmid_ref, own_ref, far_ref, out_ref, d_ref, sems = refs[sets:]
    step = pl.program_id(0)

    def fetch(k):
        return pltpu.make_async_copy(dqkv_refs[k].at[0], d_ref.at[k], sems.at[k])

    @pl.when(step == 0)
    def _():
        for k in range(sets):
            fetch(k).start()

    for k in range(sets):

        @pl.when(step == k)
        def _(k=k):
            fetch(k).wait()

    d_norm = dot(d_ref[step], w_ref[...], 0, 0)
    place_halves(out_ref, core_ref[CORE], x_own_ref[0], x_far_ref[0])
    hat, rstd = norm_parts(out_ref[...].astype(F32))
    w = d_norm * row_of(pack_ref, GAIN1)
    back = rstd * (w - jnp.mean(w, -1, keepdims=True) - hat * jnp.mean(w * hat, -1, keepdims=True))
    out_ref[...] = (gmid_ref[0].astype(F32) + back).astype(BF)
    split_halves(out_ref, core_ref[CORE], own_ref, far_ref)


def clear_rest(ref, used):
    if ref.shape[0] > used:
        ref[used:, :] = jnp.zeros((ref.shape[0] - used, ref.shape[1]), ref.dtype)


def write_halves(core, flat_ref, parts, kept_ref, sent_ref):
    start = at = 0
    for size in parts:
        half = size // 2
        mine = pl.multiple_of(start + core * half, 16)
        other = pl.multiple_of(start + (1 - core) * half, 16)
        kept_ref[at : at + half, :] = flat_ref[pl.ds(mine, half), :]
        sent_ref[at : at + half, :] = flat_ref[pl.ds(other, half), :]
        start += size
        at += half


def pack_kernel(core_ref, *refs, sets, parts):
    grad_refs = refs[:sets]
    sums_refs = refs[sets : 2 * sets]
    out_grad_ref, bias_ref, kept_ref, sent_ref, flat_ref = refs[2 * sets :]
    width = out_grad_ref.shape[0]
    used = grad_refs[0].shape[0]
    total, sums = grad_refs[0][...].astype(F32), sums_refs[0][...]
    for grad_ref, sums_ref in zip(grad_refs[1:], sums_refs[1:]):
        total = total + grad_ref[...].astype(F32)
        sums = sums + sums_ref[...]
    flat_ref[:used, :] = total.astype(BF)
    flat_ref[used : used + width, :] = out_grad_ref[...].astype(BF)
    clear_rest(flat_ref, used + width)
    write_halves(core_ref[CORE], flat_ref, parts, kept_ref, sent_ref)
    rows = lax.broadcasted_iota(jnp.int32, (8, width), 0)
    extra = jnp.zeros((8, width), F32)
    for t in range(used // width):
        row = jnp.concatenate([sums[p, 0:1, t * 128 : (t + 1) * 128] for p in range(width // 128)], 1)
        extra = jnp.where(rows == t, row, extra)
    vectors = jnp.concatenate((bias_ref[0:8, :], extra), 0).astype(BF)
    at = sum(parts) // 2
    kept_ref[at : at + EXTRA, :] = vectors
    sent_ref[at : at + EXTRA, :] = vectors


def insert_rows(info, base, came):
    def body(info_ref, came_ref, base_ref, out_ref, mark_ref):
        out_ref[...] = came_ref[...]
        mark_ref[0] = jnp.int32(0)

    return pl.pallas_call(
        body,
        grid_spec=pltpu.PrefetchScalarGridSpec(
            num_scalar_prefetch=1,
            grid=(1,),
            in_specs=[
                pl.BlockSpec(came.shape, lambda *_: (0, 0, 0)), pl.BlockSpec(memory_space=pl.ANY),
            ],
            out_specs=[
                pl.BlockSpec(came.shape, lambda s, b: (1 - b[CORE], 0, 0)),
                pl.BlockSpec(memory_space=pltpu.SMEM),
            ],
        ),
        out_shape=[jax.ShapeDtypeStruct(base.shape, base.dtype), jax.ShapeDtypeStruct((1,), jnp.int32)],
        input_output_aliases={2: 0},
        compiler_params=params(("arbitrary",)),
        name="insert",
    )(info, came, base)


def swap_cores(value):
    return lax.ppermute(value, "blk", [(0, 1), (1, 0)])


def stages(count, first=4):
    out = []
    stride = 1
    while stride < count:
        left = count // stride
        radix = first if not out and left % first == 0 else 4 if left % 4 == 0 else 2
        out.append((stride, radix))
        stride *= radix
    return out


def shifted(value, stage, steps, axis="samp"):
    stride, radix = stage
    count = lax.axis_size(axis)
    pairs = []
    for source in range(count):
        digit = (source // stride) % radix
        pairs.append((source, source + ((digit + steps) % radix - digit) * stride))
    return lax.ppermute(value, axis, pairs)


MARK = jax.ShapeDtypeStruct((1,), jnp.int32)


def small_call(kernel, args, outs, scratch=(), ties=(), name=None):
    n, t, o = len(args), len(ties), len(outs)

    def body(*refs):
        kernel(*refs[:n], *refs[n + t : n + t + o], *refs[n + t + o + 1 :])
        refs[n + t + o][0] = jnp.int32(0)

    vmem = pl.BlockSpec(memory_space=pltpu.VMEM)
    smem = pl.BlockSpec(memory_space=pltpu.SMEM)
    size = lambda a: math.prod(a.shape) * jnp.dtype(a.dtype).itemsize
    total = sum(size(a) for a in (*args[1:], *outs)) + sum(
        math.prod(a.shape) * jnp.dtype(a.dtype).itemsize for a in scratch
    )
    return pl.pallas_call(
        body,
        in_specs=[smem, *[vmem] * (n - 1), *[smem] * t],
        out_specs=[vmem] * o + [smem],
        out_shape=[*outs, MARK],
        scratch_shapes=list(scratch),
        compiler_params=pltpu.CompilerParams(vmem_limit_bytes=2 * total + 4 * 2**20),
        name=name,
    )(*args, *ties)


def hand_on(value, tie):
    def body(tie_ref, value_ref, out_ref):
        pass

    return pl.pallas_call(
        body,
        in_specs=[pl.BlockSpec(memory_space=pltpu.SMEM), pl.BlockSpec(memory_space=pl.ANY)],
        out_specs=pl.BlockSpec(memory_space=pl.ANY),
        out_shape=jax.ShapeDtypeStruct(value.shape, value.dtype),
        input_output_aliases={1: 0},
        compiler_params=pltpu.CompilerParams(vmem_limit_bytes=VMEM_BYTES),
        name="hand_on",
    )(tie, value)


def spread_kernel(info_ref, *refs, count, radix, slot, extra):
    outputs = radix + (1 if extra and radix == 1 else 0)
    outs, total_ref = refs[count : count + outputs], refs[count + outputs]
    total = refs[0][...].astype(F32)
    for ref in refs[1:count]:
        total = total + ref[...].astype(F32)
    rows = total_ref.shape[0] - extra
    size = rows // radix
    total_ref[...] = total.astype(BF)
    if radix == 1:
        outs[0][...] = total_ref[:rows, :]
        if extra:
            outs[1][...] = total[rows:]
        return
    for k in range(radix):
        start = lax.rem(info_ref[slot] + k, radix) * size
        outs[k][:size, :] = total_ref[pl.ds(pl.multiple_of(start, 16), size), :]
        if extra:
            outs[k][size:, :] = total_ref[rows:, :]


def collect_kernel(info_ref, *refs, groups):
    at, out_at = 0, sum(groups)
    for count in groups:
        size = refs[at].shape[0]
        for k in range(count):
            refs[out_at][k * size : (k + 1) * size, :] = refs[at + k][...]
        at += count
        out_at += 1


class Layout:
    def __init__(self, count, sizes):
        self.base = stages(count)
        self.count = count
        table = np.zeros((2 * count, 1 + len(self.base)), np.int32)
        for device in range(2 * count):
            table[device, 0] = device % 2
            for i in range(len(self.base)):
                table[device, 1 + i] = self.digit(device, i)
        tables = [table]
        self.place = []
        for rows in sizes:
            self.place.append(sum(t.shape[1] for t in tables))
            tables.append(np.stack([self.places(device, rows) for device in range(2 * count)]))
        self.table = np.concatenate(tables, 1).astype(np.int32)

    def digit(self, device, index):
        stride, radix = self.base[index]
        return (device // 2 // stride) % radix

    def places(self, device, rows):
        core = device % 2
        unit = rows // 2
        offsets = np.array([core * unit, (1 - core) * unit])
        for index, (_, radix) in enumerate(self.base):
            unit //= radix
            digit = (self.digit(device, index) - np.arange(radix)) % radix
            offsets = (offsets[:, None] + (digit * unit)[None, :]).reshape(-1)
        return offsets


class Chain:
    def __init__(self, layout, info, extra=0):
        self.layout = layout
        self.info = info
        self.extra = extra
        self.rounds = len(layout.base)

    def start(self, kept, sent):
        self.pending = [kept, swap_cores(sent)]

    def scatter(self, level, ties=()):
        last = level == self.rounds
        radix = 1 if last else self.layout.base[level][1]
        rows, width = self.pending[0].shape
        size = (rows - self.extra) // radix
        if last:
            outs = [jax.ShapeDtypeStruct((size, width), BF)]
            if self.extra:
                outs.append(jax.ShapeDtypeStruct((self.extra, width), F32))
        else:
            outs = [jax.ShapeDtypeStruct((size + self.extra, width), BF)] * radix
        pieces = small_call(
            functools.partial(
                spread_kernel, count=len(self.pending), radix=radix, slot=1 + level, extra=self.extra
            ),
            (self.info, *self.pending), outs, [pltpu.VMEM((rows, width), BF)], ties, "spread",
        )
        if last:
            self.value = pieces[0]
            self.vectors = pieces[1] if self.extra else None
        else:
            stage = self.layout.base[level]
            self.pending = [pieces[0]] + [shifted(pieces[k], stage, k) for k in range(1, radix)]
        return pieces[-1]

    def gather(self, level):
        stage = self.layout.base[level]
        self.pending = [self.value] + [shifted(self.value, stage, k) for k in range(1, stage[1])]

    def collect(self, ties=()):
        size, width = self.pending[0].shape
        outs = [jax.ShapeDtypeStruct((len(self.pending) * size, width), BF)]
        self.value, mark = small_call(
            functools.partial(collect_kernel, groups=(len(self.pending),)),
            (self.info, *self.pending), outs, (), ties, "collect",
        )
        return mark


def restore(place_ref, flat_ref, ref, unit, at):
    def body(i, carry):
        start = pl.multiple_of(place_ref[at + i], 16)
        source = pl.multiple_of(i * unit, 16)
        chunk = ref[pl.ds(source, unit), :]
        flat_ref[pl.ds(start, unit), :] = chunk
        return carry

    lax.fori_loop(0, ref.shape[0] // unit, body, 0)


def finish_mlp_kernel(
    info_ref, own_ref, far_ref, vectors_ref, pack_ref, w1_ref,
    fc2_ref, fc1_ref, gain_ref, shift_ref, fc1_bias_ref, fc2_bias_ref, flat_ref, *, unit, at
):
    restore(info_ref, flat_ref, own_ref, unit, at)
    restore(info_ref, flat_ref, far_ref, unit, at + own_ref.shape[0] // unit)
    hidden, width = fc2_ref.shape
    fc2_ref[...] = flat_ref[:hidden, :].astype(F32)
    columns = pack_ref[0:8, :].T
    gain = jnp.zeros((width, 1), F32)
    shift = jnp.zeros((width, 1), F32)
    for j in range(hidden // width):
        cols = slice(j * width, (j + 1) * width)
        hats = flat_ref[hidden + j * width : hidden + (j + 1) * width, :].astype(F32)
        sums = vectors_ref[j : j + 1, :]
        fc1_ref[:, cols] = hats * columns[:, GAIN2 : GAIN2 + 1] + columns[:, SHIFT2 : SHIFT2 + 1] * sums
        w = w1_ref[:, cols].astype(F32)
        gain = gain + jnp.sum(w * hats, -1, keepdims=True)
        shift = shift + jnp.sum(w * sums, -1, keepdims=True)
    lane = lax.broadcasted_iota(jnp.int32, (width, 128), 1)
    both = jnp.where(lane == 0, gain, jnp.where(lane == 1, shift, 0.0)).T[0:8]
    gain_ref[...] = both[0]
    shift_ref[...] = both[1]
    blocks = hidden // width
    for j in range(blocks):
        fc1_bias_ref[j * width : (j + 1) * width] = vectors_ref[j, :]
    fc2_bias_ref[...] = vectors_ref[blocks, :]


def finish_kernel(
    info_ref, own_ref, far_ref, vectors_ref, pack_ref, w_ref, qkv_ref, out_ref, gain_ref, shift_ref, qv_ref, out_bias_ref, flat_ref,
    *, unit, at, blocks
):
    restore(info_ref, flat_ref, own_ref, unit, at)
    restore(info_ref, flat_ref, far_ref, unit, at + own_ref.shape[0] // unit)
    width = out_ref.shape[0]
    columns = qkv_ref.shape[1]
    out_ref[...] = flat_ref[columns : columns + width, :].astype(F32)
    gain = jnp.zeros((1, width), F32)
    shift = jnp.zeros((1, width), F32)
    turned = vectors_ref[8:16, :].T
    for t in range(columns // width):
        part = slice(t * width, (t + 1) * width)
        hats = flat_ref[part, :].astype(F32)
        sums = turned[:, t : t + 1]
        result = hats * row_of(pack_ref, GAIN1) + sums * row_of(pack_ref, SHIFT1)
        qkv_ref[:, part] = result.T
        w = w_ref[part, :].astype(F32)
        gain = gain + jnp.sum(w * hats, 0, keepdims=True)
        shift = shift + jnp.sum(w * sums, 0, keepdims=True)
    gain_ref[...] = gain[0]
    shift_ref[...] = shift[0]
    qv_ref[:width] = vectors_ref[8, :]
    qv_ref[width:] = vectors_ref[10, :]
    out_bias_ref[...] = vectors_ref[blocks + 1, :]


def pad_rows(count, unit):
    return -(-count // unit) * unit


def per_device(
    tokens, view_count, norm1_gain, norm1_bias, w_qkv, qv_bias, w_out, out_bias,
    norm2_gain, norm2_bias, w_fc1, fc1_bias, w_fc2, fc2_bias, cot_tokens, cot_cls,
):
    core = lax.axis_index("blk")
    cores = lax.axis_size("blk")
    count = lax.axis_size("samp")
    samples, half, width = tokens.shape
    local = samples // cores
    rows = half * cores
    hidden = w_fc1.shape[1]
    blocks = hidden // width
    heads = width // HEAD_DIM
    pairs = heads // 2
    sds = jax.ShapeDtypeStruct

    unit = 32 * count
    parts1 = [pad_rows(2 * hidden, unit)]
    parts2 = [pad_rows(4 * width, unit)]
    layout = Layout(count, (parts1[0], parts2[0]))
    device = lax.axis_index("samp") * cores + core
    info = lax.dynamic_index_in_dim(jnp.asarray(layout.table), device, 0, keepdims=False)

    theirs = (1 - core) * local
    far_tokens = swap_cores(lax.dynamic_slice_in_dim(tokens, theirs, local, 0))
    far_cot = swap_cores(lax.dynamic_slice_in_dim(cot_tokens, theirs, local, 0))

    pack = jnp.concatenate(
        (
            norm1_gain, norm1_bias, norm2_gain, norm2_bias, out_bias, fc2_bias, qv_bias, fc1_bias,
            jnp.zeros(((8 - blocks) * width,), BF),
        )
    ).astype(F32).reshape(16, width)

    vmem = pl.BlockSpec(memory_space=pltpu.VMEM)
    half_spec = lambda f: pl.BlockSpec((1, half, width), f)
    own_map = lambda s, b, *_: (b[CORE] * local + s, 0, 0)
    by_sample = lambda s, *_: (s, 0, 0)
    rows_spec = pl.BlockSpec((1, rows, width), by_sample)
    turned_spec = pl.BlockSpec((1, width, rows), by_sample)
    rstd_spec = pl.BlockSpec((1, rows, 1), by_sample)
    hidden_spec = pl.BlockSpec((1, rows, hidden), by_sample)
    eight_spec = pl.BlockSpec((1, 8, rows), by_sample)

    def big_call(kernel, prefetch, args, in_specs, outs, out_specs, scratch=(), ties=(), grid=(local,), name=None):
        n, t, o = len(prefetch) + len(args), len(ties), len(outs)
        smem = pl.BlockSpec(memory_space=pltpu.SMEM)

        def body(*refs):
            kernel(*refs[:n], *refs[n + t : n + t + o], *refs[n + t + o + 1 :])
            refs[n + t + o][0] = jnp.int32(0)

        return pl.pallas_call(
            body,
            grid_spec=pltpu.PrefetchScalarGridSpec(
                num_scalar_prefetch=len(prefetch),
                grid=grid,
                in_specs=[*in_specs, *[smem] * t],
                out_specs=[*out_specs, smem],
                scratch_shapes=list(scratch),
            ),
            out_shape=[*outs, MARK],
            compiler_params=params(("arbitrary",) * len(grid)),
            name=name,
        )(*prefetch, *args, *ties)

    hat1, qkv, cls_rows, stats, w_turned, order, _ = big_call(
        project_kernel,
        (info, view_count),
        (tokens, far_tokens, w_qkv, pack, w_out, w_fc1, w_fc2, cot_cls),
        [half_spec(own_map), half_spec(by_sample), *[vmem] * 6],
        [
            sds((local, rows, width), BF),
            sds((local, 3 * width, rows), BF),
            sds((8, width), F32),
            sds((8, width), F32),
            sds((3 * width, width), BF),
            sds((local,), jnp.int32),
        ],
        [
            rows_spec, pl.BlockSpec((1, 3 * width, rows), by_sample), vmem, vmem, vmem,
            pl.BlockSpec(memory_space=pltpu.SMEM),
        ],
        [pltpu.VMEM((8, width), F32), pltpu.VMEM((8, width), F32), pltpu.VMEM((rows, width), BF)],
        name="project",
    )

    def add_kernel(info_ref, *refs):
        total = refs[0][...]
        for ref in refs[1:-1]:
            total = total + ref[...]
        refs[-1][...] = total

    *later, first = stages(count)

    def add_all(values, ties=()):
        return small_call(add_kernel, [info, *values], [sds((8, width), F32)], (), ties, "add")

    stats, tie = add_all([stats, swap_cores(stats)])
    stat_parts = [stats] + [shifted(stats, first, k) for k in range(1, first[1])]

    qkv_spec = lambda f: pl.BlockSpec((1, 3 * width, rows), f)
    totals, tops, plain, mixed, tie = big_call(
        attention_kernel,
        (info, view_count),
        (qkv,),
        [qkv_spec(by_sample)],
        [
            sds((local, 8, rows), F32),
            sds((local, 8, rows), F32),
            sds((local,), jnp.int32),
            sds((local, width, rows), BF),
        ],
        [eight_spec, eight_spec, pl.BlockSpec(memory_space=pltpu.SMEM), turned_spec],
        [pltpu.VMEM((2, rows, rows), BF)],
        (tie,),
        name="attention",
    )

    for stage in later:
        stats, tie = add_all(stat_parts, (tie,))
        stat_parts = [stats] + [shifted(stats, stage, k) for k in range(1, stage[1])]

    tokens_out_own, out_far, g_mid, d_mix, inner, out_grad, cls_norm, biases, kept1, sent1, _ = big_call(
        functools.partial(
            layer_kernel, samples=local * cores * count, parts=parts1, peers=len(stat_parts)
        ),
        (info,),
        (
            tokens, far_tokens, cot_tokens, far_cot, mixed, totals, cls_rows, cot_cls, *stat_parts,
            w_out, w_fc1, w_fc2, pack,
        ),
        [
            half_spec(own_map), half_spec(by_sample), half_spec(own_map), half_spec(by_sample),
            turned_spec, eight_spec, vmem, vmem, *[vmem] * len(stat_parts), vmem, vmem, vmem, vmem,
        ],
        [
            sds((samples, half, width), BF),
            sds((local, half, width), BF),
            sds((local, rows, width), BF),
            sds((local, width, rows), BF),
            sds((local, 8, rows), F32),
            sds((width, width), F32),
            sds((local, width), BF),
            sds((8, width), F32),
            sds((sum(parts1) // 2, width), BF),
            sds((sum(parts1) // 2, width), BF),
        ],
        [
            half_spec(own_map), half_spec(by_sample), rows_spec, turned_spec, eight_spec,
            vmem, vmem, vmem, vmem, vmem,
        ],
        [
            pltpu.VMEM((rows, width), BF),
            pltpu.VMEM((rows, width), F32),
            pltpu.VMEM((rows, hidden), BF),
            pltpu.VMEM((rows, hidden), BF),
            pltpu.VMEM((8, width), F32),
            pltpu.VMEM((hidden, width), F32),
            pltpu.VMEM((width, hidden), F32),
            pltpu.VMEM((sum(parts1), width), BF),
        ],
        name="layer",
    )
    chain1 = Chain(layout, info)
    chain1.start(kept1, sent1)
    out_came = swap_cores(out_far)

    def attention_back(turn, ties):
        place = lambda p, c, v, q, o: (o[turn], 0, 0)
        return big_call(
            functools.partial(attention_back_kernel, turn=turn, samples=local),
            (info, view_count, plain, order),
            (qkv.reshape(local, 3, width, rows), tops, d_mix, inner, hat1),
            [
                pl.BlockSpec((1, 3, 128, rows), lambda p, c, v, q, o: (o[turn], 0, p, 0)),
                pl.BlockSpec((1, 8, rows), place),
                pl.BlockSpec((1, 128, rows), lambda p, c, v, q, o: (o[turn], p, 0)),
                pl.BlockSpec((1, 8, rows), place),
                pl.BlockSpec((1, rows, width), place),
            ],
            [
                sds((1, 3, width, rows), BF),
                sds((3, width, width), BF),
                sds((pairs, 8, 384), F32),
            ],
            [
                pl.BlockSpec((1, 3, 128, rows), lambda p, *_: (0, 0, p, 0)),
                pl.BlockSpec((3, 128, width), lambda p, *_: (0, p, 0)),
                pl.BlockSpec((1, 8, 384), lambda p, *_: (p, 0, 0)),
            ],
            [pltpu.VMEM((2, rows, rows), BF)],
            ties,
            grid=(pairs,),
            name="attention_back",
        )

    def scatter_step(level):
        def run(ties):
            piece = chain1.scatter(level, ties)
            if level == chain1.rounds:
                chain1.gather(level - 1)
            return piece

        return run

    def collect_step(level):
        def run(ties):
            value = chain1.collect(ties)
            if level > 0:
                chain1.gather(level - 1)
            return value

        return run

    steps = [scatter_step(level) for level in range(1, chain1.rounds + 1)]
    steps += [collect_step(level) for level in reversed(range(chain1.rounds))]
    ties = (chain1.scatter(0),)
    d_parts, grads, sums = [], [], []
    for sample in range(local):
        d_part, grad, total, tie = attention_back(sample, ties)
        d_parts.append(d_part.reshape(1, 3 * width, rows))
        grads.append(grad.reshape(3 * width, width))
        sums.append(total)
        ties = (steps.pop(0)((tie,)),)
        if sample == 0:
            tokens_out, tie = insert_rows(info, tokens_out_own, out_came)
            ties = (*ties, tie)

    chain2 = Chain(layout, info, EXTRA)
    kept2, sent2, _ = small_call(
        functools.partial(pack_kernel, sets=len(grads), parts=parts2),
        (info, *grads, *sums, out_grad, biases),
        [sds((sum(parts2) // 2 + EXTRA, width), BF)] * 2,
        [pltpu.VMEM((sum(parts2), width), BF)],
        ties,
        name="pack",
    )
    chain2.start(kept2, sent2)
    tie = chain2.scatter(0)

    own_turn = lambda s, c, o: (c[CORE] * local + o[s], 0, 0)
    turn = lambda s, c, o: (o[s], 0, 0)
    grad_own, grad_far, tie = big_call(
        functools.partial(tokens_back_kernel, sets=len(d_parts)),
        (info, order),
        (*d_parts, w_turned, pack, tokens, far_tokens, g_mid),
        [
            *[pl.BlockSpec(memory_space=pl.ANY)] * len(d_parts),
            vmem, vmem, half_spec(own_turn), half_spec(turn), pl.BlockSpec((1, rows, width), turn),
        ],
        [sds((samples, half, width), BF), sds((local, half, width), BF)],
        [half_spec(own_turn), half_spec(turn)],
        [
            pltpu.VMEM((rows, width), BF),
            pltpu.VMEM((len(d_parts), 3 * width, rows), BF),
            pltpu.SemaphoreType.DMA((len(d_parts),)),
        ],
        (tie,),
        name="tokens_back",
    )
    for level in range(1, chain2.rounds + 1):
        tie = chain2.scatter(level, (tie,) if level == 1 else ())
        if level == 1:
            grad_came = swap_cores(hand_on(grad_far, tie))
            while steps:
                tie = steps.pop(0)((tie,))
            other1 = swap_cores(chain1.value)
    ties = ()
    for level in reversed(range(chain2.rounds)):
        chain2.gather(level)
        if level == chain2.rounds - 1:
            (
                grad_w_fc2, grad_w_fc1, grad_gain2, grad_shift2, grad_fc1_bias, grad_fc2_bias, tie,
            ) = small_call(
                functools.partial(
                    finish_mlp_kernel, unit=parts1[0] // (2 * count), at=layout.place[0]
                ),
                (info, chain1.value, other1, chain2.vectors, pack, w_fc1),
                [
                    sds((hidden, width), F32), sds((width, hidden), F32), sds((width,), F32),
                    sds((width,), F32), sds((hidden,), F32), sds((width,), F32),
                ],
                [pltpu.VMEM((parts1[0], width), BF)],
                name="finish_mlp",
            )
            ties = (tie,)
        if level == 0:
            grad_tokens, tie = insert_rows(info, grad_own, grad_came)
            ties = (tie,)
        chain2.collect(ties)
    other = swap_cores(chain2.value)

    grad_w_qkv, grad_w_out, grad_gain1, grad_shift1, grad_qv_bias, grad_out_bias, _ = small_call(
        functools.partial(finish_kernel, unit=parts2[0] // (2 * count), at=layout.place[1], blocks=blocks),
        (info, chain2.value, other, chain2.vectors, pack, w_turned),
        [
            sds((width, 3 * width), F32), sds((width, width), F32), sds((width,), F32), sds((width,), F32),
            sds((2 * width,), F32), sds((width,), F32),
        ],
        [pltpu.VMEM((parts2[0], width), BF)],
        name="finish",
    )
    return (
        tokens_out, cls_norm, grad_tokens, grad_gain1, grad_shift1, grad_w_qkv, grad_qv_bias,
        grad_w_out, grad_out_bias, grad_gain2, grad_shift2, grad_w_fc1, grad_fc1_bias,
        grad_w_fc2, grad_fc2_bias,
    )


def solution(mesh):
    split = P("samp", "blk", None)
    classes = P(("samp", "blk"), None)
    return jax.shard_map(
        per_device,
        mesh=mesh,
        in_specs=(split, P("samp"), *([P()] * 12), split, classes),
        out_specs=(split, classes, split, *([P()] * 12)),
        check_vma=False,
    )
```

```python
import functools
import math

import jax
import jax.numpy as jnp
import numpy as np
from jax import lax
from jax.experimental import pallas as pl
from jax.experimental.pallas import tpu as pltpu
from jax.sharding import PartitionSpec as P

HEAD_DIM = 64
VIEW_ROWS = 196
NORM_EPS = 1e-06
CLS_EPS = 1e-05
MASKED = -1e30
LOG2E = math.log2(math.e)
LN2 = math.log(2.0)
SCALE = HEAD_DIM ** (-0.5)
SUM_LOW = 1e-15
SUM_HIGH = 1e15
BF = jnp.bfloat16
F32 = jnp.float32
VMEM_BYTES = 60 * 2**20
CORE = 0
EXTRA = 16


def dot(a, b, ca, cb):
    return lax.dot_general(a, b, (((ca,), (cb,)), ((), ())), preferred_element_type=F32)


def norm_parts(values):
    centre = jnp.mean(values, -1, keepdims=True)
    offset = values - centre
    rstd = lax.rsqrt(jnp.mean(offset * offset, -1, keepdims=True) + NORM_EPS)
    return offset * rstd, rstd


def gelu_cdf(values):
    return 0.5 + 0.5 * lax.erf(values * (0.5**0.5))


def params(semantics):
    return pltpu.CompilerParams(dimension_semantics=semantics, vmem_limit_bytes=VMEM_BYTES)


def whole(shape):
    return pl.BlockSpec(shape, lambda *_: (0,) * len(shape))


def key_counts(rows):
    views = (rows - 1) // VIEW_ROWS
    return [(v, min(rows, -(-(1 + VIEW_ROWS * v) // 16) * 16)) for v in range(1, views + 1)]


GAIN1, SHIFT1, GAIN2, SHIFT2, OUT_BIAS, FC2_BIAS, QV_BIAS, FC1_BIAS = 0, 1, 2, 3, 4, 5, 6, 8


def row_of(pack_ref, index):
    return pack_ref[index : index + 1, :]


def place_halves(target_ref, core, own, far):
    half = own.shape[0]
    target_ref[pl.ds(pl.multiple_of(core * half, 16), half), :] = own
    target_ref[pl.ds(pl.multiple_of((1 - core) * half, 16), half), :] = far


def split_halves(source_ref, core, own_ref, far_ref):
    half = own_ref.shape[1]
    own_ref[0] = source_ref[pl.ds(pl.multiple_of(core * half, 16), half), :]
    far_ref[0] = source_ref[pl.ds(pl.multiple_of((1 - core) * half, 16), half), :]


def rank_samples(views_ref, base, order_ref):
    count = order_ref.shape[0]
    views = [views_ref[base + i] for i in range(count)]
    for i in range(count):
        rank = jnp.int32(0)
        for j in range(count):
            if j != i:
                ahead = views[j] >= views[i] if j < i else views[j] > views[i]
                rank = rank + ahead.astype(jnp.int32)
        order_ref[rank] = jnp.int32(i)


def project_kernel(
    blk_ref, views_ref, own_ref, far_ref, w_in_ref, pack_ref, w_out_ref, w1_ref, w2_ref, cot_ref,
    hat_ref, qkv_ref, cls_ref, stat_ref, w_ref, order_ref, mix_ref, first_ref, full_ref,
):
    step = pl.program_id(0)

    @pl.when(step == 0)
    def _():
        w_ref[...] = w_in_ref[...].T
        rank_samples(views_ref, blk_ref[CORE] * order_ref.shape[0], order_ref)

    rows = hat_ref.shape[1]
    width = own_ref.shape[2]
    place_halves(full_ref, blk_ref[0], own_ref[0], far_ref[0])
    values = full_ref[...].astype(F32)
    hat, _ = norm_parts(values)
    hat_ref[0] = hat.astype(BF)
    normed = (hat * row_of(pack_ref, GAIN1) + row_of(pack_ref, SHIFT1)).astype(BF)
    columns = pack_ref[0:8, :].T
    for third in range(3):
        part = pl.ds(third * width, width)
        piece = dot(w_ref[part, :], normed, 1, 1)
        if third == 0:
            piece = (piece + columns[:, QV_BIAS : QV_BIAS + 1]) * (SCALE * LOG2E)
        if third == 2:
            piece = piece + columns[:, QV_BIAS + 1 : QV_BIAS + 2]
        qkv_ref[0, part, :] = piece.astype(BF)

    lead = qkv_ref[0, pl.ds(0, width), :128].astype(F32).T[0:1, :]
    head_of = lax.broadcasted_iota(jnp.int32, (8, width), 1) // HEAD_DIM
    pick = head_of == lax.broadcasted_iota(jnp.int32, (8, width), 0)
    queries = jnp.where(pick, lead, 0.0).astype(BF)
    scores = dot(queries, qkv_ref[0, pl.ds(width, width), :], 1, 0)
    limit = 1 + VIEW_ROWS * views_ref[blk_ref[CORE] * pl.num_programs(0) + step]
    place = lax.broadcasted_iota(jnp.int32, (8, rows), 1)
    scores = jnp.where(place < limit, scores, MASKED)
    powers = jnp.exp2(scores - jnp.max(scores, -1, keepdims=True))
    chances = (powers / jnp.sum(powers, -1, keepdims=True)).astype(BF)
    mixed = dot(chances, qkv_ref[0, pl.ds(2 * width, width), :], 1, 1)
    mix_ref[pl.ds(step, 1), :] = jnp.sum(jnp.where(pick, mixed, 0.0), 0, keepdims=True)
    first_ref[pl.ds(step, 1), :] = values[0:1, :]

    @pl.when(step == pl.num_programs(0) - 1)
    def _():
        branch = dot(mix_ref[...].astype(BF), w_out_ref[...], 1, 0) + row_of(pack_ref, OUT_BIAS)
        middle = first_ref[...] + branch
        normed2 = norm_parts(middle)[0] * row_of(pack_ref, GAIN2) + row_of(pack_ref, SHIFT2)
        normed2 = normed2.astype(BF)
        output = middle + row_of(pack_ref, FC2_BIAS)
        for j in range(w1_ref.shape[1] // width):
            cols = slice(j * width, (j + 1) * width)
            pre = dot(normed2, w1_ref[:, cols], 1, 0) + row_of(pack_ref, FC1_BIAS + j)
            act = (pre * gelu_cdf(pre)).astype(BF)
            output = output + dot(act, w2_ref[cols, :], 1, 0)
        cls_ref[...] = output
        count = cot_ref.shape[0]
        cls = output[:count]
        cot = cot_ref[...].astype(F32)
        stat_ref[...] = jnp.zeros_like(stat_ref)
        for k, term in enumerate((cls, cls * cls, cot, cot * cls)):
            stat_ref[k : k + 1, :] = jnp.sum(term, 0, keepdims=True)


def masked_tail(scores, main, limit):
    place = main + lax.broadcasted_iota(jnp.int32, scores.shape, 0)
    return jnp.where(place < limit, scores, MASKED)


def attention_kernel(
    core_ref, views_ref, qkv_ref, sum_ref, top_ref, plain_ref, att_ref, pow_ref
):
    sample = pl.program_id(0)
    rows = qkv_ref.shape[2]
    width = att_ref.shape[1]
    heads = width // HEAD_DIM
    views = views_ref[core_ref[CORE] * pl.num_programs(0) + sample]
    limit = 1 + VIEW_ROWS * views
    ones = jnp.ones((16, rows), BF)

    def store(h, mixed):
        total = mixed[HEAD_DIM : HEAD_DIM + 1]
        sum_ref[0, pl.ds(h, 1), :] = total
        att_ref[0, head_rows(h, 0), :] = (mixed[:HEAD_DIM] * (1.0 / total)).astype(BF)

    sum_ref[0, heads:8, :] = jnp.ones((8 - heads, rows), F32)
    for count, keys in key_counts(rows):

        @pl.when(views == count)
        def _(keys=keys):
            main = keys - 16

            def pair(p, carry):
                both = range(2)
                parts = [head_parts(qkv_ref, 2 * p + k, width, keys) for k in both]
                scores = [dot(key, query, 0, 0) for query, key, _ in parts]
                for k in both:
                    pow_ref[k, :main, :] = jnp.exp2(scores[k][:main]).astype(BF)
                    tail = masked_tail(scores[k][main:], main, limit)
                    pow_ref[k, main:keys, :] = jnp.exp2(tail).astype(BF)
                lefts = [jnp.concatenate((value, ones[:, :keys]), 0) for _, _, value in parts]
                mixed = [dot(lefts[k], pow_ref[k, :keys, :], 1, 0) for k in both]
                for k in both:
                    store(2 * p + k, mixed[k])
                return carry

            lax.fori_loop(0, heads // 2, pair, 0)

    totals = sum_ref[0]
    plain = (jnp.min(totals) > SUM_LOW) & (jnp.max(totals) < SUM_HIGH)
    plain_ref[sample] = plain.astype(jnp.int32)

    @pl.when(jnp.logical_not(plain))
    def _():
        @each_head(heads)
        def _(h, slot):
            query, key, value = head_parts(qkv_ref, h, width, rows)
            scores = masked_tail(dot(key, query, 0, 0), 0, limit)
            top = jnp.max(scores, 0, keepdims=True)
            top_ref[0, pl.ds(h, 1), :] = top
            pow_ref[slot] = jnp.exp2(scores - top).astype(BF)
            left = jnp.concatenate((value, ones), 0)
            store(h, dot(left, pow_ref[slot], 1, 0))


def each_head(heads):
    def run(body):
        def pair(p, carry):
            for slot in range(2):
                body(2 * p + slot, slot)
            return carry

        lax.fori_loop(0, heads // 2, pair, 0)

    return run


def head_rows(h, base):
    return pl.ds(pl.multiple_of(base + h * HEAD_DIM, HEAD_DIM), HEAD_DIM)


def head_parts(qkv_ref, h, width, keys):
    return (
        qkv_ref[0, head_rows(h, 0), :],
        qkv_ref[0, head_rows(h, width), :keys],
        qkv_ref[0, head_rows(h, 2 * width), :keys],
    )


def layer_kernel(
    core_ref, x_own_ref, x_far_ref, own_ref, far_ref, att_ref, sum_ref, cls_ref, cot_ref, *refs,
    samples, parts, peers
):
    stat_refs = refs[:peers]
    w_out_ref, w1_ref, w2_ref, pack_ref = refs[peers : peers + 4]
    (
        out_own_ref, out_far_ref, gmid_ref, dmix_ref, inner_ref, out_grad_ref, norm_ref, bias_ref,
        kept_ref, sent_ref,
    ) = refs[peers + 4 : peers + 14]
    full_ref, g_ref, act_ref, dpre_ref, dcls_ref, acc2_ref, acc1_ref, flat_ref = refs[peers + 14 :]
    step = pl.program_id(0)
    width = own_ref.shape[2]
    hidden = w2_ref.shape[0]
    blocks = hidden // width

    @pl.when(step == 0)
    def _():
        acc2_ref[...] = jnp.zeros_like(acc2_ref)
        acc1_ref[...] = jnp.zeros_like(acc1_ref)
        bias_ref[...] = jnp.zeros_like(bias_ref)
        out_grad_ref[...] = jnp.zeros_like(out_grad_ref)
        stats = stat_refs[0][...]
        for other in stat_refs[1:]:
            stats = stats + other[...]
        local = cot_ref.shape[0]
        cls = cls_ref[...][:local]
        cot = cot_ref[...].astype(F32)
        mean = stats[0:1] / samples
        scale = lax.rsqrt(stats[1:2] / samples - mean * mean + CLS_EPS)
        hat = (cls - mean) * scale
        norm_ref[...] = hat.astype(BF)
        cross = scale * (stats[3:4] - mean * stats[2:3])
        dcls_ref[...] = jnp.zeros_like(dcls_ref)
        dcls_ref[:local, :] = scale * (cot - stats[2:3] / samples - hat * (cross / samples))

    place_halves(full_ref, core_ref[CORE], x_own_ref[0], x_far_ref[0])
    place_halves(g_ref, core_ref[CORE], own_ref[0].astype(F32), far_ref[0].astype(F32))
    g_ref[0:1, :] = g_ref[0:1, :] + dcls_ref[pl.ds(step, 1), :]
    g_mlp = g_ref[...].astype(BF)
    bias_ref[blocks : blocks + 1, :] += jnp.sum(g_mlp.astype(F32), 0, keepdims=True)

    branch = dot(att_ref[0], w_out_ref[...], 0, 0) + row_of(pack_ref, OUT_BIAS)
    middle = full_ref[...].astype(F32) + branch
    hat, rstd = norm_parts(middle)
    normed = (hat * row_of(pack_ref, GAIN2) + row_of(pack_ref, SHIFT2)).astype(BF)
    hat_low = hat.astype(BF)
    for j in range(blocks):
        cols = slice(j * width, (j + 1) * width)
        pre = dot(normed, w1_ref[:, cols], 1, 0) + row_of(pack_ref, FC1_BIAS + j)
        d_act = dot(g_mlp, w2_ref[cols, :], 1, 1)
        cdf = gelu_cdf(pre)
        bell = jnp.exp2(pre * pre * (-0.5 * LOG2E) - 0.5 * math.log2(2.0 * math.pi))
        act_ref[:, cols] = (pre * cdf).astype(BF)
        d_pre = d_act * (cdf + pre * bell)
        bias_ref[j : j + 1, :] += jnp.sum(d_pre, 0, keepdims=True)
        dpre_ref[:, cols] = d_pre.astype(BF)
    acc1_ref[...] += dot(hat_low, dpre_ref[...], 0, 0)
    acc2_ref[...] += dot(act_ref[...], g_mlp, 0, 0)
    output = middle + dot(act_ref[...], w2_ref[...], 1, 0) + row_of(pack_ref, FC2_BIAS)
    full_ref[...] = output.astype(BF)
    split_halves(full_ref, core_ref[CORE], out_own_ref, out_far_ref)

    d_norm = dot(dpre_ref[...], w1_ref[...], 1, 1)
    u = d_norm * row_of(pack_ref, GAIN2)
    g_mid = g_ref[...] + rstd * (
        u - jnp.mean(u, -1, keepdims=True) - hat * jnp.mean(u * hat, -1, keepdims=True)
    )
    g_attn = g_mid.astype(BF)
    gmid_ref[0] = g_attn
    out_grad_ref[...] += dot(att_ref[0], g_attn, 1, 0)
    bias_ref[blocks + 1 : blocks + 2, :] += jnp.sum(g_attn.astype(F32), 0, keepdims=True)
    d_mix = dot(w_out_ref[...], g_attn, 1, 1)
    for h in range(width // HEAD_DIM):
        part = slice(h * HEAD_DIM, (h + 1) * HEAD_DIM)
        piece = d_mix[part] * (1.0 / sum_ref[0, h : h + 1, :])
        dmix_ref[0, part, :] = piece.astype(BF)
        inner_ref[0, h : h + 1, :] = jnp.sum(piece * att_ref[0, part, :].astype(F32), 0, keepdims=True)

    @pl.when(step == pl.num_programs(0) - 1)
    def _():
        flat_ref[:hidden, :] = acc2_ref[...].astype(BF)
        for j in range(blocks):
            rows = slice(hidden + j * width, hidden + (j + 1) * width)
            flat_ref[rows, :] = acc1_ref[:, j * width : (j + 1) * width].astype(BF)
        clear_rest(flat_ref, 2 * hidden)
        write_halves(core_ref[CORE], flat_ref, parts, kept_ref, sent_ref)


def attention_back_kernel(
    core_ref, views_ref, plain_ref, order_ref, qkv_ref, top_ref, dmix_ref, inner_ref, hat_ref,
    dqkv_ref, grad_ref, sums_ref, pow_ref, *, turn, samples
):
    pair = pl.program_id(0)
    sample = order_ref[turn]
    rows, width = hat_ref.shape[1:]
    views = views_ref[core_ref[CORE] * samples + sample]
    limit = 1 + VIEW_ROWS * views
    plain = plain_ref[sample] == 1
    both = range(2)
    lanes = [slice(k * HEAD_DIM, (k + 1) * HEAD_DIM) for k in both]

    def back(keys, powers_of):
        query = [qkv_ref[0, 0, part, :] for part in lanes]
        key = [qkv_ref[0, 1, part, :keys] for part in lanes]
        value = [qkv_ref[0, 2, part, :keys] for part in lanes]
        d_mix = [dmix_ref[0, part, :] for part in lanes]
        scores = [dot(key[k], query[k], 0, 0) for k in both]
        for k in both:
            powers_of(k, scores[k])
        d_weights = [dot(value[k], d_mix[k], 0, 0) for k in both]
        d_scores = []
        for k in both:
            inner = inner_ref[0, pl.ds(2 * pair + k, 1), :]
            powers = pow_ref[k, :keys, :].astype(F32)
            d_scores.append((powers * (d_weights[k] - inner)).astype(BF))
        for k in both:
            d_value = dot(d_mix[k], pow_ref[k, :keys, :], 1, 1)
            dqkv_ref[0, 2, lanes[k], :keys] = d_value.astype(BF)
        for k in both:
            d_query = dot(key[k], d_scores[k], 1, 0) * SCALE
            dqkv_ref[0, 0, lanes[k], :] = d_query.astype(BF)
            d_key = dot(query[k], d_scores[k], 1, 1) * LN2
            dqkv_ref[0, 1, lanes[k], :keys] = d_key.astype(BF)
        if keys < rows:
            blank = jnp.zeros((2 * HEAD_DIM, rows - keys), BF)
            dqkv_ref[0, 1, :, keys:] = blank
            dqkv_ref[0, 2, :, keys:] = blank

    for count, keys in key_counts(rows):

        @pl.when((views == count) & plain)
        def _(keys=keys):
            main = keys - 16

            def powers_of(k, scores):
                pow_ref[k, :main, :] = jnp.exp2(scores[:main]).astype(BF)
                tail = masked_tail(scores[main:], main, limit)
                pow_ref[k, main:keys, :] = jnp.exp2(tail).astype(BF)

            back(keys, powers_of)

    @pl.when(jnp.logical_not(plain))
    def _():
        def powers_of(k, scores):
            top = top_ref[0, pl.ds(2 * pair + k, 1), :]
            pow_ref[k] = jnp.exp2(masked_tail(scores, 0, limit) - top).astype(BF)

        back(rows, powers_of)

    right = jnp.concatenate((hat_ref[0], jnp.ones((rows, 128), BF)), 1)
    result = dot(dqkv_ref[0].reshape(3 * 2 * HEAD_DIM, rows), right, 1, 0)
    grad_ref[...] = result[:, :width].astype(BF).reshape(grad_ref.shape)
    sums_ref[0] = result[:, width:].T[:8]


def tokens_back_kernel(core_ref, order_ref, *refs, sets):
    dqkv_refs = refs[:sets]
    w_ref, pack_ref, x_own_ref, x_far_ref, gmid_ref, own_ref, far_ref, out_ref, d_ref, sems = refs[sets:]
    step = pl.program_id(0)

    def fetch(k):
        return pltpu.make_async_copy(dqkv_refs[k].at[0], d_ref.at[k], sems.at[k])

    @pl.when(step == 0)
    def _():
        for k in range(sets):
            fetch(k).start()

    for k in range(sets):

        @pl.when(step == k)
        def _(k=k):
            fetch(k).wait()

    d_norm = dot(d_ref[step], w_ref[...], 0, 0)
    place_halves(out_ref, core_ref[CORE], x_own_ref[0], x_far_ref[0])
    hat, rstd = norm_parts(out_ref[...].astype(F32))
    w = d_norm * row_of(pack_ref, GAIN1)
    back = rstd * (w - jnp.mean(w, -1, keepdims=True) - hat * jnp.mean(w * hat, -1, keepdims=True))
    out_ref[...] = (gmid_ref[0].astype(F32) + back).astype(BF)
    split_halves(out_ref, core_ref[CORE], own_ref, far_ref)


def clear_rest(ref, used):
    if ref.shape[0] > used:
        ref[used:, :] = jnp.zeros((ref.shape[0] - used, ref.shape[1]), ref.dtype)


def write_halves(core, flat_ref, parts, kept_ref, sent_ref):
    start = at = 0
    for size in parts:
        half = size // 2
        mine = pl.multiple_of(start + core * half, 16)
        other = pl.multiple_of(start + (1 - core) * half, 16)
        kept_ref[at : at + half, :] = flat_ref[pl.ds(mine, half), :]
        sent_ref[at : at + half, :] = flat_ref[pl.ds(other, half), :]
        start += size
        at += half


def pack_kernel(core_ref, *refs, sets, parts):
    grad_refs = refs[:sets]
    sums_refs = refs[sets : 2 * sets]
    out_grad_ref, bias_ref, kept_ref, sent_ref, flat_ref = refs[2 * sets :]
    width = out_grad_ref.shape[0]
    used = grad_refs[0].shape[0]
    total, sums = grad_refs[0][...].astype(F32), sums_refs[0][...]
    for grad_ref, sums_ref in zip(grad_refs[1:], sums_refs[1:]):
        total = total + grad_ref[...].astype(F32)
        sums = sums + sums_ref[...]
    flat_ref[:used, :] = total.astype(BF)
    flat_ref[used : used + width, :] = out_grad_ref[...].astype(BF)
    clear_rest(flat_ref, used + width)
    write_halves(core_ref[CORE], flat_ref, parts, kept_ref, sent_ref)
    rows = lax.broadcasted_iota(jnp.int32, (8, width), 0)
    extra = jnp.zeros((8, width), F32)
    for t in range(used // width):
        row = jnp.concatenate([sums[p, 0:1, t * 128 : (t + 1) * 128] for p in range(width // 128)], 1)
        extra = jnp.where(rows == t, row, extra)
    vectors = jnp.concatenate((bias_ref[0:8, :], extra), 0).astype(BF)
    at = sum(parts) // 2
    kept_ref[at : at + EXTRA, :] = vectors
    sent_ref[at : at + EXTRA, :] = vectors


def insert_rows(info, base, came):
    def body(info_ref, came_ref, base_ref, out_ref, mark_ref):
        out_ref[...] = came_ref[...]

    return pl.pallas_call(
        body,
        grid_spec=pltpu.PrefetchScalarGridSpec(
            num_scalar_prefetch=1,
            grid=(1,),
            in_specs=[
                pl.BlockSpec(came.shape, lambda *_: (0, 0, 0)), pl.BlockSpec(memory_space=pl.ANY),
            ],
            out_specs=[
                pl.BlockSpec(came.shape, lambda s, b: (1 - b[CORE], 0, 0)),
                pl.BlockSpec(memory_space=pl.ANY),
            ],
        ),
        out_shape=[jax.ShapeDtypeStruct(base.shape, base.dtype), jax.ShapeDtypeStruct((1,), jnp.int32)],
        input_output_aliases={2: 0},
        compiler_params=params(("arbitrary",)),
        name="insert",
    )(info, came, base)


def swap_cores(value):
    return lax.ppermute(value, "blk", [(0, 1), (1, 0)])


def stages(count, first=4):
    out = []
    stride = 1
    while stride < count:
        left = count // stride
        radix = first if not out and left % first == 0 else 4 if left % 4 == 0 else 2
        out.append((stride, radix))
        stride *= radix
    return out


def shifted(value, stage, steps, axis="samp"):
    stride, radix = stage
    count = lax.axis_size(axis)
    pairs = []
    for source in range(count):
        digit = (source // stride) % radix
        pairs.append((source, source + ((digit + steps) % radix - digit) * stride))
    return lax.ppermute(value, axis, pairs)


MARK = jax.ShapeDtypeStruct((1,), jnp.int32)


def small_call(kernel, args, outs, scratch=(), ties=(), name=None):
    n, t, o = len(args), len(ties), len(outs)

    def body(*refs):
        kernel(*refs[:n], *refs[n + t : n + t + o], *refs[n + t + o + 1 :])

    vmem = pl.BlockSpec(memory_space=pltpu.VMEM)
    smem = pl.BlockSpec(memory_space=pltpu.SMEM)
    size = lambda a: math.prod(a.shape) * jnp.dtype(a.dtype).itemsize
    total = sum(size(a) for a in (*args[1:], *outs)) + sum(
        math.prod(a.shape) * jnp.dtype(a.dtype).itemsize for a in scratch
    )
    return pl.pallas_call(
        body,
        in_specs=[smem, *[vmem] * (n - 1), *[smem] * t],
        out_specs=[vmem] * o + [pl.BlockSpec(memory_space=pl.ANY)],
        out_shape=[*outs, MARK],
        scratch_shapes=list(scratch),
        compiler_params=pltpu.CompilerParams(vmem_limit_bytes=2 * total + 4 * 2**20),
        name=name,
    )(*args, *ties)


def hand_on(value, tie):
    def body(tie_ref, value_ref, out_ref):
        pass

    return pl.pallas_call(
        body,
        in_specs=[pl.BlockSpec(memory_space=pltpu.SMEM), pl.BlockSpec(memory_space=pl.ANY)],
        out_specs=pl.BlockSpec(memory_space=pl.ANY),
        out_shape=jax.ShapeDtypeStruct(value.shape, value.dtype),
        input_output_aliases={1: 0},
        compiler_params=pltpu.CompilerParams(vmem_limit_bytes=VMEM_BYTES),
        name="hand_on",
    )(tie, value)


def spread_kernel(info_ref, *refs, count, radix, slot, extra, rows, rider):
    inputs = count + (1 if rider else 0)
    outputs = radix + (1 if extra and radix == 1 else 0)
    outs, total_ref = refs[inputs : inputs + outputs], refs[inputs + outputs]
    total = refs[0][:rows, :].astype(F32)
    for ref in refs[1:count]:
        total = total + ref[:rows, :].astype(F32)
    rows = rows - extra
    size = rows // radix
    total_ref[...] = total.astype(BF)
    if radix == 1:
        outs[0][...] = total_ref[:rows, :]
        if extra:
            outs[1][...] = total[rows:]
        return
    for k in range(radix):
        start = lax.rem(info_ref[slot] + k, radix) * size
        outs[k][:size, :] = total_ref[pl.ds(pl.multiple_of(start, 16), size), :]
        if extra:
            outs[k][size : size + extra, :] = total_ref[rows:, :]
        if rider and k > 0:
            outs[k][size + extra :, :] = refs[count][...]


def collect_kernel(info_ref, own_ref, *refs):
    out_ref = refs[-1]
    size = own_ref.shape[0]
    out_ref[:size, :] = own_ref[...]
    for k, ref in enumerate(refs[:-1]):
        out_ref[(k + 1) * size : (k + 2) * size, :] = ref[ref.shape[0] - size :, :]


class Layout:
    def __init__(self, count, sizes):
        self.base = stages(count)
        self.count = count
        table = np.zeros((2 * count, 1 + len(self.base)), np.int32)
        for device in range(2 * count):
            table[device, 0] = device % 2
            for i in range(len(self.base)):
                table[device, 1 + i] = self.digit(device, i)
        tables = [table]
        self.place = []
        for rows in sizes:
            self.place.append(sum(t.shape[1] for t in tables))
            tables.append(np.stack([self.places(device, rows) for device in range(2 * count)]))
        self.table = np.concatenate(tables, 1).astype(np.int32)

    def digit(self, device, index):
        stride, radix = self.base[index]
        return (device // 2 // stride) % radix

    def places(self, device, rows):
        core = device % 2
        unit = rows // 2
        offsets = np.array([core * unit, (1 - core) * unit])
        for index, (_, radix) in enumerate(self.base):
            unit //= radix
            digit = (self.digit(device, index) - np.arange(radix)) % radix
            offsets = (offsets[:, None] + (digit * unit)[None, :]).reshape(-1)
        return offsets


class Chain:
    def __init__(self, layout, info, extra=0):
        self.layout = layout
        self.info = info
        self.extra = extra
        self.rounds = len(layout.base)

    def start(self, kept, sent):
        self.pending = [kept, swap_cores(sent)]

    def scatter(self, level, ties=(), rider=None):
        last = level == self.rounds
        radix = 1 if last else self.layout.base[level][1]
        rows, width = self.pending[0].shape
        size = (rows - self.extra) // radix
        more = () if rider is None else (rider.value,)
        if last:
            outs = [jax.ShapeDtypeStruct((size, width), BF)]
            if self.extra:
                outs.append(jax.ShapeDtypeStruct((self.extra, width), F32))
        else:
            piece = size + self.extra
            sent = piece + sum(value.shape[0] for value in more)
            outs = [jax.ShapeDtypeStruct((sent if k else piece, width), BF) for k in range(radix)]
        pieces = small_call(
            functools.partial(
                spread_kernel, count=len(self.pending), radix=radix, slot=1 + level, extra=self.extra,
                rows=rows, rider=bool(more),
            ),
            (self.info, *self.pending, *more), outs, [pltpu.VMEM((rows, width), BF)], ties, "spread",
        )
        if last:
            self.value = pieces[0]
            self.vectors = pieces[1] if self.extra else None
        else:
            stage = self.layout.base[level]
            self.pending = [pieces[0]] + [shifted(pieces[k], stage, k) for k in range(1, radix)]
            if more:
                rider.pending = [rider.value, *self.pending[1:]]
        return pieces[-1]

    def gather(self, level):
        stage = self.layout.base[level]
        self.pending = [self.value] + [shifted(self.value, stage, k) for k in range(1, stage[1])]

    def collect(self, ties=()):
        size, width = self.pending[0].shape
        outs = [jax.ShapeDtypeStruct((len(self.pending) * size, width), BF)]
        self.value, mark = small_call(
            collect_kernel, (self.info, *self.pending), outs, (), ties, "collect"
        )
        return mark


def restore(place_ref, flat_ref, ref, unit, at):
    def body(i, carry):
        start = pl.multiple_of(place_ref[at + i], 16)
        source = pl.multiple_of(i * unit, 16)
        chunk = ref[pl.ds(source, unit), :]
        flat_ref[pl.ds(start, unit), :] = chunk
        return carry

    lax.fori_loop(0, ref.shape[0] // unit, body, 0)


def finish_mlp_kernel(
    info_ref, own_ref, far_ref, vectors_ref, pack_ref, w1_ref,
    fc2_ref, fc1_ref, gain_ref, shift_ref, fc1_bias_ref, fc2_bias_ref, flat_ref, *, unit, at
):
    restore(info_ref, flat_ref, own_ref, unit, at)
    restore(info_ref, flat_ref, far_ref, unit, at + own_ref.shape[0] // unit)
    hidden, width = fc2_ref.shape
    fc2_ref[...] = flat_ref[:hidden, :].astype(F32)
    columns = pack_ref[0:8, :].T
    gain = jnp.zeros((width, 1), F32)
    shift = jnp.zeros((width, 1), F32)
    for j in range(hidden // width):
        cols = slice(j * width, (j + 1) * width)
        hats = flat_ref[hidden + j * width : hidden + (j + 1) * width, :].astype(F32)
        sums = vectors_ref[j : j + 1, :]
        fc1_ref[:, cols] = hats * columns[:, GAIN2 : GAIN2 + 1] + columns[:, SHIFT2 : SHIFT2 + 1] * sums
        w = w1_ref[:, cols].astype(F32)
        gain = gain + jnp.sum(w * hats, -1, keepdims=True)
        shift = shift + jnp.sum(w * sums, -1, keepdims=True)
    lane = lax.broadcasted_iota(jnp.int32, (width, 128), 1)
    both = jnp.where(lane == 0, gain, jnp.where(lane == 1, shift, 0.0)).T[0:8]
    gain_ref[...] = both[0]
    shift_ref[...] = both[1]
    blocks = hidden // width
    for j in range(blocks):
        fc1_bias_ref[j * width : (j + 1) * width] = vectors_ref[j, :]
    fc2_bias_ref[...] = vectors_ref[blocks, :]


def finish_kernel(
    info_ref, own_ref, far_ref, vectors_ref, pack_ref, w_ref, qkv_ref, out_ref, gain_ref, shift_ref, qv_ref, out_bias_ref, flat_ref,
    *, unit, at, blocks
):
    restore(info_ref, flat_ref, own_ref, unit, at)
    restore(info_ref, flat_ref, far_ref, unit, at + own_ref.shape[0] // unit)
    width = out_ref.shape[0]
    columns = qkv_ref.shape[1]
    out_ref[...] = flat_ref[columns : columns + width, :].astype(F32)
    gain = jnp.zeros((1, width), F32)
    shift = jnp.zeros((1, width), F32)
    turned = vectors_ref[8:16, :].T
    for t in range(columns // width):
        part = slice(t * width, (t + 1) * width)
        hats = flat_ref[part, :].astype(F32)
        sums = turned[:, t : t + 1]
        result = hats * row_of(pack_ref, GAIN1) + sums * row_of(pack_ref, SHIFT1)
        qkv_ref[:, part] = result.T
        w = w_ref[part, :].astype(F32)
        gain = gain + jnp.sum(w * hats, 0, keepdims=True)
        shift = shift + jnp.sum(w * sums, 0, keepdims=True)
    gain_ref[...] = gain[0]
    shift_ref[...] = shift[0]
    qv_ref[:width] = vectors_ref[8, :]
    qv_ref[width:] = vectors_ref[10, :]
    out_bias_ref[...] = vectors_ref[blocks + 1, :]


def pad_rows(count, unit):
    return -(-count // unit) * unit


def per_device(
    tokens, view_count, norm1_gain, norm1_bias, w_qkv, qv_bias, w_out, out_bias,
    norm2_gain, norm2_bias, w_fc1, fc1_bias, w_fc2, fc2_bias, cot_tokens, cot_cls,
):
    core = lax.axis_index("blk")
    cores = lax.axis_size("blk")
    count = lax.axis_size("samp")
    samples, half, width = tokens.shape
    local = samples // cores
    rows = half * cores
    hidden = w_fc1.shape[1]
    blocks = hidden // width
    heads = width // HEAD_DIM
    pairs = heads // 2
    sds = jax.ShapeDtypeStruct

    unit = 32 * count
    parts1 = [pad_rows(2 * hidden, unit)]
    parts2 = [pad_rows(4 * width, unit)]
    layout = Layout(count, (parts1[0], parts2[0]))
    device = lax.axis_index("samp") * cores + core
    info = lax.dynamic_index_in_dim(jnp.asarray(layout.table), device, 0, keepdims=False)

    theirs = (1 - core) * local
    far_tokens = swap_cores(lax.dynamic_slice_in_dim(tokens, theirs, local, 0))
    far_cot = swap_cores(lax.dynamic_slice_in_dim(cot_tokens, theirs, local, 0))

    pack = jnp.concatenate(
        (
            norm1_gain, norm1_bias, norm2_gain, norm2_bias, out_bias, fc2_bias, qv_bias, fc1_bias,
            jnp.zeros(((8 - blocks) * width,), BF),
        )
    ).astype(F32).reshape(16, width)

    vmem = pl.BlockSpec(memory_space=pltpu.VMEM)
    half_spec = lambda f: pl.BlockSpec((1, half, width), f)
    own_map = lambda s, b, *_: (b[CORE] * local + s, 0, 0)
    by_sample = lambda s, *_: (s, 0, 0)
    rows_spec = pl.BlockSpec((1, rows, width), by_sample)
    turned_spec = pl.BlockSpec((1, width, rows), by_sample)
    rstd_spec = pl.BlockSpec((1, rows, 1), by_sample)
    hidden_spec = pl.BlockSpec((1, rows, hidden), by_sample)
    eight_spec = pl.BlockSpec((1, 8, rows), by_sample)

    def big_call(kernel, prefetch, args, in_specs, outs, out_specs, scratch=(), ties=(), grid=(local,), name=None):
        n, t, o = len(prefetch) + len(args), len(ties), len(outs)
        smem = pl.BlockSpec(memory_space=pltpu.SMEM)

        def body(*refs):
            kernel(*refs[:n], *refs[n + t : n + t + o], *refs[n + t + o + 1 :])

        return pl.pallas_call(
            body,
            grid_spec=pltpu.PrefetchScalarGridSpec(
                num_scalar_prefetch=len(prefetch),
                grid=grid,
                in_specs=[*in_specs, *[smem] * t],
                out_specs=[*out_specs, pl.BlockSpec(memory_space=pl.ANY)],
                scratch_shapes=list(scratch),
            ),
            out_shape=[*outs, MARK],
            compiler_params=params(("arbitrary",) * len(grid)),
            name=name,
        )(*prefetch, *args, *ties)

    hat1, qkv, cls_rows, stats, w_turned, order, _ = big_call(
        project_kernel,
        (info, view_count),
        (tokens, far_tokens, w_qkv, pack, w_out, w_fc1, w_fc2, cot_cls),
        [half_spec(own_map), half_spec(by_sample), *[vmem] * 6],
        [
            sds((local, rows, width), BF),
            sds((local, 3 * width, rows), BF),
            sds((8, width), F32),
            sds((8, width), F32),
            sds((3 * width, width), BF),
            sds((local,), jnp.int32),
        ],
        [
            rows_spec, pl.BlockSpec((1, 3 * width, rows), by_sample), vmem, vmem, vmem,
            pl.BlockSpec(memory_space=pltpu.SMEM),
        ],
        [pltpu.VMEM((8, width), F32), pltpu.VMEM((8, width), F32), pltpu.VMEM((rows, width), BF)],
        name="project",
    )

    def add_kernel(info_ref, *refs):
        total = refs[0][...]
        for ref in refs[1:-1]:
            total = total + ref[...]
        refs[-1][...] = total

    *later, first = stages(count)

    def add_all(values, ties=()):
        return small_call(add_kernel, [info, *values], [sds((8, width), F32)], (), ties, "add")

    stats, tie = add_all([stats, swap_cores(stats)])
    stat_parts = [stats] + [shifted(stats, first, k) for k in range(1, first[1])]

    qkv_spec = lambda f: pl.BlockSpec((1, 3 * width, rows), f)
    totals, tops, plain, mixed, tie = big_call(
        attention_kernel,
        (info, view_count),
        (qkv,),
        [qkv_spec(by_sample)],
        [
            sds((local, 8, rows), F32),
            sds((local, 8, rows), F32),
            sds((local,), jnp.int32),
            sds((local, width, rows), BF),
        ],
        [eight_spec, eight_spec, pl.BlockSpec(memory_space=pltpu.SMEM), turned_spec],
        [pltpu.VMEM((2, rows, rows), BF)],
        (tie,),
        name="attention",
    )

    for stage in later:
        stats, tie = add_all(stat_parts, (tie,))
        stat_parts = [stats] + [shifted(stats, stage, k) for k in range(1, stage[1])]

    tokens_out_own, out_far, g_mid, d_mix, inner, out_grad, cls_norm, biases, kept1, sent1, _ = big_call(
        functools.partial(
            layer_kernel, samples=local * cores * count, parts=parts1, peers=len(stat_parts)
        ),
        (info,),
        (
            tokens, far_tokens, cot_tokens, far_cot, mixed, totals, cls_rows, cot_cls, *stat_parts,
            w_out, w_fc1, w_fc2, pack,
        ),
        [
            half_spec(own_map), half_spec(by_sample), half_spec(own_map), half_spec(by_sample),
            turned_spec, eight_spec, vmem, vmem, *[vmem] * len(stat_parts), vmem, vmem, vmem, vmem,
        ],
        [
            sds((samples, half, width), BF),
            sds((local, half, width), BF),
            sds((local, rows, width), BF),
            sds((local, width, rows), BF),
            sds((local, 8, rows), F32),
            sds((width, width), F32),
            sds((local, width), BF),
            sds((8, width), F32),
            sds((sum(parts1) // 2, width), BF),
            sds((sum(parts1) // 2, width), BF),
        ],
        [
            half_spec(own_map), half_spec(by_sample), rows_spec, turned_spec, eight_spec,
            vmem, vmem, vmem, vmem, vmem,
        ],
        [
            pltpu.VMEM((rows, width), BF),
            pltpu.VMEM((rows, width), F32),
            pltpu.VMEM((rows, hidden), BF),
            pltpu.VMEM((rows, hidden), BF),
            pltpu.VMEM((8, width), F32),
            pltpu.VMEM((hidden, width), F32),
            pltpu.VMEM((width, hidden), F32),
            pltpu.VMEM((sum(parts1), width), BF),
        ],
        name="layer",
    )
    chain1 = Chain(layout, info)
    chain1.start(kept1, sent1)
    out_came = swap_cores(out_far)

    def attention_back(turn, ties):
        place = lambda p, c, v, q, o: (o[turn], 0, 0)
        return big_call(
            functools.partial(attention_back_kernel, turn=turn, samples=local),
            (info, view_count, plain, order),
            (qkv.reshape(local, 3, width, rows), tops, d_mix, inner, hat1),
            [
                pl.BlockSpec((1, 3, 128, rows), lambda p, c, v, q, o: (o[turn], 0, p, 0)),
                pl.BlockSpec((1, 8, rows), place),
                pl.BlockSpec((1, 128, rows), lambda p, c, v, q, o: (o[turn], p, 0)),
                pl.BlockSpec((1, 8, rows), place),
                pl.BlockSpec((1, rows, width), place),
            ],
            [
                sds((1, 3, width, rows), BF),
                sds((3, width, width), BF),
                sds((pairs, 8, 384), F32),
            ],
            [
                pl.BlockSpec((1, 3, 128, rows), lambda p, *_: (0, 0, p, 0)),
                pl.BlockSpec((3, 128, width), lambda p, *_: (0, p, 0)),
                pl.BlockSpec((1, 8, 384), lambda p, *_: (p, 0, 0)),
            ],
            [pltpu.VMEM((2, rows, rows), BF)],
            ties,
            grid=(pairs,),
            name="attention_back",
        )

    def scatter_step(level):
        def run(ties):
            piece = chain1.scatter(level, ties)
            if level == chain1.rounds:
                chain1.gather(level - 1)
            return piece

        return run

    def collect_step(level):
        def run(ties):
            mark = chain1.collect(ties)
            if level > 1:
                chain1.gather(level - 1)
            return mark

        return run

    steps = [scatter_step(level) for level in range(1, chain1.rounds + 1)]
    steps += [collect_step(level) for level in reversed(range(1, chain1.rounds))]
    ties = (chain1.scatter(0),)
    d_parts, grads, sums = [], [], []
    for sample in range(local):
        d_part, grad, total, tie = attention_back(sample, ties)
        d_parts.append(d_part.reshape(1, 3 * width, rows))
        grads.append(grad.reshape(3 * width, width))
        sums.append(total)
        ties = (steps.pop(0)((tie,)),)
        if sample == 0:
            tokens_out, tie = insert_rows(info, tokens_out_own, out_came)
            ties = (*ties, tie)

    while steps:
        ties = (steps.pop(0)(()),)
    chain2 = Chain(layout, info, EXTRA)
    kept2, sent2, _ = small_call(
        functools.partial(pack_kernel, sets=len(grads), parts=parts2),
        (info, *grads, *sums, out_grad, biases),
        [sds((sum(parts2) // 2 + EXTRA, width), BF)] * 2,
        [pltpu.VMEM((sum(parts2), width), BF)],
        ties,
        name="pack",
    )
    chain2.start(kept2, sent2)
    tie = chain2.scatter(0, (), chain1)

    own_turn = lambda s, c, o: (c[CORE] * local + o[s], 0, 0)
    turn = lambda s, c, o: (o[s], 0, 0)
    grad_own, grad_far, tie = big_call(
        functools.partial(tokens_back_kernel, sets=len(d_parts)),
        (info, order),
        (*d_parts, w_turned, pack, tokens, far_tokens, g_mid),
        [
            *[pl.BlockSpec(memory_space=pl.ANY)] * len(d_parts),
            vmem, vmem, half_spec(own_turn), half_spec(turn), pl.BlockSpec((1, rows, width), turn),
        ],
        [sds((samples, half, width), BF), sds((local, half, width), BF)],
        [half_spec(own_turn), half_spec(turn)],
        [
            pltpu.VMEM((rows, width), BF),
            pltpu.VMEM((len(d_parts), 3 * width, rows), BF),
            pltpu.SemaphoreType.DMA((len(d_parts),)),
        ],
        (tie,),
        name="tokens_back",
    )
    for level in range(1, chain2.rounds + 1):
        tie = chain2.scatter(level, (tie,) if level == 1 else ())
        if level == 1:
            grad_came = swap_cores(hand_on(grad_far, tie))
            chain1.collect((tie,))
            other1 = swap_cores(chain1.value)
    ties = ()
    for level in reversed(range(chain2.rounds)):
        chain2.gather(level)
        if level == chain2.rounds - 1:
            (
                grad_w_fc2, grad_w_fc1, grad_gain2, grad_shift2, grad_fc1_bias, grad_fc2_bias, tie,
            ) = small_call(
                functools.partial(
                    finish_mlp_kernel, unit=parts1[0] // (2 * count), at=layout.place[0]
                ),
                (info, chain1.value, other1, chain2.vectors, pack, w_fc1),
                [
                    sds((hidden, width), F32), sds((width, hidden), F32), sds((width,), F32),
                    sds((width,), F32), sds((hidden,), F32), sds((width,), F32),
                ],
                [pltpu.VMEM((parts1[0], width), BF)],
                name="finish_mlp",
            )
            ties = (tie,)
        if level == 0:
            grad_tokens, tie = insert_rows(info, grad_own, grad_came)
            ties = (tie,)
        chain2.collect(ties)
    other = swap_cores(chain2.value)

    grad_w_qkv, grad_w_out, grad_gain1, grad_shift1, grad_qv_bias, grad_out_bias, _ = small_call(
        functools.partial(finish_kernel, unit=parts2[0] // (2 * count), at=layout.place[1], blocks=blocks),
        (info, chain2.value, other, chain2.vectors, pack, w_turned),
        [
            sds((width, 3 * width), F32), sds((width, width), F32), sds((width,), F32), sds((width,), F32),
            sds((2 * width,), F32), sds((width,), F32),
        ],
        [pltpu.VMEM((parts2[0], width), BF)],
        name="finish",
    )
    return (
        tokens_out, cls_norm, grad_tokens, grad_gain1, grad_shift1, grad_w_qkv, grad_qv_bias,
        grad_w_out, grad_out_bias, grad_gain2, grad_shift2, grad_w_fc1, grad_fc1_bias,
        grad_w_fc2, grad_fc2_bias,
    )


def solution(mesh):
    split = P("samp", "blk", None)
    classes = P(("samp", "blk"), None)
    return jax.shard_map(
        per_device,
        mesh=mesh,
        in_specs=(split, P("samp"), *([P()] * 12), split, classes),
        out_specs=(split, classes, split, *([P()] * 12)),
        check_vma=False,
    )
```

```python
import functools
import math

import jax
import jax.numpy as jnp
import numpy as np
from jax import lax
from jax.experimental import pallas as pl
from jax.experimental.pallas import tpu as pltpu
from jax.sharding import PartitionSpec as P

HEAD_DIM = 64
VIEW_ROWS = 196
NORM_EPS = 1e-06
CLS_EPS = 1e-05
MASKED = -1e30
LOG2E = math.log2(math.e)
LN2 = math.log(2.0)
SCALE = HEAD_DIM ** (-0.5)
SUM_LOW = 1e-15
SUM_HIGH = 1e15
BF = jnp.bfloat16
F32 = jnp.float32
VMEM_BYTES = 60 * 2**20
CORE = 0
EXTRA = 16


def dot(a, b, ca, cb):
    return lax.dot_general(a, b, (((ca,), (cb,)), ((), ())), preferred_element_type=F32)


def norm_parts(values):
    centre = jnp.mean(values, -1, keepdims=True)
    offset = values - centre
    rstd = lax.rsqrt(jnp.mean(offset * offset, -1, keepdims=True) + NORM_EPS)
    return offset * rstd, rstd


def gelu_cdf(values):
    return 0.5 + 0.5 * lax.erf(values * (0.5**0.5))


def params(semantics):
    return pltpu.CompilerParams(dimension_semantics=semantics, vmem_limit_bytes=VMEM_BYTES)


def whole(shape):
    return pl.BlockSpec(shape, lambda *_: (0,) * len(shape))


def key_counts(rows):
    views = (rows - 1) // VIEW_ROWS
    return [(v, min(rows, -(-(1 + VIEW_ROWS * v) // 16) * 16)) for v in range(1, views + 1)]


GAIN1, SHIFT1, GAIN2, SHIFT2, OUT_BIAS, FC2_BIAS, QV_BIAS, FC1_BIAS = 0, 1, 2, 3, 4, 5, 6, 8


def row_of(pack_ref, index):
    return pack_ref[index : index + 1, :]


def place_halves(target_ref, core, own, far):
    half = own.shape[0]
    target_ref[pl.ds(pl.multiple_of(core * half, 16), half), :] = own
    target_ref[pl.ds(pl.multiple_of((1 - core) * half, 16), half), :] = far


def split_halves(source_ref, core, own_ref, far_ref):
    half = own_ref.shape[1]
    own_ref[0] = source_ref[pl.ds(pl.multiple_of(core * half, 16), half), :]
    far_ref[0] = source_ref[pl.ds(pl.multiple_of((1 - core) * half, 16), half), :]


def rank_samples(views_ref, base, order_ref):
    count = order_ref.shape[0]
    views = [views_ref[base + i] for i in range(count)]
    for i in range(count):
        rank = jnp.int32(0)
        for j in range(count):
            if j != i:
                ahead = views[j] >= views[i] if j < i else views[j] > views[i]
                rank = rank + ahead.astype(jnp.int32)
        order_ref[rank] = jnp.int32(i)


def project_kernel(
    blk_ref, views_ref, own_ref, far_ref, w_in_ref, pack_ref, w_out_ref, w1_ref, w2_ref, cot_ref,
    hat_ref, qkv_ref, cls_ref, stat_ref, w_ref, order_ref, mix_ref, first_ref, full_ref,
):
    step = pl.program_id(0)

    @pl.when(step == 0)
    def _():
        w_ref[...] = w_in_ref[...].T
        rank_samples(views_ref, blk_ref[CORE] * order_ref.shape[0], order_ref)

    rows = hat_ref.shape[1]
    width = own_ref.shape[2]
    place_halves(full_ref, blk_ref[0], own_ref[0], far_ref[0])
    values = full_ref[...].astype(F32)
    hat, _ = norm_parts(values)
    hat_ref[0] = hat.astype(BF)
    normed = (hat * row_of(pack_ref, GAIN1) + row_of(pack_ref, SHIFT1)).astype(BF)
    columns = pack_ref[0:8, :].T
    for third in range(3):
        part = pl.ds(third * width, width)
        piece = dot(w_ref[part, :], normed, 1, 1)
        if third == 0:
            piece = (piece + columns[:, QV_BIAS : QV_BIAS + 1]) * (SCALE * LOG2E)
        if third == 2:
            piece = piece + columns[:, QV_BIAS + 1 : QV_BIAS + 2]
        qkv_ref[0, part, :] = piece.astype(BF)

    lead = qkv_ref[0, pl.ds(0, width), :128].astype(F32).T[0:1, :]
    head_of = lax.broadcasted_iota(jnp.int32, (8, width), 1) // HEAD_DIM
    pick = head_of == lax.broadcasted_iota(jnp.int32, (8, width), 0)
    queries = jnp.where(pick, lead, 0.0).astype(BF)
    scores = dot(queries, qkv_ref[0, pl.ds(width, width), :], 1, 0)
    limit = 1 + VIEW_ROWS * views_ref[blk_ref[CORE] * pl.num_programs(0) + step]
    place = lax.broadcasted_iota(jnp.int32, (8, rows), 1)
    scores = jnp.where(place < limit, scores, MASKED)
    powers = jnp.exp2(scores - jnp.max(scores, -1, keepdims=True))
    chances = (powers / jnp.sum(powers, -1, keepdims=True)).astype(BF)
    mixed = dot(chances, qkv_ref[0, pl.ds(2 * width, width), :], 1, 1)
    mix_ref[pl.ds(step, 1), :] = jnp.sum(jnp.where(pick, mixed, 0.0), 0, keepdims=True)
    first_ref[pl.ds(step, 1), :] = values[0:1, :]

    @pl.when(step == pl.num_programs(0) - 1)
    def _():
        branch = dot(mix_ref[...].astype(BF), w_out_ref[...], 1, 0) + row_of(pack_ref, OUT_BIAS)
        middle = first_ref[...] + branch
        normed2 = norm_parts(middle)[0] * row_of(pack_ref, GAIN2) + row_of(pack_ref, SHIFT2)
        normed2 = normed2.astype(BF)
        output = middle + row_of(pack_ref, FC2_BIAS)
        for j in range(w1_ref.shape[1] // width):
            cols = slice(j * width, (j + 1) * width)
            pre = dot(normed2, w1_ref[:, cols], 1, 0) + row_of(pack_ref, FC1_BIAS + j)
            act = (pre * gelu_cdf(pre)).astype(BF)
            output = output + dot(act, w2_ref[cols, :], 1, 0)
        cls_ref[...] = output
        count = cot_ref.shape[0]
        cls = output[:count]
        cot = cot_ref[...].astype(F32)
        stat_ref[...] = jnp.zeros_like(stat_ref)
        for k, term in enumerate((cls, cls * cls, cot, cot * cls)):
            stat_ref[k : k + 1, :] = jnp.sum(term, 0, keepdims=True)


def masked_tail(scores, main, limit):
    place = main + lax.broadcasted_iota(jnp.int32, scores.shape, 0)
    return jnp.where(place < limit, scores, MASKED)


def attention_kernel(
    core_ref, views_ref, qkv_ref, sum_ref, top_ref, plain_ref, att_ref, pow_ref
):
    sample = pl.program_id(0)
    rows = qkv_ref.shape[2]
    width = att_ref.shape[1]
    heads = width // HEAD_DIM
    views = views_ref[core_ref[CORE] * pl.num_programs(0) + sample]
    limit = 1 + VIEW_ROWS * views
    ones = jnp.ones((16, rows), BF)

    def store(h, mixed):
        total = mixed[HEAD_DIM : HEAD_DIM + 1]
        sum_ref[0, pl.ds(h, 1), :] = total
        att_ref[0, head_rows(h, 0), :] = (mixed[:HEAD_DIM] * (1.0 / total)).astype(BF)

    sum_ref[0, heads:8, :] = jnp.ones((8 - heads, rows), F32)
    for count, keys in key_counts(rows):

        @pl.when(views == count)
        def _(keys=keys):
            main = keys - 16

            def pair(p, carry):
                both = range(2)
                parts = [head_parts(qkv_ref, 2 * p + k, width, keys) for k in both]
                scores = [dot(key, query, 0, 0) for query, key, _ in parts]
                for k in both:
                    pow_ref[k, :main, :] = jnp.exp2(scores[k][:main]).astype(BF)
                    tail = masked_tail(scores[k][main:], main, limit)
                    pow_ref[k, main:keys, :] = jnp.exp2(tail).astype(BF)
                lefts = [jnp.concatenate((value, ones[:, :keys]), 0) for _, _, value in parts]
                mixed = [dot(lefts[k], pow_ref[k, :keys, :], 1, 0) for k in both]
                for k in both:
                    store(2 * p + k, mixed[k])
                return carry

            lax.fori_loop(0, heads // 2, pair, 0)

    totals = sum_ref[0]
    plain = (jnp.min(totals) > SUM_LOW) & (jnp.max(totals) < SUM_HIGH)
    plain_ref[sample] = plain.astype(jnp.int32)

    @pl.when(jnp.logical_not(plain))
    def _():
        @each_head(heads)
        def _(h, slot):
            query, key, value = head_parts(qkv_ref, h, width, rows)
            scores = masked_tail(dot(key, query, 0, 0), 0, limit)
            top = jnp.max(scores, 0, keepdims=True)
            top_ref[0, pl.ds(h, 1), :] = top
            pow_ref[slot] = jnp.exp2(scores - top).astype(BF)
            left = jnp.concatenate((value, ones), 0)
            store(h, dot(left, pow_ref[slot], 1, 0))


def each_head(heads):
    def run(body):
        def pair(p, carry):
            for slot in range(2):
                body(2 * p + slot, slot)
            return carry

        lax.fori_loop(0, heads // 2, pair, 0)

    return run


def head_rows(h, base):
    return pl.ds(pl.multiple_of(base + h * HEAD_DIM, HEAD_DIM), HEAD_DIM)


def head_parts(qkv_ref, h, width, keys):
    return (
        qkv_ref[0, head_rows(h, 0), :],
        qkv_ref[0, head_rows(h, width), :keys],
        qkv_ref[0, head_rows(h, 2 * width), :keys],
    )


def layer_kernel(
    core_ref, x_own_ref, x_far_ref, own_ref, far_ref, att_ref, sum_ref, cls_ref, cot_ref, *refs,
    samples, parts, peers
):
    stat_refs = refs[:peers]
    w_out_ref, w1_ref, w2_ref, pack_ref = refs[peers : peers + 4]
    (
        act_ref, middle_ref, gmid_ref, dmix_ref, inner_ref, out_grad_ref, norm_ref, bias_ref,
        kept_ref, sent_ref,
    ) = refs[peers + 4 : peers + 14]
    full_ref, g_ref, dpre_ref, dcls_ref, acc2_ref, acc1_ref, flat_ref = refs[peers + 14 :]
    step = pl.program_id(0)
    width = own_ref.shape[2]
    hidden = w2_ref.shape[0]
    blocks = hidden // width

    @pl.when(step == 0)
    def _():
        acc2_ref[...] = jnp.zeros_like(acc2_ref)
        acc1_ref[...] = jnp.zeros_like(acc1_ref)
        bias_ref[...] = jnp.zeros_like(bias_ref)
        out_grad_ref[...] = jnp.zeros_like(out_grad_ref)
        stats = stat_refs[0][...]
        for other in stat_refs[1:]:
            stats = stats + other[...]
        local = cot_ref.shape[0]
        cls = cls_ref[...][:local]
        cot = cot_ref[...].astype(F32)
        mean = stats[0:1] / samples
        scale = lax.rsqrt(stats[1:2] / samples - mean * mean + CLS_EPS)
        hat = (cls - mean) * scale
        norm_ref[...] = hat.astype(BF)
        cross = scale * (stats[3:4] - mean * stats[2:3])
        dcls_ref[...] = jnp.zeros_like(dcls_ref)
        dcls_ref[:local, :] = scale * (cot - stats[2:3] / samples - hat * (cross / samples))

    place_halves(full_ref, core_ref[CORE], x_own_ref[0], x_far_ref[0])
    place_halves(g_ref, core_ref[CORE], own_ref[0].astype(F32), far_ref[0].astype(F32))
    g_ref[0:1, :] = g_ref[0:1, :] + dcls_ref[pl.ds(step, 1), :]
    g_mlp = g_ref[...].astype(BF)
    bias_ref[blocks : blocks + 1, :] += jnp.sum(g_mlp.astype(F32), 0, keepdims=True)

    branch = dot(att_ref[0], w_out_ref[...], 0, 0) + row_of(pack_ref, OUT_BIAS)
    middle = full_ref[...].astype(F32) + branch
    middle_ref[0] = middle
    hat, rstd = norm_parts(middle)
    normed = (hat * row_of(pack_ref, GAIN2) + row_of(pack_ref, SHIFT2)).astype(BF)
    hat_low = hat.astype(BF)
    for j in range(blocks):
        cols = slice(j * width, (j + 1) * width)
        pre = dot(normed, w1_ref[:, cols], 1, 0) + row_of(pack_ref, FC1_BIAS + j)
        d_act = dot(g_mlp, w2_ref[cols, :], 1, 1)
        cdf = gelu_cdf(pre)
        bell = jnp.exp2(pre * pre * (-0.5 * LOG2E) - 0.5 * math.log2(2.0 * math.pi))
        act_ref[0, :, cols] = (pre * cdf).astype(BF)
        d_pre = d_act * (cdf + pre * bell)
        bias_ref[j : j + 1, :] += jnp.sum(d_pre, 0, keepdims=True)
        dpre_ref[:, cols] = d_pre.astype(BF)
    acc1_ref[...] += dot(hat_low, dpre_ref[...], 0, 0)
    acc2_ref[...] += dot(act_ref[0], g_mlp, 0, 0)
    d_norm = dot(dpre_ref[...], w1_ref[...], 1, 1)
    u = d_norm * row_of(pack_ref, GAIN2)
    g_mid = g_ref[...] + rstd * (
        u - jnp.mean(u, -1, keepdims=True) - hat * jnp.mean(u * hat, -1, keepdims=True)
    )
    g_attn = g_mid.astype(BF)
    gmid_ref[0] = g_attn
    out_grad_ref[...] += dot(att_ref[0], g_attn, 1, 0)
    bias_ref[blocks + 1 : blocks + 2, :] += jnp.sum(g_attn.astype(F32), 0, keepdims=True)
    d_mix = dot(w_out_ref[...], g_attn, 1, 1)
    for h in range(width // HEAD_DIM):
        part = slice(h * HEAD_DIM, (h + 1) * HEAD_DIM)
        piece = d_mix[part] * (1.0 / sum_ref[0, h : h + 1, :])
        dmix_ref[0, part, :] = piece.astype(BF)
        inner_ref[0, h : h + 1, :] = jnp.sum(piece * att_ref[0, part, :].astype(F32), 0, keepdims=True)

    @pl.when(step == pl.num_programs(0) - 1)
    def _():
        flat_ref[:hidden, :] = acc2_ref[...].astype(BF)
        for j in range(blocks):
            rows = slice(hidden + j * width, hidden + (j + 1) * width)
            flat_ref[rows, :] = acc1_ref[:, j * width : (j + 1) * width].astype(BF)
        clear_rest(flat_ref, 2 * hidden)
        write_halves(core_ref[CORE], flat_ref, parts, kept_ref, sent_ref)


def output_kernel(core_ref, act_ref, middle_ref, w2_ref, pack_ref, own_ref, far_ref, full_ref):
    output = middle_ref[0] + dot(act_ref[0], w2_ref[...], 1, 0) + row_of(pack_ref, FC2_BIAS)
    full_ref[...] = output.astype(BF)
    split_halves(full_ref, core_ref[CORE], own_ref, far_ref)


def attention_back_kernel(
    core_ref, views_ref, plain_ref, order_ref, qkv_ref, top_ref, dmix_ref, inner_ref, hat_ref,
    dqkv_ref, grad_ref, sums_ref, pow_ref, *, turn, samples
):
    pair = pl.program_id(0)
    sample = order_ref[turn]
    rows, width = hat_ref.shape[1:]
    views = views_ref[core_ref[CORE] * samples + sample]
    limit = 1 + VIEW_ROWS * views
    plain = plain_ref[sample] == 1
    both = range(2)
    lanes = [slice(k * HEAD_DIM, (k + 1) * HEAD_DIM) for k in both]

    def back(keys, powers_of):
        query = [qkv_ref[0, 0, part, :] for part in lanes]
        key = [qkv_ref[0, 1, part, :keys] for part in lanes]
        value = [qkv_ref[0, 2, part, :keys] for part in lanes]
        d_mix = [dmix_ref[0, part, :] for part in lanes]
        scores = [dot(key[k], query[k], 0, 0) for k in both]
        for k in both:
            powers_of(k, scores[k])
        d_weights = [dot(value[k], d_mix[k], 0, 0) for k in both]
        d_scores = []
        for k in both:
            inner = inner_ref[0, pl.ds(2 * pair + k, 1), :]
            powers = pow_ref[k, :keys, :].astype(F32)
            d_scores.append((powers * (d_weights[k] - inner)).astype(BF))
        for k in both:
            d_value = dot(d_mix[k], pow_ref[k, :keys, :], 1, 1)
            dqkv_ref[0, 2, lanes[k], :keys] = d_value.astype(BF)
        for k in both:
            d_query = dot(key[k], d_scores[k], 1, 0) * SCALE
            dqkv_ref[0, 0, lanes[k], :] = d_query.astype(BF)
            d_key = dot(query[k], d_scores[k], 1, 1) * LN2
            dqkv_ref[0, 1, lanes[k], :keys] = d_key.astype(BF)
        if keys < rows:
            blank = jnp.zeros((2 * HEAD_DIM, rows - keys), BF)
            dqkv_ref[0, 1, :, keys:] = blank
            dqkv_ref[0, 2, :, keys:] = blank

    for count, keys in key_counts(rows):

        @pl.when((views == count) & plain)
        def _(keys=keys):
            main = keys - 16

            def powers_of(k, scores):
                pow_ref[k, :main, :] = jnp.exp2(scores[:main]).astype(BF)
                tail = masked_tail(scores[main:], main, limit)
                pow_ref[k, main:keys, :] = jnp.exp2(tail).astype(BF)

            back(keys, powers_of)

    @pl.when(jnp.logical_not(plain))
    def _():
        def powers_of(k, scores):
            top = top_ref[0, pl.ds(2 * pair + k, 1), :]
            pow_ref[k] = jnp.exp2(masked_tail(scores, 0, limit) - top).astype(BF)

        back(rows, powers_of)

    right = jnp.concatenate((hat_ref[0], jnp.ones((rows, 128), BF)), 1)
    result = dot(dqkv_ref[0].reshape(3 * 2 * HEAD_DIM, rows), right, 1, 0)
    grad_ref[...] = result[:, :width].astype(BF).reshape(grad_ref.shape)
    sums_ref[0] = result[:, width:].T[:8]


def tokens_back_kernel(core_ref, order_ref, *refs, sets):
    dqkv_refs = refs[:sets]
    w_ref, pack_ref, x_own_ref, x_far_ref, gmid_ref, own_ref, far_ref, out_ref, d_ref, sems = refs[sets:]
    step = pl.program_id(0)

    def fetch(k):
        return pltpu.make_async_copy(dqkv_refs[k].at[0], d_ref.at[k], sems.at[k])

    @pl.when(step == 0)
    def _():
        for k in range(sets):
            fetch(k).start()

    for k in range(sets):

        @pl.when(step == k)
        def _(k=k):
            fetch(k).wait()

    d_norm = dot(d_ref[step], w_ref[...], 0, 0)
    place_halves(out_ref, core_ref[CORE], x_own_ref[0], x_far_ref[0])
    hat, rstd = norm_parts(out_ref[...].astype(F32))
    w = d_norm * row_of(pack_ref, GAIN1)
    back = rstd * (w - jnp.mean(w, -1, keepdims=True) - hat * jnp.mean(w * hat, -1, keepdims=True))
    out_ref[...] = (gmid_ref[0].astype(F32) + back).astype(BF)
    split_halves(out_ref, core_ref[CORE], own_ref, far_ref)


def clear_rest(ref, used):
    if ref.shape[0] > used:
        ref[used:, :] = jnp.zeros((ref.shape[0] - used, ref.shape[1]), ref.dtype)


def write_halves(core, flat_ref, parts, kept_ref, sent_ref):
    start = at = 0
    for size in parts:
        half = size // 2
        mine = pl.multiple_of(start + core * half, 16)
        other = pl.multiple_of(start + (1 - core) * half, 16)
        kept_ref[at : at + half, :] = flat_ref[pl.ds(mine, half), :]
        sent_ref[at : at + half, :] = flat_ref[pl.ds(other, half), :]
        start += size
        at += half


def pack_kernel(core_ref, *refs, sets, parts):
    grad_refs = refs[:sets]
    sums_refs = refs[sets : 2 * sets]
    out_grad_ref, bias_ref, kept_ref, sent_ref, flat_ref = refs[2 * sets :]
    width = out_grad_ref.shape[0]
    used = grad_refs[0].shape[0]
    total, sums = grad_refs[0][...].astype(F32), sums_refs[0][...]
    for grad_ref, sums_ref in zip(grad_refs[1:], sums_refs[1:]):
        total = total + grad_ref[...].astype(F32)
        sums = sums + sums_ref[...]
    flat_ref[:used, :] = total.astype(BF)
    flat_ref[used : used + width, :] = out_grad_ref[...].astype(BF)
    clear_rest(flat_ref, used + width)
    write_halves(core_ref[CORE], flat_ref, parts, kept_ref, sent_ref)
    rows = lax.broadcasted_iota(jnp.int32, (8, width), 0)
    extra = jnp.zeros((8, width), F32)
    for t in range(used // width):
        row = jnp.concatenate([sums[p, 0:1, t * 128 : (t + 1) * 128] for p in range(width // 128)], 1)
        extra = jnp.where(rows == t, row, extra)
    vectors = jnp.concatenate((bias_ref[0:8, :], extra), 0).astype(BF)
    at = sum(parts) // 2
    kept_ref[at : at + EXTRA, :] = vectors
    sent_ref[at : at + EXTRA, :] = vectors


def insert_rows(info, base, came):
    def body(info_ref, came_ref, base_ref, out_ref, mark_ref):
        out_ref[...] = came_ref[...]

    return pl.pallas_call(
        body,
        grid_spec=pltpu.PrefetchScalarGridSpec(
            num_scalar_prefetch=1,
            grid=(1,),
            in_specs=[
                pl.BlockSpec(came.shape, lambda *_: (0, 0, 0)), pl.BlockSpec(memory_space=pl.ANY),
            ],
            out_specs=[
                pl.BlockSpec(came.shape, lambda s, b: (1 - b[CORE], 0, 0)),
                pl.BlockSpec(memory_space=pl.ANY),
            ],
        ),
        out_shape=[jax.ShapeDtypeStruct(base.shape, base.dtype), jax.ShapeDtypeStruct((1,), jnp.int32)],
        input_output_aliases={2: 0},
        compiler_params=params(("arbitrary",)),
        name="insert",
    )(info, came, base)


def swap_cores(value):
    return lax.ppermute(value, "blk", [(0, 1), (1, 0)])


def stages(count, first=4):
    out = []
    stride = 1
    while stride < count:
        left = count // stride
        radix = first if not out and left % first == 0 else 4 if left % 4 == 0 else 2
        out.append((stride, radix))
        stride *= radix
    return out


def shifted(value, stage, steps, axis="samp"):
    stride, radix = stage
    count = lax.axis_size(axis)
    pairs = []
    for source in range(count):
        digit = (source // stride) % radix
        pairs.append((source, source + ((digit + steps) % radix - digit) * stride))
    return lax.ppermute(value, axis, pairs)


MARK = jax.ShapeDtypeStruct((1,), jnp.int32)


def small_call(kernel, args, outs, scratch=(), ties=(), name=None):
    n, t, o = len(args), len(ties), len(outs)

    def body(*refs):
        kernel(*refs[:n], *refs[n + t : n + t + o], *refs[n + t + o + 1 :])

    vmem = pl.BlockSpec(memory_space=pltpu.VMEM)
    smem = pl.BlockSpec(memory_space=pltpu.SMEM)
    size = lambda a: math.prod(a.shape) * jnp.dtype(a.dtype).itemsize
    total = sum(size(a) for a in (*args[1:], *outs)) + sum(
        math.prod(a.shape) * jnp.dtype(a.dtype).itemsize for a in scratch
    )
    return pl.pallas_call(
        body,
        in_specs=[smem, *[vmem] * (n - 1), *[smem] * t],
        out_specs=[vmem] * o + [pl.BlockSpec(memory_space=pl.ANY)],
        out_shape=[*outs, MARK],
        scratch_shapes=list(scratch),
        compiler_params=pltpu.CompilerParams(vmem_limit_bytes=2 * total + 4 * 2**20),
        name=name,
    )(*args, *ties)


def hand_on(values, tie):
    count = len(values)

    def body(*refs):
        pass

    anywhere = [pl.BlockSpec(memory_space=pl.ANY)] * count
    return pl.pallas_call(
        body,
        in_specs=[pl.BlockSpec(memory_space=pltpu.SMEM), *anywhere],
        out_specs=anywhere,
        out_shape=[jax.ShapeDtypeStruct(value.shape, value.dtype) for value in values],
        input_output_aliases={1 + k: k for k in range(count)},
        compiler_params=pltpu.CompilerParams(vmem_limit_bytes=VMEM_BYTES),
        name="hand_on",
    )(tie, *values)


def spread_kernel(info_ref, *refs, count, radix, slot, extra, rows, rider, unload):
    inputs = count + (1 if rider else 0) + (1 if unload else 0)
    outputs = radix + (1 if extra and radix == 1 else 0)
    outs, total_ref = refs[inputs : inputs + outputs], refs[-1]
    if unload:
        collect_kernel(info_ref, refs[inputs - 1], *refs[1:count], refs[inputs + outputs])
    total = refs[0][:rows, :].astype(F32)
    for ref in refs[1:count]:
        total = total + ref[:rows, :].astype(F32)
    rows = rows - extra
    size = rows // radix
    total_ref[...] = total.astype(BF)
    if radix == 1:
        outs[0][...] = total_ref[:rows, :]
        if extra:
            outs[1][...] = total[rows:]
        return
    for k in range(radix):
        start = lax.rem(info_ref[slot] + k, radix) * size
        outs[k][:size, :] = total_ref[pl.ds(pl.multiple_of(start, 16), size), :]
        if extra:
            outs[k][size : size + extra, :] = total_ref[rows:, :]
        if rider and k > 0:
            outs[k][size + extra :, :] = refs[count][...]


def collect_kernel(info_ref, own_ref, *refs):
    out_ref = refs[-1]
    size = own_ref.shape[0]
    out_ref[:size, :] = own_ref[...]
    for k, ref in enumerate(refs[:-1]):
        out_ref[(k + 1) * size : (k + 2) * size, :] = ref[ref.shape[0] - size :, :]


class Layout:
    def __init__(self, count, sizes):
        self.base = stages(count)
        self.count = count
        table = np.zeros((2 * count, 1 + len(self.base)), np.int32)
        for device in range(2 * count):
            table[device, 0] = device % 2
            for i in range(len(self.base)):
                table[device, 1 + i] = self.digit(device, i)
        tables = [table]
        self.place = []
        for rows in sizes:
            self.place.append(sum(t.shape[1] for t in tables))
            tables.append(np.stack([self.places(device, rows) for device in range(2 * count)]))
        self.table = np.concatenate(tables, 1).astype(np.int32)

    def digit(self, device, index):
        stride, radix = self.base[index]
        return (device // 2 // stride) % radix

    def places(self, device, rows):
        core = device % 2
        unit = rows // 2
        offsets = np.array([core * unit, (1 - core) * unit])
        for index, (_, radix) in enumerate(self.base):
            unit //= radix
            digit = (self.digit(device, index) - np.arange(radix)) % radix
            offsets = (offsets[:, None] + (digit * unit)[None, :]).reshape(-1)
        return offsets


class Chain:
    def __init__(self, layout, info, extra=0):
        self.layout = layout
        self.info = info
        self.extra = extra
        self.rounds = len(layout.base)

    def start(self, kept, sent):
        self.pending = [kept, swap_cores(sent)]

    def scatter(self, level, ties=(), rider=None, unload=None):
        last = level == self.rounds
        radix = 1 if last else self.layout.base[level][1]
        rows, width = self.pending[0].shape
        size = (rows - self.extra) // radix
        more = () if rider is None else (rider.value,)
        kept = () if unload is None else (unload.value,)
        if last:
            outs = [jax.ShapeDtypeStruct((size, width), BF)]
            if self.extra:
                outs.append(jax.ShapeDtypeStruct((self.extra, width), F32))
        else:
            piece = size + self.extra
            sent = piece + sum(value.shape[0] for value in more)
            outs = [jax.ShapeDtypeStruct((sent if k else piece, width), BF) for k in range(radix)]
        if kept:
            outs.append(jax.ShapeDtypeStruct((len(self.pending) * kept[0].shape[0], width), BF))
        pieces = small_call(
            functools.partial(
                spread_kernel, count=len(self.pending), radix=radix, slot=1 + level, extra=self.extra,
                rows=rows, rider=bool(more), unload=bool(kept),
            ),
            (self.info, *self.pending, *more, *kept), outs, [pltpu.VMEM((rows, width), BF)], ties, "spread",
        )
        if kept:
            unload.value = pieces[-2]
        if last:
            self.value = pieces[0]
            self.vectors = pieces[1] if self.extra else None
        else:
            stage = self.layout.base[level]
            self.pending = [pieces[0]] + [shifted(pieces[k], stage, k) for k in range(1, radix)]
            if more:
                rider.pending = [rider.value, *self.pending[1:]]
        return pieces[-1]

    def gather(self, level):
        stage = self.layout.base[level]
        self.pending = [self.value] + [shifted(self.value, stage, k) for k in range(1, stage[1])]

    def collect(self, ties=()):
        size, width = self.pending[0].shape
        outs = [jax.ShapeDtypeStruct((len(self.pending) * size, width), BF)]
        self.value, mark = small_call(
            collect_kernel, (self.info, *self.pending), outs, (), ties, "collect"
        )
        return mark


def restore(place_ref, flat_ref, ref, unit, at):
    def body(i, carry):
        start = pl.multiple_of(place_ref[at + i], 16)
        source = pl.multiple_of(i * unit, 16)
        chunk = ref[pl.ds(source, unit), :]
        flat_ref[pl.ds(start, unit), :] = chunk
        return carry

    lax.fori_loop(0, ref.shape[0] // unit, body, 0)


def finish_mlp_kernel(
    info_ref, own_ref, far_ref, vectors_ref, pack_ref, w1_ref,
    fc2_ref, fc1_ref, gain_ref, shift_ref, fc1_bias_ref, fc2_bias_ref, flat_ref, *, unit, at
):
    restore(info_ref, flat_ref, own_ref, unit, at)
    restore(info_ref, flat_ref, far_ref, unit, at + own_ref.shape[0] // unit)
    hidden, width = fc2_ref.shape
    fc2_ref[...] = flat_ref[:hidden, :].astype(F32)
    columns = pack_ref[0:8, :].T
    gain = jnp.zeros((width, 1), F32)
    shift = jnp.zeros((width, 1), F32)
    for j in range(hidden // width):
        cols = slice(j * width, (j + 1) * width)
        hats = flat_ref[hidden + j * width : hidden + (j + 1) * width, :].astype(F32)
        sums = vectors_ref[j : j + 1, :]
        fc1_ref[:, cols] = hats * columns[:, GAIN2 : GAIN2 + 1] + columns[:, SHIFT2 : SHIFT2 + 1] * sums
        w = w1_ref[:, cols].astype(F32)
        gain = gain + jnp.sum(w * hats, -1, keepdims=True)
        shift = shift + jnp.sum(w * sums, -1, keepdims=True)
    lane = lax.broadcasted_iota(jnp.int32, (width, 128), 1)
    both = jnp.where(lane == 0, gain, jnp.where(lane == 1, shift, 0.0)).T[0:8]
    gain_ref[...] = both[0]
    shift_ref[...] = both[1]
    blocks = hidden // width
    for j in range(blocks):
        fc1_bias_ref[j * width : (j + 1) * width] = vectors_ref[j, :]
    fc2_bias_ref[...] = vectors_ref[blocks, :]


def finish_kernel(
    info_ref, own_ref, far_ref, vectors_ref, pack_ref, w_ref, qkv_ref, out_ref, gain_ref, shift_ref, qv_ref, out_bias_ref, flat_ref,
    *, unit, at, blocks
):
    restore(info_ref, flat_ref, own_ref, unit, at)
    restore(info_ref, flat_ref, far_ref, unit, at + own_ref.shape[0] // unit)
    width = out_ref.shape[0]
    columns = qkv_ref.shape[1]
    out_ref[...] = flat_ref[columns : columns + width, :].astype(F32)
    gain = jnp.zeros((1, width), F32)
    shift = jnp.zeros((1, width), F32)
    turned = vectors_ref[8:16, :].T
    for t in range(columns // width):
        part = slice(t * width, (t + 1) * width)
        hats = flat_ref[part, :].astype(F32)
        sums = turned[:, t : t + 1]
        result = hats * row_of(pack_ref, GAIN1) + sums * row_of(pack_ref, SHIFT1)
        qkv_ref[:, part] = result.T
        w = w_ref[part, :].astype(F32)
        gain = gain + jnp.sum(w * hats, 0, keepdims=True)
        shift = shift + jnp.sum(w * sums, 0, keepdims=True)
    gain_ref[...] = gain[0]
    shift_ref[...] = shift[0]
    qv_ref[:width] = vectors_ref[8, :]
    qv_ref[width:] = vectors_ref[10, :]
    out_bias_ref[...] = vectors_ref[blocks + 1, :]


def pad_rows(count, unit):
    return -(-count // unit) * unit


def per_device(
    tokens, view_count, norm1_gain, norm1_bias, w_qkv, qv_bias, w_out, out_bias,
    norm2_gain, norm2_bias, w_fc1, fc1_bias, w_fc2, fc2_bias, cot_tokens, cot_cls,
):
    core = lax.axis_index("blk")
    cores = lax.axis_size("blk")
    count = lax.axis_size("samp")
    samples, half, width = tokens.shape
    local = samples // cores
    rows = half * cores
    hidden = w_fc1.shape[1]
    blocks = hidden // width
    heads = width // HEAD_DIM
    pairs = heads // 2
    sds = jax.ShapeDtypeStruct

    unit = 32 * count
    parts1 = [pad_rows(2 * hidden, unit)]
    parts2 = [pad_rows(4 * width, unit)]
    layout = Layout(count, (parts1[0], parts2[0]))
    device = lax.axis_index("samp") * cores + core
    info = lax.dynamic_index_in_dim(jnp.asarray(layout.table), device, 0, keepdims=False)

    theirs = (1 - core) * local
    far_tokens = swap_cores(lax.dynamic_slice_in_dim(tokens, theirs, local, 0))
    far_cot = swap_cores(lax.dynamic_slice_in_dim(cot_tokens, theirs, local, 0))

    pack = jnp.concatenate(
        (
            norm1_gain, norm1_bias, norm2_gain, norm2_bias, out_bias, fc2_bias, qv_bias, fc1_bias,
            jnp.zeros(((8 - blocks) * width,), BF),
        )
    ).astype(F32).reshape(16, width)

    vmem = pl.BlockSpec(memory_space=pltpu.VMEM)
    half_spec = lambda f: pl.BlockSpec((1, half, width), f)
    own_map = lambda s, b, *_: (b[CORE] * local + s, 0, 0)
    by_sample = lambda s, *_: (s, 0, 0)
    rows_spec = pl.BlockSpec((1, rows, width), by_sample)
    turned_spec = pl.BlockSpec((1, width, rows), by_sample)
    rstd_spec = pl.BlockSpec((1, rows, 1), by_sample)
    hidden_spec = pl.BlockSpec((1, rows, hidden), by_sample)
    eight_spec = pl.BlockSpec((1, 8, rows), by_sample)

    def big_call(kernel, prefetch, args, in_specs, outs, out_specs, scratch=(), ties=(), grid=(local,), name=None):
        n, t, o = len(prefetch) + len(args), len(ties), len(outs)
        smem = pl.BlockSpec(memory_space=pltpu.SMEM)

        def body(*refs):
            kernel(*refs[:n], *refs[n + t : n + t + o], *refs[n + t + o + 1 :])

        return pl.pallas_call(
            body,
            grid_spec=pltpu.PrefetchScalarGridSpec(
                num_scalar_prefetch=len(prefetch),
                grid=grid,
                in_specs=[*in_specs, *[smem] * t],
                out_specs=[*out_specs, pl.BlockSpec(memory_space=pl.ANY)],
                scratch_shapes=list(scratch),
            ),
            out_shape=[*outs, MARK],
            compiler_params=params(("arbitrary",) * len(grid)),
            name=name,
        )(*prefetch, *args, *ties)

    hat1, qkv, cls_rows, stats, w_turned, order, _ = big_call(
        project_kernel,
        (info, view_count),
        (tokens, far_tokens, w_qkv, pack, w_out, w_fc1, w_fc2, cot_cls),
        [half_spec(own_map), half_spec(by_sample), *[vmem] * 6],
        [
            sds((local, rows, width), BF),
            sds((local, 3 * width, rows), BF),
            sds((8, width), F32),
            sds((8, width), F32),
            sds((3 * width, width), BF),
            sds((local,), jnp.int32),
        ],
        [
            rows_spec, pl.BlockSpec((1, 3 * width, rows), by_sample), vmem, vmem, vmem,
            pl.BlockSpec(memory_space=pltpu.SMEM),
        ],
        [pltpu.VMEM((8, width), F32), pltpu.VMEM((8, width), F32), pltpu.VMEM((rows, width), BF)],
        name="project",
    )

    def add_kernel(info_ref, *refs):
        total = refs[0][...]
        for ref in refs[1:-1]:
            total = total + ref[...]
        refs[-1][...] = total

    *later, first = stages(count)

    def add_all(values, ties=()):
        return small_call(add_kernel, [info, *values], [sds((8, width), F32)], (), ties, "add")

    stats, tie = add_all([stats, swap_cores(stats)])
    stat_parts = [stats] + [shifted(stats, first, k) for k in range(1, first[1])]

    qkv_spec = lambda f: pl.BlockSpec((1, 3 * width, rows), f)
    totals, tops, plain, mixed, tie = big_call(
        attention_kernel,
        (info, view_count),
        (qkv,),
        [qkv_spec(by_sample)],
        [
            sds((local, 8, rows), F32),
            sds((local, 8, rows), F32),
            sds((local,), jnp.int32),
            sds((local, width, rows), BF),
        ],
        [eight_spec, eight_spec, pl.BlockSpec(memory_space=pltpu.SMEM), turned_spec],
        [pltpu.VMEM((2, rows, rows), BF)],
        (tie,),
        name="attention",
    )

    for stage in later:
        stats, tie = add_all(stat_parts, (tie,))
        stat_parts = [stats] + [shifted(stats, stage, k) for k in range(1, stage[1])]

    act, middle, g_mid, d_mix, inner, out_grad, cls_norm, biases, kept1, sent1, _ = big_call(
        functools.partial(
            layer_kernel, samples=local * cores * count, parts=parts1, peers=len(stat_parts)
        ),
        (info,),
        (
            tokens, far_tokens, cot_tokens, far_cot, mixed, totals, cls_rows, cot_cls, *stat_parts,
            w_out, w_fc1, w_fc2, pack,
        ),
        [
            half_spec(own_map), half_spec(by_sample), half_spec(own_map), half_spec(by_sample),
            turned_spec, eight_spec, vmem, vmem, *[vmem] * len(stat_parts), vmem, vmem, vmem, vmem,
        ],
        [
            sds((local, rows, hidden), BF),
            sds((local, rows, width), F32),
            sds((local, rows, width), BF),
            sds((local, width, rows), BF),
            sds((local, 8, rows), F32),
            sds((width, width), F32),
            sds((local, width), BF),
            sds((8, width), F32),
            sds((sum(parts1) // 2, width), BF),
            sds((sum(parts1) // 2, width), BF),
        ],
        [
            hidden_spec, rows_spec, rows_spec, turned_spec, eight_spec, vmem, vmem, vmem, vmem, vmem,
        ],
        [
            pltpu.VMEM((rows, width), BF),
            pltpu.VMEM((rows, width), F32),
            pltpu.VMEM((rows, hidden), BF),
            pltpu.VMEM((8, width), F32),
            pltpu.VMEM((hidden, width), F32),
            pltpu.VMEM((width, hidden), F32),
            pltpu.VMEM((sum(parts1), width), BF),
        ],
        name="layer",
    )
    chain1 = Chain(layout, info)
    chain1.start(kept1, sent1)

    def attention_back(turn, ties):
        place = lambda p, c, v, q, o: (o[turn], 0, 0)
        return big_call(
            functools.partial(attention_back_kernel, turn=turn, samples=local),
            (info, view_count, plain, order),
            (qkv.reshape(local, 3, width, rows), tops, d_mix, inner, hat1),
            [
                pl.BlockSpec((1, 3, 128, rows), lambda p, c, v, q, o: (o[turn], 0, p, 0)),
                pl.BlockSpec((1, 8, rows), place),
                pl.BlockSpec((1, 128, rows), lambda p, c, v, q, o: (o[turn], p, 0)),
                pl.BlockSpec((1, 8, rows), place),
                pl.BlockSpec((1, rows, width), place),
            ],
            [
                sds((1, 3, width, rows), BF),
                sds((3, width, width), BF),
                sds((pairs, 8, 384), F32),
            ],
            [
                pl.BlockSpec((1, 3, 128, rows), lambda p, *_: (0, 0, p, 0)),
                pl.BlockSpec((3, 128, width), lambda p, *_: (0, p, 0)),
                pl.BlockSpec((1, 8, 384), lambda p, *_: (p, 0, 0)),
            ],
            [pltpu.VMEM((2, rows, rows), BF)],
            ties,
            grid=(pairs,),
            name="attention_back",
        )

    def scatter_step(level):
        def run(ties):
            piece = chain1.scatter(level, ties)
            if level == chain1.rounds:
                chain1.gather(level - 1)
            return piece

        return run

    def collect_step(level):
        def run(ties):
            mark = chain1.collect(ties)
            if level > 1:
                chain1.gather(level - 1)
            return mark

        return run

    steps = [scatter_step(level) for level in range(1, chain1.rounds + 1)]
    steps += [collect_step(level) for level in reversed(range(1, chain1.rounds))]
    ties = (chain1.scatter(0),)
    d_parts, grads, sums = [], [], []
    for sample in range(local):
        d_part, grad, total, tie = attention_back(sample, ties)
        d_parts.append(d_part.reshape(1, 3 * width, rows))
        grads.append(grad.reshape(3 * width, width))
        sums.append(total)
        ties = (steps.pop(0)((tie,)),)

    while steps:
        ties = (steps.pop(0)(()),)
    chain2 = Chain(layout, info, EXTRA)
    kept2, sent2, _ = small_call(
        functools.partial(pack_kernel, sets=len(grads), parts=parts2),
        (info, *grads, *sums, out_grad, biases),
        [sds((sum(parts2) // 2 + EXTRA, width), BF)] * 2,
        [pltpu.VMEM((sum(parts2), width), BF)],
        ties,
        name="pack",
    )
    chain2.start(kept2, sent2)
    tie = chain2.scatter(0, (), chain1)

    tokens_out_own, out_far, out_tie = big_call(
        output_kernel,
        (info,),
        (act, middle, w_fc2, pack),
        [hidden_spec, rows_spec, vmem, vmem],
        [sds((samples, half, width), BF), sds((local, half, width), BF)],
        [half_spec(own_map), half_spec(by_sample)],
        [pltpu.VMEM((rows, width), BF)],
        (tie,),
        name="output",
    )
    own_turn = lambda s, c, o: (c[CORE] * local + o[s], 0, 0)
    turn = lambda s, c, o: (o[s], 0, 0)
    grad_own, grad_far, tie = big_call(
        functools.partial(tokens_back_kernel, sets=len(d_parts)),
        (info, order),
        (*d_parts, w_turned, pack, tokens, far_tokens, g_mid),
        [
            *[pl.BlockSpec(memory_space=pl.ANY)] * len(d_parts),
            vmem, vmem, half_spec(own_turn), half_spec(turn), pl.BlockSpec((1, rows, width), turn),
        ],
        [sds((samples, half, width), BF), sds((local, half, width), BF)],
        [half_spec(own_turn), half_spec(turn)],
        [
            pltpu.VMEM((rows, width), BF),
            pltpu.VMEM((len(d_parts), 3 * width, rows), BF),
            pltpu.SemaphoreType.DMA((len(d_parts),)),
        ],
        (tie,),
        name="tokens_back",
    )
    for level in range(1, chain2.rounds + 1):
        first = level == 1
        tie = chain2.scatter(level, (tie, out_tie) if first else (), None, chain1 if first else None)
        if first:
            grad_came, out_came = [swap_cores(value) for value in hand_on((grad_far, out_far), tie)]
            other1 = swap_cores(chain1.value)
    ties = ()
    for level in reversed(range(chain2.rounds)):
        chain2.gather(level)
        if level == chain2.rounds - 1:
            (
                grad_w_fc2, grad_w_fc1, grad_gain2, grad_shift2, grad_fc1_bias, grad_fc2_bias, tie,
            ) = small_call(
                functools.partial(
                    finish_mlp_kernel, unit=parts1[0] // (2 * count), at=layout.place[0]
                ),
                (info, chain1.value, other1, chain2.vectors, pack, w_fc1),
                [
                    sds((hidden, width), F32), sds((width, hidden), F32), sds((width,), F32),
                    sds((width,), F32), sds((hidden,), F32), sds((width,), F32),
                ],
                [pltpu.VMEM((parts1[0], width), BF)],
                name="finish_mlp",
            )
            ties = (tie,)
        if level == 0:
            grad_tokens, tie = insert_rows(info, grad_own, grad_came)
            tokens_out, out_tie = insert_rows(info, tokens_out_own, out_came)
            ties = (tie, out_tie)
        chain2.collect(ties)
    other = swap_cores(chain2.value)

    grad_w_qkv, grad_w_out, grad_gain1, grad_shift1, grad_qv_bias, grad_out_bias, _ = small_call(
        functools.partial(finish_kernel, unit=parts2[0] // (2 * count), at=layout.place[1], blocks=blocks),
        (info, chain2.value, other, chain2.vectors, pack, w_turned),
        [
            sds((width, 3 * width), F32), sds((width, width), F32), sds((width,), F32), sds((width,), F32),
            sds((2 * width,), F32), sds((width,), F32),
        ],
        [pltpu.VMEM((parts2[0], width), BF)],
        name="finish",
    )
    return (
        tokens_out, cls_norm, grad_tokens, grad_gain1, grad_shift1, grad_w_qkv, grad_qv_bias,
        grad_w_out, grad_out_bias, grad_gain2, grad_shift2, grad_w_fc1, grad_fc1_bias,
        grad_w_fc2, grad_fc2_bias,
    )


def solution(mesh):
    split = P("samp", "blk", None)
    classes = P(("samp", "blk"), None)
    return jax.shard_map(
        per_device,
        mesh=mesh,
        in_specs=(split, P("samp"), *([P()] * 12), split, classes),
        out_specs=(split, classes, split, *([P()] * 12)),
        check_vma=False,
    )
```

```python
import functools
import math

import jax
import jax.numpy as jnp
import numpy as np
from jax import lax
from jax.experimental import pallas as pl
from jax.experimental.pallas import tpu as pltpu
from jax.sharding import PartitionSpec as P

HEAD_DIM = 64
VIEW_ROWS = 196
NORM_EPS = 1e-06
CLS_EPS = 1e-05
MASKED = -1e30
LOG2E = math.log2(math.e)
LN2 = math.log(2.0)
SCALE = HEAD_DIM ** (-0.5)
SUM_LOW = 1e-15
SUM_HIGH = 1e15
BF = jnp.bfloat16
F32 = jnp.float32
VMEM_BYTES = 60 * 2**20
CORE = 0
EXTRA = 16


def dot(a, b, ca, cb):
    return lax.dot_general(a, b, (((ca,), (cb,)), ((), ())), preferred_element_type=F32)


def norm_parts(values):
    centre = jnp.mean(values, -1, keepdims=True)
    offset = values - centre
    rstd = lax.rsqrt(jnp.mean(offset * offset, -1, keepdims=True) + NORM_EPS)
    return offset * rstd, rstd


def gelu_cdf(values):
    return 0.5 + 0.5 * lax.erf(values * (0.5**0.5))


def params(semantics):
    return pltpu.CompilerParams(dimension_semantics=semantics, vmem_limit_bytes=VMEM_BYTES)


def whole(shape):
    return pl.BlockSpec(shape, lambda *_: (0,) * len(shape))


def key_counts(rows):
    views = (rows - 1) // VIEW_ROWS
    return [(v, min(rows, -(-(1 + VIEW_ROWS * v) // 16) * 16)) for v in range(1, views + 1)]


GAIN1, SHIFT1, GAIN2, SHIFT2, OUT_BIAS, FC2_BIAS, QV_BIAS, FC1_BIAS = 0, 1, 2, 3, 4, 5, 6, 8


def row_of(pack_ref, index):
    return pack_ref[index : index + 1, :]


def place_halves(target_ref, core, own, far):
    half = own.shape[0]
    target_ref[pl.ds(pl.multiple_of(core * half, 16), half), :] = own
    target_ref[pl.ds(pl.multiple_of((1 - core) * half, 16), half), :] = far


def split_halves(source_ref, core, own_ref, far_ref):
    half = own_ref.shape[1]
    own_ref[0] = source_ref[pl.ds(pl.multiple_of(core * half, 16), half), :]
    far_ref[0] = source_ref[pl.ds(pl.multiple_of((1 - core) * half, 16), half), :]


def rank_samples(views_ref, base, order_ref):
    count = order_ref.shape[0]
    views = [views_ref[base + i] for i in range(count)]
    for i in range(count):
        rank = jnp.int32(0)
        for j in range(count):
            if j != i:
                ahead = views[j] >= views[i] if j < i else views[j] > views[i]
                rank = rank + ahead.astype(jnp.int32)
        order_ref[rank] = jnp.int32(i)


def project_kernel(
    blk_ref, views_ref, own_ref, far_ref, w_in_ref, pack_ref, w_out_ref, w1_ref, w2_ref, cot_ref,
    hat_ref, qkv_ref, cls_ref, stat_ref, w_ref, order_ref, mix_ref, first_ref, full_ref,
):
    step = pl.program_id(0)

    @pl.when(step == 0)
    def _():
        w_ref[...] = w_in_ref[...].T
        rank_samples(views_ref, blk_ref[CORE] * order_ref.shape[0], order_ref)

    rows = hat_ref.shape[1]
    width = own_ref.shape[2]
    place_halves(full_ref, blk_ref[0], own_ref[0], far_ref[0])
    values = full_ref[...].astype(F32)
    hat, _ = norm_parts(values)
    hat_ref[0] = hat.astype(BF)
    normed = (hat * row_of(pack_ref, GAIN1) + row_of(pack_ref, SHIFT1)).astype(BF)
    columns = pack_ref[0:8, :].T
    for third in range(3):
        part = pl.ds(third * width, width)
        piece = dot(w_ref[part, :], normed, 1, 1)
        if third == 0:
            piece = (piece + columns[:, QV_BIAS : QV_BIAS + 1]) * (SCALE * LOG2E)
        if third == 2:
            piece = piece + columns[:, QV_BIAS + 1 : QV_BIAS + 2]
        qkv_ref[0, part, :] = piece.astype(BF)

    lead = qkv_ref[0, pl.ds(0, width), :128].astype(F32).T[0:1, :]
    head_of = lax.broadcasted_iota(jnp.int32, (8, width), 1) // HEAD_DIM
    pick = head_of == lax.broadcasted_iota(jnp.int32, (8, width), 0)
    queries = jnp.where(pick, lead, 0.0).astype(BF)
    scores = dot(queries, qkv_ref[0, pl.ds(width, width), :], 1, 0)
    limit = 1 + VIEW_ROWS * views_ref[blk_ref[CORE] * pl.num_programs(0) + step]
    place = lax.broadcasted_iota(jnp.int32, (8, rows), 1)
    scores = jnp.where(place < limit, scores, MASKED)
    powers = jnp.exp2(scores - jnp.max(scores, -1, keepdims=True))
    chances = (powers / jnp.sum(powers, -1, keepdims=True)).astype(BF)
    mixed = dot(chances, qkv_ref[0, pl.ds(2 * width, width), :], 1, 1)
    mix_ref[pl.ds(step, 1), :] = jnp.sum(jnp.where(pick, mixed, 0.0), 0, keepdims=True)
    first_ref[pl.ds(step, 1), :] = values[0:1, :]

    @pl.when(step == pl.num_programs(0) - 1)
    def _():
        branch = dot(mix_ref[...].astype(BF), w_out_ref[...], 1, 0) + row_of(pack_ref, OUT_BIAS)
        middle = first_ref[...] + branch
        normed2 = norm_parts(middle)[0] * row_of(pack_ref, GAIN2) + row_of(pack_ref, SHIFT2)
        normed2 = normed2.astype(BF)
        output = middle + row_of(pack_ref, FC2_BIAS)
        for j in range(w1_ref.shape[1] // width):
            cols = slice(j * width, (j + 1) * width)
            pre = dot(normed2, w1_ref[:, cols], 1, 0) + row_of(pack_ref, FC1_BIAS + j)
            act = (pre * gelu_cdf(pre)).astype(BF)
            output = output + dot(act, w2_ref[cols, :], 1, 0)
        cls_ref[...] = output
        count = cot_ref.shape[0]
        cls = output[:count]
        cot = cot_ref[...].astype(F32)
        stat_ref[...] = jnp.zeros_like(stat_ref)
        for k, term in enumerate((cls, cls * cls, cot, cot * cls)):
            stat_ref[k : k + 1, :] = jnp.sum(term, 0, keepdims=True)


def masked_tail(scores, main, limit):
    place = main + lax.broadcasted_iota(jnp.int32, scores.shape, 0)
    return jnp.where(place < limit, scores, MASKED)


def attention_kernel(
    core_ref, views_ref, qkv_ref, sum_ref, top_ref, plain_ref, att_ref, pow_ref
):
    sample = pl.program_id(0)
    rows = qkv_ref.shape[2]
    width = att_ref.shape[1]
    heads = width // HEAD_DIM
    views = views_ref[core_ref[CORE] * pl.num_programs(0) + sample]
    limit = 1 + VIEW_ROWS * views
    ones = jnp.ones((16, rows), BF)

    def store(h, mixed):
        total = mixed[HEAD_DIM : HEAD_DIM + 1]
        sum_ref[0, pl.ds(h, 1), :] = total
        att_ref[0, head_rows(h, 0), :] = (mixed[:HEAD_DIM] * (1.0 / total)).astype(BF)

    sum_ref[0, heads:8, :] = jnp.ones((8 - heads, rows), F32)
    for count, keys in key_counts(rows):

        @pl.when(views == count)
        def _(keys=keys):
            main = keys - 16

            def pair(p, carry):
                both = range(2)
                parts = [head_parts(qkv_ref, 2 * p + k, width, keys) for k in both]
                scores = [dot(key, query, 0, 0) for query, key, _ in parts]
                for k in both:
                    pow_ref[k, :main, :] = jnp.exp2(scores[k][:main]).astype(BF)
                    tail = masked_tail(scores[k][main:], main, limit)
                    pow_ref[k, main:keys, :] = jnp.exp2(tail).astype(BF)
                lefts = [jnp.concatenate((value, ones[:, :keys]), 0) for _, _, value in parts]
                mixed = [dot(lefts[k], pow_ref[k, :keys, :], 1, 0) for k in both]
                for k in both:
                    store(2 * p + k, mixed[k])
                return carry

            lax.fori_loop(0, heads // 2, pair, 0)

    totals = sum_ref[0]
    plain = (jnp.min(totals) > SUM_LOW) & (jnp.max(totals) < SUM_HIGH)
    plain_ref[sample] = plain.astype(jnp.int32)

    @pl.when(jnp.logical_not(plain))
    def _():
        @each_head(heads)
        def _(h, slot):
            query, key, value = head_parts(qkv_ref, h, width, rows)
            scores = masked_tail(dot(key, query, 0, 0), 0, limit)
            top = jnp.max(scores, 0, keepdims=True)
            top_ref[0, pl.ds(h, 1), :] = top
            pow_ref[slot] = jnp.exp2(scores - top).astype(BF)
            left = jnp.concatenate((value, ones), 0)
            store(h, dot(left, pow_ref[slot], 1, 0))


def each_head(heads):
    def run(body):
        def pair(p, carry):
            for slot in range(2):
                body(2 * p + slot, slot)
            return carry

        lax.fori_loop(0, heads // 2, pair, 0)

    return run


def head_rows(h, base):
    return pl.ds(pl.multiple_of(base + h * HEAD_DIM, HEAD_DIM), HEAD_DIM)


def head_parts(qkv_ref, h, width, keys):
    return (
        qkv_ref[0, head_rows(h, 0), :],
        qkv_ref[0, head_rows(h, width), :keys],
        qkv_ref[0, head_rows(h, 2 * width), :keys],
    )


def layer_kernel(
    core_ref, x_own_ref, x_far_ref, own_ref, far_ref, att_ref, sum_ref, cls_ref, cot_ref, *refs,
    samples, parts, peers
):
    stat_refs = refs[:peers]
    w_out_ref, w1_ref, w2_ref, pack_ref = refs[peers : peers + 4]
    (
        act_ref, middle_ref, gmid_ref, dmix_ref, inner_ref, out_grad_ref, norm_ref, bias_ref,
        kept_ref, sent_ref,
    ) = refs[peers + 4 : peers + 14]
    full_ref, g_ref, dpre_ref, dcls_ref, acc2_ref, acc1_ref, flat_ref = refs[peers + 14 :]
    step = pl.program_id(0)
    width = own_ref.shape[2]
    hidden = w2_ref.shape[0]
    blocks = hidden // width

    @pl.when(step == 0)
    def _():
        acc2_ref[...] = jnp.zeros_like(acc2_ref)
        acc1_ref[...] = jnp.zeros_like(acc1_ref)
        bias_ref[...] = jnp.zeros_like(bias_ref)
        out_grad_ref[...] = jnp.zeros_like(out_grad_ref)
        stats = stat_refs[0][...]
        for other in stat_refs[1:]:
            stats = stats + other[...]
        local = cot_ref.shape[0]
        cls = cls_ref[...][:local]
        cot = cot_ref[...].astype(F32)
        mean = stats[0:1] / samples
        scale = lax.rsqrt(stats[1:2] / samples - mean * mean + CLS_EPS)
        hat = (cls - mean) * scale
        norm_ref[...] = hat.astype(BF)
        cross = scale * (stats[3:4] - mean * stats[2:3])
        dcls_ref[...] = jnp.zeros_like(dcls_ref)
        dcls_ref[:local, :] = scale * (cot - stats[2:3] / samples - hat * (cross / samples))

    place_halves(full_ref, core_ref[CORE], x_own_ref[0], x_far_ref[0])
    place_halves(g_ref, core_ref[CORE], own_ref[0].astype(F32), far_ref[0].astype(F32))
    g_ref[0:1, :] = g_ref[0:1, :] + dcls_ref[pl.ds(step, 1), :]
    g_mlp = g_ref[...].astype(BF)
    bias_ref[blocks : blocks + 1, :] += jnp.sum(g_mlp.astype(F32), 0, keepdims=True)

    branch = dot(att_ref[0], w_out_ref[...], 0, 0) + row_of(pack_ref, OUT_BIAS)
    middle = full_ref[...].astype(F32) + branch
    middle_ref[0] = middle
    hat, rstd = norm_parts(middle)
    normed = (hat * row_of(pack_ref, GAIN2) + row_of(pack_ref, SHIFT2)).astype(BF)
    hat_low = hat.astype(BF)
    for j in range(blocks):
        cols = slice(j * width, (j + 1) * width)
        pre = dot(normed, w1_ref[:, cols], 1, 0) + row_of(pack_ref, FC1_BIAS + j)
        d_act = dot(g_mlp, w2_ref[cols, :], 1, 1)
        cdf = gelu_cdf(pre)
        bell = jnp.exp2(pre * pre * (-0.5 * LOG2E) - 0.5 * math.log2(2.0 * math.pi))
        act_ref[0, :, cols] = (pre * cdf).astype(BF)
        d_pre = d_act * (cdf + pre * bell)
        bias_ref[j : j + 1, :] += jnp.sum(d_pre, 0, keepdims=True)
        dpre_ref[:, cols] = d_pre.astype(BF)
    acc1_ref[...] += dot(hat_low, dpre_ref[...], 0, 0)
    acc2_ref[...] += dot(act_ref[0], g_mlp, 0, 0)
    d_norm = dot(dpre_ref[...], w1_ref[...], 1, 1)
    u = d_norm * row_of(pack_ref, GAIN2)
    g_mid = g_ref[...] + rstd * (
        u - jnp.mean(u, -1, keepdims=True) - hat * jnp.mean(u * hat, -1, keepdims=True)
    )
    g_attn = g_mid.astype(BF)
    gmid_ref[0] = g_attn
    out_grad_ref[...] += dot(att_ref[0], g_attn, 1, 0)
    bias_ref[blocks + 1 : blocks + 2, :] += jnp.sum(g_attn.astype(F32), 0, keepdims=True)
    d_mix = dot(w_out_ref[...], g_attn, 1, 1)
    for h in range(width // HEAD_DIM):
        part = slice(h * HEAD_DIM, (h + 1) * HEAD_DIM)
        piece = d_mix[part] * (1.0 / sum_ref[0, h : h + 1, :])
        dmix_ref[0, part, :] = piece.astype(BF)
        inner_ref[0, h : h + 1, :] = jnp.sum(piece * att_ref[0, part, :].astype(F32), 0, keepdims=True)

    @pl.when(step == pl.num_programs(0) - 1)
    def _():
        flat_ref[:hidden, :] = acc2_ref[...].astype(BF)
        for j in range(blocks):
            rows = slice(hidden + j * width, hidden + (j + 1) * width)
            flat_ref[rows, :] = acc1_ref[:, j * width : (j + 1) * width].astype(BF)
        clear_rest(flat_ref, 2 * hidden)
        write_halves(core_ref[CORE], flat_ref, parts, kept_ref, sent_ref)


def output_kernel(core_ref, act_ref, middle_ref, w2_ref, pack_ref, own_ref, far_ref, full_ref):
    output = middle_ref[0] + dot(act_ref[0], w2_ref[...], 1, 0) + row_of(pack_ref, FC2_BIAS)
    full_ref[...] = output.astype(BF)
    split_halves(full_ref, core_ref[CORE], own_ref, far_ref)


def attention_back_kernel(
    core_ref, views_ref, plain_ref, order_ref, qkv_ref, top_ref, dmix_ref, inner_ref, hat_ref,
    dqkv_ref, grad_ref, sums_ref, pow_ref, *, turn, samples
):
    pair = pl.program_id(0)
    sample = order_ref[turn]
    rows, width = hat_ref.shape[1:]
    views = views_ref[core_ref[CORE] * samples + sample]
    limit = 1 + VIEW_ROWS * views
    plain = plain_ref[sample] == 1
    both = range(2)
    lanes = [slice(k * HEAD_DIM, (k + 1) * HEAD_DIM) for k in both]

    def back(keys, powers_of):
        query = [qkv_ref[0, 0, part, :] for part in lanes]
        key = [qkv_ref[0, 1, part, :keys] for part in lanes]
        value = [qkv_ref[0, 2, part, :keys] for part in lanes]
        d_mix = [dmix_ref[0, part, :] for part in lanes]
        scores = [dot(key[k], query[k], 0, 0) for k in both]
        for k in both:
            powers_of(k, scores[k])
        d_weights = [dot(value[k], d_mix[k], 0, 0) for k in both]
        d_scores = []
        for k in both:
            inner = inner_ref[0, pl.ds(2 * pair + k, 1), :]
            powers = pow_ref[k, :keys, :].astype(F32)
            d_scores.append((powers * (d_weights[k] - inner)).astype(BF))
        for k in both:
            d_value = dot(d_mix[k], pow_ref[k, :keys, :], 1, 1)
            dqkv_ref[0, 2, lanes[k], :keys] = d_value.astype(BF)
        for k in both:
            d_query = dot(key[k], d_scores[k], 1, 0) * SCALE
            dqkv_ref[0, 0, lanes[k], :] = d_query.astype(BF)
            d_key = dot(query[k], d_scores[k], 1, 1) * LN2
            dqkv_ref[0, 1, lanes[k], :keys] = d_key.astype(BF)
        if keys < rows:
            blank = jnp.zeros((2 * HEAD_DIM, rows - keys), BF)
            dqkv_ref[0, 1, :, keys:] = blank
            dqkv_ref[0, 2, :, keys:] = blank

    for count, keys in key_counts(rows):

        @pl.when((views == count) & plain)
        def _(keys=keys):
            main = keys - 16

            def powers_of(k, scores):
                pow_ref[k, :main, :] = jnp.exp2(scores[:main]).astype(BF)
                tail = masked_tail(scores[main:], main, limit)
                pow_ref[k, main:keys, :] = jnp.exp2(tail).astype(BF)

            back(keys, powers_of)

    @pl.when(jnp.logical_not(plain))
    def _():
        def powers_of(k, scores):
            top = top_ref[0, pl.ds(2 * pair + k, 1), :]
            pow_ref[k] = jnp.exp2(masked_tail(scores, 0, limit) - top).astype(BF)

        back(rows, powers_of)

    right = jnp.concatenate((hat_ref[0], jnp.ones((rows, 128), BF)), 1)
    result = dot(dqkv_ref[0].reshape(3 * 2 * HEAD_DIM, rows), right, 1, 0)
    grad_ref[...] = result[:, :width].astype(BF).reshape(grad_ref.shape)
    sums_ref[0] = result[:, width:].T[:8]


def tokens_back_kernel(core_ref, order_ref, *refs, sets):
    dqkv_refs = refs[:sets]
    w_ref, pack_ref, x_own_ref, x_far_ref, gmid_ref, own_ref, far_ref, out_ref, d_ref, sems = refs[sets:]
    step = pl.program_id(0)

    def fetch(k):
        return pltpu.make_async_copy(dqkv_refs[k].at[0], d_ref.at[k], sems.at[k])

    @pl.when(step == 0)
    def _():
        for k in range(sets):
            fetch(k).start()

    for k in range(sets):

        @pl.when(step == k)
        def _(k=k):
            fetch(k).wait()

    d_norm = dot(d_ref[step], w_ref[...], 0, 0)
    place_halves(out_ref, core_ref[CORE], x_own_ref[0], x_far_ref[0])
    hat, rstd = norm_parts(out_ref[...].astype(F32))
    w = d_norm * row_of(pack_ref, GAIN1)
    back = rstd * (w - jnp.mean(w, -1, keepdims=True) - hat * jnp.mean(w * hat, -1, keepdims=True))
    out_ref[...] = (gmid_ref[0].astype(F32) + back).astype(BF)
    split_halves(out_ref, core_ref[CORE], own_ref, far_ref)


def clear_rest(ref, used):
    if ref.shape[0] > used:
        ref[used:, :] = jnp.zeros((ref.shape[0] - used, ref.shape[1]), ref.dtype)


def write_halves(core, flat_ref, parts, kept_ref, sent_ref):
    start = at = 0
    for size in parts:
        half = size // 2
        mine = pl.multiple_of(start + core * half, 16)
        other = pl.multiple_of(start + (1 - core) * half, 16)
        kept_ref[at : at + half, :] = flat_ref[pl.ds(mine, half), :]
        sent_ref[at : at + half, :] = flat_ref[pl.ds(other, half), :]
        start += size
        at += half


def pack_kernel(core_ref, *refs, sets, parts):
    grad_refs = refs[:sets]
    sums_refs = refs[sets : 2 * sets]
    out_grad_ref, bias_ref, kept_ref, sent_ref, flat_ref = refs[2 * sets :]
    width = out_grad_ref.shape[0]
    used = grad_refs[0].shape[0]
    total, sums = grad_refs[0][...].astype(F32), sums_refs[0][...]
    for grad_ref, sums_ref in zip(grad_refs[1:], sums_refs[1:]):
        total = total + grad_ref[...].astype(F32)
        sums = sums + sums_ref[...]
    flat_ref[:used, :] = total.astype(BF)
    flat_ref[used : used + width, :] = out_grad_ref[...].astype(BF)
    clear_rest(flat_ref, used + width)
    write_halves(core_ref[CORE], flat_ref, parts, kept_ref, sent_ref)
    rows = lax.broadcasted_iota(jnp.int32, (8, width), 0)
    extra = jnp.zeros((8, width), F32)
    for t in range(used // width):
        row = jnp.concatenate([sums[p, 0:1, t * 128 : (t + 1) * 128] for p in range(width // 128)], 1)
        extra = jnp.where(rows == t, row, extra)
    vectors = jnp.concatenate((bias_ref[0:8, :], extra), 0).astype(BF)
    at = sum(parts) // 2
    kept_ref[at : at + EXTRA, :] = vectors
    sent_ref[at : at + EXTRA, :] = vectors


def insert_rows(info, base, came):
    def body(info_ref, came_ref, base_ref, out_ref, mark_ref):
        out_ref[...] = came_ref[...]

    return pl.pallas_call(
        body,
        grid_spec=pltpu.PrefetchScalarGridSpec(
            num_scalar_prefetch=1,
            grid=(1,),
            in_specs=[
                pl.BlockSpec(came.shape, lambda *_: (0, 0, 0)), pl.BlockSpec(memory_space=pl.ANY),
            ],
            out_specs=[
                pl.BlockSpec(came.shape, lambda s, b: (1 - b[CORE], 0, 0)),
                pl.BlockSpec(memory_space=pl.ANY),
            ],
        ),
        out_shape=[jax.ShapeDtypeStruct(base.shape, base.dtype), jax.ShapeDtypeStruct((1,), jnp.int32)],
        input_output_aliases={2: 0},
        compiler_params=params(("arbitrary",)),
        name="insert",
    )(info, came, base)


def swap_cores(value):
    return lax.ppermute(value, "blk", [(0, 1), (1, 0)])


def stages(count, first=4):
    out = []
    stride = 1
    while stride < count:
        left = count // stride
        radix = first if not out and left % first == 0 else 4 if left % 4 == 0 else 2
        out.append((stride, radix))
        stride *= radix
    return out


def shifted(value, stage, steps, axis="samp"):
    stride, radix = stage
    count = lax.axis_size(axis)
    pairs = []
    for source in range(count):
        digit = (source // stride) % radix
        pairs.append((source, source + ((digit + steps) % radix - digit) * stride))
    return lax.ppermute(value, axis, pairs)


MARK = jax.ShapeDtypeStruct((1,), jnp.int32)


def small_call(kernel, args, outs, scratch=(), ties=(), name=None, through=()):
    n, t, o, m = len(args), len(ties), len(outs), len(through)

    def body(*refs):
        kernel(*refs[:n], *refs[n + t + m : n + t + m + o], *refs[n + t + 2 * m + o + 1 :])

    anywhere = pl.BlockSpec(memory_space=pl.ANY)
    vmem = pl.BlockSpec(memory_space=pltpu.VMEM)
    smem = pl.BlockSpec(memory_space=pltpu.SMEM)
    size = lambda a: math.prod(a.shape) * jnp.dtype(a.dtype).itemsize
    total = sum(size(a) for a in (*args[1:], *outs)) + sum(
        math.prod(a.shape) * jnp.dtype(a.dtype).itemsize for a in scratch
    )
    return pl.pallas_call(
        body,
        in_specs=[smem, *[vmem] * (n - 1), *[smem] * t, *[anywhere] * m],
        out_specs=[vmem] * o + [anywhere] * (m + 1),
        out_shape=[*outs, *[jax.ShapeDtypeStruct(a.shape, a.dtype) for a in through], MARK],
        input_output_aliases={n + t + k: o + k for k in range(m)},
        scratch_shapes=list(scratch),
        compiler_params=pltpu.CompilerParams(vmem_limit_bytes=2 * total + 4 * 2**20),
        name=name,
    )(*args, *ties, *through)


def spread_kernel(info_ref, *refs, count, radix, slot, extra, rows, rider, unload):
    inputs = count + (1 if rider else 0) + (1 if unload else 0)
    outputs = radix + (1 if extra and radix == 1 else 0)
    outs, total_ref = refs[inputs : inputs + outputs], refs[-1]
    if unload:
        collect_kernel(info_ref, refs[inputs - 1], *refs[1:count], refs[inputs + outputs])
    total = refs[0][:rows, :].astype(F32)
    for ref in refs[1:count]:
        total = total + ref[:rows, :].astype(F32)
    rows = rows - extra
    size = rows // radix
    total_ref[...] = total.astype(BF)
    if radix == 1:
        outs[0][...] = total_ref[:rows, :]
        if extra:
            outs[1][...] = total[rows:]
        return
    for k in range(radix):
        start = lax.rem(info_ref[slot] + k, radix) * size
        outs[k][:size, :] = total_ref[pl.ds(pl.multiple_of(start, 16), size), :]
        if extra:
            outs[k][size : size + extra, :] = total_ref[rows:, :]
        if rider and k > 0:
            outs[k][size + extra :, :] = refs[count][...]


def collect_kernel(info_ref, own_ref, *refs):
    out_ref = refs[-1]
    size = own_ref.shape[0]
    out_ref[:size, :] = own_ref[...]
    for k, ref in enumerate(refs[:-1]):
        out_ref[(k + 1) * size : (k + 2) * size, :] = ref[ref.shape[0] - size :, :]


class Layout:
    def __init__(self, count, sizes):
        self.base = stages(count)
        self.count = count
        table = np.zeros((2 * count, 1 + len(self.base)), np.int32)
        for device in range(2 * count):
            table[device, 0] = device % 2
            for i in range(len(self.base)):
                table[device, 1 + i] = self.digit(device, i)
        tables = [table]
        self.place = []
        for rows in sizes:
            self.place.append(sum(t.shape[1] for t in tables))
            tables.append(np.stack([self.places(device, rows) for device in range(2 * count)]))
        self.table = np.concatenate(tables, 1).astype(np.int32)

    def digit(self, device, index):
        stride, radix = self.base[index]
        return (device // 2 // stride) % radix

    def places(self, device, rows):
        core = device % 2
        unit = rows // 2
        offsets = np.array([core * unit, (1 - core) * unit])
        for index, (_, radix) in enumerate(self.base):
            unit //= radix
            digit = (self.digit(device, index) - np.arange(radix)) % radix
            offsets = (offsets[:, None] + (digit * unit)[None, :]).reshape(-1)
        return offsets


class Chain:
    def __init__(self, layout, info, extra=0):
        self.layout = layout
        self.info = info
        self.extra = extra
        self.rounds = len(layout.base)

    def start(self, kept, sent):
        self.pending = [kept, swap_cores(sent)]

    def scatter(self, level, ties=(), rider=None, unload=None):
        last = level == self.rounds
        radix = 1 if last else self.layout.base[level][1]
        rows, width = self.pending[0].shape
        size = (rows - self.extra) // radix
        more = () if rider is None else (rider.value,)
        kept = () if unload is None else (unload.value,)
        if last:
            outs = [jax.ShapeDtypeStruct((size, width), BF)]
            if self.extra:
                outs.append(jax.ShapeDtypeStruct((self.extra, width), F32))
        else:
            piece = size + self.extra
            sent = piece + sum(value.shape[0] for value in more)
            outs = [jax.ShapeDtypeStruct((sent if k else piece, width), BF) for k in range(radix)]
        if kept:
            outs.append(jax.ShapeDtypeStruct((len(self.pending) * kept[0].shape[0], width), BF))
        pieces = small_call(
            functools.partial(
                spread_kernel, count=len(self.pending), radix=radix, slot=1 + level, extra=self.extra,
                rows=rows, rider=bool(more), unload=bool(kept),
            ),
            (self.info, *self.pending, *more, *kept), outs, [pltpu.VMEM((rows, width), BF)], ties, "spread",
        )
        if kept:
            unload.value = pieces[-2]
        if last:
            self.value = pieces[0]
            self.vectors = pieces[1] if self.extra else None
        else:
            stage = self.layout.base[level]
            self.pending = [pieces[0]] + [shifted(pieces[k], stage, k) for k in range(1, radix)]
            if more:
                rider.pending = [rider.value, *self.pending[1:]]
        return pieces[-1]

    def gather(self, level):
        stage = self.layout.base[level]
        self.pending = [self.value] + [shifted(self.value, stage, k) for k in range(1, stage[1])]

    def collect(self, ties=(), through=()):
        size, width = self.pending[0].shape
        outs = [jax.ShapeDtypeStruct((len(self.pending) * size, width), BF)]
        self.value, *self.through, mark = small_call(
            collect_kernel, (self.info, *self.pending), outs, (), ties, "collect", through
        )
        return mark


def restore(place_ref, flat_ref, ref, unit, at):
    def body(i, carry):
        start = pl.multiple_of(place_ref[at + i], 16)
        source = pl.multiple_of(i * unit, 16)
        chunk = ref[pl.ds(source, unit), :]
        flat_ref[pl.ds(start, unit), :] = chunk
        return carry

    lax.fori_loop(0, ref.shape[0] // unit, body, 0)


def finish_mlp_kernel(
    info_ref, own_ref, far_ref, vectors_ref, pack_ref, w1_ref,
    fc2_ref, fc1_ref, gain_ref, shift_ref, fc1_bias_ref, fc2_bias_ref, flat_ref, *, unit, at
):
    restore(info_ref, flat_ref, own_ref, unit, at)
    restore(info_ref, flat_ref, far_ref, unit, at + own_ref.shape[0] // unit)
    hidden, width = fc2_ref.shape
    fc2_ref[...] = flat_ref[:hidden, :].astype(F32)
    columns = pack_ref[0:8, :].T
    gain = jnp.zeros((width, 1), F32)
    shift = jnp.zeros((width, 1), F32)
    for j in range(hidden // width):
        cols = slice(j * width, (j + 1) * width)
        hats = flat_ref[hidden + j * width : hidden + (j + 1) * width, :].astype(F32)
        sums = vectors_ref[j : j + 1, :]
        fc1_ref[:, cols] = hats * columns[:, GAIN2 : GAIN2 + 1] + columns[:, SHIFT2 : SHIFT2 + 1] * sums
        w = w1_ref[:, cols].astype(F32)
        gain = gain + jnp.sum(w * hats, -1, keepdims=True)
        shift = shift + jnp.sum(w * sums, -1, keepdims=True)
    lane = lax.broadcasted_iota(jnp.int32, (width, 128), 1)
    both = jnp.where(lane == 0, gain, jnp.where(lane == 1, shift, 0.0)).T[0:8]
    gain_ref[...] = both[0]
    shift_ref[...] = both[1]
    blocks = hidden // width
    for j in range(blocks):
        fc1_bias_ref[j * width : (j + 1) * width] = vectors_ref[j, :]
    fc2_bias_ref[...] = vectors_ref[blocks, :]


def finish_kernel(
    info_ref, own_ref, far_ref, vectors_ref, pack_ref, w_ref, qkv_ref, out_ref, gain_ref, shift_ref, qv_ref, out_bias_ref, flat_ref,
    *, unit, at, blocks
):
    restore(info_ref, flat_ref, own_ref, unit, at)
    restore(info_ref, flat_ref, far_ref, unit, at + own_ref.shape[0] // unit)
    width = out_ref.shape[0]
    columns = qkv_ref.shape[1]
    out_ref[...] = flat_ref[columns : columns + width, :].astype(F32)
    gain = jnp.zeros((1, width), F32)
    shift = jnp.zeros((1, width), F32)
    turned = vectors_ref[8:16, :].T
    for t in range(columns // width):
        part = slice(t * width, (t + 1) * width)
        hats = flat_ref[part, :].astype(F32)
        sums = turned[:, t : t + 1]
        result = hats * row_of(pack_ref, GAIN1) + sums * row_of(pack_ref, SHIFT1)
        qkv_ref[:, part] = result.T
        w = w_ref[part, :].astype(F32)
        gain = gain + jnp.sum(w * hats, 0, keepdims=True)
        shift = shift + jnp.sum(w * sums, 0, keepdims=True)
    gain_ref[...] = gain[0]
    shift_ref[...] = shift[0]
    qv_ref[:width] = vectors_ref[8, :]
    qv_ref[width:] = vectors_ref[10, :]
    out_bias_ref[...] = vectors_ref[blocks + 1, :]


def pad_rows(count, unit):
    return -(-count // unit) * unit


def per_device(
    tokens, view_count, norm1_gain, norm1_bias, w_qkv, qv_bias, w_out, out_bias,
    norm2_gain, norm2_bias, w_fc1, fc1_bias, w_fc2, fc2_bias, cot_tokens, cot_cls,
):
    core = lax.axis_index("blk")
    cores = lax.axis_size("blk")
    count = lax.axis_size("samp")
    samples, half, width = tokens.shape
    local = samples // cores
    rows = half * cores
    hidden = w_fc1.shape[1]
    blocks = hidden // width
    heads = width // HEAD_DIM
    pairs = heads // 2
    sds = jax.ShapeDtypeStruct

    unit = 32 * count
    parts1 = [pad_rows(2 * hidden, unit)]
    parts2 = [pad_rows(4 * width, unit)]
    layout = Layout(count, (parts1[0], parts2[0]))
    device = lax.axis_index("samp") * cores + core
    info = lax.dynamic_index_in_dim(jnp.asarray(layout.table), device, 0, keepdims=False)

    theirs = (1 - core) * local
    far_tokens = swap_cores(lax.dynamic_slice_in_dim(tokens, theirs, local, 0))
    far_cot = swap_cores(lax.dynamic_slice_in_dim(cot_tokens, theirs, local, 0))

    pack = jnp.concatenate(
        (
            norm1_gain, norm1_bias, norm2_gain, norm2_bias, out_bias, fc2_bias, qv_bias, fc1_bias,
            jnp.zeros(((8 - blocks) * width,), BF),
        )
    ).astype(F32).reshape(16, width)

    vmem = pl.BlockSpec(memory_space=pltpu.VMEM)
    half_spec = lambda f: pl.BlockSpec((1, half, width), f)
    own_map = lambda s, b, *_: (b[CORE] * local + s, 0, 0)
    by_sample = lambda s, *_: (s, 0, 0)
    rows_spec = pl.BlockSpec((1, rows, width), by_sample)
    turned_spec = pl.BlockSpec((1, width, rows), by_sample)
    rstd_spec = pl.BlockSpec((1, rows, 1), by_sample)
    hidden_spec = pl.BlockSpec((1, rows, hidden), by_sample)
    eight_spec = pl.BlockSpec((1, 8, rows), by_sample)

    def big_call(kernel, prefetch, args, in_specs, outs, out_specs, scratch=(), ties=(), grid=(local,), name=None):
        n, t, o = len(prefetch) + len(args), len(ties), len(outs)
        smem = pl.BlockSpec(memory_space=pltpu.SMEM)

        def body(*refs):
            kernel(*refs[:n], *refs[n + t : n + t + o], *refs[n + t + o + 1 :])

        return pl.pallas_call(
            body,
            grid_spec=pltpu.PrefetchScalarGridSpec(
                num_scalar_prefetch=len(prefetch),
                grid=grid,
                in_specs=[*in_specs, *[smem] * t],
                out_specs=[*out_specs, pl.BlockSpec(memory_space=pl.ANY)],
                scratch_shapes=list(scratch),
            ),
            out_shape=[*outs, MARK],
            compiler_params=params(("arbitrary",) * len(grid)),
            name=name,
        )(*prefetch, *args, *ties)

    hat1, qkv, cls_rows, stats, w_turned, order, _ = big_call(
        project_kernel,
        (info, view_count),
        (tokens, far_tokens, w_qkv, pack, w_out, w_fc1, w_fc2, cot_cls),
        [half_spec(own_map), half_spec(by_sample), *[vmem] * 6],
        [
            sds((local, rows, width), BF),
            sds((local, 3 * width, rows), BF),
            sds((8, width), F32),
            sds((8, width), F32),
            sds((3 * width, width), BF),
            sds((local,), jnp.int32),
        ],
        [
            rows_spec, pl.BlockSpec((1, 3 * width, rows), by_sample), vmem, vmem, vmem,
            pl.BlockSpec(memory_space=pltpu.SMEM),
        ],
        [pltpu.VMEM((8, width), F32), pltpu.VMEM((8, width), F32), pltpu.VMEM((rows, width), BF)],
        name="project",
    )

    def add_kernel(info_ref, *refs):
        total = refs[0][...]
        for ref in refs[1:-1]:
            total = total + ref[...]
        refs[-1][...] = total

    *later, first = stages(count)

    def add_all(values, ties=()):
        return small_call(add_kernel, [info, *values], [sds((8, width), F32)], (), ties, "add")

    stats, tie = add_all([stats, swap_cores(stats)])
    stat_parts = [stats] + [shifted(stats, first, k) for k in range(1, first[1])]

    qkv_spec = lambda f: pl.BlockSpec((1, 3 * width, rows), f)
    totals, tops, plain, mixed, tie = big_call(
        attention_kernel,
        (info, view_count),
        (qkv,),
        [qkv_spec(by_sample)],
        [
            sds((local, 8, rows), F32),
            sds((local, 8, rows), F32),
            sds((local,), jnp.int32),
            sds((local, width, rows), BF),
        ],
        [eight_spec, eight_spec, pl.BlockSpec(memory_space=pltpu.SMEM), turned_spec],
        [pltpu.VMEM((2, rows, rows), BF)],
        (tie,),
        name="attention",
    )

    for stage in later:
        stats, tie = add_all(stat_parts, (tie,))
        stat_parts = [stats] + [shifted(stats, stage, k) for k in range(1, stage[1])]

    act, middle, g_mid, d_mix, inner, out_grad, cls_norm, biases, kept1, sent1, _ = big_call(
        functools.partial(
            layer_kernel, samples=local * cores * count, parts=parts1, peers=len(stat_parts)
        ),
        (info,),
        (
            tokens, far_tokens, cot_tokens, far_cot, mixed, totals, cls_rows, cot_cls, *stat_parts,
            w_out, w_fc1, w_fc2, pack,
        ),
        [
            half_spec(own_map), half_spec(by_sample), half_spec(own_map), half_spec(by_sample),
            turned_spec, eight_spec, vmem, vmem, *[vmem] * len(stat_parts), vmem, vmem, vmem, vmem,
        ],
        [
            sds((local, rows, hidden), BF),
            sds((local, rows, width), F32),
            sds((local, rows, width), BF),
            sds((local, width, rows), BF),
            sds((local, 8, rows), F32),
            sds((width, width), F32),
            sds((local, width), BF),
            sds((8, width), F32),
            sds((sum(parts1) // 2, width), BF),
            sds((sum(parts1) // 2, width), BF),
        ],
        [
            hidden_spec, rows_spec, rows_spec, turned_spec, eight_spec, vmem, vmem, vmem, vmem, vmem,
        ],
        [
            pltpu.VMEM((rows, width), BF),
            pltpu.VMEM((rows, width), F32),
            pltpu.VMEM((rows, hidden), BF),
            pltpu.VMEM((8, width), F32),
            pltpu.VMEM((hidden, width), F32),
            pltpu.VMEM((width, hidden), F32),
            pltpu.VMEM((sum(parts1), width), BF),
        ],
        name="layer",
    )
    chain1 = Chain(layout, info)
    chain1.start(kept1, sent1)

    def attention_back(turn, ties):
        place = lambda p, c, v, q, o: (o[turn], 0, 0)
        return big_call(
            functools.partial(attention_back_kernel, turn=turn, samples=local),
            (info, view_count, plain, order),
            (qkv.reshape(local, 3, width, rows), tops, d_mix, inner, hat1),
            [
                pl.BlockSpec((1, 3, 128, rows), lambda p, c, v, q, o: (o[turn], 0, p, 0)),
                pl.BlockSpec((1, 8, rows), place),
                pl.BlockSpec((1, 128, rows), lambda p, c, v, q, o: (o[turn], p, 0)),
                pl.BlockSpec((1, 8, rows), place),
                pl.BlockSpec((1, rows, width), place),
            ],
            [
                sds((1, 3, width, rows), BF),
                sds((3, width, width), BF),
                sds((pairs, 8, 384), F32),
            ],
            [
                pl.BlockSpec((1, 3, 128, rows), lambda p, *_: (0, 0, p, 0)),
                pl.BlockSpec((3, 128, width), lambda p, *_: (0, p, 0)),
                pl.BlockSpec((1, 8, 384), lambda p, *_: (p, 0, 0)),
            ],
            [pltpu.VMEM((2, rows, rows), BF)],
            ties,
            grid=(pairs,),
            name="attention_back",
        )

    def scatter_step(level):
        def run(ties):
            piece = chain1.scatter(level, ties)
            if level == chain1.rounds:
                chain1.gather(level - 1)
            return piece

        return run

    def collect_step(level):
        def run(ties):
            mark = chain1.collect(ties)
            if level > 1:
                chain1.gather(level - 1)
            return mark

        return run

    steps = [scatter_step(level) for level in range(1, chain1.rounds + 1)]
    steps += [collect_step(level) for level in reversed(range(1, chain1.rounds))]
    ties = (chain1.scatter(0),)
    d_parts, grads, sums = [], [], []
    for sample in range(local):
        d_part, grad, total, tie = attention_back(sample, ties)
        d_parts.append(d_part.reshape(1, 3 * width, rows))
        grads.append(grad.reshape(3 * width, width))
        sums.append(total)
        ties = (steps.pop(0)((tie,)),)

    while steps:
        ties = (steps.pop(0)(()),)
    chain2 = Chain(layout, info, EXTRA)
    kept2, sent2, _ = small_call(
        functools.partial(pack_kernel, sets=len(grads), parts=parts2),
        (info, *grads, *sums, out_grad, biases),
        [sds((sum(parts2) // 2 + EXTRA, width), BF)] * 2,
        [pltpu.VMEM((sum(parts2), width), BF)],
        ties,
        name="pack",
    )
    chain2.start(kept2, sent2)
    tie = chain2.scatter(0, (), chain1)

    own_turn = lambda s, c, o: (c[CORE] * local + o[s], 0, 0)
    turn = lambda s, c, o: (o[s], 0, 0)
    grad_own, grad_far, tie = big_call(
        functools.partial(tokens_back_kernel, sets=len(d_parts)),
        (info, order),
        (*d_parts, w_turned, pack, tokens, far_tokens, g_mid),
        [
            *[pl.BlockSpec(memory_space=pl.ANY)] * len(d_parts),
            vmem, vmem, half_spec(own_turn), half_spec(turn), pl.BlockSpec((1, rows, width), turn),
        ],
        [sds((samples, half, width), BF), sds((local, half, width), BF)],
        [half_spec(own_turn), half_spec(turn)],
        [
            pltpu.VMEM((rows, width), BF),
            pltpu.VMEM((len(d_parts), 3 * width, rows), BF),
            pltpu.SemaphoreType.DMA((len(d_parts),)),
        ],
        (tie,),
        name="tokens_back",
    )
    tokens_out_own, out_far, out_tie = big_call(
        output_kernel,
        (info,),
        (act, middle, w_fc2, pack),
        [hidden_spec, rows_spec, vmem, vmem],
        [sds((samples, half, width), BF), sds((local, half, width), BF)],
        [half_spec(own_map), half_spec(by_sample)],
        [pltpu.VMEM((rows, width), BF)],
        (tie,),
        name="output",
    )
    grad_came = swap_cores(grad_far)
    for level in range(1, chain2.rounds + 1):
        first = level == 1
        tie = chain2.scatter(level, (out_tie,) if first else (), None, chain1 if first else None)
        if first:
            other1 = swap_cores(chain1.value)
    ties = ()
    for level in reversed(range(chain2.rounds)):
        chain2.gather(level)
        if level == chain2.rounds - 1:
            (
                grad_w_fc2, grad_w_fc1, grad_gain2, grad_shift2, grad_fc1_bias, grad_fc2_bias, tie,
            ) = small_call(
                functools.partial(
                    finish_mlp_kernel, unit=parts1[0] // (2 * count), at=layout.place[0]
                ),
                (info, chain1.value, other1, chain2.vectors, pack, w_fc1),
                [
                    sds((hidden, width), F32), sds((width, hidden), F32), sds((width,), F32),
                    sds((width,), F32), sds((hidden,), F32), sds((width,), F32),
                ],
                [pltpu.VMEM((parts1[0], width), BF)],
                name="finish_mlp",
            )
            ties = (tie,)
        if level == 0:
            grad_tokens, tie = insert_rows(info, grad_own, grad_came)
            ties = (tie,)
        chain2.collect(ties, (out_far,) if level == chain2.rounds - 1 else ())
        if level == chain2.rounds - 1:
            out_came = swap_cores(chain2.through[0])
    other = swap_cores(chain2.value)
    tokens_out, out_tie = insert_rows(info, tokens_out_own, out_came)

    grad_w_qkv, grad_w_out, grad_gain1, grad_shift1, grad_qv_bias, grad_out_bias, _ = small_call(
        functools.partial(finish_kernel, unit=parts2[0] // (2 * count), at=layout.place[1], blocks=blocks),
        (info, chain2.value, other, chain2.vectors, pack, w_turned),
        [
            sds((width, 3 * width), F32), sds((width, width), F32), sds((width,), F32), sds((width,), F32),
            sds((2 * width,), F32), sds((width,), F32),
        ],
        [pltpu.VMEM((parts2[0], width), BF)],
        (out_tie,),
        name="finish",
    )
    return (
        tokens_out, cls_norm, grad_tokens, grad_gain1, grad_shift1, grad_w_qkv, grad_qv_bias,
        grad_w_out, grad_out_bias, grad_gain2, grad_shift2, grad_w_fc1, grad_fc1_bias,
        grad_w_fc2, grad_fc2_bias,
    )


def solution(mesh):
    split = P("samp", "blk", None)
    classes = P(("samp", "blk"), None)
    return jax.shard_map(
        per_device,
        mesh=mesh,
        in_specs=(split, P("samp"), *([P()] * 12), split, classes),
        out_specs=(split, classes, split, *([P()] * 12)),
        check_vma=False,
    )
```

```python
import functools
import math

import jax
import jax.numpy as jnp
import numpy as np
from jax import lax
from jax.experimental import pallas as pl
from jax.experimental.pallas import tpu as pltpu
from jax.sharding import PartitionSpec as P

HEAD_DIM = 64
VIEW_ROWS = 196
NORM_EPS = 1e-06
CLS_EPS = 1e-05
MASKED = -1e30
LOG2E = math.log2(math.e)
LN2 = math.log(2.0)
SCALE = HEAD_DIM ** (-0.5)
SUM_LOW = 1e-15
SUM_HIGH = 1e15
BF = jnp.bfloat16
F32 = jnp.float32
VMEM_BYTES = 60 * 2**20
CORE = 0
EXTRA = 16


def dot(a, b, ca, cb):
    return lax.dot_general(a, b, (((ca,), (cb,)), ((), ())), preferred_element_type=F32)


def norm_parts(values):
    centre = jnp.mean(values, -1, keepdims=True)
    offset = values - centre
    rstd = lax.rsqrt(jnp.mean(offset * offset, -1, keepdims=True) + NORM_EPS)
    return offset * rstd, rstd


def gelu_cdf(values):
    return 0.5 + 0.5 * lax.erf(values * (0.5**0.5))


def params(semantics):
    return pltpu.CompilerParams(dimension_semantics=semantics, vmem_limit_bytes=VMEM_BYTES)


def whole(shape):
    return pl.BlockSpec(shape, lambda *_: (0,) * len(shape))


def key_counts(rows):
    views = (rows - 1) // VIEW_ROWS
    return [(v, min(rows, -(-(1 + VIEW_ROWS * v) // 16) * 16)) for v in range(1, views + 1)]


GAIN1, SHIFT1, GAIN2, SHIFT2, OUT_BIAS, FC2_BIAS, QV_BIAS, FC1_BIAS = 0, 1, 2, 3, 4, 5, 6, 8


def row_of(pack_ref, index):
    return pack_ref[index : index + 1, :]


def place_halves(target_ref, core, own, far):
    half = own.shape[0]
    target_ref[pl.ds(pl.multiple_of(core * half, 16), half), :] = own
    target_ref[pl.ds(pl.multiple_of((1 - core) * half, 16), half), :] = far


def split_halves(source_ref, core, own_ref, far_ref):
    half = own_ref.shape[1]
    own_ref[0] = source_ref[pl.ds(pl.multiple_of(core * half, 16), half), :]
    far_ref[0] = source_ref[pl.ds(pl.multiple_of((1 - core) * half, 16), half), :]


def rank_samples(views_ref, base, order_ref):
    count = order_ref.shape[0]
    views = [views_ref[base + i] for i in range(count)]
    for i in range(count):
        rank = jnp.int32(0)
        for j in range(count):
            if j != i:
                ahead = views[j] >= views[i] if j < i else views[j] > views[i]
                rank = rank + ahead.astype(jnp.int32)
        order_ref[rank] = jnp.int32(i)


def project_kernel(
    blk_ref, views_ref, own_ref, far_ref, w_in_ref, pack_ref, w_out_ref, w1_ref, w2_ref, cot_ref,
    hat_ref, qkv_ref, cls_ref, stat_ref, w_ref, order_ref, mix_ref, first_ref, full_ref,
):
    step = pl.program_id(0)

    @pl.when(step == 0)
    def _():
        w_ref[...] = w_in_ref[...].T
        rank_samples(views_ref, blk_ref[CORE] * order_ref.shape[0], order_ref)

    rows = hat_ref.shape[1]
    width = own_ref.shape[2]
    place_halves(full_ref, blk_ref[0], own_ref[0], far_ref[0])
    values = full_ref[...].astype(F32)
    hat, _ = norm_parts(values)
    hat_ref[0] = hat.astype(BF)
    normed = (hat * row_of(pack_ref, GAIN1) + row_of(pack_ref, SHIFT1)).astype(BF)
    columns = pack_ref[0:8, :].T
    for third in range(3):
        part = pl.ds(third * width, width)
        piece = dot(w_ref[part, :], normed, 1, 1)
        if third == 0:
            piece = (piece + columns[:, QV_BIAS : QV_BIAS + 1]) * (SCALE * LOG2E)
        if third == 2:
            piece = piece + columns[:, QV_BIAS + 1 : QV_BIAS + 2]
        qkv_ref[0, part, :] = piece.astype(BF)

    lead = qkv_ref[0, pl.ds(0, width), :128].astype(F32).T[0:1, :]
    head_of = lax.broadcasted_iota(jnp.int32, (8, width), 1) // HEAD_DIM
    pick = head_of == lax.broadcasted_iota(jnp.int32, (8, width), 0)
    queries = jnp.where(pick, lead, 0.0).astype(BF)
    scores = dot(queries, qkv_ref[0, pl.ds(width, width), :], 1, 0)
    limit = 1 + VIEW_ROWS * views_ref[blk_ref[CORE] * pl.num_programs(0) + step]
    place = lax.broadcasted_iota(jnp.int32, (8, rows), 1)
    scores = jnp.where(place < limit, scores, MASKED)
    powers = jnp.exp2(scores - jnp.max(scores, -1, keepdims=True))
    chances = (powers / jnp.sum(powers, -1, keepdims=True)).astype(BF)
    mixed = dot(chances, qkv_ref[0, pl.ds(2 * width, width), :], 1, 1)
    mix_ref[pl.ds(step, 1), :] = jnp.sum(jnp.where(pick, mixed, 0.0), 0, keepdims=True)
    first_ref[pl.ds(step, 1), :] = values[0:1, :]

    @pl.when(step == pl.num_programs(0) - 1)
    def _():
        branch = dot(mix_ref[...].astype(BF), w_out_ref[...], 1, 0) + row_of(pack_ref, OUT_BIAS)
        middle = first_ref[...] + branch
        normed2 = norm_parts(middle)[0] * row_of(pack_ref, GAIN2) + row_of(pack_ref, SHIFT2)
        normed2 = normed2.astype(BF)
        output = middle + row_of(pack_ref, FC2_BIAS)
        for j in range(w1_ref.shape[1] // width):
            cols = slice(j * width, (j + 1) * width)
            pre = dot(normed2, w1_ref[:, cols], 1, 0) + row_of(pack_ref, FC1_BIAS + j)
            act = (pre * gelu_cdf(pre)).astype(BF)
            output = output + dot(act, w2_ref[cols, :], 1, 0)
        cls_ref[...] = output
        count = cot_ref.shape[0]
        cls = output[:count]
        cot = cot_ref[...].astype(F32)
        stat_ref[...] = jnp.zeros_like(stat_ref)
        for k, term in enumerate((cls, cls * cls, cot, cot * cls)):
            stat_ref[k : k + 1, :] = jnp.sum(term, 0, keepdims=True)


def masked_tail(scores, main, limit):
    place = main + lax.broadcasted_iota(jnp.int32, scores.shape, 0)
    return jnp.where(place < limit, scores, MASKED)


def attention_kernel(
    core_ref, views_ref, qkv_ref, sum_ref, top_ref, plain_ref, att_ref, pow_ref
):
    sample = pl.program_id(0)
    rows = qkv_ref.shape[2]
    width = att_ref.shape[1]
    heads = width // HEAD_DIM
    views = views_ref[core_ref[CORE] * pl.num_programs(0) + sample]
    limit = 1 + VIEW_ROWS * views
    ones = jnp.ones((16, rows), BF)

    def store(h, mixed):
        total = mixed[HEAD_DIM : HEAD_DIM + 1]
        sum_ref[0, pl.ds(h, 1), :] = total
        att_ref[0, head_rows(h, 0), :] = (mixed[:HEAD_DIM] * (1.0 / total)).astype(BF)

    sum_ref[0, heads:8, :] = jnp.ones((8 - heads, rows), F32)
    for count, keys in key_counts(rows):

        @pl.when(views == count)
        def _(keys=keys):
            main = keys - 16

            def pair(p, carry):
                both = range(2)
                parts = [head_parts(qkv_ref, 2 * p + k, width, keys) for k in both]
                scores = [dot(key, query, 0, 0) for query, key, _ in parts]
                for k in both:
                    pow_ref[k, :main, :] = jnp.exp2(scores[k][:main]).astype(BF)
                    tail = masked_tail(scores[k][main:], main, limit)
                    pow_ref[k, main:keys, :] = jnp.exp2(tail).astype(BF)
                lefts = [jnp.concatenate((value, ones[:, :keys]), 0) for _, _, value in parts]
                mixed = [dot(lefts[k], pow_ref[k, :keys, :], 1, 0) for k in both]
                for k in both:
                    store(2 * p + k, mixed[k])
                return carry

            lax.fori_loop(0, heads // 2, pair, 0)

    totals = sum_ref[0]
    plain = (jnp.min(totals) > SUM_LOW) & (jnp.max(totals) < SUM_HIGH)
    plain_ref[sample] = plain.astype(jnp.int32)

    @pl.when(jnp.logical_not(plain))
    def _():
        @each_head(heads)
        def _(h, slot):
            query, key, value = head_parts(qkv_ref, h, width, rows)
            scores = masked_tail(dot(key, query, 0, 0), 0, limit)
            top = jnp.max(scores, 0, keepdims=True)
            top_ref[0, pl.ds(h, 1), :] = top
            pow_ref[slot] = jnp.exp2(scores - top).astype(BF)
            left = jnp.concatenate((value, ones), 0)
            store(h, dot(left, pow_ref[slot], 1, 0))


def each_head(heads):
    def run(body):
        def pair(p, carry):
            for slot in range(2):
                body(2 * p + slot, slot)
            return carry

        lax.fori_loop(0, heads // 2, pair, 0)

    return run


def head_rows(h, base):
    return pl.ds(pl.multiple_of(base + h * HEAD_DIM, HEAD_DIM), HEAD_DIM)


def head_parts(qkv_ref, h, width, keys):
    return (
        qkv_ref[0, head_rows(h, 0), :],
        qkv_ref[0, head_rows(h, width), :keys],
        qkv_ref[0, head_rows(h, 2 * width), :keys],
    )


def layer_kernel(
    core_ref, x_own_ref, x_far_ref, own_ref, far_ref, att_ref, sum_ref, cls_ref, cot_ref, *refs,
    samples, parts, peers
):
    stat_refs = refs[:peers]
    w_out_ref, w1_ref, w2_ref, pack_ref = refs[peers : peers + 4]
    (
        act_ref, middle_ref, gmid_ref, dmix_ref, inner_ref, out_grad_ref, norm_ref, bias_ref,
        kept_ref, sent_ref,
    ) = refs[peers + 4 : peers + 14]
    full_ref, g_ref, dpre_ref, dcls_ref, acc2_ref, acc1_ref, flat_ref = refs[peers + 14 :]
    step = pl.program_id(0)
    width = own_ref.shape[2]
    hidden = w2_ref.shape[0]
    blocks = hidden // width

    @pl.when(step == 0)
    def _():
        acc2_ref[...] = jnp.zeros_like(acc2_ref)
        acc1_ref[...] = jnp.zeros_like(acc1_ref)
        bias_ref[...] = jnp.zeros_like(bias_ref)
        out_grad_ref[...] = jnp.zeros_like(out_grad_ref)
        stats = stat_refs[0][...]
        for other in stat_refs[1:]:
            stats = stats + other[...]
        local = cot_ref.shape[0]
        cls = cls_ref[...][:local]
        cot = cot_ref[...].astype(F32)
        mean = stats[0:1] / samples
        scale = lax.rsqrt(stats[1:2] / samples - mean * mean + CLS_EPS)
        hat = (cls - mean) * scale
        norm_ref[...] = hat.astype(BF)
        cross = scale * (stats[3:4] - mean * stats[2:3])
        dcls_ref[...] = jnp.zeros_like(dcls_ref)
        dcls_ref[:local, :] = scale * (cot - stats[2:3] / samples - hat * (cross / samples))

    place_halves(full_ref, core_ref[CORE], x_own_ref[0], x_far_ref[0])
    place_halves(g_ref, core_ref[CORE], own_ref[0].astype(F32), far_ref[0].astype(F32))
    g_ref[0:1, :] = g_ref[0:1, :] + dcls_ref[pl.ds(step, 1), :]
    g_mlp = g_ref[...].astype(BF)
    bias_ref[blocks : blocks + 1, :] += jnp.sum(g_mlp.astype(F32), 0, keepdims=True)

    branch = dot(att_ref[0], w_out_ref[...], 0, 0) + row_of(pack_ref, OUT_BIAS)
    middle = full_ref[...].astype(F32) + branch
    middle_ref[0] = middle
    hat, rstd = norm_parts(middle)
    normed = (hat * row_of(pack_ref, GAIN2) + row_of(pack_ref, SHIFT2)).astype(BF)
    hat_low = hat.astype(BF)
    for j in range(blocks):
        cols = slice(j * width, (j + 1) * width)
        pre = dot(normed, w1_ref[:, cols], 1, 0) + row_of(pack_ref, FC1_BIAS + j)
        d_act = dot(g_mlp, w2_ref[cols, :], 1, 1)
        cdf = gelu_cdf(pre)
        bell = jnp.exp2(pre * pre * (-0.5 * LOG2E) - 0.5 * math.log2(2.0 * math.pi))
        act_ref[0, :, cols] = (pre * cdf).astype(BF)
        d_pre = d_act * (cdf + pre * bell)
        bias_ref[j : j + 1, :] += jnp.sum(d_pre, 0, keepdims=True)
        dpre_ref[:, cols] = d_pre.astype(BF)
    acc1_ref[...] += dot(hat_low, dpre_ref[...], 0, 0)
    acc2_ref[...] += dot(act_ref[0], g_mlp, 0, 0)
    d_norm = dot(dpre_ref[...], w1_ref[...], 1, 1)
    u = d_norm * row_of(pack_ref, GAIN2)
    g_mid = g_ref[...] + rstd * (
        u - jnp.mean(u, -1, keepdims=True) - hat * jnp.mean(u * hat, -1, keepdims=True)
    )
    g_attn = g_mid.astype(BF)
    gmid_ref[0] = g_attn
    out_grad_ref[...] += dot(att_ref[0], g_attn, 1, 0)
    bias_ref[blocks + 1 : blocks + 2, :] += jnp.sum(g_attn.astype(F32), 0, keepdims=True)
    d_mix = dot(w_out_ref[...], g_attn, 1, 1)
    for h in range(width // HEAD_DIM):
        part = slice(h * HEAD_DIM, (h + 1) * HEAD_DIM)
        piece = d_mix[part] * (1.0 / sum_ref[0, h : h + 1, :])
        dmix_ref[0, part, :] = piece.astype(BF)
        inner_ref[0, h : h + 1, :] = jnp.sum(piece * att_ref[0, part, :].astype(F32), 0, keepdims=True)

    @pl.when(step == pl.num_programs(0) - 1)
    def _():
        flat_ref[:hidden, :] = acc2_ref[...].astype(BF)
        for j in range(blocks):
            rows = slice(hidden + j * width, hidden + (j + 1) * width)
            flat_ref[rows, :] = acc1_ref[:, j * width : (j + 1) * width].astype(BF)
        clear_rest(flat_ref, 2 * hidden)
        write_halves(core_ref[CORE], flat_ref, parts, kept_ref, sent_ref)


def output_kernel(core_ref, act_ref, middle_ref, w2_ref, pack_ref, own_ref, far_ref, full_ref):
    output = middle_ref[0] + dot(act_ref[0], w2_ref[...], 1, 0) + row_of(pack_ref, FC2_BIAS)
    full_ref[...] = output.astype(BF)
    split_halves(full_ref, core_ref[CORE], own_ref, far_ref)


def attention_back_kernel(
    core_ref, views_ref, plain_ref, order_ref, qkv_ref, top_ref, dmix_ref, inner_ref, hat_ref,
    *refs, turn, samples, parts
):
    last = turn == samples - 1
    if last:
        earlier = refs[:turn], refs[turn : 2 * turn]
        out_grad_ref, bias_ref = refs[2 * turn : 2 * turn + 2]
        dqkv_ref, kept_ref, sent_ref, pow_ref, flat_ref, vector_ref = refs[2 * turn + 2 :]
    else:
        dqkv_ref, grad_ref, sums_ref, pow_ref = refs
    pair = pl.program_id(0)
    sample = order_ref[turn]
    rows, width = hat_ref.shape[1:]
    views = views_ref[core_ref[CORE] * samples + sample]
    limit = 1 + VIEW_ROWS * views
    plain = plain_ref[sample] == 1
    both = range(2)
    lanes = [slice(k * HEAD_DIM, (k + 1) * HEAD_DIM) for k in both]

    def back(keys, powers_of):
        query = [qkv_ref[0, 0, part, :] for part in lanes]
        key = [qkv_ref[0, 1, part, :keys] for part in lanes]
        value = [qkv_ref[0, 2, part, :keys] for part in lanes]
        d_mix = [dmix_ref[0, part, :] for part in lanes]
        scores = [dot(key[k], query[k], 0, 0) for k in both]
        for k in both:
            powers_of(k, scores[k])
        d_weights = [dot(value[k], d_mix[k], 0, 0) for k in both]
        d_scores = []
        for k in both:
            inner = inner_ref[0, pl.ds(2 * pair + k, 1), :]
            powers = pow_ref[k, :keys, :].astype(F32)
            d_scores.append((powers * (d_weights[k] - inner)).astype(BF))
        for k in both:
            d_value = dot(d_mix[k], pow_ref[k, :keys, :], 1, 1)
            dqkv_ref[0, 2, lanes[k], :keys] = d_value.astype(BF)
        for k in both:
            d_query = dot(key[k], d_scores[k], 1, 0) * SCALE
            dqkv_ref[0, 0, lanes[k], :] = d_query.astype(BF)
            d_key = dot(query[k], d_scores[k], 1, 1) * LN2
            dqkv_ref[0, 1, lanes[k], :keys] = d_key.astype(BF)
        if keys < rows:
            blank = jnp.zeros((2 * HEAD_DIM, rows - keys), BF)
            dqkv_ref[0, 1, :, keys:] = blank
            dqkv_ref[0, 2, :, keys:] = blank

    for count, keys in key_counts(rows):

        @pl.when((views == count) & plain)
        def _(keys=keys):
            main = keys - 16

            def powers_of(k, scores):
                pow_ref[k, :main, :] = jnp.exp2(scores[:main]).astype(BF)
                tail = masked_tail(scores[main:], main, limit)
                pow_ref[k, main:keys, :] = jnp.exp2(tail).astype(BF)

            back(keys, powers_of)

    @pl.when(jnp.logical_not(plain))
    def _():
        def powers_of(k, scores):
            top = top_ref[0, pl.ds(2 * pair + k, 1), :]
            pow_ref[k] = jnp.exp2(masked_tail(scores, 0, limit) - top).astype(BF)

        back(rows, powers_of)

    right = jnp.concatenate((hat_ref[0], jnp.ones((rows, 128), BF)), 1)
    result = dot(dqkv_ref[0].reshape(3 * 2 * HEAD_DIM, rows), right, 1, 0)
    sums = result[:, width:].T[:8]
    if not last:
        grad_ref[...] = result[:, :width].astype(BF).reshape(grad_ref.shape)
        sums_ref[0] = sums
        return

    @pl.when(pair == 0)
    def _():
        vector_ref[0:8, :] = bias_ref[...]
        vector_ref[8:16, :] = jnp.zeros((8, width), F32)

    for ref in earlier[1]:
        sums = sums + ref[0]
    at = pl.multiple_of(pair * 128, 128)
    for t in range(3):
        own = slice(t * 128, (t + 1) * 128)
        total = result[own, :width]
        for ref in earlier[0]:
            total = total + ref[t].astype(F32)
        flat_ref[pl.ds(t * width + at, 128), :] = total.astype(BF)
        vector_ref[8 + t : 9 + t, pl.ds(at, 128)] = sums[0:1, own]

    @pl.when(pair == pl.num_programs(0) - 1)
    def _():
        flat_ref[3 * width : 4 * width, :] = out_grad_ref[...].astype(BF)
        clear_rest(flat_ref, 4 * width)
        write_halves(core_ref[CORE], flat_ref, parts, kept_ref, sent_ref)
        half = sum(parts) // 2
        kept_ref[half : half + EXTRA, :] = vector_ref[...].astype(BF)
        sent_ref[half : half + EXTRA, :] = vector_ref[...].astype(BF)


def tokens_back_kernel(core_ref, order_ref, *refs, sets):
    dqkv_refs = refs[:sets]
    w_ref, pack_ref, x_own_ref, x_far_ref, gmid_ref, own_ref, far_ref, out_ref, d_ref, sems = refs[sets:]
    step = pl.program_id(0)

    def fetch(k):
        return pltpu.make_async_copy(dqkv_refs[k].at[0], d_ref.at[k], sems.at[k])

    @pl.when(step == 0)
    def _():
        for k in range(sets):
            fetch(k).start()

    for k in range(sets):

        @pl.when(step == k)
        def _(k=k):
            fetch(k).wait()

    d_norm = dot(d_ref[step], w_ref[...], 0, 0)
    place_halves(out_ref, core_ref[CORE], x_own_ref[0], x_far_ref[0])
    hat, rstd = norm_parts(out_ref[...].astype(F32))
    w = d_norm * row_of(pack_ref, GAIN1)
    back = rstd * (w - jnp.mean(w, -1, keepdims=True) - hat * jnp.mean(w * hat, -1, keepdims=True))
    out_ref[...] = (gmid_ref[0].astype(F32) + back).astype(BF)
    split_halves(out_ref, core_ref[CORE], own_ref, far_ref)


def clear_rest(ref, used):
    if ref.shape[0] > used:
        ref[used:, :] = jnp.zeros((ref.shape[0] - used, ref.shape[1]), ref.dtype)


def write_halves(core, flat_ref, parts, kept_ref, sent_ref):
    start = at = 0
    for size in parts:
        half = size // 2
        mine = pl.multiple_of(start + core * half, 16)
        other = pl.multiple_of(start + (1 - core) * half, 16)
        kept_ref[at : at + half, :] = flat_ref[pl.ds(mine, half), :]
        sent_ref[at : at + half, :] = flat_ref[pl.ds(other, half), :]
        start += size
        at += half


def insert_rows(info, base, came):
    def body(info_ref, came_ref, base_ref, out_ref, mark_ref):
        out_ref[...] = came_ref[...]

    return pl.pallas_call(
        body,
        grid_spec=pltpu.PrefetchScalarGridSpec(
            num_scalar_prefetch=1,
            grid=(1,),
            in_specs=[
                pl.BlockSpec(came.shape, lambda *_: (0, 0, 0)), pl.BlockSpec(memory_space=pl.ANY),
            ],
            out_specs=[
                pl.BlockSpec(came.shape, lambda s, b: (1 - b[CORE], 0, 0)),
                pl.BlockSpec(memory_space=pl.ANY),
            ],
        ),
        out_shape=[jax.ShapeDtypeStruct(base.shape, base.dtype), jax.ShapeDtypeStruct((1,), jnp.int32)],
        input_output_aliases={2: 0},
        compiler_params=params(("arbitrary",)),
        name="insert",
    )(info, came, base)


def swap_cores(value):
    return lax.ppermute(value, "blk", [(0, 1), (1, 0)])


def stages(count, first=4):
    out = []
    stride = 1
    while stride < count:
        left = count // stride
        radix = first if not out and left % first == 0 else 4 if left % 4 == 0 else 2
        out.append((stride, radix))
        stride *= radix
    return out


def shifted(value, stage, steps, axis="samp"):
    stride, radix = stage
    count = lax.axis_size(axis)
    pairs = []
    for source in range(count):
        digit = (source // stride) % radix
        pairs.append((source, source + ((digit + steps) % radix - digit) * stride))
    return lax.ppermute(value, axis, pairs)


MARK = jax.ShapeDtypeStruct((1,), jnp.int32)


def small_call(kernel, args, outs, scratch=(), ties=(), name=None, through=()):
    n, t, o, m = len(args), len(ties), len(outs), len(through)

    def body(*refs):
        kernel(*refs[:n], *refs[n + t + m : n + t + m + o], *refs[n + t + 2 * m + o + 1 :])

    anywhere = pl.BlockSpec(memory_space=pl.ANY)
    vmem = pl.BlockSpec(memory_space=pltpu.VMEM)
    smem = pl.BlockSpec(memory_space=pltpu.SMEM)
    size = lambda a: math.prod(a.shape) * jnp.dtype(a.dtype).itemsize
    total = sum(size(a) for a in (*args[1:], *outs)) + sum(
        math.prod(a.shape) * jnp.dtype(a.dtype).itemsize for a in scratch
    )
    return pl.pallas_call(
        body,
        in_specs=[smem, *[vmem] * (n - 1), *[smem] * t, *[anywhere] * m],
        out_specs=[vmem] * o + [anywhere] * (m + 1),
        out_shape=[*outs, *[jax.ShapeDtypeStruct(a.shape, a.dtype) for a in through], MARK],
        input_output_aliases={n + t + k: o + k for k in range(m)},
        scratch_shapes=list(scratch),
        compiler_params=pltpu.CompilerParams(vmem_limit_bytes=2 * total + 4 * 2**20),
        name=name,
    )(*args, *ties, *through)


def spread_kernel(info_ref, *refs, count, radix, slot, extra, rows, rider, unload):
    inputs = count + (1 if rider else 0) + (1 if unload else 0)
    outputs = radix + (1 if extra and radix == 1 else 0)
    outs, total_ref = refs[inputs : inputs + outputs], refs[-1]
    if unload:
        collect_kernel(info_ref, refs[inputs - 1], *refs[1:count], refs[inputs + outputs])
    total = refs[0][:rows, :].astype(F32)
    for ref in refs[1:count]:
        total = total + ref[:rows, :].astype(F32)
    rows = rows - extra
    size = rows // radix
    total_ref[...] = total.astype(BF)
    if radix == 1:
        outs[0][...] = total_ref[:rows, :]
        if extra:
            outs[1][...] = total[rows:]
        return
    for k in range(radix):
        start = lax.rem(info_ref[slot] + k, radix) * size
        outs[k][:size, :] = total_ref[pl.ds(pl.multiple_of(start, 16), size), :]
        if extra:
            outs[k][size : size + extra, :] = total_ref[rows:, :]
        if rider and k > 0:
            outs[k][size + extra :, :] = refs[count][...]


def collect_kernel(info_ref, own_ref, *refs):
    out_ref = refs[-1]
    size = own_ref.shape[0]
    out_ref[:size, :] = own_ref[...]
    for k, ref in enumerate(refs[:-1]):
        out_ref[(k + 1) * size : (k + 2) * size, :] = ref[ref.shape[0] - size :, :]


class Layout:
    def __init__(self, count, sizes):
        self.base = stages(count)
        self.count = count
        table = np.zeros((2 * count, 1 + len(self.base)), np.int32)
        for device in range(2 * count):
            table[device, 0] = device % 2
            for i in range(len(self.base)):
                table[device, 1 + i] = self.digit(device, i)
        tables = [table]
        self.place = []
        for rows in sizes:
            self.place.append(sum(t.shape[1] for t in tables))
            tables.append(np.stack([self.places(device, rows) for device in range(2 * count)]))
        self.table = np.concatenate(tables, 1).astype(np.int32)

    def digit(self, device, index):
        stride, radix = self.base[index]
        return (device // 2 // stride) % radix

    def places(self, device, rows):
        core = device % 2
        unit = rows // 2
        offsets = np.array([core * unit, (1 - core) * unit])
        for index, (_, radix) in enumerate(self.base):
            unit //= radix
            digit = (self.digit(device, index) - np.arange(radix)) % radix
            offsets = (offsets[:, None] + (digit * unit)[None, :]).reshape(-1)
        return offsets


class Chain:
    def __init__(self, layout, info, extra=0):
        self.layout = layout
        self.info = info
        self.extra = extra
        self.rounds = len(layout.base)

    def start(self, kept, sent):
        self.pending = [kept, swap_cores(sent)]

    def scatter(self, level, ties=(), rider=None, unload=None):
        last = level == self.rounds
        radix = 1 if last else self.layout.base[level][1]
        rows, width = self.pending[0].shape
        size = (rows - self.extra) // radix
        more = () if rider is None else (rider.value,)
        kept = () if unload is None else (unload.value,)
        if last:
            outs = [jax.ShapeDtypeStruct((size, width), BF)]
            if self.extra:
                outs.append(jax.ShapeDtypeStruct((self.extra, width), F32))
        else:
            piece = size + self.extra
            sent = piece + sum(value.shape[0] for value in more)
            outs = [jax.ShapeDtypeStruct((sent if k else piece, width), BF) for k in range(radix)]
        if kept:
            outs.append(jax.ShapeDtypeStruct((len(self.pending) * kept[0].shape[0], width), BF))
        pieces = small_call(
            functools.partial(
                spread_kernel, count=len(self.pending), radix=radix, slot=1 + level, extra=self.extra,
                rows=rows, rider=bool(more), unload=bool(kept),
            ),
            (self.info, *self.pending, *more, *kept), outs, [pltpu.VMEM((rows, width), BF)], ties, "spread",
        )
        if kept:
            unload.value = pieces[-2]
        if last:
            self.value = pieces[0]
            self.vectors = pieces[1] if self.extra else None
        else:
            stage = self.layout.base[level]
            self.pending = [pieces[0]] + [shifted(pieces[k], stage, k) for k in range(1, radix)]
            if more:
                rider.pending = [rider.value, *self.pending[1:]]
        return pieces[-1]

    def gather(self, level):
        stage = self.layout.base[level]
        self.pending = [self.value] + [shifted(self.value, stage, k) for k in range(1, stage[1])]

    def collect(self, ties=(), through=()):
        size, width = self.pending[0].shape
        outs = [jax.ShapeDtypeStruct((len(self.pending) * size, width), BF)]
        self.value, *self.through, mark = small_call(
            collect_kernel, (self.info, *self.pending), outs, (), ties, "collect", through
        )
        return mark


def restore(place_ref, flat_ref, ref, unit, at):
    def body(i, carry):
        start = pl.multiple_of(place_ref[at + i], 16)
        source = pl.multiple_of(i * unit, 16)
        chunk = ref[pl.ds(source, unit), :]
        flat_ref[pl.ds(start, unit), :] = chunk
        return carry

    lax.fori_loop(0, ref.shape[0] // unit, body, 0)


def finish_mlp_kernel(
    info_ref, own_ref, far_ref, vectors_ref, pack_ref, w1_ref,
    fc2_ref, fc1_ref, gain_ref, shift_ref, fc1_bias_ref, fc2_bias_ref, flat_ref, *, unit, at
):
    restore(info_ref, flat_ref, own_ref, unit, at)
    restore(info_ref, flat_ref, far_ref, unit, at + own_ref.shape[0] // unit)
    hidden, width = fc2_ref.shape
    fc2_ref[...] = flat_ref[:hidden, :].astype(F32)
    columns = pack_ref[0:8, :].T
    gain = jnp.zeros((width, 1), F32)
    shift = jnp.zeros((width, 1), F32)
    for j in range(hidden // width):
        cols = slice(j * width, (j + 1) * width)
        hats = flat_ref[hidden + j * width : hidden + (j + 1) * width, :].astype(F32)
        sums = vectors_ref[j : j + 1, :]
        fc1_ref[:, cols] = hats * columns[:, GAIN2 : GAIN2 + 1] + columns[:, SHIFT2 : SHIFT2 + 1] * sums
        w = w1_ref[:, cols].astype(F32)
        gain = gain + jnp.sum(w * hats, -1, keepdims=True)
        shift = shift + jnp.sum(w * sums, -1, keepdims=True)
    lane = lax.broadcasted_iota(jnp.int32, (width, 128), 1)
    both = jnp.where(lane == 0, gain, jnp.where(lane == 1, shift, 0.0)).T[0:8]
    gain_ref[...] = both[0]
    shift_ref[...] = both[1]
    blocks = hidden // width
    for j in range(blocks):
        fc1_bias_ref[j * width : (j + 1) * width] = vectors_ref[j, :]
    fc2_bias_ref[...] = vectors_ref[blocks, :]


def finish_kernel(
    info_ref, own_ref, far_ref, vectors_ref, pack_ref, w_ref, qkv_ref, out_ref, gain_ref, shift_ref, qv_ref, out_bias_ref, flat_ref,
    *, unit, at, blocks
):
    restore(info_ref, flat_ref, own_ref, unit, at)
    restore(info_ref, flat_ref, far_ref, unit, at + own_ref.shape[0] // unit)
    width = out_ref.shape[0]
    columns = qkv_ref.shape[1]
    out_ref[...] = flat_ref[columns : columns + width, :].astype(F32)
    gain = jnp.zeros((1, width), F32)
    shift = jnp.zeros((1, width), F32)
    turned = vectors_ref[8:16, :].T
    for t in range(columns // width):
        part = slice(t * width, (t + 1) * width)
        hats = flat_ref[part, :].astype(F32)
        sums = turned[:, t : t + 1]
        result = hats * row_of(pack_ref, GAIN1) + sums * row_of(pack_ref, SHIFT1)
        qkv_ref[:, part] = result.T
        w = w_ref[part, :].astype(F32)
        gain = gain + jnp.sum(w * hats, 0, keepdims=True)
        shift = shift + jnp.sum(w * sums, 0, keepdims=True)
    gain_ref[...] = gain[0]
    shift_ref[...] = shift[0]
    qv_ref[:width] = vectors_ref[8, :]
    qv_ref[width:] = vectors_ref[10, :]
    out_bias_ref[...] = vectors_ref[blocks + 1, :]


def pad_rows(count, unit):
    return -(-count // unit) * unit


def per_device(
    tokens, view_count, norm1_gain, norm1_bias, w_qkv, qv_bias, w_out, out_bias,
    norm2_gain, norm2_bias, w_fc1, fc1_bias, w_fc2, fc2_bias, cot_tokens, cot_cls,
):
    core = lax.axis_index("blk")
    cores = lax.axis_size("blk")
    count = lax.axis_size("samp")
    samples, half, width = tokens.shape
    local = samples // cores
    rows = half * cores
    hidden = w_fc1.shape[1]
    blocks = hidden // width
    heads = width // HEAD_DIM
    pairs = heads // 2
    sds = jax.ShapeDtypeStruct

    unit = 32 * count
    parts1 = [pad_rows(2 * hidden, unit)]
    parts2 = [pad_rows(4 * width, unit)]
    layout = Layout(count, (parts1[0], parts2[0]))
    device = lax.axis_index("samp") * cores + core
    info = lax.dynamic_index_in_dim(jnp.asarray(layout.table), device, 0, keepdims=False)

    theirs = (1 - core) * local
    far_tokens = swap_cores(lax.dynamic_slice_in_dim(tokens, theirs, local, 0))
    far_cot = swap_cores(lax.dynamic_slice_in_dim(cot_tokens, theirs, local, 0))

    pack = jnp.concatenate(
        (
            norm1_gain, norm1_bias, norm2_gain, norm2_bias, out_bias, fc2_bias, qv_bias, fc1_bias,
            jnp.zeros(((8 - blocks) * width,), BF),
        )
    ).astype(F32).reshape(16, width)

    vmem = pl.BlockSpec(memory_space=pltpu.VMEM)
    half_spec = lambda f: pl.BlockSpec((1, half, width), f)
    own_map = lambda s, b, *_: (b[CORE] * local + s, 0, 0)
    by_sample = lambda s, *_: (s, 0, 0)
    rows_spec = pl.BlockSpec((1, rows, width), by_sample)
    turned_spec = pl.BlockSpec((1, width, rows), by_sample)
    rstd_spec = pl.BlockSpec((1, rows, 1), by_sample)
    hidden_spec = pl.BlockSpec((1, rows, hidden), by_sample)
    eight_spec = pl.BlockSpec((1, 8, rows), by_sample)

    def big_call(kernel, prefetch, args, in_specs, outs, out_specs, scratch=(), ties=(), grid=(local,), name=None):
        n, t, o = len(prefetch) + len(args), len(ties), len(outs)
        smem = pl.BlockSpec(memory_space=pltpu.SMEM)

        def body(*refs):
            kernel(*refs[:n], *refs[n + t : n + t + o], *refs[n + t + o + 1 :])

        return pl.pallas_call(
            body,
            grid_spec=pltpu.PrefetchScalarGridSpec(
                num_scalar_prefetch=len(prefetch),
                grid=grid,
                in_specs=[*in_specs, *[smem] * t],
                out_specs=[*out_specs, pl.BlockSpec(memory_space=pl.ANY)],
                scratch_shapes=list(scratch),
            ),
            out_shape=[*outs, MARK],
            compiler_params=params(("arbitrary",) * len(grid)),
            name=name,
        )(*prefetch, *args, *ties)

    hat1, qkv, cls_rows, stats, w_turned, order, _ = big_call(
        project_kernel,
        (info, view_count),
        (tokens, far_tokens, w_qkv, pack, w_out, w_fc1, w_fc2, cot_cls),
        [half_spec(own_map), half_spec(by_sample), *[vmem] * 6],
        [
            sds((local, rows, width), BF),
            sds((local, 3 * width, rows), BF),
            sds((8, width), F32),
            sds((8, width), F32),
            sds((3 * width, width), BF),
            sds((local,), jnp.int32),
        ],
        [
            rows_spec, pl.BlockSpec((1, 3 * width, rows), by_sample), vmem, vmem, vmem,
            pl.BlockSpec(memory_space=pltpu.SMEM),
        ],
        [pltpu.VMEM((8, width), F32), pltpu.VMEM((8, width), F32), pltpu.VMEM((rows, width), BF)],
        name="project",
    )

    def add_kernel(info_ref, *refs):
        total = refs[0][...]
        for ref in refs[1:-1]:
            total = total + ref[...]
        refs[-1][...] = total

    *later, first = stages(count)

    def add_all(values, ties=()):
        return small_call(add_kernel, [info, *values], [sds((8, width), F32)], (), ties, "add")

    stats, tie = add_all([stats, swap_cores(stats)])
    stat_parts = [stats] + [shifted(stats, first, k) for k in range(1, first[1])]

    qkv_spec = lambda f: pl.BlockSpec((1, 3 * width, rows), f)
    totals, tops, plain, mixed, tie = big_call(
        attention_kernel,
        (info, view_count),
        (qkv,),
        [qkv_spec(by_sample)],
        [
            sds((local, 8, rows), F32),
            sds((local, 8, rows), F32),
            sds((local,), jnp.int32),
            sds((local, width, rows), BF),
        ],
        [eight_spec, eight_spec, pl.BlockSpec(memory_space=pltpu.SMEM), turned_spec],
        [pltpu.VMEM((2, rows, rows), BF)],
        (tie,),
        name="attention",
    )

    for stage in later:
        stats, tie = add_all(stat_parts, (tie,))
        stat_parts = [stats] + [shifted(stats, stage, k) for k in range(1, stage[1])]

    act, middle, g_mid, d_mix, inner, out_grad, cls_norm, biases, kept1, sent1, _ = big_call(
        functools.partial(
            layer_kernel, samples=local * cores * count, parts=parts1, peers=len(stat_parts)
        ),
        (info,),
        (
            tokens, far_tokens, cot_tokens, far_cot, mixed, totals, cls_rows, cot_cls, *stat_parts,
            w_out, w_fc1, w_fc2, pack,
        ),
        [
            half_spec(own_map), half_spec(by_sample), half_spec(own_map), half_spec(by_sample),
            turned_spec, eight_spec, vmem, vmem, *[vmem] * len(stat_parts), vmem, vmem, vmem, vmem,
        ],
        [
            sds((local, rows, hidden), BF),
            sds((local, rows, width), F32),
            sds((local, rows, width), BF),
            sds((local, width, rows), BF),
            sds((local, 8, rows), F32),
            sds((width, width), F32),
            sds((local, width), BF),
            sds((8, width), F32),
            sds((sum(parts1) // 2, width), BF),
            sds((sum(parts1) // 2, width), BF),
        ],
        [
            hidden_spec, rows_spec, rows_spec, turned_spec, eight_spec, vmem, vmem, vmem, vmem, vmem,
        ],
        [
            pltpu.VMEM((rows, width), BF),
            pltpu.VMEM((rows, width), F32),
            pltpu.VMEM((rows, hidden), BF),
            pltpu.VMEM((8, width), F32),
            pltpu.VMEM((hidden, width), F32),
            pltpu.VMEM((width, hidden), F32),
            pltpu.VMEM((sum(parts1), width), BF),
        ],
        name="layer",
    )
    chain1 = Chain(layout, info)
    chain1.start(kept1, sent1)

    def attention_back(turn, ties, grads, sums):
        place = lambda p, c, v, q, o: (o[turn], 0, 0)
        grad_spec = pl.BlockSpec((3, 128, width), lambda p, *_: (0, p, 0))
        sums_spec = pl.BlockSpec((1, 8, 384), lambda p, *_: (p, 0, 0))
        last = turn == local - 1
        half_rows = sum(parts2) // 2 + EXTRA
        more = [*grads, *sums, out_grad, biases] if last else []
        return big_call(
            functools.partial(attention_back_kernel, turn=turn, samples=local, parts=parts2),
            (info, view_count, plain, order),
            (qkv.reshape(local, 3, width, rows), tops, d_mix, inner, hat1, *more),
            [
                pl.BlockSpec((1, 3, 128, rows), lambda p, c, v, q, o: (o[turn], 0, p, 0)),
                pl.BlockSpec((1, 8, rows), place),
                pl.BlockSpec((1, 128, rows), lambda p, c, v, q, o: (o[turn], p, 0)),
                pl.BlockSpec((1, 8, rows), place),
                pl.BlockSpec((1, rows, width), place),
                *([grad_spec] * turn + [sums_spec] * turn + [vmem, vmem] if last else []),
            ],
            [
                sds((1, 3, width, rows), BF),
                *(
                    [sds((half_rows, width), BF)] * 2
                    if last
                    else [sds((3, width, width), BF), sds((pairs, 8, 384), F32)]
                ),
            ],
            [
                pl.BlockSpec((1, 3, 128, rows), lambda p, *_: (0, 0, p, 0)),
                *([vmem, vmem] if last else [grad_spec, sums_spec]),
            ],
            [
                pltpu.VMEM((2, rows, rows), BF),
                *([pltpu.VMEM((sum(parts2), width), BF), pltpu.VMEM((16, width), F32)] if last else []),
            ],
            ties,
            grid=(pairs,),
            name="attention_back",
        )

    def scatter_step(level):
        def run(ties):
            piece = chain1.scatter(level, ties)
            if level == chain1.rounds:
                chain1.gather(level - 1)
            return piece

        return run

    def collect_step(level):
        def run(ties, through=()):
            mark = chain1.collect(ties, through)
            if level > 1:
                chain1.gather(level - 1)
            return mark

        return run

    steps = [scatter_step(level) for level in range(1, chain1.rounds + 1)]
    steps += [collect_step(level) for level in reversed(range(1, chain1.rounds))]
    ties = (chain1.scatter(0),)
    d_parts, grads, sums = [], [], []
    chain2 = Chain(layout, info, EXTRA)
    for sample in range(local):
        d_part, grad, total, tie = attention_back(sample, ties, grads, sums)
        d_parts.append(d_part.reshape(1, 3 * width, rows))
        if sample == local - 1:
            if chain1.rounds == sample:
                ties = (steps.pop(0)((tie,), (total,)),)
                total = chain1.through[0]
            chain2.start(grad, total)
            break
        grads.append(grad)
        sums.append(total)
        if steps:
            ties = (steps.pop(0)((tie,)),)
    while steps:
        ties = (steps.pop(0)(()),)
    tie = chain2.scatter(0, (), chain1)

    own_turn = lambda s, c, o: (c[CORE] * local + o[s], 0, 0)
    turn = lambda s, c, o: (o[s], 0, 0)
    grad_own, grad_far, tie = big_call(
        functools.partial(tokens_back_kernel, sets=len(d_parts)),
        (info, order),
        (*d_parts, w_turned, pack, tokens, far_tokens, g_mid),
        [
            *[pl.BlockSpec(memory_space=pl.ANY)] * len(d_parts),
            vmem, vmem, half_spec(own_turn), half_spec(turn), pl.BlockSpec((1, rows, width), turn),
        ],
        [sds((samples, half, width), BF), sds((local, half, width), BF)],
        [half_spec(own_turn), half_spec(turn)],
        [
            pltpu.VMEM((rows, width), BF),
            pltpu.VMEM((len(d_parts), 3 * width, rows), BF),
            pltpu.SemaphoreType.DMA((len(d_parts),)),
        ],
        (tie,),
        name="tokens_back",
    )
    tokens_out_own, out_far, out_tie = big_call(
        output_kernel,
        (info,),
        (act, middle, w_fc2, pack),
        [hidden_spec, rows_spec, vmem, vmem],
        [sds((samples, half, width), BF), sds((local, half, width), BF)],
        [half_spec(own_map), half_spec(by_sample)],
        [pltpu.VMEM((rows, width), BF)],
        (tie,),
        name="output",
    )
    grad_came = swap_cores(grad_far)
    for level in range(1, chain2.rounds + 1):
        first = level == 1
        tie = chain2.scatter(level, (out_tie,) if first else (), None, chain1 if first else None)
        if first:
            other1 = swap_cores(chain1.value)
    ties = ()
    for level in reversed(range(chain2.rounds)):
        chain2.gather(level)
        if level == chain2.rounds - 1:
            (
                grad_w_fc2, grad_w_fc1, grad_gain2, grad_shift2, grad_fc1_bias, grad_fc2_bias, tie,
            ) = small_call(
                functools.partial(
                    finish_mlp_kernel, unit=parts1[0] // (2 * count), at=layout.place[0]
                ),
                (info, chain1.value, other1, chain2.vectors, pack, w_fc1),
                [
                    sds((hidden, width), F32), sds((width, hidden), F32), sds((width,), F32),
                    sds((width,), F32), sds((hidden,), F32), sds((width,), F32),
                ],
                [pltpu.VMEM((parts1[0], width), BF)],
                name="finish_mlp",
            )
            ties = (tie,)
        if level == 0:
            grad_tokens, tie = insert_rows(info, grad_own, grad_came)
            ties = (tie,)
        chain2.collect(ties, (out_far,) if level == chain2.rounds - 1 else ())
        if level == chain2.rounds - 1:
            out_came = swap_cores(chain2.through[0])
    other = swap_cores(chain2.value)
    tokens_out, out_tie = insert_rows(info, tokens_out_own, out_came)

    grad_w_qkv, grad_w_out, grad_gain1, grad_shift1, grad_qv_bias, grad_out_bias, _ = small_call(
        functools.partial(finish_kernel, unit=parts2[0] // (2 * count), at=layout.place[1], blocks=blocks),
        (info, chain2.value, other, chain2.vectors, pack, w_turned),
        [
            sds((width, 3 * width), F32), sds((width, width), F32), sds((width,), F32), sds((width,), F32),
            sds((2 * width,), F32), sds((width,), F32),
        ],
        [pltpu.VMEM((parts2[0], width), BF)],
        (out_tie,),
        name="finish",
    )
    return (
        tokens_out, cls_norm, grad_tokens, grad_gain1, grad_shift1, grad_w_qkv, grad_qv_bias,
        grad_w_out, grad_out_bias, grad_gain2, grad_shift2, grad_w_fc1, grad_fc1_bias,
        grad_w_fc2, grad_fc2_bias,
    )


def solution(mesh):
    split = P("samp", "blk", None)
    classes = P(("samp", "blk"), None)
    return jax.shard_map(
        per_device,
        mesh=mesh,
        in_specs=(split, P("samp"), *([P()] * 12), split, classes),
        out_specs=(split, classes, split, *([P()] * 12)),
        check_vma=False,
    )
```

```python
import functools
import math

import jax
import jax.numpy as jnp
import numpy as np
from jax import lax
from jax.experimental import pallas as pl
from jax.experimental.pallas import tpu as pltpu
from jax.sharding import PartitionSpec as P

HEAD_DIM = 64
VIEW_ROWS = 196
NORM_EPS = 1e-06
CLS_EPS = 1e-05
MASKED = -1e30
LOG2E = math.log2(math.e)
LN2 = math.log(2.0)
SCALE = HEAD_DIM ** (-0.5)
SUM_LOW = 1e-15
SUM_HIGH = 1e15
BF = jnp.bfloat16
F32 = jnp.float32
VMEM_BYTES = 60 * 2**20
CORE = 0
EXTRA = 16


def dot(a, b, ca, cb):
    return lax.dot_general(a, b, (((ca,), (cb,)), ((), ())), preferred_element_type=F32)


def norm_parts(values):
    centre = jnp.mean(values, -1, keepdims=True)
    offset = values - centre
    rstd = lax.rsqrt(jnp.mean(offset * offset, -1, keepdims=True) + NORM_EPS)
    return offset * rstd, rstd


def gelu_cdf(values):
    return 0.5 + 0.5 * lax.erf(values * (0.5**0.5))


def params(semantics):
    return pltpu.CompilerParams(dimension_semantics=semantics, vmem_limit_bytes=VMEM_BYTES)


def whole(shape):
    return pl.BlockSpec(shape, lambda *_: (0,) * len(shape))


def key_counts(rows):
    views = (rows - 1) // VIEW_ROWS
    return [(v, min(rows, -(-(1 + VIEW_ROWS * v) // 16) * 16)) for v in range(1, views + 1)]


GAIN1, SHIFT1, GAIN2, SHIFT2, OUT_BIAS, FC2_BIAS, QV_BIAS, FC1_BIAS = 0, 1, 2, 3, 4, 5, 6, 8


def row_of(pack_ref, index):
    return pack_ref[index : index + 1, :]


def place_halves(target_ref, core, own, far):
    half = own.shape[0]
    target_ref[pl.ds(pl.multiple_of(core * half, 16), half), :] = own
    target_ref[pl.ds(pl.multiple_of((1 - core) * half, 16), half), :] = far


def split_halves(source_ref, core, own_ref, far_ref):
    half = own_ref.shape[1]
    own_ref[0] = source_ref[pl.ds(pl.multiple_of(core * half, 16), half), :]
    far_ref[0] = source_ref[pl.ds(pl.multiple_of((1 - core) * half, 16), half), :]


def rank_samples(views_ref, base, order_ref):
    count = order_ref.shape[0]
    views = [views_ref[base + i] for i in range(count)]
    for i in range(count):
        rank = jnp.int32(0)
        for j in range(count):
            if j != i:
                ahead = views[j] >= views[i] if j < i else views[j] > views[i]
                rank = rank + ahead.astype(jnp.int32)
        order_ref[rank] = jnp.int32(i)


def project_kernel(
    blk_ref, views_ref, own_ref, far_ref, w_in_ref, w_out_ref, w1_ref, w2_ref, cot_ref,
    gain1_ref, shift1_ref, gain2_ref, shift2_ref, out_bias_ref, fc2_bias_ref, qv_bias_ref, fc1_bias_ref,
    hat_ref, qkv_ref, cls_ref, stat_ref, w_ref, order_ref, pack_ref, mix_ref, first_ref, full_ref,
):
    step = pl.program_id(0)

    @pl.when(step == 0)
    def _():
        pack_ref[...] = jnp.zeros_like(pack_ref)
        singles = gain1_ref, shift1_ref, gain2_ref, shift2_ref, out_bias_ref, fc2_bias_ref
        for k, ref in enumerate(singles):
            pack_ref[k, :] = ref[...].astype(F32)
        for first, ref in ((QV_BIAS, qv_bias_ref), (FC1_BIAS, fc1_bias_ref)):
            for k in range(ref.shape[0] // pack_ref.shape[1]):
                part = slice(k * pack_ref.shape[1], (k + 1) * pack_ref.shape[1])
                pack_ref[first + k, :] = ref[part].astype(F32)
        w_ref[...] = w_in_ref[...].T
        rank_samples(views_ref, blk_ref[CORE] * order_ref.shape[0], order_ref)

    rows = hat_ref.shape[1]
    width = own_ref.shape[2]
    place_halves(full_ref, blk_ref[0], own_ref[0], far_ref[0])
    values = full_ref[...].astype(F32)
    hat, _ = norm_parts(values)
    hat_ref[0] = hat.astype(BF)
    normed = (hat * row_of(pack_ref, GAIN1) + row_of(pack_ref, SHIFT1)).astype(BF)
    columns = pack_ref[0:8, :].T
    for third in range(3):
        part = pl.ds(third * width, width)
        piece = dot(w_ref[part, :], normed, 1, 1)
        if third == 0:
            piece = (piece + columns[:, QV_BIAS : QV_BIAS + 1]) * (SCALE * LOG2E)
        if third == 2:
            piece = piece + columns[:, QV_BIAS + 1 : QV_BIAS + 2]
        qkv_ref[0, part, :] = piece.astype(BF)

    lead = qkv_ref[0, pl.ds(0, width), :128].astype(F32).T[0:1, :]
    head_of = lax.broadcasted_iota(jnp.int32, (8, width), 1) // HEAD_DIM
    pick = head_of == lax.broadcasted_iota(jnp.int32, (8, width), 0)
    queries = jnp.where(pick, lead, 0.0).astype(BF)
    scores = dot(queries, qkv_ref[0, pl.ds(width, width), :], 1, 0)
    limit = 1 + VIEW_ROWS * views_ref[blk_ref[CORE] * pl.num_programs(0) + step]
    place = lax.broadcasted_iota(jnp.int32, (8, rows), 1)
    scores = jnp.where(place < limit, scores, MASKED)
    powers = jnp.exp2(scores - jnp.max(scores, -1, keepdims=True))
    chances = (powers / jnp.sum(powers, -1, keepdims=True)).astype(BF)
    mixed = dot(chances, qkv_ref[0, pl.ds(2 * width, width), :], 1, 1)
    mix_ref[pl.ds(step, 1), :] = jnp.sum(jnp.where(pick, mixed, 0.0), 0, keepdims=True)
    first_ref[pl.ds(step, 1), :] = values[0:1, :]

    @pl.when(step == pl.num_programs(0) - 1)
    def _():
        branch = dot(mix_ref[...].astype(BF), w_out_ref[...], 1, 0) + row_of(pack_ref, OUT_BIAS)
        middle = first_ref[...] + branch
        normed2 = norm_parts(middle)[0] * row_of(pack_ref, GAIN2) + row_of(pack_ref, SHIFT2)
        normed2 = normed2.astype(BF)
        output = middle + row_of(pack_ref, FC2_BIAS)
        for j in range(w1_ref.shape[1] // width):
            cols = slice(j * width, (j + 1) * width)
            pre = dot(normed2, w1_ref[:, cols], 1, 0) + row_of(pack_ref, FC1_BIAS + j)
            act = (pre * gelu_cdf(pre)).astype(BF)
            output = output + dot(act, w2_ref[cols, :], 1, 0)
        cls_ref[...] = output
        count = cot_ref.shape[0]
        cls = output[:count]
        cot = cot_ref[...].astype(F32)
        stat_ref[...] = jnp.zeros_like(stat_ref)
        for k, term in enumerate((cls, cls * cls, cot, cot * cls)):
            stat_ref[k : k + 1, :] = jnp.sum(term, 0, keepdims=True)


def masked_tail(scores, main, limit):
    place = main + lax.broadcasted_iota(jnp.int32, scores.shape, 0)
    return jnp.where(place < limit, scores, MASKED)


def attention_kernel(
    core_ref, views_ref, qkv_ref, sum_ref, top_ref, plain_ref, att_ref, pow_ref
):
    sample = pl.program_id(0)
    rows = qkv_ref.shape[2]
    width = att_ref.shape[1]
    heads = width // HEAD_DIM
    views = views_ref[core_ref[CORE] * pl.num_programs(0) + sample]
    limit = 1 + VIEW_ROWS * views
    ones = jnp.ones((16, rows), BF)

    def store(h, mixed):
        total = mixed[HEAD_DIM : HEAD_DIM + 1]
        sum_ref[0, pl.ds(h, 1), :] = total
        att_ref[0, head_rows(h, 0), :] = (mixed[:HEAD_DIM] * (1.0 / total)).astype(BF)

    sum_ref[0, heads:8, :] = jnp.ones((8 - heads, rows), F32)
    for count, keys in key_counts(rows):

        @pl.when(views == count)
        def _(keys=keys):
            main = keys - 16

            def pair(p, carry):
                both = range(2)
                parts = [head_parts(qkv_ref, 2 * p + k, width, keys) for k in both]
                scores = [dot(key, query, 0, 0) for query, key, _ in parts]
                for k in both:
                    pow_ref[k, :main, :] = jnp.exp2(scores[k][:main]).astype(BF)
                    tail = masked_tail(scores[k][main:], main, limit)
                    pow_ref[k, main:keys, :] = jnp.exp2(tail).astype(BF)
                lefts = [jnp.concatenate((value, ones[:, :keys]), 0) for _, _, value in parts]
                mixed = [dot(lefts[k], pow_ref[k, :keys, :], 1, 0) for k in both]
                for k in both:
                    store(2 * p + k, mixed[k])
                return carry

            lax.fori_loop(0, heads // 2, pair, 0)

    totals = sum_ref[0]
    plain = (jnp.min(totals) > SUM_LOW) & (jnp.max(totals) < SUM_HIGH)
    plain_ref[sample] = plain.astype(jnp.int32)

    @pl.when(jnp.logical_not(plain))
    def _():
        @each_head(heads)
        def _(h, slot):
            query, key, value = head_parts(qkv_ref, h, width, rows)
            scores = masked_tail(dot(key, query, 0, 0), 0, limit)
            top = jnp.max(scores, 0, keepdims=True)
            top_ref[0, pl.ds(h, 1), :] = top
            pow_ref[slot] = jnp.exp2(scores - top).astype(BF)
            left = jnp.concatenate((value, ones), 0)
            store(h, dot(left, pow_ref[slot], 1, 0))


def each_head(heads):
    def run(body):
        def pair(p, carry):
            for slot in range(2):
                body(2 * p + slot, slot)
            return carry

        lax.fori_loop(0, heads // 2, pair, 0)

    return run


def head_rows(h, base):
    return pl.ds(pl.multiple_of(base + h * HEAD_DIM, HEAD_DIM), HEAD_DIM)


def head_parts(qkv_ref, h, width, keys):
    return (
        qkv_ref[0, head_rows(h, 0), :],
        qkv_ref[0, head_rows(h, width), :keys],
        qkv_ref[0, head_rows(h, 2 * width), :keys],
    )


def layer_kernel(
    core_ref, x_own_ref, x_far_ref, own_ref, far_ref, att_ref, sum_ref, cls_ref, cot_ref, *refs,
    samples, parts, peers
):
    stat_refs = refs[:peers]
    w_out_ref, w1_ref, w2_ref, pack_ref = refs[peers : peers + 4]
    (
        act_ref, middle_ref, gmid_ref, dmix_ref, inner_ref, out_grad_ref, norm_ref, bias_ref,
        kept_ref, sent_ref,
    ) = refs[peers + 4 : peers + 14]
    full_ref, g_ref, dpre_ref, dcls_ref, acc2_ref, acc1_ref, flat_ref = refs[peers + 14 :]
    step = pl.program_id(0)
    width = own_ref.shape[2]
    hidden = w2_ref.shape[0]
    blocks = hidden // width

    @pl.when(step == 0)
    def _():
        acc2_ref[...] = jnp.zeros_like(acc2_ref)
        acc1_ref[...] = jnp.zeros_like(acc1_ref)
        bias_ref[...] = jnp.zeros_like(bias_ref)
        out_grad_ref[...] = jnp.zeros_like(out_grad_ref)
        stats = stat_refs[0][...]
        for other in stat_refs[1:]:
            stats = stats + other[...]
        local = cot_ref.shape[0]
        cls = cls_ref[...][:local]
        cot = cot_ref[...].astype(F32)
        mean = stats[0:1] / samples
        scale = lax.rsqrt(stats[1:2] / samples - mean * mean + CLS_EPS)
        hat = (cls - mean) * scale
        norm_ref[...] = hat.astype(BF)
        cross = scale * (stats[3:4] - mean * stats[2:3])
        dcls_ref[...] = jnp.zeros_like(dcls_ref)
        dcls_ref[:local, :] = scale * (cot - stats[2:3] / samples - hat * (cross / samples))

    place_halves(full_ref, core_ref[CORE], x_own_ref[0], x_far_ref[0])
    place_halves(g_ref, core_ref[CORE], own_ref[0].astype(F32), far_ref[0].astype(F32))
    g_ref[0:1, :] = g_ref[0:1, :] + dcls_ref[pl.ds(step, 1), :]
    g_mlp = g_ref[...].astype(BF)
    bias_ref[blocks : blocks + 1, :] += jnp.sum(g_mlp.astype(F32), 0, keepdims=True)

    branch = dot(att_ref[0], w_out_ref[...], 0, 0) + row_of(pack_ref, OUT_BIAS)
    middle = full_ref[...].astype(F32) + branch
    middle_ref[0] = middle
    hat, rstd = norm_parts(middle)
    normed = (hat * row_of(pack_ref, GAIN2) + row_of(pack_ref, SHIFT2)).astype(BF)
    hat_low = hat.astype(BF)
    for j in range(blocks):
        cols = slice(j * width, (j + 1) * width)
        pre = dot(normed, w1_ref[:, cols], 1, 0) + row_of(pack_ref, FC1_BIAS + j)
        d_act = dot(g_mlp, w2_ref[cols, :], 1, 1)
        cdf = gelu_cdf(pre)
        bell = jnp.exp2(pre * pre * (-0.5 * LOG2E) - 0.5 * math.log2(2.0 * math.pi))
        act_ref[0, :, cols] = (pre * cdf).astype(BF)
        d_pre = d_act * (cdf + pre * bell)
        bias_ref[j : j + 1, :] += jnp.sum(d_pre, 0, keepdims=True)
        dpre_ref[:, cols] = d_pre.astype(BF)
    acc1_ref[...] += dot(hat_low, dpre_ref[...], 0, 0)
    acc2_ref[...] += dot(act_ref[0], g_mlp, 0, 0)
    d_norm = dot(dpre_ref[...], w1_ref[...], 1, 1)
    u = d_norm * row_of(pack_ref, GAIN2)
    g_mid = g_ref[...] + rstd * (
        u - jnp.mean(u, -1, keepdims=True) - hat * jnp.mean(u * hat, -1, keepdims=True)
    )
    g_attn = g_mid.astype(BF)
    gmid_ref[0] = g_attn
    out_grad_ref[...] += dot(att_ref[0], g_attn, 1, 0)
    bias_ref[blocks + 1 : blocks + 2, :] += jnp.sum(g_attn.astype(F32), 0, keepdims=True)
    d_mix = dot(w_out_ref[...], g_attn, 1, 1)
    for h in range(width // HEAD_DIM):
        part = slice(h * HEAD_DIM, (h + 1) * HEAD_DIM)
        piece = d_mix[part] * (1.0 / sum_ref[0, h : h + 1, :])
        dmix_ref[0, part, :] = piece.astype(BF)
        inner_ref[0, h : h + 1, :] = jnp.sum(piece * att_ref[0, part, :].astype(F32), 0, keepdims=True)

    @pl.when(step == pl.num_programs(0) - 1)
    def _():
        flat_ref[:hidden, :] = acc2_ref[...].astype(BF)
        for j in range(blocks):
            rows = slice(hidden + j * width, hidden + (j + 1) * width)
            flat_ref[rows, :] = acc1_ref[:, j * width : (j + 1) * width].astype(BF)
        clear_rest(flat_ref, 2 * hidden)
        write_halves(core_ref[CORE], flat_ref, parts, kept_ref, sent_ref)


def output_kernel(core_ref, act_ref, middle_ref, w2_ref, pack_ref, own_ref, far_ref, full_ref):
    output = middle_ref[0] + dot(act_ref[0], w2_ref[...], 1, 0) + row_of(pack_ref, FC2_BIAS)
    full_ref[...] = output.astype(BF)
    split_halves(full_ref, core_ref[CORE], own_ref, far_ref)


def attention_back_kernel(
    core_ref, views_ref, plain_ref, order_ref, qkv_ref, top_ref, dmix_ref, inner_ref, hat_ref,
    *refs, turn, samples, parts
):
    last = turn == samples - 1
    if last:
        earlier = refs[:turn], refs[turn : 2 * turn]
        out_grad_ref, bias_ref = refs[2 * turn : 2 * turn + 2]
        dqkv_ref, kept_ref, sent_ref, pow_ref, flat_ref, vector_ref = refs[2 * turn + 2 :]
    else:
        dqkv_ref, grad_ref, sums_ref, pow_ref = refs
    pair = pl.program_id(0)
    sample = order_ref[turn]
    rows, width = hat_ref.shape[1:]
    views = views_ref[core_ref[CORE] * samples + sample]
    limit = 1 + VIEW_ROWS * views
    plain = plain_ref[sample] == 1
    both = range(2)
    lanes = [slice(k * HEAD_DIM, (k + 1) * HEAD_DIM) for k in both]

    def back(keys, powers_of):
        query = [qkv_ref[0, 0, part, :] for part in lanes]
        key = [qkv_ref[0, 1, part, :keys] for part in lanes]
        value = [qkv_ref[0, 2, part, :keys] for part in lanes]
        d_mix = [dmix_ref[0, part, :] for part in lanes]
        scores = [dot(key[k], query[k], 0, 0) for k in both]
        for k in both:
            powers_of(k, scores[k])
        d_weights = [dot(value[k], d_mix[k], 0, 0) for k in both]
        d_scores = []
        for k in both:
            inner = inner_ref[0, pl.ds(2 * pair + k, 1), :]
            powers = pow_ref[k, :keys, :].astype(F32)
            d_scores.append((powers * (d_weights[k] - inner)).astype(BF))
        for k in both:
            d_value = dot(d_mix[k], pow_ref[k, :keys, :], 1, 1)
            dqkv_ref[0, 2, lanes[k], :keys] = d_value.astype(BF)
        for k in both:
            d_query = dot(key[k], d_scores[k], 1, 0) * SCALE
            dqkv_ref[0, 0, lanes[k], :] = d_query.astype(BF)
            d_key = dot(query[k], d_scores[k], 1, 1) * LN2
            dqkv_ref[0, 1, lanes[k], :keys] = d_key.astype(BF)
        if keys < rows:
            blank = jnp.zeros((2 * HEAD_DIM, rows - keys), BF)
            dqkv_ref[0, 1, :, keys:] = blank
            dqkv_ref[0, 2, :, keys:] = blank

    for count, keys in key_counts(rows):

        @pl.when((views == count) & plain)
        def _(keys=keys):
            main = keys - 16

            def powers_of(k, scores):
                pow_ref[k, :main, :] = jnp.exp2(scores[:main]).astype(BF)
                tail = masked_tail(scores[main:], main, limit)
                pow_ref[k, main:keys, :] = jnp.exp2(tail).astype(BF)

            back(keys, powers_of)

    @pl.when(jnp.logical_not(plain))
    def _():
        def powers_of(k, scores):
            top = top_ref[0, pl.ds(2 * pair + k, 1), :]
            pow_ref[k] = jnp.exp2(masked_tail(scores, 0, limit) - top).astype(BF)

        back(rows, powers_of)

    right = jnp.concatenate((hat_ref[0], jnp.ones((rows, 128), BF)), 1)
    result = dot(dqkv_ref[0].reshape(3 * 2 * HEAD_DIM, rows), right, 1, 0)
    sums = result[:, width:].T[:8]
    if not last:
        grad_ref[...] = result[:, :width].astype(BF).reshape(grad_ref.shape)
        sums_ref[0] = sums
        return

    @pl.when(pair == 0)
    def _():
        vector_ref[0:8, :] = bias_ref[...]
        vector_ref[8:16, :] = jnp.zeros((8, width), F32)

    for ref in earlier[1]:
        sums = sums + ref[0]
    at = pl.multiple_of(pair * 128, 128)
    for t in range(3):
        own = slice(t * 128, (t + 1) * 128)
        total = result[own, :width]
        for ref in earlier[0]:
            total = total + ref[t].astype(F32)
        flat_ref[pl.ds(t * width + at, 128), :] = total.astype(BF)
        vector_ref[8 + t : 9 + t, pl.ds(at, 128)] = sums[0:1, own]

    @pl.when(pair == pl.num_programs(0) - 1)
    def _():
        flat_ref[3 * width : 4 * width, :] = out_grad_ref[...].astype(BF)
        clear_rest(flat_ref, 4 * width)
        write_halves(core_ref[CORE], flat_ref, parts, kept_ref, sent_ref)
        half = sum(parts) // 2
        kept_ref[half : half + EXTRA, :] = vector_ref[...].astype(BF)
        sent_ref[half : half + EXTRA, :] = vector_ref[...].astype(BF)


def tokens_back_kernel(core_ref, order_ref, *refs, sets):
    dqkv_refs = refs[:sets]
    w_ref, pack_ref, x_own_ref, x_far_ref, gmid_ref, own_ref, far_ref, out_ref, d_ref, sems = refs[sets:]
    step = pl.program_id(0)

    def fetch(k):
        return pltpu.make_async_copy(dqkv_refs[k].at[0], d_ref.at[k], sems.at[k])

    @pl.when(step == 0)
    def _():
        for k in range(sets):
            fetch(k).start()

    for k in range(sets):

        @pl.when(step == k)
        def _(k=k):
            fetch(k).wait()

    d_norm = dot(d_ref[step], w_ref[...], 0, 0)
    place_halves(out_ref, core_ref[CORE], x_own_ref[0], x_far_ref[0])
    hat, rstd = norm_parts(out_ref[...].astype(F32))
    w = d_norm * row_of(pack_ref, GAIN1)
    back = rstd * (w - jnp.mean(w, -1, keepdims=True) - hat * jnp.mean(w * hat, -1, keepdims=True))
    out_ref[...] = (gmid_ref[0].astype(F32) + back).astype(BF)
    split_halves(out_ref, core_ref[CORE], own_ref, far_ref)


def clear_rest(ref, used):
    if ref.shape[0] > used:
        ref[used:, :] = jnp.zeros((ref.shape[0] - used, ref.shape[1]), ref.dtype)


def write_halves(core, flat_ref, parts, kept_ref, sent_ref):
    start = at = 0
    for size in parts:
        half = size // 2
        mine = pl.multiple_of(start + core * half, 16)
        other = pl.multiple_of(start + (1 - core) * half, 16)
        kept_ref[at : at + half, :] = flat_ref[pl.ds(mine, half), :]
        sent_ref[at : at + half, :] = flat_ref[pl.ds(other, half), :]
        start += size
        at += half


def insert_rows(info, base, came):
    def body(info_ref, came_ref, base_ref, out_ref, mark_ref):
        out_ref[...] = came_ref[...]

    return pl.pallas_call(
        body,
        grid_spec=pltpu.PrefetchScalarGridSpec(
            num_scalar_prefetch=1,
            grid=(1,),
            in_specs=[
                pl.BlockSpec(came.shape, lambda *_: (0, 0, 0)), pl.BlockSpec(memory_space=pl.ANY),
            ],
            out_specs=[
                pl.BlockSpec(came.shape, lambda s, b: (1 - b[CORE], 0, 0)),
                pl.BlockSpec(memory_space=pl.ANY),
            ],
        ),
        out_shape=[jax.ShapeDtypeStruct(base.shape, base.dtype), jax.ShapeDtypeStruct((1,), jnp.int32)],
        input_output_aliases={2: 0},
        compiler_params=params(("arbitrary",)),
        name="insert",
    )(info, came, base)


def swap_cores(value):
    return lax.ppermute(value, "blk", [(0, 1), (1, 0)])


def stages(count, first=4):
    out = []
    stride = 1
    while stride < count:
        left = count // stride
        radix = first if not out and left % first == 0 else 4 if left % 4 == 0 else 2
        out.append((stride, radix))
        stride *= radix
    return out


def shifted(value, stage, steps, axis="samp"):
    stride, radix = stage
    count = lax.axis_size(axis)
    pairs = []
    for source in range(count):
        digit = (source // stride) % radix
        pairs.append((source, source + ((digit + steps) % radix - digit) * stride))
    return lax.ppermute(value, axis, pairs)


MARK = jax.ShapeDtypeStruct((1,), jnp.int32)


def small_call(kernel, args, outs, scratch=(), ties=(), name=None, through=()):
    n, t, o, m = len(args), len(ties), len(outs), len(through)

    def body(*refs):
        kernel(*refs[:n], *refs[n + t + m : n + t + m + o], *refs[n + t + 2 * m + o + 1 :])

    anywhere = pl.BlockSpec(memory_space=pl.ANY)
    vmem = pl.BlockSpec(memory_space=pltpu.VMEM)
    smem = pl.BlockSpec(memory_space=pltpu.SMEM)
    size = lambda a: math.prod(a.shape) * jnp.dtype(a.dtype).itemsize
    total = sum(size(a) for a in (*args[1:], *outs)) + sum(
        math.prod(a.shape) * jnp.dtype(a.dtype).itemsize for a in scratch
    )
    return pl.pallas_call(
        body,
        in_specs=[smem, *[vmem] * (n - 1), *[smem] * t, *[anywhere] * m],
        out_specs=[vmem] * o + [anywhere] * (m + 1),
        out_shape=[*outs, *[jax.ShapeDtypeStruct(a.shape, a.dtype) for a in through], MARK],
        input_output_aliases={n + t + k: o + k for k in range(m)},
        scratch_shapes=list(scratch),
        compiler_params=pltpu.CompilerParams(vmem_limit_bytes=2 * total + 4 * 2**20),
        name=name,
    )(*args, *ties, *through)


def spread_kernel(info_ref, *refs, count, radix, slot, extra, rows, rider, unload):
    inputs = count + (1 if rider else 0) + (1 if unload else 0)
    outputs = radix + (1 if extra and radix == 1 else 0)
    outs, total_ref = refs[inputs : inputs + outputs], refs[-1]
    if unload:
        collect_kernel(info_ref, refs[inputs - 1], *refs[1:count], refs[inputs + outputs])
    total = refs[0][:rows, :].astype(F32)
    for ref in refs[1:count]:
        total = total + ref[:rows, :].astype(F32)
    rows = rows - extra
    size = rows // radix
    total_ref[...] = total.astype(BF)
    if radix == 1:
        outs[0][...] = total_ref[:rows, :]
        if extra:
            outs[1][...] = total[rows:]
        return
    for k in range(radix):
        start = lax.rem(info_ref[slot] + k, radix) * size
        outs[k][:size, :] = total_ref[pl.ds(pl.multiple_of(start, 16), size), :]
        if extra:
            outs[k][size : size + extra, :] = total_ref[rows:, :]
        if rider and k > 0:
            outs[k][size + extra :, :] = refs[count][...]


def collect_kernel(info_ref, own_ref, *refs):
    out_ref = refs[-1]
    size = own_ref.shape[0]
    out_ref[:size, :] = own_ref[...]
    for k, ref in enumerate(refs[:-1]):
        out_ref[(k + 1) * size : (k + 2) * size, :] = ref[ref.shape[0] - size :, :]


class Layout:
    def __init__(self, count, sizes):
        self.base = stages(count)
        self.count = count
        table = np.zeros((2 * count, 1 + len(self.base)), np.int32)
        for device in range(2 * count):
            table[device, 0] = device % 2
            for i in range(len(self.base)):
                table[device, 1 + i] = self.digit(device, i)
        tables = [table]
        self.place = []
        for rows in sizes:
            self.place.append(sum(t.shape[1] for t in tables))
            tables.append(np.stack([self.places(device, rows) for device in range(2 * count)]))
        self.table = np.concatenate(tables, 1).astype(np.int32)

    def digit(self, device, index):
        stride, radix = self.base[index]
        return (device // 2 // stride) % radix

    def places(self, device, rows):
        core = device % 2
        unit = rows // 2
        offsets = np.array([core * unit, (1 - core) * unit])
        for index, (_, radix) in enumerate(self.base):
            unit //= radix
            digit = (self.digit(device, index) - np.arange(radix)) % radix
            offsets = (offsets[:, None] + (digit * unit)[None, :]).reshape(-1)
        return offsets


class Chain:
    def __init__(self, layout, info, extra=0):
        self.layout = layout
        self.info = info
        self.extra = extra
        self.rounds = len(layout.base)

    def start(self, kept, sent):
        self.pending = [kept, swap_cores(sent)]

    def scatter(self, level, ties=(), rider=None, unload=None):
        last = level == self.rounds
        radix = 1 if last else self.layout.base[level][1]
        rows, width = self.pending[0].shape
        size = (rows - self.extra) // radix
        more = () if rider is None else (rider.value,)
        kept = () if unload is None else (unload.value,)
        if last:
            outs = [jax.ShapeDtypeStruct((size, width), BF)]
            if self.extra:
                outs.append(jax.ShapeDtypeStruct((self.extra, width), F32))
        else:
            piece = size + self.extra
            sent = piece + sum(value.shape[0] for value in more)
            outs = [jax.ShapeDtypeStruct((sent if k else piece, width), BF) for k in range(radix)]
        if kept:
            outs.append(jax.ShapeDtypeStruct((len(self.pending) * kept[0].shape[0], width), BF))
        pieces = small_call(
            functools.partial(
                spread_kernel, count=len(self.pending), radix=radix, slot=1 + level, extra=self.extra,
                rows=rows, rider=bool(more), unload=bool(kept),
            ),
            (self.info, *self.pending, *more, *kept), outs, [pltpu.VMEM((rows, width), BF)], ties, "spread",
        )
        if kept:
            unload.value = pieces[-2]
        if last:
            self.value = pieces[0]
            self.vectors = pieces[1] if self.extra else None
        else:
            stage = self.layout.base[level]
            self.pending = [pieces[0]] + [shifted(pieces[k], stage, k) for k in range(1, radix)]
            if more:
                rider.pending = [rider.value, *self.pending[1:]]
        return pieces[-1]

    def gather(self, level):
        stage = self.layout.base[level]
        self.pending = [self.value] + [shifted(self.value, stage, k) for k in range(1, stage[1])]

    def collect(self, ties=(), through=()):
        size, width = self.pending[0].shape
        outs = [jax.ShapeDtypeStruct((len(self.pending) * size, width), BF)]
        self.value, *self.through, mark = small_call(
            collect_kernel, (self.info, *self.pending), outs, (), ties, "collect", through
        )
        return mark


def restore(place_ref, flat_ref, ref, unit, at):
    def body(i, carry):
        start = pl.multiple_of(place_ref[at + i], 16)
        source = pl.multiple_of(i * unit, 16)
        chunk = ref[pl.ds(source, unit), :]
        flat_ref[pl.ds(start, unit), :] = chunk
        return carry

    lax.fori_loop(0, ref.shape[0] // unit, body, 0)


def finish_mlp_kernel(
    info_ref, own_ref, far_ref, vectors_ref, pack_ref, w1_ref,
    fc2_ref, fc1_ref, gain_ref, shift_ref, fc1_bias_ref, fc2_bias_ref, flat_ref, *, unit, at
):
    restore(info_ref, flat_ref, own_ref, unit, at)
    restore(info_ref, flat_ref, far_ref, unit, at + own_ref.shape[0] // unit)
    hidden, width = fc2_ref.shape
    fc2_ref[...] = flat_ref[:hidden, :].astype(F32)
    columns = pack_ref[0:8, :].T
    gain = jnp.zeros((width, 1), F32)
    shift = jnp.zeros((width, 1), F32)
    for j in range(hidden // width):
        cols = slice(j * width, (j + 1) * width)
        hats = flat_ref[hidden + j * width : hidden + (j + 1) * width, :].astype(F32)
        sums = vectors_ref[j : j + 1, :]
        fc1_ref[:, cols] = hats * columns[:, GAIN2 : GAIN2 + 1] + columns[:, SHIFT2 : SHIFT2 + 1] * sums
        w = w1_ref[:, cols].astype(F32)
        gain = gain + jnp.sum(w * hats, -1, keepdims=True)
        shift = shift + jnp.sum(w * sums, -1, keepdims=True)
    lane = lax.broadcasted_iota(jnp.int32, (width, 128), 1)
    both = jnp.where(lane == 0, gain, jnp.where(lane == 1, shift, 0.0)).T[0:8]
    gain_ref[...] = both[0]
    shift_ref[...] = both[1]
    blocks = hidden // width
    for j in range(blocks):
        fc1_bias_ref[j * width : (j + 1) * width] = vectors_ref[j, :]
    fc2_bias_ref[...] = vectors_ref[blocks, :]


def finish_kernel(
    info_ref, own_ref, far_ref, vectors_ref, pack_ref, w_ref, qkv_ref, out_ref, gain_ref, shift_ref, qv_ref, out_bias_ref, flat_ref,
    *, unit, at, blocks
):
    restore(info_ref, flat_ref, own_ref, unit, at)
    restore(info_ref, flat_ref, far_ref, unit, at + own_ref.shape[0] // unit)
    width = out_ref.shape[0]
    columns = qkv_ref.shape[1]
    out_ref[...] = flat_ref[columns : columns + width, :].astype(F32)
    gain = jnp.zeros((1, width), F32)
    shift = jnp.zeros((1, width), F32)
    turned = vectors_ref[8:16, :].T
    for t in range(columns // width):
        part = slice(t * width, (t + 1) * width)
        hats = flat_ref[part, :].astype(F32)
        sums = turned[:, t : t + 1]
        result = hats * row_of(pack_ref, GAIN1) + sums * row_of(pack_ref, SHIFT1)
        qkv_ref[:, part] = result.T
        w = w_ref[part, :].astype(F32)
        gain = gain + jnp.sum(w * hats, 0, keepdims=True)
        shift = shift + jnp.sum(w * sums, 0, keepdims=True)
    gain_ref[...] = gain[0]
    shift_ref[...] = shift[0]
    qv_ref[:width] = vectors_ref[8, :]
    qv_ref[width:] = vectors_ref[10, :]
    out_bias_ref[...] = vectors_ref[blocks + 1, :]


def pad_rows(count, unit):
    return -(-count // unit) * unit


def per_device(
    tokens, view_count, norm1_gain, norm1_bias, w_qkv, qv_bias, w_out, out_bias,
    norm2_gain, norm2_bias, w_fc1, fc1_bias, w_fc2, fc2_bias, cot_tokens, cot_cls,
):
    core = lax.axis_index("blk")
    cores = lax.axis_size("blk")
    count = lax.axis_size("samp")
    samples, half, width = tokens.shape
    local = samples // cores
    rows = half * cores
    hidden = w_fc1.shape[1]
    blocks = hidden // width
    heads = width // HEAD_DIM
    pairs = heads // 2
    sds = jax.ShapeDtypeStruct

    unit = 32 * count
    parts1 = [pad_rows(2 * hidden, unit)]
    parts2 = [pad_rows(4 * width, unit)]
    layout = Layout(count, (parts1[0], parts2[0]))
    device = lax.axis_index("samp") * cores + core
    info = lax.dynamic_index_in_dim(jnp.asarray(layout.table), device, 0, keepdims=False)

    theirs = (1 - core) * local
    far_tokens = swap_cores(lax.dynamic_slice_in_dim(tokens, theirs, local, 0))
    far_cot = swap_cores(lax.dynamic_slice_in_dim(cot_tokens, theirs, local, 0))

    vmem = pl.BlockSpec(memory_space=pltpu.VMEM)
    half_spec = lambda f: pl.BlockSpec((1, half, width), f)
    own_map = lambda s, b, *_: (b[CORE] * local + s, 0, 0)
    by_sample = lambda s, *_: (s, 0, 0)
    rows_spec = pl.BlockSpec((1, rows, width), by_sample)
    turned_spec = pl.BlockSpec((1, width, rows), by_sample)
    rstd_spec = pl.BlockSpec((1, rows, 1), by_sample)
    hidden_spec = pl.BlockSpec((1, rows, hidden), by_sample)
    eight_spec = pl.BlockSpec((1, 8, rows), by_sample)

    def big_call(kernel, prefetch, args, in_specs, outs, out_specs, scratch=(), ties=(), grid=(local,), name=None):
        n, t, o = len(prefetch) + len(args), len(ties), len(outs)
        smem = pl.BlockSpec(memory_space=pltpu.SMEM)

        def body(*refs):
            kernel(*refs[:n], *refs[n + t : n + t + o], *refs[n + t + o + 1 :])

        return pl.pallas_call(
            body,
            grid_spec=pltpu.PrefetchScalarGridSpec(
                num_scalar_prefetch=len(prefetch),
                grid=grid,
                in_specs=[*in_specs, *[smem] * t],
                out_specs=[*out_specs, pl.BlockSpec(memory_space=pl.ANY)],
                scratch_shapes=list(scratch),
            ),
            out_shape=[*outs, MARK],
            compiler_params=params(("arbitrary",) * len(grid)),
            name=name,
        )(*prefetch, *args, *ties)

    hat1, qkv, cls_rows, stats, w_turned, order, pack, _ = big_call(
        project_kernel,
        (info, view_count),
        (
            tokens, far_tokens, w_qkv, w_out, w_fc1, w_fc2, cot_cls, norm1_gain, norm1_bias,
            norm2_gain, norm2_bias, out_bias, fc2_bias, qv_bias, fc1_bias,
        ),
        [half_spec(own_map), half_spec(by_sample), *[vmem] * 13],
        [
            sds((local, rows, width), BF),
            sds((local, 3 * width, rows), BF),
            sds((8, width), F32),
            sds((8, width), F32),
            sds((3 * width, width), BF),
            sds((local,), jnp.int32),
            sds((16, width), F32),
        ],
        [
            rows_spec, pl.BlockSpec((1, 3 * width, rows), by_sample), vmem, vmem, vmem,
            pl.BlockSpec(memory_space=pltpu.SMEM), vmem,
        ],
        [pltpu.VMEM((8, width), F32), pltpu.VMEM((8, width), F32), pltpu.VMEM((rows, width), BF)],
        name="project",
    )

    def add_kernel(info_ref, *refs):
        total = refs[0][...]
        for ref in refs[1:-1]:
            total = total + ref[...]
        refs[-1][...] = total

    *later, first = stages(count)

    def add_all(values, ties=()):
        return small_call(add_kernel, [info, *values], [sds((8, width), F32)], (), ties, "add")

    stats, tie = add_all([stats, swap_cores(stats)])
    stat_parts = [stats] + [shifted(stats, first, k) for k in range(1, first[1])]

    qkv_spec = lambda f: pl.BlockSpec((1, 3 * width, rows), f)
    totals, tops, plain, mixed, tie = big_call(
        attention_kernel,
        (info, view_count),
        (qkv,),
        [qkv_spec(by_sample)],
        [
            sds((local, 8, rows), F32),
            sds((local, 8, rows), F32),
            sds((local,), jnp.int32),
            sds((local, width, rows), BF),
        ],
        [eight_spec, eight_spec, pl.BlockSpec(memory_space=pltpu.SMEM), turned_spec],
        [pltpu.VMEM((2, rows, rows), BF)],
        (tie,),
        name="attention",
    )

    for stage in later:
        stats, tie = add_all(stat_parts, (tie,))
        stat_parts = [stats] + [shifted(stats, stage, k) for k in range(1, stage[1])]

    act, middle, g_mid, d_mix, inner, out_grad, cls_norm, biases, kept1, sent1, _ = big_call(
        functools.partial(
            layer_kernel, samples=local * cores * count, parts=parts1, peers=len(stat_parts)
        ),
        (info,),
        (
            tokens, far_tokens, cot_tokens, far_cot, mixed, totals, cls_rows, cot_cls, *stat_parts,
            w_out, w_fc1, w_fc2, pack,
        ),
        [
            half_spec(own_map), half_spec(by_sample), half_spec(own_map), half_spec(by_sample),
            turned_spec, eight_spec, vmem, vmem, *[vmem] * len(stat_parts), vmem, vmem, vmem, vmem,
        ],
        [
            sds((local, rows, hidden), BF),
            sds((local, rows, width), F32),
            sds((local, rows, width), BF),
            sds((local, width, rows), BF),
            sds((local, 8, rows), F32),
            sds((width, width), F32),
            sds((local, width), BF),
            sds((8, width), F32),
            sds((sum(parts1) // 2, width), BF),
            sds((sum(parts1) // 2, width), BF),
        ],
        [
            hidden_spec, rows_spec, rows_spec, turned_spec, eight_spec, vmem, vmem, vmem, vmem, vmem,
        ],
        [
            pltpu.VMEM((rows, width), BF),
            pltpu.VMEM((rows, width), F32),
            pltpu.VMEM((rows, hidden), BF),
            pltpu.VMEM((8, width), F32),
            pltpu.VMEM((hidden, width), F32),
            pltpu.VMEM((width, hidden), F32),
            pltpu.VMEM((sum(parts1), width), BF),
        ],
        name="layer",
    )
    chain1 = Chain(layout, info)
    chain1.start(kept1, sent1)

    def attention_back(turn, ties, grads, sums):
        place = lambda p, c, v, q, o: (o[turn], 0, 0)
        grad_spec = pl.BlockSpec((3, 128, width), lambda p, *_: (0, p, 0))
        sums_spec = pl.BlockSpec((1, 8, 384), lambda p, *_: (p, 0, 0))
        last = turn == local - 1
        half_rows = sum(parts2) // 2 + EXTRA
        more = [*grads, *sums, out_grad, biases] if last else []
        return big_call(
            functools.partial(attention_back_kernel, turn=turn, samples=local, parts=parts2),
            (info, view_count, plain, order),
            (qkv.reshape(local, 3, width, rows), tops, d_mix, inner, hat1, *more),
            [
                pl.BlockSpec((1, 3, 128, rows), lambda p, c, v, q, o: (o[turn], 0, p, 0)),
                pl.BlockSpec((1, 8, rows), place),
                pl.BlockSpec((1, 128, rows), lambda p, c, v, q, o: (o[turn], p, 0)),
                pl.BlockSpec((1, 8, rows), place),
                pl.BlockSpec((1, rows, width), place),
                *([grad_spec] * turn + [sums_spec] * turn + [vmem, vmem] if last else []),
            ],
            [
                sds((1, 3, width, rows), BF),
                *(
                    [sds((half_rows, width), BF)] * 2
                    if last
                    else [sds((3, width, width), BF), sds((pairs, 8, 384), F32)]
                ),
            ],
            [
                pl.BlockSpec((1, 3, 128, rows), lambda p, *_: (0, 0, p, 0)),
                *([vmem, vmem] if last else [grad_spec, sums_spec]),
            ],
            [
                pltpu.VMEM((2, rows, rows), BF),
                *([pltpu.VMEM((sum(parts2), width), BF), pltpu.VMEM((16, width), F32)] if last else []),
            ],
            ties,
            grid=(pairs,),
            name="attention_back",
        )

    def scatter_step(level):
        def run(ties):
            piece = chain1.scatter(level, ties)
            if level == chain1.rounds:
                chain1.gather(level - 1)
            return piece

        return run

    def collect_step(level):
        def run(ties, through=()):
            mark = chain1.collect(ties, through)
            if level > 1:
                chain1.gather(level - 1)
            return mark

        return run

    steps = [scatter_step(level) for level in range(1, chain1.rounds + 1)]
    steps += [collect_step(level) for level in reversed(range(1, chain1.rounds))]
    ties = (chain1.scatter(0),)
    d_parts, grads, sums = [], [], []
    chain2 = Chain(layout, info, EXTRA)
    for sample in range(local):
        d_part, grad, total, tie = attention_back(sample, ties, grads, sums)
        d_parts.append(d_part.reshape(1, 3 * width, rows))
        if sample == local - 1:
            if chain1.rounds == sample:
                ties = (steps.pop(0)((tie,), (total,)),)
                total = chain1.through[0]
            chain2.start(grad, total)
            break
        grads.append(grad)
        sums.append(total)
        if steps:
            ties = (steps.pop(0)((tie,)),)
    while steps:
        ties = (steps.pop(0)(()),)
    tie = chain2.scatter(0, (), chain1)

    own_turn = lambda s, c, o: (c[CORE] * local + o[s], 0, 0)
    turn = lambda s, c, o: (o[s], 0, 0)
    grad_own, grad_far, tie = big_call(
        functools.partial(tokens_back_kernel, sets=len(d_parts)),
        (info, order),
        (*d_parts, w_turned, pack, tokens, far_tokens, g_mid),
        [
            *[pl.BlockSpec(memory_space=pl.ANY)] * len(d_parts),
            vmem, vmem, half_spec(own_turn), half_spec(turn), pl.BlockSpec((1, rows, width), turn),
        ],
        [sds((samples, half, width), BF), sds((local, half, width), BF)],
        [half_spec(own_turn), half_spec(turn)],
        [
            pltpu.VMEM((rows, width), BF),
            pltpu.VMEM((len(d_parts), 3 * width, rows), BF),
            pltpu.SemaphoreType.DMA((len(d_parts),)),
        ],
        (tie,),
        name="tokens_back",
    )
    tokens_out_own, out_far, out_tie = big_call(
        output_kernel,
        (info,),
        (act, middle, w_fc2, pack),
        [hidden_spec, rows_spec, vmem, vmem],
        [sds((samples, half, width), BF), sds((local, half, width), BF)],
        [half_spec(own_map), half_spec(by_sample)],
        [pltpu.VMEM((rows, width), BF)],
        (tie,),
        name="output",
    )
    grad_came = swap_cores(grad_far)
    for level in range(1, chain2.rounds + 1):
        first = level == 1
        tie = chain2.scatter(level, (out_tie,) if first else (), None, chain1 if first else None)
        if first:
            other1 = swap_cores(chain1.value)
    ties = ()
    for level in reversed(range(chain2.rounds)):
        chain2.gather(level)
        if level == chain2.rounds - 1:
            (
                grad_w_fc2, grad_w_fc1, grad_gain2, grad_shift2, grad_fc1_bias, grad_fc2_bias, tie,
            ) = small_call(
                functools.partial(
                    finish_mlp_kernel, unit=parts1[0] // (2 * count), at=layout.place[0]
                ),
                (info, chain1.value, other1, chain2.vectors, pack, w_fc1),
                [
                    sds((hidden, width), F32), sds((width, hidden), F32), sds((width,), F32),
                    sds((width,), F32), sds((hidden,), F32), sds((width,), F32),
                ],
                [pltpu.VMEM((parts1[0], width), BF)],
                name="finish_mlp",
            )
            ties = (tie,)
        if level == 0:
            grad_tokens, tie = insert_rows(info, grad_own, grad_came)
            ties = (tie,)
        chain2.collect(ties, (out_far,) if level == chain2.rounds - 1 else ())
        if level == chain2.rounds - 1:
            out_came = swap_cores(chain2.through[0])
    other = swap_cores(chain2.value)
    tokens_out, out_tie = insert_rows(info, tokens_out_own, out_came)

    grad_w_qkv, grad_w_out, grad_gain1, grad_shift1, grad_qv_bias, grad_out_bias, _ = small_call(
        functools.partial(finish_kernel, unit=parts2[0] // (2 * count), at=layout.place[1], blocks=blocks),
        (info, chain2.value, other, chain2.vectors, pack, w_turned),
        [
            sds((width, 3 * width), F32), sds((width, width), F32), sds((width,), F32), sds((width,), F32),
            sds((2 * width,), F32), sds((width,), F32),
        ],
        [pltpu.VMEM((parts2[0], width), BF)],
        (out_tie,),
        name="finish",
    )
    return (
        tokens_out, cls_norm, grad_tokens, grad_gain1, grad_shift1, grad_w_qkv, grad_qv_bias,
        grad_w_out, grad_out_bias, grad_gain2, grad_shift2, grad_w_fc1, grad_fc1_bias,
        grad_w_fc2, grad_fc2_bias,
    )


def solution(mesh):
    split = P("samp", "blk", None)
    classes = P(("samp", "blk"), None)
    return jax.shard_map(
        per_device,
        mesh=mesh,
        in_specs=(split, P("samp"), *([P()] * 12), split, classes),
        out_specs=(split, classes, split, *([P()] * 12)),
        check_vma=False,
    )
```
